32 devices in a mesh: seq: 8 (over y, x, core), fsdp: 4 (over z).
Axes of the slice: x: 2, y: 2, z: 4, core: 2. Of those that a mesh axis runs over, the one named last changes fastest.
Arguments:
- tokens: bfloat16 [4, 2048, 1024], P('fsdp', 'seq'), may hold values from -6 to 6
- norm1_gain: bfloat16 [1024], P(('seq', 'fsdp')), may hold values from 0.5 to 1.5
- qkv_weight: bfloat16 [1024, 3072], P(('seq', 'fsdp')), may hold values from -0.1875 to 0.1875
- gate_weight: bfloat16 [1024, 48], P(('seq', 'fsdp')), may hold values from -0.1875 to 0.1875
- conv_weight: bfloat16 [4, 3072], P(None, ('seq', 'fsdp')), may hold values from -2.5 to 2.5
- memory_w1: bfloat16 [16, 64, 256], P(None, None, ('seq', 'fsdp')), may hold values from -0.75 to 0.75
- memory_w2: bfloat16 [16, 256, 64], P(None, ('seq', 'fsdp')), may hold values from -0.375 to 0.375
- persistent_keys: bfloat16 [16, 1024], P(None, ('seq', 'fsdp')), may hold values from -9 to 9
- persistent_values: bfloat16 [16, 1024], P(None, ('seq', 'fsdp')), may hold values from -6 to 6
- out_weight: bfloat16 [1024, 1024], P(('seq', 'fsdp')), may hold values from -0.5 to 0.5
- norm2_gain: bfloat16 [1024], P(('seq', 'fsdp')), may hold values from 0.5 to 1.5
- ffn_gate: bfloat16 [1024, 4096], P('seq', 'fsdp'), may hold values from -0.1875 to 0.1875
- ffn_up: bfloat16 [1024, 4096], P('seq', 'fsdp'), may hold values from -0.1875 to 0.1875
- ffn_down: bfloat16 [4096, 1024], P('fsdp', 'seq'), may hold values from -0.09375 to 0.09375
- gate_bias: float32 [3, 16], replicated, may hold values from -1.5 to 1.5
- doc_lengths: int32 [4, 4], P('fsdp'), may hold values from 1 to 2045, as said below
- live_mask: int32 [4, 2048], P('fsdp', 'seq'), may hold values 0 or 1
- cotangent: bfloat16 [4, 2048, 1024], P('fsdp', 'seq'), may hold values from -6 to 6
Outputs:
- output: bfloat16 [4, 2048, 1024], P('fsdp', 'seq')
- input_grad: float32 [4, 2048, 1024], P('fsdp', 'seq')
- grad_norm1_gain: float32 [1024], P(('seq', 'fsdp'))
- grad_qkv_weight: float32 [1024, 3072], P(('seq', 'fsdp'))
- grad_gate_weight: float32 [1024, 48], P(('seq', 'fsdp'))
- grad_conv_weight: float32 [4, 3072], P(None, ('seq', 'fsdp'))
- grad_memory_w1: float32 [16, 64, 256], P(None, None, ('seq', 'fsdp'))
- grad_memory_w2: float32 [16, 256, 64], P(None, ('seq', 'fsdp'))
- grad_persistent_keys: float32 [16, 1024], P(None, ('seq', 'fsdp'))
- grad_persistent_values: float32 [16, 1024], P(None, ('seq', 'fsdp'))
- grad_out_weight: float32 [1024, 1024], P(('seq', 'fsdp'))
- grad_norm2_gain: float32 [1024], P(('seq', 'fsdp'))
- grad_ffn_gate: float32 [1024, 4096], P('seq', 'fsdp')
- grad_ffn_up: float32 [1024, 4096], P('seq', 'fsdp')
- grad_ffn_down: float32 [4096, 1024], P('fsdp', 'seq')
- grad_gate_bias: float32 [3, 16], replicated
The draws below stay inside these ranges and needn't reach their ends.
Inputs may be any that keep to these rules, and one draw needn't show every extreme that they name: `doc_lengths`: each row's 4 lengths sum to 2048; one document of each row, at a place drawn from the seed, spans all but fewer than 256 of its positions, and every other holds at most 64; in every row the document after the long one (cyclically) holds 1, and in one row all others hold 1.
All inputs are finite; a program needn't handle non-finite values. No bound on the sum of `live_mask` on one device may be relied on, other than what follows from the above.
Results may differ from the reference program's by a relative error of at most 0.023.
Values may be sent and summed in bfloat16 or wider, within the bound.
A program may use at most 512 MiB of HBM per device.

```python
import jax
import jax.numpy as jnp
from jax import lax

HEAD_COUNT = 16
HEAD_SIZE = 64
D = 1024
FF = 4096
MH = 256
P_SIZE = 16
SEG = 256
NDOC = 4
ROWS = 4
ROW_LEN = 2048


def draw_doc_lengths(key, part):
    key = jax.random.fold_in(key, 11)
    short_key, place_key, row_key = jax.random.split(key, 3)
    short_rows = jax.random.randint(short_key, (ROWS, NDOC), 1, SEG // 4 + 1)
    longest = jax.random.randint(place_key, (ROWS, 1), 0, NDOC)
    unit_row = jax.random.randint(row_key, (1, 1), 0, ROWS)
    columns = jnp.arange(NDOC)[None, :]
    chosen = columns == longest
    after_long = columns == (longest + 1) % NDOC
    all_unit = jnp.arange(ROWS)[:, None] == unit_row
    short_rows = jnp.where(after_long | all_unit, 1, short_rows)
    others = jnp.sum(jnp.where(chosen, 0, short_rows), axis=1, keepdims=True)
    return jnp.where(chosen, ROW_LEN - others, short_rows).astype(jnp.int32)


def with_ends(values, own_key, least, high):
    shape = values.shape
    index_at = [jax.random.randint(jax.random.fold_in(own_key, axis), (), 0, shape[axis]) for axis in range(len(shape))]
    values = values.at[tuple(index_at)].set(least)
    longest = shape.index(max(shape))
    index_at[longest] = (index_at[longest] + 1) % shape[longest]
    return values.at[tuple(index_at)].set(high)


def shard_levels(stream_key, shape, pieces, low, largest):
    level = 1.0
    for position, shards_of in pieces:
        heights = jax.random.uniform(jax.random.fold_in(jax.random.fold_in(stream_key, 6), position), (shards_of,), jnp.float32, low / len(pieces), largest / len(pieces))
        level = level * jnp.repeat(jnp.exp(heights), shape[position] // shards_of).reshape((-1,) + (1,) * (len(shape) - 1 - position))
    return level


def noise(key, extent, scale, bound, cuts=(), kind=jnp.bfloat16):
    array = scale * jax.random.normal(key, extent, jnp.float32)
    if cuts:
        array = array * shard_levels(key, extent, cuts, -0.22, 0.18)
    return jnp.clip(array, -bound, bound).astype(kind)


def setup_inputs(seed: int = 0) -> dict:
    key_of = jax.random.split(jax.random.key(seed), 19)
    tokens = noise(key_of[0], (ROWS, ROW_LEN, D), 1.0, 6.0, ((0, 4), (1, 8)))
    norm1_gain = jnp.clip(1.0 + 0.1 * jax.random.normal(key_of[1], (D,), jnp.float32), 0.5, 1.5).astype(jnp.bfloat16)
    qkv_weight = noise(key_of[2], (D, 3 * D), D ** -0.5, 0.1875, ((0, 32),))
    gate_weight = noise(key_of[3], (D, 3 * HEAD_COUNT), D ** -0.5, 0.1875, ((0, 32),))
    conv_weight = noise(key_of[4], (4, 3 * D), 0.5, 2.5, ((1, 32),))
    memory_w1 = noise(key_of[5], (HEAD_COUNT, HEAD_SIZE, MH), HEAD_SIZE ** -0.5, 0.75, ((2, 32),))
    memory_w2 = noise(key_of[6], (HEAD_COUNT, MH, HEAD_SIZE), MH ** -0.5, 0.375, ((1, 32),))
    persistent_keys = noise(key_of[7], (P_SIZE, D), 1.5, 9.0, ((1, 32),))
    persistent_values = noise(key_of[8], (P_SIZE, D), 1.0, 6.0, ((1, 32),))
    out_weight = noise(key_of[9], (D, D), (D // 8) ** -0.5, 0.5, ((0, 32),))
    norm2_gain = jnp.clip(1.0 + 0.1 * jax.random.normal(key_of[10], (D,), jnp.float32), 0.5, 1.5).astype(jnp.bfloat16)
    ffn_gate = noise(key_of[11], (D, FF), D ** -0.5, 0.1875, ((0, 8), (1, 4)))
    ffn_up = noise(key_of[12], (D, FF), D ** -0.5, 0.1875, ((0, 8), (1, 4)))
    ffn_down = noise(key_of[13], (FF, D), FF ** -0.5, 0.09375, ((0, 4), (1, 8)))
    gate_bias = jnp.clip(jax.random.uniform(key_of[14], (3, HEAD_COUNT), jnp.float32, -1.5, 1.5), -1.5, 1.5)
    doc_lengths = draw_doc_lengths(jax.random.fold_in(key_of[18], 71), 0)
    live_mask = with_ends((jax.random.randint(key_of[16], (ROWS, ROW_LEN), 0, 8) < 7).astype(jnp.int32), jax.random.fold_in(key_of[16], 1), 0, 1)
    cotangent = noise(key_of[17], (ROWS, ROW_LEN, D), 1.0, 6.0, ((0, 4), (1, 8)))
    return {"tokens": tokens, "norm1_gain": norm1_gain, "qkv_weight": qkv_weight, "gate_weight": gate_weight, "conv_weight": conv_weight, "memory_w1": memory_w1, "memory_w2": memory_w2, "persistent_keys": persistent_keys, "persistent_values": persistent_values, "out_weight": out_weight, "norm2_gain": norm2_gain, "ffn_gate": ffn_gate, "ffn_up": ffn_up, "ffn_down": ffn_down, "gate_bias": gate_bias, "doc_lengths": doc_lengths, "live_mask": live_mask, "cotangent": cotangent}


EXACT_PRECISION = lax.Precision.HIGHEST
NORM_EPS = 1e-05
UNIT_EPS = 1e-06
SCORE_SCALE = 8.0
MEMORY_SCALE = 8.0
THETA_SCALE = 0.0005
MASKED = -1000000000.0

@jax.custom_vjp
def low(v):
    return lax.optimization_barrier(v.astype(jnp.bfloat16)).astype(jnp.float32)

@jax.custom_vjp
def low_back(v):
    return v

def low_keep(v):
    return (low(v), None)

def low_pass(kept, grad):
    return (grad,)

def back_keep(v):
    return (v, None)

def back_low(kept, grad):
    return (low(grad),)
low.defvjp(low_keep, low_pass)
low_back.defvjp(back_keep, back_low)

def dense_product(left_rows, right_rows):
    return jnp.dot(left_rows, right_rows, precision=EXACT_PRECISION)

def rms_scale(values, gain_row):
    return values * lax.rsqrt(lax.optimization_barrier(jnp.mean(values * values, axis=-1, keepdims=True)) + NORM_EPS) * gain_row

def unit_heads(values):
    shaped = values.reshape(values.shape[0], HEAD_COUNT, HEAD_SIZE)
    shaped = shaped * lax.rsqrt(lax.optimization_barrier(jnp.sum(shaped * shaped, axis=-1, keepdims=True)) + UNIT_EPS)
    return shaped.reshape(values.shape[0], HEAD_COUNT * HEAD_SIZE)

def swish_derivative(values):
    sigmoid_rows = jax.nn.sigmoid(values)
    return sigmoid_rows * (1.0 + values * (1.0 - sigmoid_rows))

def doc_table(lengths, positions):
    starts = (jnp.cumsum(lengths) - lengths).astype(jnp.int32)
    inside = starts[None, :] <= positions[:, None]
    doc_number = (lax.optimization_barrier(jnp.sum(inside.astype(jnp.int32), axis=1)) - 1).astype(jnp.int32)
    doc_begin = lax.optimization_barrier(jnp.max(jnp.where(inside, starts[None, :], -1), axis=1)).astype(jnp.int32)
    return (doc_number, doc_begin)

def same_table(ext_number, doc_number):
    length = doc_number.shape[0]
    return jnp.stack([(ext_number[3 - offset:3 - offset + length] == doc_number).astype(jnp.float32) for offset in range(4)])

def gate_values(gate_input, gate_shift):
    forget_rate = jax.nn.sigmoid(gate_input[:, :HEAD_COUNT] + 3.0 * gate_shift[0] - 7.5)
    momentum_rate = jax.nn.sigmoid(gate_input[:, HEAD_COUNT:2 * HEAD_COUNT] + gate_shift[1] + 1.5)
    step_size = THETA_SCALE * jax.nn.sigmoid(gate_input[:, 2 * HEAD_COUNT:] + gate_shift[2])
    return (forget_rate, momentum_rate, step_size)

def compose_pairs(later_pair, earlier_pair):
    return (later_pair[0] * earlier_pair[0], later_pair[1] * earlier_pair[0] + later_pair[2] * earlier_pair[1], later_pair[2] * earlier_pair[2])

def transition(key_rows, value_rows, gate_input, gate_shift, first_layer, layer_second_output, live_rows, fresh_rows):
    forget_rate, momentum_rate, step_size = gate_values(gate_input, gate_shift)
    element_count = key_rows.shape[0]
    key_heads = key_rows.reshape(element_count, HEAD_COUNT, HEAD_SIZE)
    value_head_split = value_rows.reshape(element_count, HEAD_COUNT, HEAD_SIZE)
    inner_hidden_rows = jnp.einsum('thd,hdm->thm', key_heads, first_layer, precision=EXACT_PRECISION)
    hidden_activation = jax.nn.silu(inner_hidden_rows)
    residual_error_rows = jnp.einsum('fwq,wqz->fwz', hidden_activation, layer_second_output, precision=EXACT_PRECISION) - value_head_split
    derivative_rows = jnp.einsum('zkx,ksx->zks', residual_error_rows, layer_second_output, precision=EXACT_PRECISION) * swish_derivative(inner_hidden_rows)
    keeping = 1.0 - fresh_rows[:, None]
    carry_gate = keeping * momentum_rate
    fade_gate = keeping * (1.0 - forget_rate)
    flipped = (jnp.flip(carry_gate, 0), jnp.flip(carry_gate, 0), jnp.flip(fade_gate, 0))
    inclusive = lax.associative_scan(compose_pairs, flipped)
    inclusive = tuple((jnp.flip(member, 0) for member in inclusive))
    ones_row = jnp.ones((1, HEAD_COUNT), jnp.float32)
    zeros_row = jnp.zeros((1, HEAD_COUNT), jnp.float32)
    after_keep = jnp.concatenate([inclusive[0][1:], ones_row], axis=0)
    after_mix = jnp.concatenate([inclusive[1][1:], zeros_row], axis=0)
    after_fade = jnp.concatenate([inclusive[2][1:], ones_row], axis=0)
    written = -step_size * live_rows[:, None]
    state_weight_matrix = written * after_keep
    memory_weight_matrix = written * (after_mix + after_fade)
    add_s1 = jnp.einsum('thd,thm->hdm', state_weight_matrix[:, :, None] * key_heads, derivative_rows, precision=EXACT_PRECISION)
    increment_second_state = jnp.einsum('aig,ais->igs', state_weight_matrix[:, :, None] * hidden_activation, residual_error_rows, precision=EXACT_PRECISION)
    add_w1 = jnp.einsum('thd,thm->hdm', memory_weight_matrix[:, :, None] * key_heads, derivative_rows, precision=EXACT_PRECISION)
    increment_second_weight = jnp.einsum('aig,ais->igs', memory_weight_matrix[:, :, None] * hidden_activation, residual_error_rows, precision=EXACT_PRECISION)
    return (inclusive[0][0], inclusive[2][0], inclusive[1][0], add_s1, increment_second_state, add_w1, increment_second_weight)

def recall(queries, first_layer, layer_second_output):
    element_count = queries.shape[0]
    query_heads = queries.reshape(element_count, HEAD_COUNT, HEAD_SIZE)
    hidden_activation = jax.nn.silu(jnp.einsum('thd,hdm->thm', query_heads, first_layer, precision=EXACT_PRECISION))
    return jnp.einsum('fwq,wqz->fwz', hidden_activation, layer_second_output, precision=EXACT_PRECISION).reshape(element_count, HEAD_COUNT * HEAD_SIZE)

def memory_read(queries, first_layer, layer_second_output, state_first, state_second, older):
    carried = recall(queries, first_layer + state_first, layer_second_output + state_second)
    initial = recall(queries, first_layer, layer_second_output)
    return older[:, None] * carried + (1.0 - older[:, None]) * initial

def conv_mix(extended, conv_taps, same_doc):
    length = extended.shape[0] - 3
    summed = jnp.zeros((length, extended.shape[1]), jnp.float32)
    for offset in range(4):
        summed = summed + conv_taps[offset] * extended[3 - offset:3 - offset + length] * same_doc[offset][:, None]
    return summed

def attend(queries, key_rows, value_rows, persist_keys, persist_values, visible):
    query_heads = queries.reshape(SEG, HEAD_COUNT, HEAD_SIZE)
    key_heads = key_rows.reshape(2 * SEG, HEAD_COUNT, HEAD_SIZE)
    value_head_split = value_rows.reshape(2 * SEG, HEAD_COUNT, HEAD_SIZE)
    pkey_heads = persist_keys.reshape(P_SIZE, HEAD_COUNT, HEAD_SIZE)
    pvalue_heads = persist_values.reshape(P_SIZE, HEAD_COUNT, HEAD_SIZE)
    fixed = jnp.einsum('qhd,phd->hqp', query_heads, pkey_heads, precision=EXACT_PRECISION)
    window = SCORE_SCALE * jnp.einsum('qhd,khd->hqk', query_heads, key_heads, precision=EXACT_PRECISION)
    scores = low_back(jnp.concatenate([fixed, window], axis=-1))
    scores = jnp.concatenate([scores[..., :P_SIZE], jnp.where(visible[None], scores[..., P_SIZE:], MASKED)], axis=-1)
    highest = lax.optimization_barrier(jnp.max(scores, axis=-1, keepdims=True))
    weights = jnp.exp(scores - highest)
    weights = low(weights / lax.optimization_barrier(jnp.sum(weights, axis=-1, keepdims=True)))
    merged = jnp.einsum('hqp,phd->qhd', weights[..., :P_SIZE], pvalue_heads, precision=EXACT_PRECISION)
    merged = merged + jnp.einsum('hqk,khd->qhd', weights[..., P_SIZE:], value_head_split, precision=EXACT_PRECISION)
    return merged.reshape(SEG, HEAD_COUNT * HEAD_SIZE)

def layer_block(tokens_block, live_block, lengths, number, state, params):
    gain_one, qkv_matrix, gate_matrix, conv_taps, memory_first, memory_second, persist_keys, persist_values, out_matrix, gain_two, up_gate, up_matrix, down_matrix, gate_shift = params
    state_s1, state_s2, state_w1, state_w2, prev_rows, prev_keys, prev_values, prev_live = state
    width = HEAD_COUNT * HEAD_SIZE
    block_start = number * SEG
    positions = block_start + jnp.arange(SEG, dtype=jnp.int32)
    doc_number, doc_begin = doc_table(lengths, positions)
    prev_number = doc_table(lengths, positions - SEG)[0]
    normed = low(rms_scale(tokens_block, gain_one))
    raw_rows = low(low_back(dense_product(normed, qkv_matrix)))
    gate_input = dense_product(normed, gate_matrix)
    extended = jnp.concatenate([prev_rows, raw_rows], axis=0)
    same_doc = same_table(jnp.concatenate([prev_number[SEG - 3:], doc_number]), doc_number)
    mixed_rows = conv_mix(extended, conv_taps, same_doc)
    query_unit = unit_heads(mixed_rows[:, :width])
    key_unit = unit_heads(mixed_rows[:, width:2 * width])
    value_rows = mixed_rows[:, 2 * width:]
    query_att = low(query_unit)
    key_att = low(key_unit)
    value_att = low(value_rows)
    live_rows = live_block.astype(jnp.float32)
    fresh_rows = (doc_begin == positions).astype(jnp.float32)
    older = (doc_begin < block_start).astype(jnp.float32)
    change = transition(MEMORY_SCALE * key_unit, value_rows, gate_input, gate_shift, memory_first, memory_second, live_rows, fresh_rows)
    recalled = memory_read(MEMORY_SCALE * query_unit, memory_first, memory_second, state_w1, state_w2, older)
    key_positions = jnp.concatenate([positions - SEG, positions])
    key_number = jnp.concatenate([prev_number, doc_number])
    key_live = jnp.concatenate([prev_live, live_rows])
    distance = positions[:, None] - key_positions[None, :]
    visible = (key_number[None, :] == doc_number[:, None]) & (key_live[None, :] > 0.5) & (distance >= 0) & (distance < SEG)
    attended = attend(query_att, jnp.concatenate([prev_keys, key_att]), jnp.concatenate([prev_values, value_att]), persist_keys, persist_values, visible)
    combined = low(low_back(attended + recalled))
    middle = tokens_block + low_back(dense_product(combined, out_matrix))
    normed_two = low(rms_scale(middle, gain_two))
    gate_rows = low_back(dense_product(normed_two, up_gate))
    up_rows = low_back(dense_product(normed_two, up_matrix))
    hidden = low(jax.nn.silu(gate_rows) * up_rows)
    output = middle + dense_product(hidden, down_matrix)
    keep_factor = change[0][:, None, None]
    fade_factor = change[1][:, None, None]
    mix_factor = change[2][:, None, None]
    next_state = (keep_factor * state_s1 + change[3], keep_factor * state_s2 + change[4], fade_factor * state_w1 + mix_factor * state_s1 + change[5], fade_factor * state_w2 + mix_factor * state_s2 + change[6], raw_rows[SEG - 3:], key_att, value_att, live_rows)
    return (output, next_state)

def reference(tokens, norm1_gain, qkv_weight, gate_weight, conv_weight, memory_w1, memory_w2, persistent_keys, persistent_values, out_weight, norm2_gain, ffn_gate, ffn_up, ffn_down, gate_bias, doc_lengths, live_mask, cotangent):
    blocks = ROW_LEN // SEG
    floats = tuple((member.astype(jnp.float32) for member in (norm1_gain, qkv_weight, gate_weight, conv_weight, memory_w1, memory_w2, persistent_keys, persistent_values, out_weight, norm2_gain, ffn_gate, ffn_up, ffn_down, gate_bias)))

    def whole_layer(inputs, *params):

        def block_step(state, number):
            tokens_block = lax.dynamic_slice_in_dim(inputs, number * SEG, SEG, 1)
            live_block = lax.dynamic_slice_in_dim(live_mask, number * SEG, SEG, 1)
            row_batch = jax.vmap(layer_block, in_axes=(0, 0, 0, None, 0, None))
            output, next_state = row_batch(tokens_block, live_block, doc_lengths, number, state, params)
            return (next_state, output)
        start_state = (jnp.zeros((ROWS, HEAD_COUNT, HEAD_SIZE, MH), jnp.float32), jnp.zeros((ROWS, HEAD_COUNT, MH, HEAD_SIZE), jnp.float32), jnp.zeros((ROWS, HEAD_COUNT, HEAD_SIZE, MH), jnp.float32), jnp.zeros((ROWS, HEAD_COUNT, MH, HEAD_SIZE), jnp.float32), jnp.zeros((ROWS, 3, 3 * HEAD_COUNT * HEAD_SIZE), jnp.float32), jnp.zeros((ROWS, SEG, HEAD_COUNT * HEAD_SIZE), jnp.float32), jnp.zeros((ROWS, SEG, HEAD_COUNT * HEAD_SIZE), jnp.float32), jnp.zeros((ROWS, SEG), jnp.float32))
        final_state, outputs = lax.scan(jax.checkpoint(block_step), start_state, jnp.arange(blocks, dtype=jnp.int32))
        return jnp.moveaxis(outputs, 0, 1).reshape(ROWS, ROW_LEN, HEAD_COUNT * HEAD_SIZE)
    result, pullback = jax.vjp(whole_layer, tokens.astype(jnp.float32), *floats)
    gradients = pullback(cotangent.astype(jnp.float32))
    return (result.astype(jnp.bfloat16), gradients[0], gradients[1], gradients[2], gradients[3], gradients[4], gradients[5], gradients[6], gradients[7], gradients[8], gradients[9], gradients[10], gradients[11], gradients[12], gradients[13], gradients[14])
```

```python
from functools import partial

import jax
import jax.numpy as jnp
from jax import lax
from jax.experimental import pallas as pl
from jax.experimental.pallas import tpu as pltpu
from jax.sharding import PartitionSpec as P

HEAD_COUNT = 16
HEAD_SIZE = 64
D = 1024
MH = 256
P_SIZE = 16
SEG = 256
LANES = 128

NORM_EPS = 1e-05
UNIT_EPS = 1e-06
SCORE_SCALE = 8.0
MEMORY_SCALE = 8.0
THETA_SCALE = 0.0005
MASKED = -1000000000.0
VMEM_GRANT = 56 * 1024 * 1024
MESH = pl.DeviceIdType.MESH

f32 = jnp.float32
bf16 = jnp.bfloat16


def dot_nt(left, right):
    return lax.dot_general(left, right, (((1,), (1,)), ((), ())), preferred_element_type=f32)


def dot_nn(left, right):
    return lax.dot_general(left, right, (((1,), (0,)), ((), ())), preferred_element_type=f32)


def dot_tn(left, right):
    return lax.dot_general(left, right, (((0,), (0,)), ((), ())), preferred_element_type=f32)


def lane_index(shape):
    return lax.broadcasted_iota(jnp.int32, shape, 1)


def to_low(rows, head):
    return rows if head == 0 else pltpu.roll(rows, HEAD_SIZE, 1)


def swap_halves(rows):
    return pltpu.roll(rows, HEAD_SIZE, 1)


def lane_sum(rows):
    return jnp.sum(rows, axis=1, keepdims=True)


def unit_pair(rows, low):
    squares = rows * rows
    first = lane_sum(jnp.where(low, squares, 0.0))
    second = lane_sum(jnp.where(low, 0.0, squares))
    inverse = jnp.where(low, lax.rsqrt(first + UNIT_EPS), lax.rsqrt(second + UNIT_EPS))
    return rows * inverse, inverse


def unit_pair_pull(unit, inverse, grad, low):
    along = unit * grad
    first = lane_sum(jnp.where(low, along, 0.0))
    second = lane_sum(jnp.where(low, 0.0, along))
    return inverse * (grad - unit * jnp.where(low, first, second))


def mix_taps(ext_ref, conv_ref, place):
    mixed = conv_ref[0:1, :] * ext_ref[8 : 8 + SEG, :]
    for offset in range(1, 4):
        kept = jnp.where(place >= offset, ext_ref[8 - offset : 8 - offset + SEG, :], 0.0)
        mixed = mixed + conv_ref[offset : offset + 1, :] * kept
    return mixed


def gate_scan(gate_rows):
    lane = lane_index((8, SEG))
    keep = jnp.where(gate_rows[24:25] < 0.5, 0.0, 1.0)
    live = gate_rows[25:26]
    forget = jax.nn.sigmoid(gate_rows[0:8])
    momentum = jax.nn.sigmoid(gate_rows[8:16])
    step = jax.nn.sigmoid(gate_rows[16:24])
    carry = keep * momentum
    fade = keep * (1.0 - forget)
    keep_all, mix_all, fade_all = carry, carry, fade
    distance = 1
    while distance < SEG:
        inside = lane < SEG - distance
        turn = SEG - distance
        keep_next = jnp.where(inside, pltpu.roll(keep_all, turn, 1), 1.0)
        mix_next = jnp.where(inside, pltpu.roll(mix_all, turn, 1), 0.0)
        fade_next = jnp.where(inside, pltpu.roll(fade_all, turn, 1), 1.0)
        mix_all = mix_next * keep_all + fade_next * mix_all
        keep_all = keep_next * keep_all
        fade_all = fade_next * fade_all
        distance *= 2
    inside = lane < SEG - 1
    keep_after = jnp.where(inside, pltpu.roll(keep_all, SEG - 1, 1), 1.0)
    mix_after = jnp.where(inside, pltpu.roll(mix_all, SEG - 1, 1), 0.0)
    fade_after = jnp.where(inside, pltpu.roll(fade_all, SEG - 1, 1), 1.0)
    written = -THETA_SCALE * step * live
    return dict(
        keep=keep,
        live=live,
        forget=forget,
        momentum=momentum,
        step=step,
        carry=carry,
        fade=fade,
        keep_after=keep_after,
        reach=mix_after + fade_after,
        fade_after=fade_after,
        written=written,
        totals=(keep_all, mix_all, fade_all),
    )


def write_columns(scan):
    rows = jnp.concatenate(
        [scan["written"] * scan["keep_after"], scan["written"] * scan["reach"]], axis=0
    )
    return jnp.transpose(rows)


def state_factors(totals, head, low):
    keep_all, mix_all, fade_all = (member[head : head + 1, 0:1] for member in totals)
    return jnp.where(low, keep_all, fade_all), mix_all


def visible_masks(place, live_prev, live_now):
    row = lax.broadcasted_iota(jnp.int32, (SEG, SEG), 0)
    gap = row - lane_index((SEG, SEG))
    now = (gap >= 0) & (gap <= place) & (live_now > 0.5)
    prev = (gap < 0) & (gap + SEG <= place) & (live_prev > 0.5)
    return prev, now


def layer_scores(query, key_prev, key_now, pkeys, masks):
    fixed = dot_nt(query, pkeys)
    prev = jnp.where(masks[0], SCORE_SCALE * dot_nt(query, key_prev), MASKED)
    now = jnp.where(masks[1], SCORE_SCALE * dot_nt(query, key_now), MASKED)
    return fixed, prev, now


def forward_kernel(
    heads,
    raw_ref,
    gate_ref,
    place_ref,
    conv_ref,
    mem_ref,
    swap_ref,
    pkey_ref,
    pvalue_ref,
    comb_ref,
    key_out,
    value_out,
    total_out,
    state_out,
    ext,
    key_prev,
    value_prev,
    live_prev,
    state,
):
    at = pl.program_id(0)

    @pl.when(at == 0)
    def _():
        ext[0:8, :] = jnp.zeros((8, 3 * LANES), f32)
        key_prev[...] = jnp.zeros_like(key_prev)
        value_prev[...] = jnp.zeros_like(value_prev)
        live_prev[...] = jnp.zeros_like(live_prev)
        state[...] = jnp.zeros_like(state)

    low = lane_index((SEG, LANES)) < HEAD_SIZE
    ext[8 : 8 + SEG, :] = raw_ref[...].astype(f32)
    place = place_ref[...]
    mixed = mix_taps(ext, conv_ref, place)
    ext[0:8, :] = ext[SEG : SEG + 8, :]
    query_unit, _ = unit_pair(mixed[:, :LANES], low)
    key_unit, _ = unit_pair(mixed[:, LANES : 2 * LANES], low)
    value = mixed[:, 2 * LANES :]
    key_now = key_unit.astype(bf16)
    value_now = value.astype(bf16)
    key_out[...] = key_now
    value_out[...] = value_now
    scan = gate_scan(gate_ref[0])
    columns = write_columns(scan)
    masks = visible_masks(place, live_prev[0:1, :], scan["live"])
    older = jnp.where(place > lax.broadcasted_iota(jnp.int32, (SEG, 1), 0), 1.0, 0.0)
    kept_prev, kept_value = key_prev[...], value_prev[...]
    combined = jnp.zeros((SEG, LANES), f32)
    log_totals = jnp.zeros((SEG, 8), f32)
    for head in range(heads):
        own = low if head == 0 else jnp.logical_not(low)
        query = jnp.where(own, query_unit, 0.0).astype(bf16)
        fixed, prev, now = layer_scores(query, kept_prev, key_now, pkey_ref[...], masks)
        highest = jnp.maximum(
            jnp.max(fixed, axis=1, keepdims=True),
            jnp.maximum(
                jnp.max(prev, axis=1, keepdims=True), jnp.max(now, axis=1, keepdims=True)
            ),
        )
        fixed, prev, now = (jnp.exp(member - highest) for member in (fixed, prev, now))
        summed = lane_sum(fixed) + lane_sum(prev + now)
        inverse = 1.0 / summed
        attended = dot_nn((prev * inverse).astype(bf16), kept_value)
        attended = attended + dot_nn((now * inverse).astype(bf16), value_now)
        attended = attended + dot_nn((fixed * inverse).astype(bf16), pvalue_ref[...])
        log_totals = jnp.where(lane_index((SEG, 8)) == head, highest + jnp.log(summed), log_totals)

        key_low = to_low(key_unit, head) * MEMORY_SCALE
        value_low = to_low(value, head)
        query_low = to_low(query_unit, head) * MEMORY_SCALE
        mem, swap = mem_ref[head], swap_ref[head]
        state_one, state_two = state[head, 0], state[head, 1]
        state_out[0, head, 0] = state_one.astype(bf16)
        state_out[0, head, 1] = state_two.astype(bf16)

        first = jnp.where(low, mem.astype(f32), state_one).astype(bf16)
        second = jnp.where(low, swap.astype(f32), state_two).astype(bf16)
        asked = jnp.where(low, query_low, older * swap_halves(query_low)).astype(bf16)
        inner = dot_nt(asked, first)
        answer = dot_nn((inner * jax.nn.sigmoid(inner)).astype(bf16), second)
        recalled = jnp.where(low, answer, 0.0) + jnp.where(low, older * swap_halves(answer), 0.0)
        if head:
            recalled = swap_halves(recalled)
        combined = combined + jnp.where(own, attended, 0.0) + recalled

        key_cut = jnp.where(low, key_low, 0.0)
        inner = dot_nt(key_cut.astype(bf16), mem)
        sigmoid = jax.nn.sigmoid(inner)
        active = inner * sigmoid
        slope = sigmoid * (1.0 + inner - active)
        active = active.astype(bf16)
        error = jnp.where(low, dot_nn(active, swap) - value_low, 0.0)
        descent = (dot_nt(error.astype(bf16), swap) * slope).astype(bf16)
        scale = jnp.where(low, columns[:, head : head + 1], columns[:, 8 + head : 9 + head])
        key_scaled = ((key_cut + swap_halves(key_cut)) * scale).astype(bf16)
        error_scaled = ((error + swap_halves(error)) * scale).astype(bf16)
        factor, blend = state_factors(scan["totals"], head, low)
        for member, old, added in (
            (0, state_one, dot_tn(descent, key_scaled)),
            (1, state_two, dot_tn(active, error_scaled)),
        ):
            turned = jnp.where(low, 0.0, blend * swap_halves(old))
            state[head, member] = factor * old + turned + added
    comb_ref[...] = combined.astype(bf16)
    total_out[...] = log_totals
    key_prev[...] = key_now
    value_prev[...] = value_now
    live_prev[...] = jnp.broadcast_to(scan["live"], (8, SEG))


def chain_rows(factor, term, start, lane):
    distance = 1
    while distance < SEG:
        inside = lane >= distance
        factor_before = jnp.where(inside, pltpu.roll(factor, distance, 1), 1.0)
        term_before = jnp.where(inside, pltpu.roll(term, distance, 1), 0.0)
        term = term + factor * term_before
        factor = factor * factor_before
        distance *= 2
    after = factor * start + term
    return jnp.where(lane == 0, start, pltpu.roll(after, 1, 1))


def backward_kernel(
    heads,
    raw_ref,
    tail_ref,
    gate_ref,
    gate_prev_ref,
    place_ref,
    key_ref,
    key_prev_ref,
    value_ref,
    value_prev_ref,
    total_ref,
    state_ref,
    grad_ref,
    conv_ref,
    mem_ref,
    swap_ref,
    pkey_ref,
    pvalue_ref,
    draw_ref,
    dgate_ref,
    dmem_ref,
    dconv_ref,
    dpkey_ref,
    dpvalue_ref,
    ext,
    shifted_rows,
    key_carry,
    value_carry,
    late,
):
    at = pl.program_id(0)

    @pl.when(at == 0)
    def _():
        dmem_ref[...] = jnp.zeros_like(dmem_ref)
        dconv_ref[...] = jnp.zeros_like(dconv_ref)
        dpkey_ref[...] = jnp.zeros_like(dpkey_ref)
        dpvalue_ref[...] = jnp.zeros_like(dpvalue_ref)
        shifted_rows[:, 0:8, :] = jnp.zeros((3, 8, 3 * LANES), f32)
        key_carry[...] = jnp.zeros_like(key_carry)
        value_carry[...] = jnp.zeros_like(value_carry)
        late[...] = jnp.zeros_like(late)

    low = lane_index((SEG, LANES)) < HEAD_SIZE
    ext[0:8, :] = tail_ref[8:16, :].astype(f32)
    ext[8 : 8 + SEG, :] = raw_ref[...].astype(f32)
    place = place_ref[...]
    mixed = mix_taps(ext, conv_ref, place)
    query_unit, query_inverse = unit_pair(mixed[:, :LANES], low)
    key_unit, key_inverse = unit_pair(mixed[:, LANES : 2 * LANES], low)
    value = mixed[:, 2 * LANES :]
    key_now, key_prev = key_ref[...], key_prev_ref[...]
    value_now, value_prev = value_ref[...], value_prev_ref[...]
    gate_rows = gate_ref[0]
    scan = gate_scan(gate_rows)
    columns = write_columns(scan)
    masks = visible_masks(place, gate_prev_ref[0, 25:26, :], scan["live"])
    older = jnp.where(place > lax.broadcasted_iota(jnp.int32, (SEG, 1), 0), 1.0, 0.0)
    grad = grad_ref[...].astype(f32)
    grad_query = jnp.zeros((SEG, LANES), f32)
    grad_key = key_carry[...]
    grad_value = value_carry[...]
    carry_key = jnp.zeros((SEG, LANES), f32)
    carry_value = jnp.zeros((SEG, LANES), f32)
    wide = lane_index((SEG, LANES))
    write_grads = jnp.zeros((SEG, LANES), f32)
    sublane = lax.broadcasted_iota(jnp.int32, (8, 1), 0)
    keep_start = jnp.zeros((8, 1), f32)
    mix_start = jnp.zeros((8, 1), f32)
    fade_start = jnp.zeros((8, 1), f32)
    for head in range(heads):
        own = low if head == 0 else jnp.logical_not(low)
        query = jnp.where(own, query_unit, 0.0).astype(bf16)
        grad_own = jnp.where(own, grad, 0.0).astype(bf16)
        total = total_ref[:, head : head + 1]
        scores = layer_scores(query, key_prev, key_now, pkey_ref[...], masks)
        probs = [jnp.exp(member - total) for member in scores]
        grads = [
            dot_nt(grad_own, pvalue_ref[...]),
            dot_nt(grad_own, value_prev),
            dot_nt(grad_own, value_now),
        ]
        spread = lane_sum(probs[0] * grads[0]) + lane_sum(probs[1] * grads[1] + probs[2] * grads[2])
        score_grads = [(one * (other - spread)).astype(bf16) for one, other in zip(probs, grads)]
        probs = [member.astype(bf16) for member in probs]
        back = dot_nn(score_grads[1], key_prev) + dot_nn(score_grads[2], key_now)
        back = SCORE_SCALE * back + dot_nn(score_grads[0], pkey_ref[...])
        grad_query = grad_query + jnp.where(own, back, 0.0)
        carry_key = carry_key + SCORE_SCALE * dot_tn(score_grads[1], query)
        grad_key = grad_key + SCORE_SCALE * dot_tn(score_grads[2], query)
        carry_value = carry_value + dot_tn(probs[1], grad_own)
        grad_value = grad_value + dot_tn(probs[2], grad_own)
        dpkey_ref[...] += dot_tn(score_grads[0], query)
        dpvalue_ref[...] += dot_tn(probs[0], grad_own)

        mem, swap = mem_ref[head], swap_ref[head]
        state_one, state_two = (state_ref[0, head, member].astype(f32) for member in range(2))
        late_one, late_two = late[head, 0], late[head, 1]

        query_low = to_low(query_unit, head) * MEMORY_SCALE
        grad_low = to_low(grad, head)
        first = jnp.where(low, mem.astype(f32), state_one).astype(bf16)
        second = jnp.where(low, swap.astype(f32), state_two).astype(bf16)
        asked = jnp.where(low, query_low, older * swap_halves(query_low)).astype(bf16)
        told = jnp.where(low, grad_low, older * swap_halves(grad_low)).astype(bf16)
        inner = dot_nt(asked, first)
        sigmoid = jax.nn.sigmoid(inner)
        active = inner * sigmoid
        slope = sigmoid * (1.0 + inner - active)
        grad_inner = (dot_nt(told, second) * slope).astype(bf16)
        back = dot_nn(grad_inner, first)
        back = jnp.where(low, MEMORY_SCALE * (back + older * swap_halves(back)), 0.0)
        grad_query = grad_query + (back if head == 0 else swap_halves(back))
        read_one = dot_tn(grad_inner, asked)
        read_two = dot_tn(active.astype(bf16), told)

        key_low = to_low(key_unit, head) * MEMORY_SCALE
        key_cut = jnp.where(low, key_low, 0.0)
        key_bf = key_cut.astype(bf16)
        inner = dot_nt(key_bf, mem)
        sigmoid = jax.nn.sigmoid(inner)
        active = inner * sigmoid
        slope = sigmoid * (1.0 + inner - active)
        curve = sigmoid * (1.0 - sigmoid) * (2.0 + inner - 2.0 * active)
        active = active.astype(bf16)
        error = jnp.where(low, dot_nn(active, swap) - to_low(value, head), 0.0)
        error_bf = error.astype(bf16)
        pulled = dot_nt(error_bf, swap)
        descent = (pulled * slope).astype(bf16)
        scale = jnp.where(low, columns[:, head : head + 1], columns[:, 8 + head : 9 + head])
        key_twice = key_cut + swap_halves(key_cut)
        error_twice = error + swap_halves(error)
        key_scaled = (key_twice * scale).astype(bf16)
        error_scaled = (error_twice * scale).astype(bf16)
        late_one_bf, late_two_bf = late_one.astype(bf16), late_two.astype(bf16)
        grad_descent = dot_nt(key_scaled, late_one_bf)
        back_key = dot_nn(descent, late_one_bf)
        back_error = dot_nn(active, late_two_bf)
        weight_grad = key_twice * back_key + error_twice * back_error
        grad_state_weight = lane_sum(jnp.where(low, weight_grad, 0.0))
        grad_write_weight = lane_sum(jnp.where(low, 0.0, weight_grad))
        write_grads = jnp.where(wide == head, grad_state_weight, write_grads)
        write_grads = jnp.where(wide == 8 + head, grad_write_weight, write_grads)
        grad_pulled = (grad_descent * slope).astype(bf16)
        back_error = back_error * scale
        back_error = back_error + swap_halves(back_error) + dot_nn(grad_pulled, swap)
        back_error = jnp.where(low, back_error, 0.0)
        back_error_bf = back_error.astype(bf16)
        grad_active = dot_nt(error_scaled, late_two_bf) + dot_nt(back_error_bf, swap)
        grad_inner = (grad_descent * pulled * curve + grad_active * slope).astype(bf16)
        back_key = back_key * scale
        back_key = back_key + swap_halves(back_key) + dot_nn(grad_inner, mem)
        back_key = jnp.where(low, MEMORY_SCALE * back_key, 0.0)
        grad_key = grad_key + (back_key if head == 0 else swap_halves(back_key))
        grad_value = grad_value - (back_error if head == 0 else swap_halves(back_error))
        write_one = dot_tn(grad_inner, key_bf)
        write_two = dot_tn(grad_pulled, error_bf) + dot_tn(active, back_error_bf)
        dmem_ref[head] += jnp.where(low, read_one + write_one, swap_halves(read_two + write_two))

        factor, blend = state_factors(scan["totals"], head, low)
        same = late_one * state_one + late_two * state_two
        cross = late_one * swap_halves(state_one) + late_two * swap_halves(state_two)
        same_low = jnp.sum(lane_sum(jnp.where(low, same, 0.0)), axis=0, keepdims=True)
        same_high = jnp.sum(lane_sum(jnp.where(low, 0.0, same)), axis=0, keepdims=True)
        cross_high = jnp.sum(lane_sum(jnp.where(low, 0.0, cross)), axis=0, keepdims=True)
        keep_start = jnp.where(sublane == head, same_low, keep_start)
        fade_start = jnp.where(sublane == head, same_high, fade_start)
        mix_start = jnp.where(sublane == head, cross_high, mix_start)
        for member, old, read in ((0, late_one, read_one), (1, late_two, read_two)):
            turned = jnp.where(low, blend * swap_halves(old), read)
            late[head, member] = factor * old + turned

    lane = lane_index((8, SEG))
    write_rows = jnp.transpose(write_grads)
    grad_state_rows, grad_write_rows = write_rows[0:8], write_rows[8:16]
    written = scan["written"]
    keep_grads = chain_rows(scan["carry"], grad_state_rows * written, keep_start, lane)
    mix_grads = chain_rows(scan["carry"], grad_write_rows * written, mix_start, lane)
    mix_next = scan["carry"] * mix_grads + grad_write_rows * written
    fade_grads = chain_rows(scan["fade"], mix_next, fade_start, lane)
    grad_written = grad_state_rows * scan["keep_after"] + grad_write_rows * scan["reach"]
    grad_carry = keep_grads * scan["keep_after"] + mix_grads * scan["reach"]
    grad_fade = fade_grads * scan["fade_after"]
    used = sublane < heads
    forget, momentum, step = scan["forget"], scan["momentum"], scan["step"]
    forget_back = -grad_fade * scan["keep"] * forget * (1.0 - forget)
    momentum_back = grad_carry * scan["keep"] * momentum * (1.0 - momentum)
    step_back = -THETA_SCALE * grad_written * scan["live"] * step * (1.0 - step)
    dgate_ref[0, 0:8] = jnp.where(used, forget_back, 0.0)
    dgate_ref[0, 8:16] = jnp.where(used, momentum_back, 0.0)
    dgate_ref[0, 16:24] = jnp.where(used, step_back, 0.0)

    key_carry[...] = carry_key
    value_carry[...] = carry_value
    grad_mixed = jnp.concatenate(
        [
            unit_pair_pull(query_unit, query_inverse, grad_query, low),
            unit_pair_pull(key_unit, key_inverse, grad_key, low),
            grad_value,
        ],
        axis=1,
    )
    back = conv_ref[0:1, :] * grad_mixed
    dconv_ref[0:1, :] += jnp.sum(grad_mixed * ext[8 : 8 + SEG, :], axis=0, keepdims=True)
    for offset in range(1, 4):
        kept = jnp.where(place >= offset, grad_mixed, 0.0)
        member = offset - 1
        shifted_rows[member, SEG : SEG + 8, :] = shifted_rows[member, 0:8, :]
        shifted_rows[member, 0:SEG, :] = kept
        back = back + conv_ref[offset : offset + 1, :] * shifted_rows[
            member, offset : offset + SEG, :
        ]
        dconv_ref[offset : offset + 1, :] += jnp.sum(
            kept * ext[8 - offset : 8 - offset + SEG, :], axis=0, keepdims=True
        )
    draw_ref[...] = back.astype(bf16)


def block_of(shape, index):
    return pl.BlockSpec(shape, index)


def whole_of(array):
    zeros = (0,) * array.ndim
    return pl.BlockSpec(array.shape, lambda n: zeros)


def mix_forward(heads, raw, gates, place, conv, mem, swap, pkeys, pvalues):
    length = raw.shape[0]
    count = length // SEG
    row_block = pl.BlockSpec((SEG, LANES), lambda n: (n, 0))
    return pl.pallas_call(
        partial(forward_kernel, heads),
        grid=(count,),
        in_specs=[
            pl.BlockSpec((SEG, 3 * LANES), lambda n: (n, 0)),
            pl.BlockSpec((1, 32, SEG), lambda n: (n, 0, 0)),
            pl.BlockSpec((SEG, 1), lambda n: (n, 0)),
        ]
        + [whole_of(member) for member in (conv, mem, swap, pkeys, pvalues)],
        out_specs=[
            row_block,
            row_block,
            row_block,
            pl.BlockSpec((SEG, 8), lambda n: (n, 0)),
            pl.BlockSpec((1, heads, 2, MH, LANES), lambda n: (n, 0, 0, 0, 0)),
        ],
        out_shape=[
            jax.ShapeDtypeStruct((length, LANES), bf16),
            jax.ShapeDtypeStruct((length, LANES), bf16),
            jax.ShapeDtypeStruct((length, LANES), bf16),
            jax.ShapeDtypeStruct((length, 8), f32),
            jax.ShapeDtypeStruct((count, heads, 2, MH, LANES), bf16),
        ],
        scratch_shapes=[
            pltpu.VMEM((SEG + 8, 3 * LANES), f32),
            pltpu.VMEM((SEG, LANES), bf16),
            pltpu.VMEM((SEG, LANES), bf16),
            pltpu.VMEM((8, SEG), f32),
            pltpu.VMEM((heads, 2, MH, LANES), f32),
        ],
        compiler_params=pltpu.CompilerParams(
            dimension_semantics=("arbitrary",), vmem_limit_bytes=VMEM_GRANT
        ),
        name="mix_forward",
    )(raw, gates, place, conv, mem, swap, pkeys, pvalues)


def mix_backward(
    heads, raw, gates, place, keys, values, totals, states, grad, conv, mem, swap, pkeys, pvalues
):
    length = raw.shape[0]
    count = length // SEG

    def here(n):
        return count - 1 - n

    def before(n):
        return jnp.maximum(count - 2 - n, 0)

    row_block = pl.BlockSpec((SEG, LANES), lambda n: (here(n), 0))
    prev_block = pl.BlockSpec((SEG, LANES), lambda n: (before(n), 0))
    tail_rows = SEG // 16
    return pl.pallas_call(
        partial(backward_kernel, heads),
        grid=(count,),
        in_specs=[
            pl.BlockSpec((SEG, 3 * LANES), lambda n: (here(n), 0)),
            pl.BlockSpec((16, 3 * LANES), lambda n: (jnp.maximum(here(n) * tail_rows - 1, 0), 0)),
            pl.BlockSpec((1, 32, SEG), lambda n: (here(n), 0, 0)),
            pl.BlockSpec((1, 32, SEG), lambda n: (before(n), 0, 0)),
            pl.BlockSpec((SEG, 1), lambda n: (here(n), 0)),
            row_block,
            prev_block,
            row_block,
            prev_block,
            pl.BlockSpec((SEG, 8), lambda n: (here(n), 0)),
            pl.BlockSpec((1, heads, 2, MH, LANES), lambda n: (here(n), 0, 0, 0, 0)),
            row_block,
        ]
        + [whole_of(member) for member in (conv, mem, swap, pkeys, pvalues)],
        out_specs=[
            pl.BlockSpec((SEG, 3 * LANES), lambda n: (here(n), 0)),
            pl.BlockSpec((1, 24, SEG), lambda n: (here(n), 0, 0)),
            pl.BlockSpec((heads, MH, LANES), lambda n: (0, 0, 0)),
            pl.BlockSpec((8, 3 * LANES), lambda n: (0, 0)),
            pl.BlockSpec((P_SIZE, LANES), lambda n: (0, 0)),
            pl.BlockSpec((P_SIZE, LANES), lambda n: (0, 0)),
        ],
        out_shape=[
            jax.ShapeDtypeStruct((length, 3 * LANES), bf16),
            jax.ShapeDtypeStruct((count, 24, SEG), f32),
            jax.ShapeDtypeStruct((heads, MH, LANES), f32),
            jax.ShapeDtypeStruct((8, 3 * LANES), f32),
            jax.ShapeDtypeStruct((P_SIZE, LANES), f32),
            jax.ShapeDtypeStruct((P_SIZE, LANES), f32),
        ],
        scratch_shapes=[
            pltpu.VMEM((SEG + 8, 3 * LANES), f32),
            pltpu.VMEM((3, SEG + 8, 3 * LANES), f32),
            pltpu.VMEM((SEG, LANES), f32),
            pltpu.VMEM((SEG, LANES), f32),
            pltpu.VMEM((heads, 2, MH, LANES), f32),
        ],
        compiler_params=pltpu.CompilerParams(
            dimension_semantics=("arbitrary",), vmem_limit_bytes=VMEM_GRANT
        ),
        name="mix_backward",
    )(
        raw,
        raw,
        gates,
        gates,
        place,
        keys,
        keys,
        values,
        values,
        totals,
        states,
        grad,
        conv,
        mem,
        swap,
        pkeys,
        pvalues,
    )


def exchange_kernel(name, axes, counts, *refs):
    seqs, lines = axes
    chips = seqs // 2
    devices = seqs * lines
    gathers, planes, rows_to, everys, alls, scatters = counts
    total_in = sum(counts)
    inputs, outputs, scratch = refs[:total_in], refs[total_in : 2 * total_in], refs[2 * total_in :]
    seq, line = lax.axis_index("seq"), lax.axis_index("fsdp")
    me = seq * lines + line
    chip, core = seq // 2, lax.rem(seq, 2)
    sibling = (2 * chip + 1 - core, line)

    def twin(q):
        return (2 * q + core, line)

    def point(i):
        return (i // lines, lax.rem(i, lines))

    def loop(first, last, body):
        def step(k, carry):
            body(k)
            return carry

        lax.fori_loop(first, last, step, 0)

    barrier = pltpu.get_barrier_semaphore()
    if everys or alls or rows_to:

        def greet(k):
            pl.semaphore_signal(
                barrier, inc=1, device_id=point(lax.rem(me + k, devices)), device_id_type=MESH
            )

        loop(1, devices, greet)
        pl.semaphore_wait(barrier, devices - 1)
    else:

        def greet(k):
            pl.semaphore_signal(
                barrier, inc=1, device_id=(lax.rem(seq + k, seqs), line), device_id_type=MESH
            )

        loop(1, seqs, greet)
        pl.semaphore_wait(barrier, seqs - 1)

    position = 0
    groups = []
    for count in counts:
        groups.append((inputs[position : position + count], outputs[position : position + count]))
        position += count
    scratch = list(scratch)

    def take(number):
        taken = scratch[:number]
        del scratch[:number]
        return taken

    sums = []
    for source, target in zip(*groups[5]):
        pair, landed, pair_send, pair_recv, far_send, far_recv = take(6)

        def pair_copy(q, source=source, pair=pair, send=pair_send, recv=pair_recv):
            return pltpu.make_async_remote_copy(
                src_ref=source.at[2 * q + 1 - core],
                dst_ref=pair.at[q],
                send_sem=send.at[q],
                recv_sem=recv.at[q],
                device_id=sibling,
                device_id_type=MESH,
            )

        def far_copy(q, slot, pair=pair, landed=landed, send=far_send, recv=far_recv):
            return pltpu.make_async_remote_copy(
                src_ref=pair.at[q],
                dst_ref=landed.at[slot],
                send_sem=send.at[q],
                recv_sem=recv.at[slot],
                device_id=twin(q),
                device_id_type=MESH,
            )

        loop(1, chips + 1, lambda k, f=pair_copy: f(lax.rem(chip + k, chips)).start())
        sums.append((source, target, pair, landed, pair_copy, far_copy))

    spread = []
    for source, target in zip(*groups[0]):
        local, far_send, far_recv, near_send, near_recv = take(5)

        def own(target=target, source=source, local=local):
            return pltpu.make_async_copy(source, target.at[seq], local.at[0])

        def far(q, slot, source=source, target=target, send=far_send, recv=far_recv):
            return pltpu.make_async_remote_copy(
                src_ref=source,
                dst_ref=target.at[2 * slot + core],
                send_sem=send.at[q],
                recv_sem=recv.at[slot],
                device_id=twin(q),
                device_id_type=MESH,
            )

        def near_own(source=source, target=target, send=near_send, recv=near_recv):
            return pltpu.make_async_remote_copy(
                src_ref=source,
                dst_ref=target.at[seq],
                send_sem=send.at[chip],
                recv_sem=recv.at[chip],
                device_id=sibling,
                device_id_type=MESH,
            )

        def near(q, target=target, send=near_send, recv=near_recv):
            return pltpu.make_async_remote_copy(
                src_ref=target.at[2 * q + core],
                dst_ref=target.at[2 * q + core],
                send_sem=send.at[q],
                recv_sem=recv.at[q],
                device_id=sibling,
                device_id_type=MESH,
            )

        def near_arrival(q, target=target, send=near_send, recv=near_recv):
            return pltpu.make_async_remote_copy(
                src_ref=target.at[2 * q + 1 - core],
                dst_ref=target.at[2 * q + 1 - core],
                send_sem=send.at[q],
                recv_sem=recv.at[q],
                device_id=sibling,
                device_id_type=MESH,
            )

        loop(1, chips, lambda k, f=far: f(lax.rem(chip + k, chips), chip).start())
        near_own().start()
        own().start()
        spread.append((own, far, near_own, near, near_arrival))

    direct = []
    for kind, (sources, targets) in (
        ("plane", groups[1]),
        ("line", groups[2]),
        ("every", groups[3]),
        ("all", groups[4]),
    ):
        for source, target in zip(sources, targets):
            local, send, recv = take(3)
            if kind == "plane":
                number, mine = seqs, seq
            elif kind == "line":
                number, mine = lines, line
            else:
                number, mine = devices, me

            def piece(i, source=source, kind=kind, number=number):
                if kind in ("line", "all"):
                    return source
                if kind == "every" and source.shape[0] != number:
                    return source.at[i // lines]
                return source.at[i]

            def place(i, kind=kind):
                if kind == "plane":
                    return (i, line)
                if kind == "line":
                    return (seq, i)
                return point(i)

            def copy(i, slot, target=target, send=send, recv=recv, piece=piece, place=place):
                return pltpu.make_async_remote_copy(
                    src_ref=piece(i),
                    dst_ref=target.at[slot],
                    send_sem=send.at[i],
                    recv_sem=recv.at[slot],
                    device_id=place(i),
                    device_id_type=MESH,
                )

            def own(target=target, local=local, piece=piece, mine=mine):
                return pltpu.make_async_copy(piece(mine), target.at[mine], local.at[0])

            loop(
                1,
                number,
                lambda k, f=copy, m=mine, c=number: f(lax.rem(m + k, c), m).start(),
            )
            own().start()
            direct.append((own, copy, mine, number))

    rows = 32
    for source, target, pair, landed, pair_copy, far_copy in sums:

        def combine(k, source=source, pair=pair, pair_copy=pair_copy, far_copy=far_copy):
            q = lax.rem(chip + k, chips)
            pair_copy(q).wait_recv()

            def add(r):
                part = pl.ds(pl.multiple_of(r * rows, rows), rows)
                both = source[2 * q + core, part, :].astype(f32) + pair[q, part, :].astype(f32)
                pair[q, part, :] = both.astype(bf16)

            loop(0, source.shape[1] // rows, add)

            @pl.when(k < chips)
            def _():
                far_copy(q, chip).start()

        loop(1, chips + 1, combine)
    for own, far, near_own, near, near_arrival in spread:

        def forward(k, far=far, near=near):
            q = lax.rem(chip + k, chips)
            far(q, q).wait_recv()
            near(q).start()

        loop(1, chips, forward)

    for own, copy, mine, number in direct:

        def end(k, copy=copy, mine=mine, number=number):
            i = lax.rem(mine + k, number)
            copy(i, i).wait_recv()
            copy(i, i).wait_send()

        loop(1, number, end)
        own().wait()
    for own, far, near_own, near, near_arrival in spread:
        own().wait()
        near_own().wait_send()

        def end_far(k, far=far, near=near):
            q = lax.rem(chip + k, chips)
            far(q, q).wait_send()
            near(q).wait_send()

        loop(1, chips, end_far)
        loop(0, chips, lambda q, f=near_arrival: f(q).wait_recv())
    for source, target, pair, landed, pair_copy, far_copy in sums:

        def end_sum(k, far_copy=far_copy, pair_copy=pair_copy):
            q = lax.rem(chip + k, chips)
            far_copy(q, q).wait_recv()

        loop(1, chips, end_sum)

        def add_all(r, target=target, pair=pair, landed=landed):
            part = pl.ds(pl.multiple_of(r * rows, rows), rows)
            whole = pair[chip, part, :].astype(f32)
            for k in range(1, chips):
                whole = whole + landed[lax.rem(chip + k, chips), part, :].astype(f32)
            target[part, :] = whole

        loop(0, target.shape[0] // rows, add_all)
        loop(1, chips, lambda k, f=far_copy: f(lax.rem(chip + k, chips), chip).wait_send())
        loop(0, chips, lambda q, f=pair_copy: f(q).wait_send())


def exchange(
    name, collective, gathers=(), planes=(), to_line=(), everys=(), alls=(), scatters=()
):
    seqs, lines = lax.axis_size("seq"), lax.axis_size("fsdp")
    chips, devices = seqs // 2, seqs * lines
    arrays = [*gathers, *planes, *to_line, *everys, *alls, *scatters]
    counts = tuple(len(kind) for kind in (gathers, planes, to_line, everys, alls, scatters))
    dma = pltpu.SemaphoreType.DMA
    scratch = []
    for array in scatters:
        half = (chips,) + array.shape[1:]
        scratch += [pltpu.VMEM(half, bf16), pltpu.VMEM(half, bf16)] + [dma((chips,))] * 4
    for array in gathers:
        scratch += [dma((1,))] + [dma((chips,))] * 4
    shapes = [jax.ShapeDtypeStruct((seqs,) + array.shape, array.dtype) for array in gathers]
    for array in planes:
        scratch += [dma((1,)), dma((seqs,)), dma((seqs,))]
        shapes.append(jax.ShapeDtypeStruct(array.shape, array.dtype))
    for array in to_line:
        scratch += [dma((1,)), dma((lines,)), dma((lines,))]
        shapes.append(jax.ShapeDtypeStruct((lines,) + array.shape, array.dtype))
    for array in everys:
        scratch += [dma((1,)), dma((devices,)), dma((devices,))]
        shapes.append(jax.ShapeDtypeStruct((devices,) + array.shape[1:], array.dtype))
    for array in alls:
        scratch += [dma((1,)), dma((devices,)), dma((devices,))]
        shapes.append(jax.ShapeDtypeStruct((devices,) + array.shape, array.dtype))
    for array in scatters:
        shapes.append(jax.ShapeDtypeStruct(array.shape[1:], f32))
    plain = len(arrays) - len(scatters)
    any_spec, vmem_spec = pl.BlockSpec(memory_space=pl.ANY), pl.BlockSpec(memory_space=pltpu.VMEM)
    specs = [any_spec] * plain + [vmem_spec] * len(scatters)
    return pl.pallas_call(
        partial(exchange_kernel, name, (seqs, lines), counts),
        out_shape=shapes,
        in_specs=specs,
        out_specs=specs,
        scratch_shapes=scratch,
        compiler_params=pltpu.CompilerParams(
            collective_id=collective, has_side_effects=True, vmem_limit_bytes=VMEM_GRANT
        ),
        name=name,
    )(*arrays)


def norm_scale(values):
    return lax.rsqrt(jnp.mean(values * values, axis=-1, keepdims=True) + NORM_EPS)


def norm_pull(values, scale, gain, grad):
    inner = jnp.mean(grad * gain * values, axis=-1, keepdims=True)
    return scale * (grad * gain - values * (scale * scale) * inner)


def swish_slope(values, sigmoid):
    return sigmoid * (1.0 + values * (1.0 - sigmoid))


def widen(rows, width):
    return jnp.pad(rows, [(0, 0)] * (rows.ndim - 1) + [(0, width - rows.shape[-1])])


def on_device(
    tokens,
    norm1_gain,
    qkv_weight,
    gate_weight,
    conv_weight,
    memory_w1,
    memory_w2,
    persistent_keys,
    persistent_values,
    out_weight,
    norm2_gain,
    ffn_gate,
    ffn_up,
    ffn_down,
    gate_bias,
    doc_lengths,
    live_mask,
    cotangent,
):
    seqs, lines = lax.axis_size("seq"), lax.axis_size("fsdp")
    devices = seqs * lines
    seq, line = lax.axis_index("seq"), lax.axis_index("fsdp")
    me = seq * lines + line
    groups = min(HEAD_COUNT, seqs)
    copies = seqs // groups
    heads = HEAD_COUNT // groups
    width = heads * HEAD_SIZE
    group = seq // copies
    first_copy = (seq % copies == 0).astype(f32)
    share = D // devices
    hidden_share = MH // devices
    length = seqs * SEG
    piece = D // seqs
    slab = ffn_gate.shape[1] // seqs

    def for_copies(array):
        return jnp.repeat(array, copies, axis=0) if copies > 1 else array

    def head_columns(array):
        rows = array.shape[0]
        split = array.reshape(rows, 3, groups, width).transpose(2, 0, 1, 3)
        return for_copies(widen(split, LANES).reshape(groups, rows, 3 * LANES))

    qkv_blocks = head_columns(qkv_weight)
    memory_pack = jnp.concatenate([memory_w1.transpose(0, 2, 1), memory_w2], axis=2)
    memory_blocks = for_copies(memory_pack.reshape(groups, heads * hidden_share, LANES))
    live_rows = live_mask[0].astype(bf16).reshape(SEG // LANES, LANES)
    small = [
        gate_weight,
        conv_weight,
        persistent_keys,
        persistent_values,
        norm1_gain[None],
        norm2_gain[None],
        live_rows,
    ]
    small_at = [0]
    for member in small:
        small_at.append(small_at[-1] + member.shape[0])
    small_pack = jnp.concatenate([widen(member, LANES) for member in small], axis=0)
    small_pack = jnp.pad(small_pack, ((0, -small_pack.shape[0] % 16), (0, 0)))
    ffn_local = jnp.stack([ffn_gate, ffn_up, ffn_down.T])
    ffn_blocks = ffn_local.reshape(3, piece, seqs, slab).transpose(2, 0, 1, 3)
    ffn_blocks = ffn_blocks.reshape(seqs, 3 * piece, slab)
    token_rows, ffn_got, qkv_got, memory_got, small_got = exchange(
        "first_exchange",
        0,
        gathers=[tokens[0]],
        planes=[ffn_blocks],
        everys=[qkv_blocks, memory_blocks],
        alls=[small_pack],
    )
    out_matrix = lax.all_gather(out_weight, ("seq", "fsdp"), axis=0, tiled=True)
    ffn_part = ffn_got.reshape(seqs, 3, piece, slab).transpose(1, 0, 2, 3).reshape(3 * D, slab)
    ffn_full = lax.all_gather(ffn_part, "fsdp", axis=1, tiled=True).reshape(3, D, lines * slab)
    cot_rows = lax.all_gather(cotangent[0], "seq", axis=0, tiled=True)

    token_rows = token_rows.reshape(length, D)
    qkv_matrix = qkv_got.reshape(D, 3 * LANES)
    memory_both = memory_got.reshape(devices, heads, hidden_share, LANES)
    memory_both = memory_both.transpose(1, 0, 2, 3).reshape(heads, MH, LANES)
    memory_turned = jnp.concatenate(
        [memory_both[..., HEAD_SIZE:], memory_both[..., :HEAD_SIZE]], axis=-1
    )

    def small_part(number, columns):
        return small_got[:, small_at[number] : small_at[number + 1], :columns]

    gate_matrix = small_part(0, 3 * HEAD_COUNT).reshape(D, 3, HEAD_COUNT).transpose(1, 2, 0)
    gate_rows = lax.dynamic_slice_in_dim(gate_matrix, group * heads, heads, 1)
    gate_rows = jnp.pad(gate_rows, ((0, 0), (0, 8 - heads), (0, 0))).reshape(24, D)
    taps = small_part(1, 3 * share).transpose(1, 0, 2).reshape(4, 3, groups, width)
    taps = lax.dynamic_slice_in_dim(taps, group, 1, 2)[:, :, 0]
    taps = jnp.pad(widen(taps, LANES).reshape(4, 3 * LANES), ((0, 4), (0, 0))).astype(f32)

    def own_columns(number):
        whole = small_part(number, share).transpose(1, 0, 2).reshape(P_SIZE, D)
        return widen(lax.dynamic_slice_in_dim(whole, group * width, width, 1), LANES)

    pkeys, pvalues = own_columns(2), own_columns(3)
    gain_one = small_part(4, share).reshape(1, D).astype(f32)
    gain_two = small_part(5, share).reshape(1, D).astype(f32)
    live_all = small_part(6, LANES).reshape(seqs, lines, SEG)
    live_all = lax.dynamic_index_in_dim(live_all, line, 1, False).astype(f32)

    lengths = doc_lengths[0]
    starts = jnp.cumsum(lengths) - lengths

    def place_of(positions):
        inside = starts <= positions[..., None]
        return positions - jnp.max(jnp.where(inside, starts, -1), axis=-1)

    place_rows = place_of(jnp.arange(length, dtype=jnp.int32).reshape(seqs, SEG))
    place_column = place_of(jnp.arange(length, dtype=jnp.int32).reshape(length, 1))

    wide_tokens = token_rows.astype(f32)
    normed = (wide_tokens * norm_scale(wide_tokens) * gain_one).astype(bf16)
    raw = jnp.dot(normed, qkv_matrix, preferred_element_type=f32).astype(bf16)
    gate_input = dot_nt(gate_rows, normed)
    shift = lax.dynamic_slice_in_dim(gate_bias, group * heads, heads, 1)
    shift = shift * jnp.array([[3.0], [1.0], [1.0]], f32) + jnp.array([[-7.5], [1.5], [0.0]], f32)
    shift = jnp.pad(shift, ((0, 0), (0, 8 - heads))).reshape(24, 1)
    gate_input = (gate_input + shift).reshape(24, seqs, SEG).transpose(1, 0, 2)
    extra = jnp.stack([place_rows.astype(f32), live_all], axis=1)
    gates = jnp.concatenate([gate_input, jnp.pad(extra, ((0, 0), (0, 6), (0, 0)))], axis=1)
    constants = (taps, memory_both, memory_turned, pkeys, pvalues)
    mixed, keys, values, totals, states = mix_forward(heads, raw, gates, place_column, *constants)

    (mixed_got,) = exchange("to_segments", 1, planes=[mixed.reshape(seqs, SEG, LANES)])
    combined = mixed_got[::copies, :, :width].transpose(1, 0, 2).reshape(SEG, D)
    inputs = tokens[0].astype(f32)
    middle = inputs + jnp.dot(combined, out_matrix, preferred_element_type=f32)
    scale_two = norm_scale(middle)
    normed_two_own = (middle * scale_two * gain_two).astype(bf16)
    (normed_two,) = exchange("second_rows", 2, gathers=[normed_two_own])
    normed_two = normed_two.reshape(length, D)

    up_gate, up_matrix, down_matrix = ffn_full[0], ffn_full[1], ffn_full[2]
    gate_act = jnp.dot(normed_two, up_gate, preferred_element_type=f32)
    up_act = jnp.dot(normed_two, up_matrix, preferred_element_type=f32)
    sigmoid = jax.nn.sigmoid(gate_act)
    swish = gate_act * sigmoid
    hidden = (swish * up_act).astype(bf16)
    grad_hidden = jnp.dot(cot_rows, down_matrix, preferred_element_type=f32)
    grad_gate = (grad_hidden * up_act * swish_slope(gate_act, sigmoid)).astype(bf16)
    grad_up = (grad_hidden * swish).astype(bf16)
    normed_part = dot_nt(grad_gate, up_gate) + dot_nt(grad_up, up_matrix)
    (grad_normed_two,) = exchange(
        "second_sums", 3, scatters=[normed_part.astype(bf16).reshape(seqs, SEG, D)]
    )
    down_part = dot_nt(hidden, down_matrix).astype(bf16)
    down_sum = lax.psum_scatter(down_part, "seq", scatter_dimension=0, tiled=True)
    output = (middle + down_sum.astype(f32)).astype(bf16)
    ffn_grads = jnp.concatenate(
        [dot_tn(normed_two, grad_gate), dot_tn(normed_two, grad_up), dot_tn(cot_rows, hidden)],
        axis=0,
    ).astype(bf16)
    ffn_grads = lax.psum_scatter(ffn_grads, "fsdp", scatter_dimension=1, tiled=True)

    grad_middle = cotangent[0].astype(f32) + norm_pull(middle, scale_two, gain_two, grad_normed_two)
    grad_gain_two = jnp.sum(grad_normed_two * middle * scale_two, axis=0, keepdims=True)
    grad_branch = grad_middle.astype(bf16)
    grad_combined = dot_nt(grad_branch, out_matrix).astype(bf16)
    grad_out = dot_tn(combined, grad_branch).astype(bf16)
    grad_out = lax.psum_scatter(grad_out, ("seq", "fsdp"), scatter_dimension=0, tiled=True)
    blocks = widen(grad_combined.reshape(SEG, groups, width).transpose(1, 0, 2), LANES)
    (grad_mixed,) = exchange("to_heads", 4, planes=[for_copies(blocks)])

    grad_raw, grad_gates, grad_memory, grad_taps, grad_pkeys, grad_pvalues = mix_backward(
        heads,
        raw,
        gates,
        place_column,
        keys,
        values,
        totals,
        states,
        grad_mixed.reshape(length, LANES),
        *constants,
    )
    grad_gates = grad_gates.transpose(1, 0, 2).reshape(24, length)
    grad_gates_low = grad_gates.astype(bf16)
    grad_qkv = dot_tn(normed, grad_raw)
    grad_gate_rows = dot_nn(grad_gates_low, normed)
    grad_normed = dot_nt(grad_raw, qkv_matrix) + dot_tn(grad_gates_low, gate_rows)
    grad_normed = (grad_normed * first_copy).astype(bf16).reshape(seqs, SEG, D)

    def to_owners(rows):
        return rows.reshape(rows.shape[0], devices, share).transpose(1, 0, 2)

    memory_part = grad_memory.reshape(heads, devices, hidden_share, LANES).transpose(1, 0, 2, 3)
    memory_part = memory_part.reshape(devices, heads * hidden_share, LANES)
    owner_rows = widen(to_owners(jnp.concatenate([grad_gate_rows, grad_gain_two], axis=0)), LANES)
    owner_pack = jnp.concatenate([memory_part, owner_rows], axis=1).astype(bf16)
    owner_pack = jnp.pad(owner_pack, ((0, 0), (0, -owner_pack.shape[1] % 16), (0, 0)))
    bias_sums = widen(jnp.sum(grad_gates, axis=1)[None], LANES)
    shared_pack = jnp.concatenate(
        [grad_taps[:4].reshape(12, LANES), bias_sums, jnp.zeros((3, LANES), f32)], axis=0
    )
    line_pack = jnp.concatenate([grad_pkeys, grad_pvalues], axis=0)
    ffn_out = ffn_grads.reshape(3, seqs, piece, slab).transpose(1, 0, 2, 3)
    ffn_got, line_got, qkv_got, owner_got, shared_got, grad_normed = exchange(
        "last_exchange",
        5,
        planes=[ffn_out.reshape(seqs, 3 * piece, slab)],
        to_line=[line_pack],
        everys=[grad_qkv.astype(bf16).reshape(devices, share, 3 * LANES), owner_pack],
        alls=[shared_pack],
        scatters=[grad_normed],
    )

    scale_one = norm_scale(inputs)
    input_grad = grad_middle + norm_pull(inputs, scale_one, gain_one, grad_normed)

    def over_rows(got):
        summed = jnp.sum(got.astype(f32).reshape((seqs, lines) + got.shape[1:]), axis=1)
        return summed[::copies]

    grad_qkv = over_rows(qkv_got).reshape(groups, share, 3, LANES)[..., :width]
    grad_qkv = grad_qkv.transpose(1, 2, 0, 3).reshape(share, 3 * D)
    owner_sums = over_rows(owner_got)
    memory_rows = heads * hidden_share
    grad_memory = owner_sums[:, :memory_rows].reshape(HEAD_COUNT, hidden_share, LANES)
    grad_memory_w1 = grad_memory[..., :HEAD_SIZE].transpose(0, 2, 1)
    grad_memory_w2 = grad_memory[..., HEAD_SIZE:]
    grad_gate = owner_sums[:, memory_rows : memory_rows + 24, :share]
    grad_gate = grad_gate.reshape(groups, 3, 8, share)[:, :, :heads].transpose(3, 1, 0, 2)
    grad_gate = grad_gate.reshape(share, 3 * HEAD_COUNT)
    grad_gain_two = jnp.sum(owner_got[:, memory_rows + 24, :share].astype(f32), axis=0)
    own_gain = norm1_gain.astype(f32)
    along = jnp.sum(grad_qkv * qkv_weight.astype(f32), axis=1)
    along = along + jnp.sum(grad_gate * gate_weight.astype(f32), axis=1)
    grad_gain_one = along / own_gain
    shared_sums = over_rows(shared_got)
    grad_conv = shared_sums[:, :12].reshape(groups, 4, 3, LANES)[..., :width]
    grad_conv = grad_conv.transpose(1, 2, 0, 3).reshape(4, 3 * D)
    grad_conv = lax.dynamic_slice_in_dim(grad_conv, me * 3 * share, 3 * share, 1)
    grad_bias = shared_sums[:, 12, :24].reshape(groups, 3, 8)[:, :, :heads]
    grad_bias = grad_bias.transpose(1, 0, 2).reshape(3, HEAD_COUNT)
    grad_bias = grad_bias * jnp.array([[3.0], [1.0], [1.0]], f32)
    line_sums = jnp.sum(line_got, axis=0)
    line_sums = lax.dynamic_slice_in_dim(line_sums, me * share - group * width, share, 1)
    ffn_sums = ffn_got.astype(f32).reshape(seqs, 3, piece, slab).transpose(1, 2, 0, 3)
    ffn_sums = ffn_sums.reshape(3, piece, seqs * slab)
    return (
        output[None],
        input_grad[None],
        grad_gain_one,
        grad_qkv,
        grad_gate,
        grad_conv,
        grad_memory_w1,
        grad_memory_w2,
        line_sums[:P_SIZE],
        line_sums[P_SIZE:],
        grad_out.astype(f32),
        grad_gain_two,
        ffn_sums[0],
        ffn_sums[1],
        ffn_sums[2].T,
        grad_bias,
    )


def solution(mesh):
    return jax.shard_map(
        on_device,
        mesh=mesh,
        in_specs=(
            P("fsdp", "seq", None),
            P(("seq", "fsdp")),
            P(("seq", "fsdp"), None),
            P(("seq", "fsdp"), None),
            P(None, ("seq", "fsdp")),
            P(None, None, ("seq", "fsdp")),
            P(None, ("seq", "fsdp"), None),
            P(None, ("seq", "fsdp")),
            P(None, ("seq", "fsdp")),
            P(("seq", "fsdp"), None),
            P(("seq", "fsdp")),
            P("seq", "fsdp"),
            P("seq", "fsdp"),
            P("fsdp", "seq"),
            P(),
            P("fsdp", None),
            P("fsdp", "seq"),
            P("fsdp", "seq", None),
        ),
        out_specs=(
            P("fsdp", "seq", None),
            P("fsdp", "seq", None),
            P(("seq", "fsdp")),
            P(("seq", "fsdp"), None),
            P(("seq", "fsdp"), None),
            P(None, ("seq", "fsdp")),
            P(None, None, ("seq", "fsdp")),
            P(None, ("seq", "fsdp"), None),
            P(None, ("seq", "fsdp")),
            P(None, ("seq", "fsdp")),
            P(("seq", "fsdp"), None),
            P(("seq", "fsdp")),
            P("seq", "fsdp"),
            P("seq", "fsdp"),
            P("fsdp", "seq"),
            P(),
        ),
        check_vma=False,
    )
```

```python
import math
from functools import partial

import jax
import jax.numpy as jnp
from jax import lax
from jax.experimental import pallas as pl
from jax.experimental.pallas import tpu as pltpu
from jax.sharding import PartitionSpec as P

HEAD_COUNT = 16
HEAD_SIZE = 64
D = 1024
MH = 256
P_SIZE = 16
SEG = 256
LANES = 128

NORM_EPS = 1e-05
UNIT_EPS = 1e-06
SCORE_SCALE = 8.0
MEMORY_SCALE = 8.0
THETA_SCALE = 0.0005
MASKED = -1000000000.0
VMEM_GRANT = 56 * 1024 * 1024
MESH = pl.DeviceIdType.MESH

f32 = jnp.float32
bf16 = jnp.bfloat16


def dot_nt(left, right):
    return lax.dot_general(left, right, (((1,), (1,)), ((), ())), preferred_element_type=f32)


def dot_nn(left, right):
    return lax.dot_general(left, right, (((1,), (0,)), ((), ())), preferred_element_type=f32)


def dot_tn(left, right):
    return lax.dot_general(left, right, (((0,), (0,)), ((), ())), preferred_element_type=f32)


def lane_index(shape):
    return lax.broadcasted_iota(jnp.int32, shape, 1)


def to_low(rows, head):
    return rows if head == 0 else pltpu.roll(rows, HEAD_SIZE, 1)


def swap_halves(rows):
    return pltpu.roll(rows, HEAD_SIZE, 1)


def lane_sum(rows):
    return jnp.sum(rows, axis=1, keepdims=True)


def unit_pair(rows, low):
    squares = rows * rows
    first = lane_sum(jnp.where(low, squares, 0.0))
    second = lane_sum(jnp.where(low, 0.0, squares))
    inverse = jnp.where(low, lax.rsqrt(first + UNIT_EPS), lax.rsqrt(second + UNIT_EPS))
    return rows * inverse, inverse


def unit_pair_pull(unit, inverse, grad, low):
    along = unit * grad
    first = lane_sum(jnp.where(low, along, 0.0))
    second = lane_sum(jnp.where(low, 0.0, along))
    return inverse * (grad - unit * jnp.where(low, first, second))


def mix_taps(ext_ref, conv_ref, place):
    mixed = conv_ref[0:1, :] * ext_ref[8 : 8 + SEG, :]
    for offset in range(1, 4):
        kept = jnp.where(place >= offset, ext_ref[8 - offset : 8 - offset + SEG, :], 0.0)
        mixed = mixed + conv_ref[offset : offset + 1, :] * kept
    return mixed


def gate_scan(gate_rows):
    lane = lane_index((8, SEG))
    keep = jnp.where(gate_rows[24:25] < 0.5, 0.0, 1.0)
    live = gate_rows[25:26]
    forget = jax.nn.sigmoid(gate_rows[0:8])
    momentum = jax.nn.sigmoid(gate_rows[8:16])
    step = jax.nn.sigmoid(gate_rows[16:24])
    carry = keep * momentum
    fade = keep * (1.0 - forget)
    keep_all, mix_all, fade_all = carry, carry, fade
    distance = 1
    while distance < SEG:
        inside = lane < SEG - distance
        turn = SEG - distance
        keep_next = jnp.where(inside, pltpu.roll(keep_all, turn, 1), 1.0)
        mix_next = jnp.where(inside, pltpu.roll(mix_all, turn, 1), 0.0)
        fade_next = jnp.where(inside, pltpu.roll(fade_all, turn, 1), 1.0)
        mix_all = mix_next * keep_all + fade_next * mix_all
        keep_all = keep_next * keep_all
        fade_all = fade_next * fade_all
        distance *= 2
    inside = lane < SEG - 1
    keep_after = jnp.where(inside, pltpu.roll(keep_all, SEG - 1, 1), 1.0)
    mix_after = jnp.where(inside, pltpu.roll(mix_all, SEG - 1, 1), 0.0)
    fade_after = jnp.where(inside, pltpu.roll(fade_all, SEG - 1, 1), 1.0)
    written = -THETA_SCALE * step * live
    return dict(
        keep=keep,
        live=live,
        forget=forget,
        momentum=momentum,
        step=step,
        carry=carry,
        fade=fade,
        keep_after=keep_after,
        reach=mix_after + fade_after,
        fade_after=fade_after,
        written=written,
        totals=(keep_all, mix_all, fade_all),
    )


def write_columns(scan):
    rows = jnp.concatenate(
        [scan["written"] * scan["keep_after"], scan["written"] * scan["reach"]], axis=0
    )
    return jnp.transpose(rows)


def state_factors(totals, head, low):
    keep_all, mix_all, fade_all = (member[head : head + 1, 0:1] for member in totals)
    return jnp.where(low, keep_all, fade_all), mix_all


def visible_masks(place, live_prev, live_now):
    row = lax.broadcasted_iota(jnp.int32, (SEG, SEG), 0)
    gap = row - lane_index((SEG, SEG))
    now = (gap >= 0) & (gap <= place) & (live_now > 0.5)
    prev = (gap < 0) & (gap + SEG <= place) & (live_prev > 0.5)
    return prev, now


def layer_scores(query, key_prev, key_now, pkeys, masks):
    fixed = dot_nt(query, pkeys)
    prev = jnp.where(masks[0], SCORE_SCALE * dot_nt(query, key_prev), MASKED)
    now = jnp.where(masks[1], SCORE_SCALE * dot_nt(query, key_now), MASKED)
    return fixed, prev, now


def forward_kernel(heads, plan, *refs):
    carried = len(plan.arrays)
    own, refs = refs[:8], refs[8:]
    sent, refs = refs[:carried], refs[carried:]
    made, refs = refs[:5], refs[5:]
    got, refs = refs[:carried], refs[carried:]
    begin, middle, finish = plan.phases(sent, got, refs[5:])
    at, last = pl.program_id(0), pl.num_programs(0) - 1

    @pl.when(at == 0)
    def _():
        greet_all(plan.axes, plan.kinds)
        begin()

    forward_step(heads, *own, *made, *refs[:5])

    @pl.when(at == last)
    def _():
        middle()
        finish()


def forward_step(
    heads,
    raw_ref,
    gate_ref,
    place_ref,
    conv_ref,
    mem_ref,
    swap_ref,
    pkey_ref,
    pvalue_ref,
    comb_ref,
    key_out,
    value_out,
    total_out,
    state_out,
    ext,
    key_prev,
    value_prev,
    live_prev,
    state,
):
    at = pl.program_id(0)

    @pl.when(at == 0)
    def _():
        ext[0:8, :] = jnp.zeros((8, 3 * LANES), f32)
        key_prev[...] = jnp.zeros_like(key_prev)
        value_prev[...] = jnp.zeros_like(value_prev)
        live_prev[...] = jnp.zeros_like(live_prev)
        state[...] = jnp.zeros_like(state)

    low = lane_index((SEG, LANES)) < HEAD_SIZE
    ext[8 : 8 + SEG, :] = raw_ref[...].astype(f32)
    place = place_ref[...]
    mixed = mix_taps(ext, conv_ref, place)
    ext[0:8, :] = ext[SEG : SEG + 8, :]
    query_unit, _ = unit_pair(mixed[:, :LANES], low)
    key_unit, _ = unit_pair(mixed[:, LANES : 2 * LANES], low)
    value = mixed[:, 2 * LANES :]
    key_now = key_unit.astype(bf16)
    value_now = value.astype(bf16)
    key_out[...] = key_now
    value_out[...] = value_now
    scan = gate_scan(gate_ref[0])
    columns = write_columns(scan)
    masks = visible_masks(place, live_prev[0:1, :], scan["live"])
    older = jnp.where(place > lax.broadcasted_iota(jnp.int32, (SEG, 1), 0), 1.0, 0.0)
    kept_prev, kept_value = key_prev[...], value_prev[...]
    combined = jnp.zeros((SEG, LANES), f32)
    log_totals = jnp.zeros((SEG, 8), f32)
    for head in range(heads):
        own = low if head == 0 else jnp.logical_not(low)
        query = jnp.where(own, query_unit, 0.0).astype(bf16)
        fixed, prev, now = layer_scores(query, kept_prev, key_now, pkey_ref[...], masks)
        highest = jnp.maximum(
            jnp.max(fixed, axis=1, keepdims=True),
            jnp.maximum(
                jnp.max(prev, axis=1, keepdims=True), jnp.max(now, axis=1, keepdims=True)
            ),
        )
        fixed, prev, now = (jnp.exp(member - highest) for member in (fixed, prev, now))
        summed = lane_sum(fixed) + lane_sum(prev + now)
        inverse = 1.0 / summed
        attended = dot_nn((prev * inverse).astype(bf16), kept_value)
        attended = attended + dot_nn((now * inverse).astype(bf16), value_now)
        attended = attended + dot_nn((fixed * inverse).astype(bf16), pvalue_ref[...])
        log_totals = jnp.where(lane_index((SEG, 8)) == head, highest + jnp.log(summed), log_totals)

        key_low = to_low(key_unit, head) * MEMORY_SCALE
        value_low = to_low(value, head)
        query_low = to_low(query_unit, head) * MEMORY_SCALE
        mem, swap = mem_ref[head], swap_ref[head]
        state_one, state_two = state[head, 0], state[head, 1]
        state_out[0, head, 0] = state_one.astype(bf16)
        state_out[0, head, 1] = state_two.astype(bf16)

        first = jnp.where(low, mem.astype(f32), state_one).astype(bf16)
        second = jnp.where(low, swap.astype(f32), state_two).astype(bf16)
        asked = jnp.where(low, query_low, older * swap_halves(query_low)).astype(bf16)
        inner = dot_nt(asked, first)
        answer = dot_nn((inner * jax.nn.sigmoid(inner)).astype(bf16), second)
        recalled = jnp.where(low, answer, 0.0) + jnp.where(low, older * swap_halves(answer), 0.0)
        if head:
            recalled = swap_halves(recalled)
        combined = combined + jnp.where(own, attended, 0.0) + recalled

        key_cut = jnp.where(low, key_low, 0.0)
        inner = dot_nt(key_cut.astype(bf16), mem)
        sigmoid = jax.nn.sigmoid(inner)
        active = inner * sigmoid
        slope = sigmoid * (1.0 + inner - active)
        active = active.astype(bf16)
        error = jnp.where(low, dot_nn(active, swap) - value_low, 0.0)
        descent = (dot_nt(error.astype(bf16), swap) * slope).astype(bf16)
        scale = jnp.where(low, columns[:, head : head + 1], columns[:, 8 + head : 9 + head])
        key_scaled = ((key_cut + swap_halves(key_cut)) * scale).astype(bf16)
        error_scaled = ((error + swap_halves(error)) * scale).astype(bf16)
        factor, blend = state_factors(scan["totals"], head, low)
        for member, old, added in (
            (0, state_one, dot_tn(descent, key_scaled)),
            (1, state_two, dot_tn(active, error_scaled)),
        ):
            turned = jnp.where(low, 0.0, blend * swap_halves(old))
            state[head, member] = factor * old + turned + added
    comb_ref[...] = combined.astype(bf16)
    total_out[...] = log_totals
    key_prev[...] = key_now
    value_prev[...] = value_now
    live_prev[...] = jnp.broadcast_to(scan["live"], (8, SEG))


def chain_rows(factor, term, start, lane):
    distance = 1
    while distance < SEG:
        inside = lane >= distance
        factor_before = jnp.where(inside, pltpu.roll(factor, distance, 1), 1.0)
        term_before = jnp.where(inside, pltpu.roll(term, distance, 1), 0.0)
        term = term + factor * term_before
        factor = factor * factor_before
        distance *= 2
    after = factor * start + term
    return jnp.where(lane == 0, start, pltpu.roll(after, 1, 1))


def backward_kernel(heads, plan, *refs):
    carried = len(plan.arrays)
    own, refs = refs[:17], refs[17:]
    sent, refs = refs[:carried], refs[carried:]
    made, refs = refs[:6], refs[6:]
    got, refs = refs[:carried], refs[carried:]
    begin, middle, finish = plan.phases(sent, got, refs[5:])
    at, last = pl.program_id(0), pl.num_programs(0) - 1

    @pl.when(at == 0)
    def _():
        greet_all(plan.axes, plan.kinds)
        begin()

    backward_step(heads, *own, *made, *refs[:5])

    @pl.when(at == 1)
    def _():
        middle()

    @pl.when(at == last)
    def _():
        finish()


def backward_step(
    heads,
    raw_ref,
    tail_ref,
    gate_ref,
    gate_prev_ref,
    place_ref,
    key_ref,
    key_prev_ref,
    value_ref,
    value_prev_ref,
    total_ref,
    state_ref,
    grad_ref,
    conv_ref,
    mem_ref,
    swap_ref,
    pkey_ref,
    pvalue_ref,
    draw_ref,
    dgate_ref,
    dmem_ref,
    dconv_ref,
    dpkey_ref,
    dpvalue_ref,
    ext,
    shifted_rows,
    key_carry,
    value_carry,
    late,
):
    at = pl.program_id(0)

    @pl.when(at == 0)
    def _():
        dmem_ref[...] = jnp.zeros_like(dmem_ref)
        dconv_ref[...] = jnp.zeros_like(dconv_ref)
        dpkey_ref[...] = jnp.zeros_like(dpkey_ref)
        dpvalue_ref[...] = jnp.zeros_like(dpvalue_ref)
        shifted_rows[:, 0:8, :] = jnp.zeros((3, 8, 3 * LANES), f32)
        key_carry[...] = jnp.zeros_like(key_carry)
        value_carry[...] = jnp.zeros_like(value_carry)
        late[...] = jnp.zeros_like(late)

    low = lane_index((SEG, LANES)) < HEAD_SIZE
    ext[0:8, :] = tail_ref[8:16, :].astype(f32)
    ext[8 : 8 + SEG, :] = raw_ref[...].astype(f32)
    place = place_ref[...]
    mixed = mix_taps(ext, conv_ref, place)
    query_unit, query_inverse = unit_pair(mixed[:, :LANES], low)
    key_unit, key_inverse = unit_pair(mixed[:, LANES : 2 * LANES], low)
    value = mixed[:, 2 * LANES :]
    key_now, key_prev = key_ref[...], key_prev_ref[...]
    value_now, value_prev = value_ref[...], value_prev_ref[...]
    gate_rows = gate_ref[0]
    scan = gate_scan(gate_rows)
    columns = write_columns(scan)
    masks = visible_masks(place, gate_prev_ref[0, 25:26, :], scan["live"])
    older = jnp.where(place > lax.broadcasted_iota(jnp.int32, (SEG, 1), 0), 1.0, 0.0)
    grad = grad_ref[...].astype(f32)
    grad_query = jnp.zeros((SEG, LANES), f32)
    grad_key = key_carry[...]
    grad_value = value_carry[...]
    carry_key = jnp.zeros((SEG, LANES), f32)
    carry_value = jnp.zeros((SEG, LANES), f32)
    wide = lane_index((SEG, LANES))
    write_grads = jnp.zeros((SEG, LANES), f32)
    sublane = lax.broadcasted_iota(jnp.int32, (8, 1), 0)
    keep_start = jnp.zeros((8, 1), f32)
    mix_start = jnp.zeros((8, 1), f32)
    fade_start = jnp.zeros((8, 1), f32)
    for head in range(heads):
        own = low if head == 0 else jnp.logical_not(low)
        query = jnp.where(own, query_unit, 0.0).astype(bf16)
        grad_own = jnp.where(own, grad, 0.0).astype(bf16)
        total = total_ref[:, head : head + 1]
        scores = layer_scores(query, key_prev, key_now, pkey_ref[...], masks)
        probs = [jnp.exp(member - total) for member in scores]
        grads = [
            dot_nt(grad_own, pvalue_ref[...]),
            dot_nt(grad_own, value_prev),
            dot_nt(grad_own, value_now),
        ]
        spread = lane_sum(probs[0] * grads[0]) + lane_sum(probs[1] * grads[1] + probs[2] * grads[2])
        score_grads = [(one * (other - spread)).astype(bf16) for one, other in zip(probs, grads)]
        probs = [member.astype(bf16) for member in probs]
        back = dot_nn(score_grads[1], key_prev) + dot_nn(score_grads[2], key_now)
        back = SCORE_SCALE * back + dot_nn(score_grads[0], pkey_ref[...])
        grad_query = grad_query + jnp.where(own, back, 0.0)
        carry_key = carry_key + SCORE_SCALE * dot_tn(score_grads[1], query)
        grad_key = grad_key + SCORE_SCALE * dot_tn(score_grads[2], query)
        carry_value = carry_value + dot_tn(probs[1], grad_own)
        grad_value = grad_value + dot_tn(probs[2], grad_own)
        dpkey_ref[...] += dot_tn(score_grads[0], query)
        dpvalue_ref[...] += dot_tn(probs[0], grad_own)

        mem, swap = mem_ref[head], swap_ref[head]
        state_one, state_two = (state_ref[0, head, member].astype(f32) for member in range(2))
        late_one, late_two = late[head, 0], late[head, 1]

        query_low = to_low(query_unit, head) * MEMORY_SCALE
        grad_low = to_low(grad, head)
        first = jnp.where(low, mem.astype(f32), state_one).astype(bf16)
        second = jnp.where(low, swap.astype(f32), state_two).astype(bf16)
        asked = jnp.where(low, query_low, older * swap_halves(query_low)).astype(bf16)
        told = jnp.where(low, grad_low, older * swap_halves(grad_low)).astype(bf16)
        inner = dot_nt(asked, first)
        sigmoid = jax.nn.sigmoid(inner)
        active = inner * sigmoid
        slope = sigmoid * (1.0 + inner - active)
        grad_inner = (dot_nt(told, second) * slope).astype(bf16)
        back = dot_nn(grad_inner, first)
        back = jnp.where(low, MEMORY_SCALE * (back + older * swap_halves(back)), 0.0)
        grad_query = grad_query + (back if head == 0 else swap_halves(back))
        read_one = dot_tn(grad_inner, asked)
        read_two = dot_tn(active.astype(bf16), told)

        key_low = to_low(key_unit, head) * MEMORY_SCALE
        key_cut = jnp.where(low, key_low, 0.0)
        key_bf = key_cut.astype(bf16)
        inner = dot_nt(key_bf, mem)
        sigmoid = jax.nn.sigmoid(inner)
        active = inner * sigmoid
        slope = sigmoid * (1.0 + inner - active)
        curve = sigmoid * (1.0 - sigmoid) * (2.0 + inner - 2.0 * active)
        active = active.astype(bf16)
        error = jnp.where(low, dot_nn(active, swap) - to_low(value, head), 0.0)
        error_bf = error.astype(bf16)
        pulled = dot_nt(error_bf, swap)
        descent = (pulled * slope).astype(bf16)
        scale = jnp.where(low, columns[:, head : head + 1], columns[:, 8 + head : 9 + head])
        key_twice = key_cut + swap_halves(key_cut)
        error_twice = error + swap_halves(error)
        key_scaled = (key_twice * scale).astype(bf16)
        error_scaled = (error_twice * scale).astype(bf16)
        late_one_bf, late_two_bf = late_one.astype(bf16), late_two.astype(bf16)
        grad_descent = dot_nt(key_scaled, late_one_bf)
        back_key = dot_nn(descent, late_one_bf)
        back_error = dot_nn(active, late_two_bf)
        weight_grad = key_twice * back_key + error_twice * back_error
        grad_state_weight = lane_sum(jnp.where(low, weight_grad, 0.0))
        grad_write_weight = lane_sum(jnp.where(low, 0.0, weight_grad))
        write_grads = jnp.where(wide == head, grad_state_weight, write_grads)
        write_grads = jnp.where(wide == 8 + head, grad_write_weight, write_grads)
        grad_pulled = (grad_descent * slope).astype(bf16)
        back_error = back_error * scale
        back_error = back_error + swap_halves(back_error) + dot_nn(grad_pulled, swap)
        back_error = jnp.where(low, back_error, 0.0)
        back_error_bf = back_error.astype(bf16)
        grad_active = dot_nt(error_scaled, late_two_bf) + dot_nt(back_error_bf, swap)
        grad_inner = (grad_descent * pulled * curve + grad_active * slope).astype(bf16)
        back_key = back_key * scale
        back_key = back_key + swap_halves(back_key) + dot_nn(grad_inner, mem)
        back_key = jnp.where(low, MEMORY_SCALE * back_key, 0.0)
        grad_key = grad_key + (back_key if head == 0 else swap_halves(back_key))
        grad_value = grad_value - (back_error if head == 0 else swap_halves(back_error))
        write_one = dot_tn(grad_inner, key_bf)
        write_two = dot_tn(grad_pulled, error_bf) + dot_tn(active, back_error_bf)
        dmem_ref[head] += jnp.where(low, read_one + write_one, swap_halves(read_two + write_two))

        factor, blend = state_factors(scan["totals"], head, low)
        same = late_one * state_one + late_two * state_two
        cross = late_one * swap_halves(state_one) + late_two * swap_halves(state_two)
        same_low = jnp.sum(lane_sum(jnp.where(low, same, 0.0)), axis=0, keepdims=True)
        same_high = jnp.sum(lane_sum(jnp.where(low, 0.0, same)), axis=0, keepdims=True)
        cross_high = jnp.sum(lane_sum(jnp.where(low, 0.0, cross)), axis=0, keepdims=True)
        keep_start = jnp.where(sublane == head, same_low, keep_start)
        fade_start = jnp.where(sublane == head, same_high, fade_start)
        mix_start = jnp.where(sublane == head, cross_high, mix_start)
        for member, old, read in ((0, late_one, read_one), (1, late_two, read_two)):
            turned = jnp.where(low, blend * swap_halves(old), read)
            late[head, member] = factor * old + turned

    lane = lane_index((8, SEG))
    write_rows = jnp.transpose(write_grads)
    grad_state_rows, grad_write_rows = write_rows[0:8], write_rows[8:16]
    written = scan["written"]
    keep_grads = chain_rows(scan["carry"], grad_state_rows * written, keep_start, lane)
    mix_grads = chain_rows(scan["carry"], grad_write_rows * written, mix_start, lane)
    mix_next = scan["carry"] * mix_grads + grad_write_rows * written
    fade_grads = chain_rows(scan["fade"], mix_next, fade_start, lane)
    grad_written = grad_state_rows * scan["keep_after"] + grad_write_rows * scan["reach"]
    grad_carry = keep_grads * scan["keep_after"] + mix_grads * scan["reach"]
    grad_fade = fade_grads * scan["fade_after"]
    used = sublane < heads
    forget, momentum, step = scan["forget"], scan["momentum"], scan["step"]
    forget_back = -grad_fade * scan["keep"] * forget * (1.0 - forget)
    momentum_back = grad_carry * scan["keep"] * momentum * (1.0 - momentum)
    step_back = -THETA_SCALE * grad_written * scan["live"] * step * (1.0 - step)
    dgate_ref[0, 0:8] = jnp.where(used, forget_back, 0.0)
    dgate_ref[0, 8:16] = jnp.where(used, momentum_back, 0.0)
    dgate_ref[0, 16:24] = jnp.where(used, step_back, 0.0)

    key_carry[...] = carry_key
    value_carry[...] = carry_value
    grad_mixed = jnp.concatenate(
        [
            unit_pair_pull(query_unit, query_inverse, grad_query, low),
            unit_pair_pull(key_unit, key_inverse, grad_key, low),
            grad_value,
        ],
        axis=1,
    )
    back = conv_ref[0:1, :] * grad_mixed
    dconv_ref[0:1, :] += jnp.sum(grad_mixed * ext[8 : 8 + SEG, :], axis=0, keepdims=True)
    for offset in range(1, 4):
        kept = jnp.where(place >= offset, grad_mixed, 0.0)
        member = offset - 1
        shifted_rows[member, SEG : SEG + 8, :] = shifted_rows[member, 0:8, :]
        shifted_rows[member, 0:SEG, :] = kept
        back = back + conv_ref[offset : offset + 1, :] * shifted_rows[
            member, offset : offset + SEG, :
        ]
        dconv_ref[offset : offset + 1, :] += jnp.sum(
            kept * ext[8 - offset : 8 - offset + SEG, :], axis=0, keepdims=True
        )
    draw_ref[...] = back.astype(bf16)


def block_of(shape, index):
    return pl.BlockSpec(shape, index)


def whole_of(array):
    zeros = (0,) * array.ndim
    return pl.BlockSpec(array.shape, lambda n: zeros)


def mix_forward(collective, plan, heads, raw, gates, place, conv, mem, swap, pkeys, pvalues):
    length = raw.shape[0]
    count = length // SEG
    row_block = pl.BlockSpec((SEG, LANES), lambda n: (n, 0))
    return pl.pallas_call(
        partial(forward_kernel, heads, plan),
        grid=(count,),
        in_specs=[
            pl.BlockSpec((SEG, 3 * LANES), lambda n: (n, 0)),
            pl.BlockSpec((1, 32, SEG), lambda n: (n, 0, 0)),
            pl.BlockSpec((SEG, 1), lambda n: (n, 0)),
        ]
        + [whole_of(member) for member in (conv, mem, swap, pkeys, pvalues)]
        + plan.specs(True)[0],
        out_specs=[
            row_block,
            row_block,
            row_block,
            pl.BlockSpec((SEG, 8), lambda n: (n, 0)),
            pl.BlockSpec((1, heads, 2, MH, LANES), lambda n: (n, 0, 0, 0, 0)),
        ]
        + plan.specs(True)[1],
        out_shape=[
            jax.ShapeDtypeStruct((length, LANES), bf16),
            jax.ShapeDtypeStruct((length, LANES), bf16),
            jax.ShapeDtypeStruct((length, LANES), bf16),
            jax.ShapeDtypeStruct((length, 8), f32),
            jax.ShapeDtypeStruct((count, heads, 2, MH, LANES), bf16),
        ]
        + plan.shapes,
        scratch_shapes=[
            pltpu.VMEM((SEG + 8, 3 * LANES), f32),
            pltpu.VMEM((SEG, LANES), bf16),
            pltpu.VMEM((SEG, LANES), bf16),
            pltpu.VMEM((8, SEG), f32),
            pltpu.VMEM((heads, 2, MH, LANES), f32),
        ]
        + plan.scratch,
        compiler_params=pltpu.CompilerParams(
            dimension_semantics=("arbitrary",),
            collective_id=collective,
            has_side_effects=True,
            vmem_limit_bytes=VMEM_GRANT,
        ),
        name="mix_forward",
    )(raw, gates, place, conv, mem, swap, pkeys, pvalues, *plan.arrays)


def mix_backward(
    collective,
    plan,
    heads,
    raw,
    gates,
    place,
    keys,
    values,
    totals,
    states,
    grad,
    conv,
    mem,
    swap,
    pkeys,
    pvalues,
):
    length = raw.shape[0]
    count = length // SEG

    def here(n):
        return count - 1 - n

    def before(n):
        return jnp.maximum(count - 2 - n, 0)

    row_block = pl.BlockSpec((SEG, LANES), lambda n: (here(n), 0))
    prev_block = pl.BlockSpec((SEG, LANES), lambda n: (before(n), 0))
    tail_rows = SEG // 16
    return pl.pallas_call(
        partial(backward_kernel, heads, plan),
        grid=(count,),
        in_specs=[
            pl.BlockSpec((SEG, 3 * LANES), lambda n: (here(n), 0)),
            pl.BlockSpec((16, 3 * LANES), lambda n: (jnp.maximum(here(n) * tail_rows - 1, 0), 0)),
            pl.BlockSpec((1, 32, SEG), lambda n: (here(n), 0, 0)),
            pl.BlockSpec((1, 32, SEG), lambda n: (before(n), 0, 0)),
            pl.BlockSpec((SEG, 1), lambda n: (here(n), 0)),
            row_block,
            prev_block,
            row_block,
            prev_block,
            pl.BlockSpec((SEG, 8), lambda n: (here(n), 0)),
            pl.BlockSpec((1, heads, 2, MH, LANES), lambda n: (here(n), 0, 0, 0, 0)),
            row_block,
        ]
        + [whole_of(member) for member in (conv, mem, swap, pkeys, pvalues)]
        + plan.specs(True)[0],
        out_specs=[
            pl.BlockSpec((SEG, 3 * LANES), lambda n: (here(n), 0)),
            pl.BlockSpec((1, 24, SEG), lambda n: (here(n), 0, 0)),
            pl.BlockSpec((heads, MH, LANES), lambda n: (0, 0, 0)),
            pl.BlockSpec((8, 3 * LANES), lambda n: (0, 0)),
            pl.BlockSpec((P_SIZE, LANES), lambda n: (0, 0)),
            pl.BlockSpec((P_SIZE, LANES), lambda n: (0, 0)),
        ]
        + plan.specs(True)[1],
        out_shape=[
            jax.ShapeDtypeStruct((length, 3 * LANES), bf16),
            jax.ShapeDtypeStruct((count, 24, SEG), f32),
            jax.ShapeDtypeStruct((heads, MH, LANES), f32),
            jax.ShapeDtypeStruct((8, 3 * LANES), f32),
            jax.ShapeDtypeStruct((P_SIZE, LANES), f32),
            jax.ShapeDtypeStruct((P_SIZE, LANES), f32),
        ]
        + plan.shapes,
        scratch_shapes=[
            pltpu.VMEM((SEG + 8, 3 * LANES), f32),
            pltpu.VMEM((3, SEG + 8, 3 * LANES), f32),
            pltpu.VMEM((SEG, LANES), f32),
            pltpu.VMEM((SEG, LANES), f32),
            pltpu.VMEM((heads, 2, MH, LANES), f32),
        ]
        + plan.scratch,
        compiler_params=pltpu.CompilerParams(
            dimension_semantics=("arbitrary",),
            collective_id=collective,
            has_side_effects=True,
            vmem_limit_bytes=VMEM_GRANT,
        ),
        name="mix_backward",
    )(
        raw,
        raw,
        gates,
        gates,
        place,
        keys,
        keys,
        values,
        values,
        totals,
        states,
        grad,
        conv,
        mem,
        swap,
        pkeys,
        pvalues,
        *plan.arrays,
    )


def exchange_phases(axes, counts, inputs, outputs, scratch):
    seqs, lines = axes
    chips = seqs // 2
    devices = seqs * lines
    seq, line = lax.axis_index("seq"), lax.axis_index("fsdp")
    me = seq * lines + line
    chip, core = seq // 2, lax.rem(seq, 2)
    sibling = (2 * chip + 1 - core, line)

    def twin(q):
        return (2 * q + core, line)

    def point(i):
        return (i // lines, lax.rem(i, lines))

    def loop(first, last, body):
        def step(k, carry):
            body(k)
            return carry

        lax.fori_loop(first, last, step, 0)

    position = 0
    groups = []
    for count in counts:
        groups.append((inputs[position : position + count], outputs[position : position + count]))
        position += count
    scratch = list(scratch)

    def take(number):
        taken = scratch[:number]
        del scratch[:number]
        return taken

    starts = []

    sums = []
    for source, target in zip(*groups[5]):
        pair, landed, pair_send, pair_recv, far_send, far_recv = take(6)

        def pair_copy(q, source=source, pair=pair, send=pair_send, recv=pair_recv):
            return pltpu.make_async_remote_copy(
                src_ref=source.at[2 * q + 1 - core],
                dst_ref=pair.at[q],
                send_sem=send.at[q],
                recv_sem=recv.at[q],
                device_id=sibling,
                device_id_type=MESH,
            )

        def far_copy(q, slot, pair=pair, landed=landed, send=far_send, recv=far_recv):
            return pltpu.make_async_remote_copy(
                src_ref=pair.at[q],
                dst_ref=landed.at[slot],
                send_sem=send.at[q],
                recv_sem=recv.at[slot],
                device_id=twin(q),
                device_id_type=MESH,
            )

        starts.append(
            lambda f=pair_copy: loop(1, chips + 1, lambda k: f(lax.rem(chip + k, chips)).start())
        )
        sums.append((source, target, pair, landed, pair_copy, far_copy))

    spread = []
    for source, target in zip(*groups[0]):
        local, far_send, far_recv, near_send, near_recv = take(5)

        def own(target=target, source=source, local=local):
            return pltpu.make_async_copy(source, target.at[seq], local.at[0])

        def far(q, slot, source=source, target=target, send=far_send, recv=far_recv):
            return pltpu.make_async_remote_copy(
                src_ref=source,
                dst_ref=target.at[2 * slot + core],
                send_sem=send.at[q],
                recv_sem=recv.at[slot],
                device_id=twin(q),
                device_id_type=MESH,
            )

        def near_own(source=source, target=target, send=near_send, recv=near_recv):
            return pltpu.make_async_remote_copy(
                src_ref=source,
                dst_ref=target.at[seq],
                send_sem=send.at[chip],
                recv_sem=recv.at[chip],
                device_id=sibling,
                device_id_type=MESH,
            )

        def near(q, target=target, send=near_send, recv=near_recv):
            return pltpu.make_async_remote_copy(
                src_ref=target.at[2 * q + core],
                dst_ref=target.at[2 * q + core],
                send_sem=send.at[q],
                recv_sem=recv.at[q],
                device_id=sibling,
                device_id_type=MESH,
            )

        def near_arrival(q, target=target, send=near_send, recv=near_recv):
            return pltpu.make_async_remote_copy(
                src_ref=target.at[2 * q + 1 - core],
                dst_ref=target.at[2 * q + 1 - core],
                send_sem=send.at[q],
                recv_sem=recv.at[q],
                device_id=sibling,
                device_id_type=MESH,
            )

        def start(far=far, near_own=near_own, own=own):
            loop(1, chips, lambda k: far(lax.rem(chip + k, chips), chip).start())
            near_own().start()
            own().start()

        starts.append(start)
        spread.append((own, far, near_own, near, near_arrival))

    direct = []
    for kind, (sources, targets) in (
        ("plane", groups[1]),
        ("line", groups[2]),
        ("every", groups[3]),
        ("all", groups[4]),
    ):
        for source, target in zip(sources, targets):
            local, send, recv = take(3)
            if kind == "plane":
                number, mine = seqs, seq
            elif kind == "line":
                number, mine = lines, line
            else:
                number, mine = devices, me

            def piece(i, source=source, kind=kind, number=number):
                if kind == "all" or (kind == "line" and source.ndim == 2):
                    return source
                if kind == "every" and source.shape[0] != number:
                    return source.at[i // lines]
                return source.at[i]

            def place(i, kind=kind):
                if kind == "plane":
                    return (i, line)
                if kind == "line":
                    return (seq, i)
                return point(i)

            def copy(i, slot, target=target, send=send, recv=recv, piece=piece, place=place):
                return pltpu.make_async_remote_copy(
                    src_ref=piece(i),
                    dst_ref=target.at[slot],
                    send_sem=send.at[i],
                    recv_sem=recv.at[slot],
                    device_id=place(i),
                    device_id_type=MESH,
                )

            def own(target=target, local=local, piece=piece, mine=mine):
                return pltpu.make_async_copy(piece(mine), target.at[mine], local.at[0])

            def start(copy=copy, own=own, mine=mine, number=number):
                loop(1, number, lambda k: copy(lax.rem(mine + k, number), mine).start())
                own().start()

            starts.append(start)
            direct.append((own, copy, mine, number))

    relays = []
    for source, target in zip(*groups[6]):
        local, plane_send, plane_recv, line_send, line_recv = take(5)

        def copy(i, slot, source=source, target=target, send=plane_send, recv=plane_recv):
            return pltpu.make_async_remote_copy(
                src_ref=source.at[i],
                dst_ref=target.at[line, slot],
                send_sem=send.at[i],
                recv_sem=recv.at[slot],
                device_id=(i, line),
                device_id_type=MESH,
            )

        def own(source=source, target=target, local=local):
            return pltpu.make_async_copy(source.at[seq], target.at[line, seq], local.at[0])

        def onward(i, slot, target=target, send=line_send, recv=line_recv):
            return pltpu.make_async_remote_copy(
                src_ref=target.at[slot],
                dst_ref=target.at[slot],
                send_sem=send.at[i],
                recv_sem=recv.at[slot],
                device_id=(seq, i),
                device_id_type=MESH,
            )

        def start(copy=copy, own=own):
            loop(1, seqs, lambda k: copy(lax.rem(seq + k, seqs), seq).start())
            own().start()

        starts.insert(0, start)
        relays.append((own, copy, onward))

    merges = []
    rows = 32
    for source, target in zip(*groups[7]):
        landed, summed, local, line_send, line_recv, plane_send, plane_recv = take(7)

        def copy(i, slot, source=source, landed=landed, send=line_send, recv=line_recv):
            return pltpu.make_async_remote_copy(
                src_ref=source.at[i],
                dst_ref=landed.at[slot],
                send_sem=send.at[i],
                recv_sem=recv.at[slot],
                device_id=(seq, i),
                device_id_type=MESH,
            )

        def own(source=source, landed=landed, local=local):
            return pltpu.make_async_copy(source.at[line], landed.at[line], local.at[0])

        def onward(i, slot, summed=summed, target=target, send=plane_send, recv=plane_recv):
            return pltpu.make_async_remote_copy(
                src_ref=summed.at[i],
                dst_ref=target.at[slot],
                send_sem=send.at[i],
                recv_sem=recv.at[slot],
                device_id=(i, line),
                device_id_type=MESH,
            )

        def keep(summed=summed, target=target, local=local):
            return pltpu.make_async_copy(summed.at[seq], target.at[seq], local.at[0])

        def start(copy=copy, own=own):
            loop(1, lines, lambda k: copy(lax.rem(line + k, lines), line).start())
            own().start()

        starts.insert(0, start)
        merges.append((landed, summed, own, copy, onward, keep))

    def begin():
        for start in starts:
            start()

    def middle():
        for source, target, pair, landed, pair_copy, far_copy in sums:

            def combine(k, source=source, pair=pair, pair_copy=pair_copy, far_copy=far_copy):
                q = lax.rem(chip + k, chips)
                pair_copy(q).wait_recv()

                def add(r):
                    part = pl.ds(pl.multiple_of(r * rows, rows), rows)
                    both = source[2 * q + core, part, :].astype(f32) + pair[q, part, :].astype(f32)
                    pair[q, part, :] = both.astype(bf16)

                loop(0, source.shape[1] // rows, add)

                @pl.when(k < chips)
                def _():
                    far_copy(q, chip).start()

            loop(1, chips + 1, combine)
        for own, copy, onward in relays:
            loop(1, seqs, lambda k, f=copy: f(lax.rem(seq + k, seqs), lax.rem(seq + k, seqs)).wait_recv())
            own().wait()
            loop(1, lines, lambda k, f=onward: f(lax.rem(line + k, lines), line).start())
        for own, far, near_own, near, near_arrival in spread:

            def forward(k, far=far, near=near):
                q = lax.rem(chip + k, chips)
                far(q, q).wait_recv()
                near(q).start()

            loop(1, chips, forward)
        for landed, summed, own, copy, onward, keep in merges:
            loop(1, lines, lambda k, f=copy: f(lax.rem(line + k, lines), lax.rem(line + k, lines)).wait_recv())
            own().wait()

            def add_up(k, landed=landed, summed=summed, onward=onward):
                i = lax.rem(seq + k, seqs)
                whole = landed[0, i].astype(f32)
                for member in range(1, lines):
                    whole = whole + landed[member, i].astype(f32)
                summed[i] = whole.astype(bf16)

                @pl.when(k < seqs)
                def _():
                    onward(i, seq).start()

            loop(1, seqs + 1, add_up)
            keep().start()

    def finish():
        for own, copy, mine, number in direct:

            def end(k, copy=copy, mine=mine, number=number):
                i = lax.rem(mine + k, number)
                copy(i, i).wait_recv()
                copy(i, i).wait_send()

            loop(1, number, end)
            own().wait()
        for own, copy, onward in relays:
            loop(1, seqs, lambda k, f=copy: f(lax.rem(seq + k, seqs), seq).wait_send())

            def end_relay(k, onward=onward):
                i = lax.rem(line + k, lines)
                onward(i, i).wait_recv()
                onward(i, line).wait_send()

            loop(1, lines, end_relay)
        for own, far, near_own, near, near_arrival in spread:
            own().wait()
            near_own().wait_send()

            def end_far(k, far=far, near=near):
                q = lax.rem(chip + k, chips)
                far(q, q).wait_send()
                near(q).wait_send()

            loop(1, chips, end_far)
            loop(0, chips, lambda q, f=near_arrival: f(q).wait_recv())
        for source, target, pair, landed, pair_copy, far_copy in sums:

            def end_sum(k, far_copy=far_copy):
                q = lax.rem(chip + k, chips)
                far_copy(q, q).wait_recv()

            loop(1, chips, end_sum)

            def add_all(r, target=target, pair=pair, landed=landed):
                part = pl.ds(pl.multiple_of(r * rows, rows), rows)
                whole = pair[chip, part, :].astype(f32)
                for k in range(1, chips):
                    whole = whole + landed[lax.rem(chip + k, chips), part, :].astype(f32)
                target[part, :] = whole

            loop(0, target.shape[0] // rows, add_all)
            loop(1, chips, lambda k, f=far_copy: f(lax.rem(chip + k, chips), chip).wait_send())
            loop(0, chips, lambda q, f=pair_copy: f(q).wait_send())
        for landed, summed, own, copy, onward, keep in merges:
            loop(1, lines, lambda k, f=copy: f(lax.rem(line + k, lines), line).wait_send())

            def end_merge(k, onward=onward):
                i = lax.rem(seq + k, seqs)
                onward(i, i).wait_recv()
                onward(i, seq).wait_send()

            loop(1, seqs, end_merge)
            keep().wait()

    return begin, middle, finish


def greet_all(axes, kinds):
    seqs, lines = axes
    seq, line = lax.axis_index("seq"), lax.axis_index("fsdp")
    barrier = pltpu.get_barrier_semaphore()

    def signal(place):
        pl.semaphore_signal(barrier, inc=1, device_id=place, device_id_type=MESH)

    def loop(last, body):
        def step(k, carry):
            body(k)
            return carry

        lax.fori_loop(1, last, step, 0)

    if "all" in kinds:
        devices = seqs * lines
        me = seq * lines + line

        def greet(k):
            i = lax.rem(me + k, devices)
            signal((i // lines, lax.rem(i, lines)))

        loop(devices, greet)
        pl.semaphore_wait(barrier, devices - 1)
        return
    met = 0
    if "plane" in kinds:
        loop(seqs, lambda k: signal((lax.rem(seq + k, seqs), line)))
        met += seqs - 1
    if "line" in kinds:
        loop(lines, lambda k: signal((seq, lax.rem(line + k, lines))))
        met += lines - 1
    pl.semaphore_wait(barrier, met)


KINDS = ("gathers", "planes", "to_line", "everys", "alls", "scatters", "relays", "merges")


class Exchange:
    def __init__(self, **arrays):
        self.axes = seqs, lines = lax.axis_size("seq"), lax.axis_size("fsdp")
        chips, devices = seqs // 2, seqs * lines
        dma = pltpu.SemaphoreType.DMA
        groups = [tuple(arrays.get(kind, ())) for kind in KINDS]
        self.counts = tuple(len(group) for group in groups)
        self.arrays = [array for group in groups for array in group]
        scratch = {kind: [] for kind in KINDS}
        shapes, self.in_vmem = [], []
        kinds = set()
        for kind, group in zip(KINDS, groups):
            for array in group:
                shape, dtype = array.shape, array.dtype
                if kind == "gathers":
                    scratch[kind] += [dma((1,))] + [dma((chips,))] * 4
                    shape = (seqs,) + shape
                elif kind == "planes":
                    scratch[kind] += [dma((1,)), dma((seqs,)), dma((seqs,))]
                elif kind == "to_line":
                    scratch[kind] += [dma((1,)), dma((lines,)), dma((lines,))]
                    shape = (lines,) + shape[-2:]
                elif kind == "everys":
                    scratch[kind] += [dma((1,)), dma((devices,)), dma((devices,))]
                    shape = (devices,) + shape[1:]
                elif kind == "alls":
                    scratch[kind] += [dma((1,)), dma((devices,)), dma((devices,))]
                    shape = (devices,) + shape
                elif kind == "scatters":
                    half = pltpu.VMEM((chips,) + shape[1:], bf16)
                    scratch[kind] += [half, half] + [dma((chips,))] * 4
                    shape, dtype = shape[1:], f32
                elif kind == "relays":
                    scratch[kind] += [dma((1,))] + [dma((seqs,))] * 2 + [dma((lines,))] * 2
                    shape = (lines,) + shape
                else:
                    scratch[kind] += [pltpu.VMEM(shape, bf16), pltpu.VMEM(shape[1:], bf16), dma((1,))]
                    scratch[kind] += [dma((lines,))] * 2 + [dma((seqs,))] * 2
                    shape = shape[1:]
                shapes.append(jax.ShapeDtypeStruct(shape, dtype))
                self.in_vmem.append(kind == "scatters")
                if kind in ("everys", "alls"):
                    kinds.add("all")
                if kind not in ("to_line",):
                    kinds.add("plane")
                if kind in ("to_line", "relays", "merges"):
                    kinds.add("line")
        self.kinds = kinds
        self.shapes = shapes
        order = ("scatters", "gathers", "planes", "to_line", "everys", "alls", "relays", "merges")
        self.scratch = [member for kind in order for member in scratch[kind]]

    def specs(self, gridded):
        if gridded:
            vmem = [
                pl.BlockSpec(
                    array.shape, lambda n, z=(0,) * array.ndim: z, pipeline_mode=pl.Buffered(1)
                )
                for array in self.arrays
            ]
            out = [
                pl.BlockSpec(array.shape, lambda n, z=(0,) * len(array.shape): z)
                for array in self.shapes
            ]
        else:
            vmem = out = [pl.BlockSpec(memory_space=pltpu.VMEM)] * len(self.arrays)
        plain = pl.BlockSpec(memory_space=pl.ANY)
        first = [one if inside else plain for one, inside in zip(vmem, self.in_vmem)]
        second = [one if inside else plain for one, inside in zip(out, self.in_vmem)]
        return first, second

    def phases(self, inputs, outputs, scratch):
        return exchange_phases(self.axes, self.counts, inputs, outputs, scratch)


def exchange_kernel(plan, *refs):
    number = len(plan.arrays)
    greet_all(plan.axes, plan.kinds)
    for phase in plan.phases(refs[:number], refs[number : 2 * number], refs[2 * number :]):
        phase()


def exchange(name, collective, **arrays):
    plan = Exchange(**arrays)
    in_specs, out_specs = plan.specs(False)
    return pl.pallas_call(
        partial(exchange_kernel, plan),
        out_shape=plan.shapes,
        in_specs=in_specs,
        out_specs=out_specs,
        scratch_shapes=plan.scratch,
        compiler_params=pltpu.CompilerParams(
            collective_id=collective, has_side_effects=True, vmem_limit_bytes=VMEM_GRANT
        ),
        name=name,
    )(*plan.arrays)


def ffn_kernel(
    axes,
    rows_ref,
    cot_ref,
    weight_ref,
    sum_ref,
    down_ref,
    grad_ref,
    rows_all,
    other,
    pair,
    landed,
    cot_slot,
    down_slot,
    grad_sum,
    far_send,
    far_recv,
    near_send,
    near_recv,
    pair_send,
    pair_recv,
    back_send,
    back_recv,
    cot_sem,
    down_sem,
    grad_sem,
):
    seqs, lines = axes
    chips = seqs // 2
    side = math.isqrt(chips)
    seq, line = lax.axis_index("seq"), lax.axis_index("fsdp")
    chip, core = seq // 2, lax.rem(seq, 2)
    sibling = (2 * chip + 1 - core, line)

    def at_step(k):
        across = lax.rem(lax.rem(chip, side) + lax.rem(k, side), side)
        along = lax.rem(chip // side + k // side, side)
        return along * side + across

    def loop(first, last, body):
        def step(k, carry):
            body(k)
            return carry

        lax.fori_loop(first, last, step, 0)

    barrier = pltpu.get_barrier_semaphore()

    def greet(k):
        pl.semaphore_signal(
            barrier, inc=1, device_id=(lax.rem(seq + k, seqs), line), device_id_type=MESH
        )

    loop(1, seqs, greet)
    pl.semaphore_wait(barrier, seqs - 1)

    def remote(source, target, send, recv, place):
        return pltpu.make_async_remote_copy(
            src_ref=source,
            dst_ref=target,
            send_sem=send,
            recv_sem=recv,
            device_id=place,
            device_id_type=MESH,
        )

    def far(q, slot):
        return remote(
            rows_ref,
            rows_all.at[2 * slot + core],
            far_send.at[q],
            far_recv.at[slot],
            (2 * q + core, line),
        )

    def near(q):
        block = rows_all.at[2 * q + core]
        return remote(block, block, near_send.at[q], near_recv.at[q], sibling)

    def near_own():
        return remote(
            rows_ref, rows_all.at[seq], near_send.at[chip], near_recv.at[chip], sibling
        )

    def near_arrival(q):
        block = rows_all.at[2 * q + 1 - core]
        return remote(block, block, near_send.at[q], near_recv.at[q], sibling)

    def to_pair(q):
        return remote(other.at[q], pair.at[q], pair_send.at[q], pair_recv.at[q], sibling)

    def back(q, slot):
        return remote(
            pair.at[q],
            landed.at[slot],
            back_send.at[q],
            back_recv.at[slot],
            (2 * q + core, line),
        )

    def block_at(step):
        q = at_step(step // 2)
        return 2 * q + jnp.where(lax.rem(step, 2) == 0, 1 - core, core)

    def cot_copy(step):
        slot = lax.rem(step, 2)
        return pltpu.make_async_copy(
            cot_ref.at[block_at(step)], cot_slot.at[slot], cot_sem.at[slot]
        )

    def down_copy(step):
        slot = lax.rem(step, 2)
        return pltpu.make_async_copy(
            down_slot.at[slot], down_ref.at[block_at(step)], down_sem.at[slot]
        )

    near_own().start()
    loop(1, chips, lambda k: far(at_step(k), chip).start())
    cot_copy(0).start()
    rows_all[seq] = rows_ref[...]
    grad_sum[...] = jnp.zeros_like(grad_sum)

    def work(step):
        k = step // 2
        q = at_step(k)
        mine = lax.rem(step, 2)
        block = block_at(step)
        slot = lax.rem(step, 2)

        @pl.when(step + 1 < seqs)
        def _():
            cot_copy(step + 1).start()

        @pl.when(jnp.logical_and(mine == 0, k > 0))
        def _():
            far(q, q).wait_recv()
            near(q).start()

        @pl.when(mine == 0)
        def _():
            near_arrival(q).wait_recv()

        cot_copy(step).wait()

        @pl.when(step >= 2)
        def _():
            down_copy(step - 2).wait()

        rows = rows_all[block]
        cot = cot_slot[slot]
        up_gate, up_matrix, down_matrix = weight_ref[0], weight_ref[1], weight_ref[2]
        gate_act = dot_nn(rows, up_gate)
        up_act = dot_nn(rows, up_matrix)
        grad_hidden = dot_nn(cot, down_matrix)
        sigmoid = jax.nn.sigmoid(gate_act)
        swish = gate_act * sigmoid
        hidden = (swish * up_act).astype(bf16)
        slope = sigmoid * (1.0 + gate_act - swish)
        grad_gate = (grad_hidden * up_act * slope).astype(bf16)
        grad_up = (grad_hidden * swish).astype(bf16)
        part = dot_nt(grad_gate, up_gate) + dot_nt(grad_up, up_matrix)

        @pl.when(mine == 0)
        def _():
            other[q] = part.astype(bf16)
            to_pair(q).start()

        @pl.when(mine == 1)
        def _():
            to_pair(q).wait_recv()
            both = part + pair[q].astype(f32)

            @pl.when(k == 0)
            def _():
                sum_ref[...] = both

            @pl.when(k > 0)
            def _():
                pair[q] = both.astype(bf16)
                back(q, chip).start()

        down_slot[slot] = dot_nt(hidden, down_matrix).astype(bf16)
        down_copy(step).start()
        grad_sum[0] += dot_tn(rows, grad_gate)
        grad_sum[1] += dot_tn(rows, grad_up)
        grad_sum[2] += dot_tn(cot, hidden)

    loop(0, seqs, work)
    for member in range(3):
        other_grad = grad_sum[member].astype(bf16)
        grad_ref[member] = other_grad
    down_copy(seqs - 2).wait()
    down_copy(seqs - 1).wait()
    near_own().wait_send()
    loop(0, chips, lambda q: to_pair(q).wait_send())

    def end(k):
        q = at_step(k)
        far(q, q).wait_send()
        near(q).wait_send()
        back(q, chip).wait_send()
        back(q, q).wait_recv()
        sum_ref[...] += landed[q].astype(f32)

    loop(1, chips, end)


def feed_forward(collective, rows, cot, weights):
    seqs, lines = lax.axis_size("seq"), lax.axis_size("fsdp")
    chips = seqs // 2
    hidden = weights.shape[2]
    dma = pltpu.SemaphoreType.DMA
    any_spec, vmem_spec = pl.BlockSpec(memory_space=pl.ANY), pl.BlockSpec(memory_space=pltpu.VMEM)
    half = pltpu.VMEM((chips, SEG, D), bf16)
    return pl.pallas_call(
        partial(ffn_kernel, (seqs, lines)),
        out_shape=[
            jax.ShapeDtypeStruct((SEG, D), f32),
            jax.ShapeDtypeStruct((seqs, SEG, D), bf16),
            jax.ShapeDtypeStruct((3, D, hidden), bf16),
        ],
        in_specs=[vmem_spec, any_spec, vmem_spec],
        out_specs=[vmem_spec, any_spec, vmem_spec],
        scratch_shapes=[
            pltpu.VMEM((seqs, SEG, D), bf16),
            half,
            half,
            half,
            pltpu.VMEM((2, SEG, D), bf16),
            pltpu.VMEM((2, SEG, D), bf16),
            pltpu.VMEM((3, D, hidden), f32),
        ]
        + [dma((chips,))] * 8
        + [dma((2,)), dma((2,)), dma((1,))],
        compiler_params=pltpu.CompilerParams(
            collective_id=collective, has_side_effects=True, vmem_limit_bytes=VMEM_GRANT
        ),
        name="feed_forward",
    )(rows, cot, weights)


def norm_scale(values):
    return lax.rsqrt(jnp.mean(values * values, axis=-1, keepdims=True) + NORM_EPS)


def norm_pull(values, scale, gain, grad):
    inner = jnp.mean(grad * gain * values, axis=-1, keepdims=True)
    return scale * (grad * gain - values * (scale * scale) * inner)


def swish_slope(values, sigmoid):
    return sigmoid * (1.0 + values * (1.0 - sigmoid))


def widen(rows, width):
    return jnp.pad(rows, [(0, 0)] * (rows.ndim - 1) + [(0, width - rows.shape[-1])])


def on_device(
    tokens,
    norm1_gain,
    qkv_weight,
    gate_weight,
    conv_weight,
    memory_w1,
    memory_w2,
    persistent_keys,
    persistent_values,
    out_weight,
    norm2_gain,
    ffn_gate,
    ffn_up,
    ffn_down,
    gate_bias,
    doc_lengths,
    live_mask,
    cotangent,
):
    seqs, lines = lax.axis_size("seq"), lax.axis_size("fsdp")
    devices = seqs * lines
    seq, line = lax.axis_index("seq"), lax.axis_index("fsdp")
    me = seq * lines + line
    groups = min(HEAD_COUNT, seqs)
    copies = seqs // groups
    heads = HEAD_COUNT // groups
    width = heads * HEAD_SIZE
    group = seq // copies
    first_copy = (seq % copies == 0).astype(f32)
    share = D // devices
    hidden_share = MH // devices
    length = seqs * SEG
    piece = D // seqs
    slab = ffn_gate.shape[1] // seqs

    def for_copies(array):
        return jnp.repeat(array, copies, axis=0) if copies > 1 else array

    qkv_blocks = qkv_weight.reshape(share, 3, groups, width).transpose(2, 1, 0, 3)
    qkv_blocks = widen(qkv_blocks, LANES).reshape(groups, 3 * share, LANES)
    memory_pack = jnp.concatenate([memory_w1.transpose(0, 2, 1), memory_w2], axis=2)
    memory_blocks = memory_pack.reshape(groups, heads * hidden_share, LANES)
    persistent = jnp.concatenate([persistent_keys, persistent_values], axis=0)
    gate_part = jnp.pad(gate_weight, ((0, 2 * P_SIZE - share), (0, HEAD_SIZE - 3 * HEAD_COUNT)))
    small_pack = jnp.concatenate(
        [
            jnp.concatenate([gate_part, widen(persistent, HEAD_SIZE)], axis=1),
            widen(conv_weight, LANES),
            widen(norm1_gain[None], LANES),
            widen(norm2_gain[None], LANES),
            live_mask[0].astype(bf16).reshape(SEG // LANES, LANES),
        ],
        axis=0,
    )
    small_pack = jnp.broadcast_to(small_pack, (groups,) + small_pack.shape)
    weight_pack = jnp.concatenate([qkv_blocks, memory_blocks, small_pack], axis=1)
    weight_pack = jnp.pad(weight_pack, ((0, 0), (0, -weight_pack.shape[1] % 16), (0, 0)))
    ffn_local = jnp.stack([ffn_gate, ffn_up, ffn_down.T])
    ffn_blocks = ffn_local.reshape(3, piece, seqs, slab).transpose(2, 0, 1, 3)
    ffn_blocks = ffn_blocks.reshape(seqs, 3 * piece, slab)
    token_rows, ffn_got, out_rows, weights_got = exchange(
        "first_exchange",
        0,
        gathers=[tokens[0]],
        planes=[ffn_blocks],
        to_line=[out_weight],
        relays=[for_copies(weight_pack)],
    )
    ffn_part = ffn_got.reshape(seqs, 3, piece, slab).transpose(1, 0, 2, 3).reshape(3 * D, slab)
    ffn_full = lax.all_gather(ffn_part, "fsdp", axis=1, tiled=True).reshape(3, D, lines * slab)

    token_rows = token_rows.reshape(length, D)
    memory_at = 3 * share
    small_at = memory_at + heads * hidden_share
    qkv_matrix = weights_got[:, :, :memory_at].reshape(lines, seqs, 3, share, LANES)
    qkv_matrix = qkv_matrix.transpose(1, 0, 3, 2, 4).reshape(D, 3 * LANES)
    memory_both = weights_got[:, :, memory_at:small_at]
    memory_both = memory_both.reshape(lines, seqs, heads, hidden_share, LANES)
    memory_both = memory_both.transpose(2, 1, 0, 3, 4).reshape(heads, MH, LANES)
    memory_turned = jnp.concatenate(
        [memory_both[..., HEAD_SIZE:], memory_both[..., :HEAD_SIZE]], axis=-1
    )
    small_got = weights_got[:, :, small_at:].transpose(1, 0, 2, 3)
    small_all = small_got.reshape((devices,) + small_got.shape[2:])
    gate_matrix = small_all[:, :share, : 3 * HEAD_COUNT].reshape(D, 3, HEAD_COUNT)
    gate_rows = gate_matrix.transpose(1, 2, 0)
    gate_rows = lax.dynamic_slice_in_dim(gate_rows, group * heads, heads, 1)
    gate_rows = jnp.pad(gate_rows, ((0, 0), (0, 8 - heads), (0, 0))).reshape(24, D)
    after = 2 * P_SIZE
    taps = small_all[:, after : after + 4, : 3 * share].transpose(1, 0, 2)
    taps = taps.reshape(4, 3, groups, width)
    taps = lax.dynamic_slice_in_dim(taps, group, 1, 2)[:, :, 0]
    taps = jnp.pad(widen(taps, LANES).reshape(4, 3 * LANES), ((0, 4), (0, 0))).astype(f32)
    persistent = small_all[:, :after, HEAD_SIZE : HEAD_SIZE + share].transpose(1, 0, 2)
    persistent = persistent.reshape(after, D)
    persistent = widen(lax.dynamic_slice_in_dim(persistent, group * width, width, 1), LANES)
    pkeys, pvalues = persistent[:P_SIZE], persistent[P_SIZE:]
    gain_one = small_all[:, after + 4, :share].reshape(1, D).astype(f32)
    gain_two = small_all[:, after + 5, :share].reshape(1, D).astype(f32)
    live_all = small_got[:, :, after + 6 : after + 6 + SEG // LANES].reshape(seqs, lines, SEG)
    live_all = lax.dynamic_index_in_dim(live_all, line, 1, False).astype(f32)

    lengths = doc_lengths[0]
    starts = jnp.cumsum(lengths) - lengths

    def place_of(positions):
        inside = starts <= positions[..., None]
        return positions - jnp.max(jnp.where(inside, starts, -1), axis=-1)

    place_rows = place_of(jnp.arange(length, dtype=jnp.int32).reshape(seqs, SEG))
    place_column = place_of(jnp.arange(length, dtype=jnp.int32).reshape(length, 1))

    wide_tokens = token_rows.astype(f32)
    normed = (wide_tokens * norm_scale(wide_tokens) * gain_one).astype(bf16)
    raw = jnp.dot(normed, qkv_matrix, preferred_element_type=f32).astype(bf16)
    gate_input = dot_nt(gate_rows, normed)
    shift = lax.dynamic_slice_in_dim(gate_bias, group * heads, heads, 1)
    shift = shift * jnp.array([[3.0], [1.0], [1.0]], f32) + jnp.array([[-7.5], [1.5], [0.0]], f32)
    shift = jnp.pad(shift, ((0, 0), (0, 8 - heads))).reshape(24, 1)
    gate_input = (gate_input + shift).reshape(24, seqs, SEG).transpose(1, 0, 2)
    extra = jnp.stack([place_rows.astype(f32), live_all], axis=1)
    gates = jnp.concatenate([gate_input, jnp.pad(extra, ((0, 0), (0, 6), (0, 0)))], axis=1)
    constants = (taps, memory_both, memory_turned, pkeys, pvalues)
    plan = Exchange(gathers=[out_rows.reshape(lines * share, D), cotangent[0]])
    mixed, keys, values, totals, states, out_matrix, cot_rows = mix_forward(
        6, plan, heads, raw, gates, place_column, *constants
    )
    out_matrix = out_matrix.reshape(D, D)

    (mixed_got,) = exchange("to_segments", 1, planes=[mixed.reshape(seqs, SEG, LANES)])
    combined = mixed_got[::copies, :, :width].transpose(1, 0, 2).reshape(SEG, D)
    inputs = tokens[0].astype(f32)
    middle = inputs + jnp.dot(combined, out_matrix, preferred_element_type=f32)
    scale_two = norm_scale(middle)
    normed_two_own = (middle * scale_two * gain_two).astype(bf16)
    grad_normed_two, down_part, ffn_grads = feed_forward(
        2, normed_two_own, cot_rows, ffn_full
    )
    ffn_grads = ffn_grads.reshape(3 * D, lines * slab)
    ffn_grads = lax.psum_scatter(ffn_grads, "fsdp", scatter_dimension=1, tiled=True)

    grad_middle = cotangent[0].astype(f32) + norm_pull(middle, scale_two, gain_two, grad_normed_two)
    grad_gain_two = jnp.sum(grad_normed_two * middle * scale_two, axis=0, keepdims=True)
    grad_branch = grad_middle.astype(bf16)
    grad_combined = dot_nt(grad_branch, out_matrix).astype(bf16)
    grad_out = dot_tn(combined, grad_branch).astype(bf16)
    plan = Exchange(scatters=[down_part, grad_out.reshape(seqs, piece, D)])
    blocks = widen(grad_combined.reshape(SEG, groups, width).transpose(1, 0, 2), LANES)
    (grad_mixed,) = exchange("to_heads", 4, planes=[for_copies(blocks)])

    grad_raw, grad_gates, grad_memory, grad_taps, grad_pkeys, grad_pvalues, down_sum, grad_out = mix_backward(
        7,
        plan,
        heads,
        raw,
        gates,
        place_column,
        keys,
        values,
        totals,
        states,
        grad_mixed.reshape(length, LANES),
        *constants,
    )
    output = (middle + down_sum).astype(bf16)
    grad_gates = grad_gates.transpose(1, 0, 2).reshape(24, length)
    grad_gates_low = grad_gates.astype(bf16)
    grad_gate_rows = dot_nn(grad_gates_low, normed)
    grad_normed = dot_nt(grad_raw, qkv_matrix) + dot_tn(grad_gates_low, gate_rows)
    grad_normed = (grad_normed * first_copy).astype(bf16).reshape(seqs, SEG, D)

    qkv_part = dot_tn(normed, grad_raw).astype(bf16).reshape(seqs, lines, share, 3, LANES)
    qkv_part = qkv_part.transpose(1, 0, 3, 2, 4).reshape(lines, seqs, 3 * share, LANES)
    memory_part = grad_memory.astype(bf16).reshape(heads, seqs, lines, hidden_share, LANES)
    memory_part = memory_part.transpose(2, 1, 0, 3, 4)
    memory_part = memory_part.reshape(lines, seqs, heads * hidden_share, LANES)
    owner_rows = jnp.concatenate([grad_gate_rows, grad_gain_two], axis=0).astype(bf16)
    owner_rows = owner_rows.reshape(25, seqs, lines, share).transpose(2, 1, 0, 3)
    bias_sums = widen(jnp.sum(grad_gates, axis=1)[None], LANES)
    shared_rows = jnp.concatenate([grad_taps[:4].reshape(12, LANES), bias_sums], axis=0)
    shared_rows = jnp.broadcast_to(shared_rows.astype(bf16), (lines, seqs, 13, LANES))
    grad_pack = jnp.concatenate(
        [qkv_part, memory_part, widen(owner_rows, LANES), shared_rows], axis=2
    )
    grad_pack = jnp.pad(grad_pack, ((0, 0), (0, 0), (0, -grad_pack.shape[2] % 16), (0, 0)))
    line_pack = jnp.concatenate([grad_pkeys, grad_pvalues], axis=0)
    out_part = grad_out.astype(bf16).reshape(lines, share, D)
    ffn_out = ffn_grads.reshape(3, seqs, piece, slab).transpose(1, 0, 2, 3)
    ffn_got, out_got, line_got, grad_normed, grads_got = exchange(
        "last_exchange",
        5,
        planes=[ffn_out.reshape(seqs, 3 * piece, slab)],
        to_line=[out_part, line_pack],
        scatters=[grad_normed],
        merges=[grad_pack],
    )

    scale_one = norm_scale(inputs)
    input_grad = grad_middle + norm_pull(inputs, scale_one, gain_one, grad_normed)

    grad_sums = grads_got[::copies].astype(f32)
    grad_qkv = grad_sums[:, : 3 * share].reshape(groups, 3, share, LANES)[..., :width]
    grad_qkv = grad_qkv.transpose(2, 1, 0, 3).reshape(share, 3 * D)
    owner_at = small_at
    grad_memory = grad_sums[:, memory_at:owner_at].reshape(HEAD_COUNT, hidden_share, LANES)
    grad_memory_w1 = grad_memory[..., :HEAD_SIZE].transpose(0, 2, 1)
    grad_memory_w2 = grad_memory[..., HEAD_SIZE:]
    grad_gate = grad_sums[:, owner_at : owner_at + 24, :share]
    grad_gate = grad_gate.reshape(groups, 3, 8, share)[:, :, :heads].transpose(3, 1, 0, 2)
    grad_gate = grad_gate.reshape(share, 3 * HEAD_COUNT)
    grad_gain_two = jnp.sum(grads_got[:, owner_at + 24, :share].astype(f32), axis=0)
    own_gain = norm1_gain.astype(f32)
    along = jnp.sum(grad_qkv * qkv_weight.astype(f32), axis=1)
    along = along + jnp.sum(grad_gate * gate_weight.astype(f32), axis=1)
    grad_gain_one = along / own_gain
    shared_at = owner_at + 25
    grad_conv = grad_sums[:, shared_at : shared_at + 12].reshape(groups, 4, 3, LANES)[..., :width]
    grad_conv = grad_conv.transpose(1, 2, 0, 3).reshape(4, 3 * D)
    grad_conv = lax.dynamic_slice_in_dim(grad_conv, me * 3 * share, 3 * share, 1)
    grad_bias = grad_sums[:, shared_at + 12, :24].reshape(groups, 3, 8)[:, :, :heads]
    grad_bias = grad_bias.transpose(1, 0, 2).reshape(3, HEAD_COUNT)
    grad_bias = grad_bias * jnp.array([[3.0], [1.0], [1.0]], f32)
    line_sums = jnp.sum(line_got, axis=0)
    line_sums = lax.dynamic_slice_in_dim(line_sums, me * share - group * width, share, 1)
    ffn_sums = ffn_got.astype(f32).reshape(seqs, 3, piece, slab).transpose(1, 2, 0, 3)
    ffn_sums = ffn_sums.reshape(3, piece, seqs * slab)
    return (
        output[None],
        input_grad[None],
        grad_gain_one,
        grad_qkv,
        grad_gate,
        grad_conv,
        grad_memory_w1,
        grad_memory_w2,
        line_sums[:P_SIZE],
        line_sums[P_SIZE:],
        jnp.sum(out_got.astype(f32), axis=0),
        grad_gain_two,
        ffn_sums[0],
        ffn_sums[1],
        ffn_sums[2].T,
        grad_bias,
    )


def solution(mesh):
    return jax.shard_map(
        on_device,
        mesh=mesh,
        in_specs=(
            P("fsdp", "seq", None),
            P(("seq", "fsdp")),
            P(("seq", "fsdp"), None),
            P(("seq", "fsdp"), None),
            P(None, ("seq", "fsdp")),
            P(None, None, ("seq", "fsdp")),
            P(None, ("seq", "fsdp"), None),
            P(None, ("seq", "fsdp")),
            P(None, ("seq", "fsdp")),
            P(("seq", "fsdp"), None),
            P(("seq", "fsdp")),
            P("seq", "fsdp"),
            P("seq", "fsdp"),
            P("fsdp", "seq"),
            P(),
            P("fsdp", None),
            P("fsdp", "seq"),
            P("fsdp", "seq", None),
        ),
        out_specs=(
            P("fsdp", "seq", None),
            P("fsdp", "seq", None),
            P(("seq", "fsdp")),
            P(("seq", "fsdp"), None),
            P(("seq", "fsdp"), None),
            P(None, ("seq", "fsdp")),
            P(None, None, ("seq", "fsdp")),
            P(None, ("seq", "fsdp"), None),
            P(None, ("seq", "fsdp")),
            P(None, ("seq", "fsdp")),
            P(("seq", "fsdp"), None),
            P(("seq", "fsdp")),
            P("seq", "fsdp"),
            P("seq", "fsdp"),
            P("fsdp", "seq"),
            P(),
        ),
        check_vma=False,
    )
```

```python
import math
from functools import partial

import jax
import jax.numpy as jnp
from jax import lax
from jax.experimental import pallas as pl
from jax.experimental.pallas import tpu as pltpu
from jax.sharding import PartitionSpec as P

HEAD_COUNT = 16
HEAD_SIZE = 64
D = 1024
FF = 4096
MH = 256
P_SIZE = 16
SEG = 256
LANES = 128

NORM_EPS = 1e-05
UNIT_EPS = 1e-06
SCORE_SCALE = 8.0
MEMORY_SCALE = 8.0
THETA_SCALE = 0.0005
MASKED = -1000000000.0
VMEM_GRANT = 56 * 1024 * 1024
MESH = pl.DeviceIdType.MESH

f32 = jnp.float32
bf16 = jnp.bfloat16


def dot_nt(left, right):
    return lax.dot_general(left, right, (((1,), (1,)), ((), ())), preferred_element_type=f32)


def dot_nn(left, right):
    return lax.dot_general(left, right, (((1,), (0,)), ((), ())), preferred_element_type=f32)


def dot_tn(left, right):
    return lax.dot_general(left, right, (((0,), (0,)), ((), ())), preferred_element_type=f32)


def lane_index(shape):
    return lax.broadcasted_iota(jnp.int32, shape, 1)


def to_low(rows, head):
    return rows if head == 0 else pltpu.roll(rows, HEAD_SIZE, 1)


def swap_halves(rows):
    return pltpu.roll(rows, HEAD_SIZE, 1)


def lane_sum(rows):
    return jnp.sum(rows, axis=1, keepdims=True)


def unit_pair(rows, low):
    squares = rows * rows
    first = lane_sum(jnp.where(low, squares, 0.0))
    second = lane_sum(jnp.where(low, 0.0, squares))
    inverse = jnp.where(low, lax.rsqrt(first + UNIT_EPS), lax.rsqrt(second + UNIT_EPS))
    return rows * inverse, inverse


def unit_pair_pull(unit, inverse, grad, low):
    along = unit * grad
    first = lane_sum(jnp.where(low, along, 0.0))
    second = lane_sum(jnp.where(low, 0.0, along))
    return inverse * (grad - unit * jnp.where(low, first, second))


def mix_taps(ext_ref, conv_ref, place):
    mixed = conv_ref[0:1, :] * ext_ref[8 : 8 + SEG, :]
    for offset in range(1, 4):
        kept = jnp.where(place >= offset, ext_ref[8 - offset : 8 - offset + SEG, :], 0.0)
        mixed = mixed + conv_ref[offset : offset + 1, :] * kept
    return mixed


def places(length_ref, positions):
    start = jnp.int32(0)
    begin = jnp.zeros_like(positions)
    for document in range(1, length_ref.shape[1]):
        start = start + length_ref[0, document - 1]
        begin = jnp.where(positions >= start, start, begin)
    return positions - begin


def gate_scan(heads, first_head, gate_columns, bias_ref, place_row, live):
    lane = lane_index((8, SEG))
    sublane = lax.broadcasted_iota(jnp.int32, (8, SEG), 0)
    gate_rows = jnp.transpose(gate_columns)
    shifts = []
    for kind, (scale, shift) in enumerate(((3.0, -7.5), (1.0, 1.5), (1.0, 0.0))):
        bias = jnp.zeros((8, SEG), f32)
        for head in range(heads):
            own = scale * bias_ref[kind, first_head + head] + shift
            bias = jnp.where(sublane == head, own, bias)
        shifts.append(bias)
    keep = jnp.where(place_row < 1, 0.0, 1.0)
    forget = jax.nn.sigmoid(gate_rows[0:8] + shifts[0])
    momentum = jax.nn.sigmoid(gate_rows[8:16] + shifts[1])
    step = jax.nn.sigmoid(gate_rows[16:24] + shifts[2])
    carry = keep * momentum
    fade = keep * (1.0 - forget)
    keep_all, mix_all, fade_all = carry, carry, fade
    distance = 1
    while distance < SEG:
        inside = lane < SEG - distance
        turn = SEG - distance
        keep_next = jnp.where(inside, pltpu.roll(keep_all, turn, 1), 1.0)
        mix_next = jnp.where(inside, pltpu.roll(mix_all, turn, 1), 0.0)
        fade_next = jnp.where(inside, pltpu.roll(fade_all, turn, 1), 1.0)
        mix_all = mix_next * keep_all + fade_next * mix_all
        keep_all = keep_next * keep_all
        fade_all = fade_next * fade_all
        distance *= 2
    inside = lane < SEG - 1
    keep_after = jnp.where(inside, pltpu.roll(keep_all, SEG - 1, 1), 1.0)
    mix_after = jnp.where(inside, pltpu.roll(mix_all, SEG - 1, 1), 0.0)
    fade_after = jnp.where(inside, pltpu.roll(fade_all, SEG - 1, 1), 1.0)
    written = -THETA_SCALE * step * live
    return dict(
        keep=keep,
        live=live,
        forget=forget,
        momentum=momentum,
        step=step,
        carry=carry,
        fade=fade,
        keep_after=keep_after,
        reach=mix_after + fade_after,
        fade_after=fade_after,
        written=written,
        totals=(keep_all, mix_all, fade_all),
    )


def write_columns(scan):
    rows = jnp.concatenate(
        [scan["written"] * scan["keep_after"], scan["written"] * scan["reach"]], axis=0
    )
    return jnp.transpose(rows)


def state_factors(totals, head, low):
    keep_all, mix_all, fade_all = (member[head : head + 1, 0:1] for member in totals)
    return jnp.where(low, keep_all, fade_all), mix_all


def visible_masks(place, live_prev, live_now):
    row = lax.broadcasted_iota(jnp.int32, (SEG, SEG), 0)
    gap = row - lane_index((SEG, SEG))
    now = (gap >= 0) & (gap <= place) & (live_now > 0.5)
    prev = (gap < 0) & (gap + SEG <= place) & (live_prev > 0.5)
    return prev, now


def layer_scores(query, key_prev, key_now, pkeys, masks):
    fixed = dot_nt(query, pkeys)
    prev = jnp.where(masks[0], SCORE_SCALE * dot_nt(query, key_prev), MASKED)
    now = jnp.where(masks[1], SCORE_SCALE * dot_nt(query, key_now), MASKED)
    return fixed, prev, now


def forward_kernel(heads, plan, *refs):
    carried = len(plan.arrays)
    own, refs = refs[:9], refs[9:]
    sent, refs = refs[:carried], refs[carried:]
    made, refs = refs[:5], refs[5:]
    got, refs = refs[:carried], refs[carried:]
    begin, middle, finish = plan.phases(sent, got, refs[5:])
    at, last = pl.program_id(0), pl.num_programs(0) - 1

    @pl.when(at == 0)
    def _():
        greet_all(plan.axes, plan.kinds)
        begin()

    forward_step(heads, *own, *made, *refs[:5])

    @pl.when(at == (5 * last) // 8)
    def _():
        middle()

    @pl.when(at == last)
    def _():
        finish()


def forward_step(
    heads,
    raw_ref,
    gate_ref,
    live_ref,
    conv_ref,
    mem_ref,
    swap_ref,
    persist_ref,
    length_ref,
    bias_ref,
    comb_ref,
    key_out,
    value_out,
    total_out,
    state_out,
    ext,
    key_prev,
    value_prev,
    live_prev,
    state,
):
    at = pl.program_id(0)

    @pl.when(at == 0)
    def _():
        ext[0:8, :] = jnp.zeros((8, 3 * LANES), f32)
        key_prev[...] = jnp.zeros_like(key_prev)
        value_prev[...] = jnp.zeros_like(value_prev)
        live_prev[...] = jnp.zeros_like(live_prev)
        state[...] = jnp.zeros_like(state)

    low = lane_index((SEG, LANES)) < HEAD_SIZE
    ext[8 : 8 + SEG, :] = raw_ref[...].astype(f32)
    place = places(length_ref, at * SEG + lax.broadcasted_iota(jnp.int32, (SEG, 1), 0))
    place_row = places(length_ref, at * SEG + lane_index((1, SEG)))
    pkeys, pvalues = persist_ref[0:P_SIZE, :], persist_ref[P_SIZE:, :]
    first_head = (lax.axis_index("seq") * HEAD_COUNT) // lax.axis_size("seq")
    mixed = mix_taps(ext, conv_ref, place)
    ext[0:8, :] = ext[SEG : SEG + 8, :]
    query_unit, _ = unit_pair(mixed[:, :LANES], low)
    key_unit, _ = unit_pair(mixed[:, LANES : 2 * LANES], low)
    value = mixed[:, 2 * LANES :]
    key_now = key_unit.astype(bf16)
    value_now = value.astype(bf16)
    key_out[...] = key_now
    value_out[...] = value_now
    scan = gate_scan(heads, first_head, gate_ref[...], bias_ref, place_row, live_ref[0, 0:1, :])
    columns = write_columns(scan)
    masks = visible_masks(place, live_prev[0:1, :], scan["live"])
    older = jnp.where(place > lax.broadcasted_iota(jnp.int32, (SEG, 1), 0), 1.0, 0.0)
    kept_prev, kept_value = key_prev[...], value_prev[...]
    combined = jnp.zeros((SEG, LANES), f32)
    log_totals = jnp.zeros((SEG, 8), f32)
    for head in range(heads):
        own = low if head == 0 else jnp.logical_not(low)
        query = jnp.where(own, query_unit, 0.0).astype(bf16)
        fixed, prev, now = layer_scores(query, kept_prev, key_now, pkeys, masks)
        highest = jnp.maximum(
            jnp.max(fixed, axis=1, keepdims=True),
            jnp.maximum(
                jnp.max(prev, axis=1, keepdims=True), jnp.max(now, axis=1, keepdims=True)
            ),
        )
        fixed, prev, now = (jnp.exp(member - highest) for member in (fixed, prev, now))
        summed = lane_sum(fixed) + lane_sum(prev + now)
        inverse = 1.0 / summed
        attended = dot_nn((prev * inverse).astype(bf16), kept_value)
        attended = attended + dot_nn((now * inverse).astype(bf16), value_now)
        attended = attended + dot_nn((fixed * inverse).astype(bf16), pvalues)
        log_totals = jnp.where(lane_index((SEG, 8)) == head, highest + jnp.log(summed), log_totals)

        key_low = to_low(key_unit, head) * MEMORY_SCALE
        value_low = to_low(value, head)
        query_low = to_low(query_unit, head) * MEMORY_SCALE
        mem, swap = mem_ref[head], swap_ref[head]
        state_one, state_two = state[head, 0], state[head, 1]
        state_out[0, head, 0] = state_one.astype(bf16)
        state_out[0, head, 1] = state_two.astype(bf16)

        first = jnp.where(low, mem.astype(f32), state_one).astype(bf16)
        second = jnp.where(low, swap.astype(f32), state_two).astype(bf16)
        asked = jnp.where(low, query_low, older * swap_halves(query_low)).astype(bf16)
        inner = dot_nt(asked, first)
        answer = dot_nn((inner * jax.nn.sigmoid(inner)).astype(bf16), second)
        recalled = jnp.where(low, answer, 0.0) + jnp.where(low, older * swap_halves(answer), 0.0)
        if head:
            recalled = swap_halves(recalled)
        combined = combined + jnp.where(own, attended, 0.0) + recalled

        key_cut = jnp.where(low, key_low, 0.0)
        inner = dot_nt(key_cut.astype(bf16), mem)
        sigmoid = jax.nn.sigmoid(inner)
        active = inner * sigmoid
        slope = sigmoid * (1.0 + inner - active)
        active = active.astype(bf16)
        error = jnp.where(low, dot_nn(active, swap) - value_low, 0.0)
        descent = (dot_nt(error.astype(bf16), swap) * slope).astype(bf16)
        scale = jnp.where(low, columns[:, head : head + 1], columns[:, 8 + head : 9 + head])
        key_scaled = ((key_cut + swap_halves(key_cut)) * scale).astype(bf16)
        error_scaled = ((error + swap_halves(error)) * scale).astype(bf16)
        factor, blend = state_factors(scan["totals"], head, low)
        for member, old, added in (
            (0, state_one, dot_tn(descent, key_scaled)),
            (1, state_two, dot_tn(active, error_scaled)),
        ):
            turned = jnp.where(low, 0.0, blend * swap_halves(old))
            state[head, member] = factor * old + turned + added
    comb_ref[...] = combined.astype(bf16)
    total_out[...] = log_totals
    key_prev[...] = key_now
    value_prev[...] = value_now
    live_prev[...] = jnp.broadcast_to(scan["live"], (8, SEG))


def chain_rows(factor, term, start, lane):
    distance = 1
    while distance < SEG:
        inside = lane >= distance
        factor_before = jnp.where(inside, pltpu.roll(factor, distance, 1), 1.0)
        term_before = jnp.where(inside, pltpu.roll(term, distance, 1), 0.0)
        term = term + factor * term_before
        factor = factor * factor_before
        distance *= 2
    after = factor * start + term
    return jnp.where(lane == 0, start, pltpu.roll(after, 1, 1))


def backward_kernel(heads, plan, *refs):
    carried = len(plan.arrays)
    own, refs = refs[:18], refs[18:]
    sent, refs = refs[:carried], refs[carried:]
    made, refs = refs[:5], refs[5:]
    got, refs = refs[:carried], refs[carried:]
    begin, middle, finish = plan.phases(sent, got, refs[5:])
    at, last = pl.program_id(0), pl.num_programs(0) - 1

    @pl.when(at == 0)
    def _():
        greet_all(plan.axes, plan.kinds)
        begin()

    backward_step(heads, *own, *made, *refs[:5])

    @pl.when(at == 1)
    def _():
        middle()

    @pl.when(at == last)
    def _():
        finish()


def backward_step(
    heads,
    raw_ref,
    tail_ref,
    gate_ref,
    live_ref,
    live_prev_ref,
    key_ref,
    key_prev_ref,
    value_ref,
    value_prev_ref,
    total_ref,
    state_ref,
    grad_ref,
    conv_ref,
    mem_ref,
    swap_ref,
    persist_ref,
    length_ref,
    bias_ref,
    draw_ref,
    dmem_ref,
    dconv_ref,
    dpersist_ref,
    dbias_ref,
    ext,
    shifted_rows,
    key_carry,
    value_carry,
    late,
):
    at = pl.program_id(0)

    @pl.when(at == 0)
    def _():
        dmem_ref[...] = jnp.zeros_like(dmem_ref)
        dconv_ref[...] = jnp.zeros_like(dconv_ref)
        dpersist_ref[...] = jnp.zeros_like(dpersist_ref)
        dbias_ref[...] = jnp.zeros_like(dbias_ref)
        shifted_rows[:, 0:8, :] = jnp.zeros((3, 8, 3 * LANES), f32)
        key_carry[...] = jnp.zeros_like(key_carry)
        value_carry[...] = jnp.zeros_like(value_carry)
        late[...] = jnp.zeros_like(late)

    low = lane_index((SEG, LANES)) < HEAD_SIZE
    ext[0:8, :] = tail_ref[8:16, :].astype(f32)
    ext[8 : 8 + SEG, :] = raw_ref[...].astype(f32)
    here = (pl.num_programs(0) - 1 - at) * SEG
    place = places(length_ref, here + lax.broadcasted_iota(jnp.int32, (SEG, 1), 0))
    place_row = places(length_ref, here + lane_index((1, SEG)))
    pkeys, pvalues = persist_ref[0:P_SIZE, :], persist_ref[P_SIZE:, :]
    first_head = (lax.axis_index("seq") * HEAD_COUNT) // lax.axis_size("seq")
    mixed = mix_taps(ext, conv_ref, place)
    query_unit, query_inverse = unit_pair(mixed[:, :LANES], low)
    key_unit, key_inverse = unit_pair(mixed[:, LANES : 2 * LANES], low)
    value = mixed[:, 2 * LANES :]
    key_now, key_prev = key_ref[...], key_prev_ref[...]
    value_now, value_prev = value_ref[...], value_prev_ref[...]
    scan = gate_scan(heads, first_head, gate_ref[...], bias_ref, place_row, live_ref[0, 0:1, :])
    columns = write_columns(scan)
    masks = visible_masks(place, live_prev_ref[0, 0:1, :], scan["live"])
    older = jnp.where(place > lax.broadcasted_iota(jnp.int32, (SEG, 1), 0), 1.0, 0.0)
    grad = grad_ref[...].astype(f32)
    grad_query = jnp.zeros((SEG, LANES), f32)
    grad_key = key_carry[...]
    grad_value = value_carry[...]
    carry_key = jnp.zeros((SEG, LANES), f32)
    carry_value = jnp.zeros((SEG, LANES), f32)
    wide = lane_index((SEG, LANES))
    write_grads = jnp.zeros((SEG, LANES), f32)
    sublane = lax.broadcasted_iota(jnp.int32, (8, 1), 0)
    keep_start = jnp.zeros((8, 1), f32)
    mix_start = jnp.zeros((8, 1), f32)
    fade_start = jnp.zeros((8, 1), f32)
    for head in range(heads):
        own = low if head == 0 else jnp.logical_not(low)
        query = jnp.where(own, query_unit, 0.0).astype(bf16)
        grad_own = jnp.where(own, grad, 0.0).astype(bf16)
        total = total_ref[:, head : head + 1]
        scores = layer_scores(query, key_prev, key_now, pkeys, masks)
        probs = [jnp.exp(member - total) for member in scores]
        grads = [
            dot_nt(grad_own, pvalues),
            dot_nt(grad_own, value_prev),
            dot_nt(grad_own, value_now),
        ]
        spread = lane_sum(probs[0] * grads[0]) + lane_sum(probs[1] * grads[1] + probs[2] * grads[2])
        score_grads = [(one * (other - spread)).astype(bf16) for one, other in zip(probs, grads)]
        probs = [member.astype(bf16) for member in probs]
        back = dot_nn(score_grads[1], key_prev) + dot_nn(score_grads[2], key_now)
        back = SCORE_SCALE * back + dot_nn(score_grads[0], pkeys)
        grad_query = grad_query + jnp.where(own, back, 0.0)
        carry_key = carry_key + SCORE_SCALE * dot_tn(score_grads[1], query)
        grad_key = grad_key + SCORE_SCALE * dot_tn(score_grads[2], query)
        carry_value = carry_value + dot_tn(probs[1], grad_own)
        grad_value = grad_value + dot_tn(probs[2], grad_own)
        dpersist_ref[0:P_SIZE, :] += dot_tn(score_grads[0], query)
        dpersist_ref[P_SIZE:, :] += dot_tn(probs[0], grad_own)

        mem, swap = mem_ref[head], swap_ref[head]
        state_one, state_two = (state_ref[0, head, member].astype(f32) for member in range(2))
        late_one, late_two = late[head, 0], late[head, 1]

        query_low = to_low(query_unit, head) * MEMORY_SCALE
        grad_low = to_low(grad, head)
        first = jnp.where(low, mem.astype(f32), state_one).astype(bf16)
        second = jnp.where(low, swap.astype(f32), state_two).astype(bf16)
        asked = jnp.where(low, query_low, older * swap_halves(query_low)).astype(bf16)
        told = jnp.where(low, grad_low, older * swap_halves(grad_low)).astype(bf16)
        inner = dot_nt(asked, first)
        sigmoid = jax.nn.sigmoid(inner)
        active = inner * sigmoid
        slope = sigmoid * (1.0 + inner - active)
        grad_inner = (dot_nt(told, second) * slope).astype(bf16)
        back = dot_nn(grad_inner, first)
        back = jnp.where(low, MEMORY_SCALE * (back + older * swap_halves(back)), 0.0)
        grad_query = grad_query + (back if head == 0 else swap_halves(back))
        read_one = dot_tn(grad_inner, asked)
        read_two = dot_tn(active.astype(bf16), told)

        key_low = to_low(key_unit, head) * MEMORY_SCALE
        key_cut = jnp.where(low, key_low, 0.0)
        key_bf = key_cut.astype(bf16)
        inner = dot_nt(key_bf, mem)
        sigmoid = jax.nn.sigmoid(inner)
        active = inner * sigmoid
        slope = sigmoid * (1.0 + inner - active)
        curve = sigmoid * (1.0 - sigmoid) * (2.0 + inner - 2.0 * active)
        active = active.astype(bf16)
        error = jnp.where(low, dot_nn(active, swap) - to_low(value, head), 0.0)
        error_bf = error.astype(bf16)
        pulled = dot_nt(error_bf, swap)
        descent = (pulled * slope).astype(bf16)
        scale = jnp.where(low, columns[:, head : head + 1], columns[:, 8 + head : 9 + head])
        key_twice = key_cut + swap_halves(key_cut)
        error_twice = error + swap_halves(error)
        key_scaled = (key_twice * scale).astype(bf16)
        error_scaled = (error_twice * scale).astype(bf16)
        late_one_bf, late_two_bf = late_one.astype(bf16), late_two.astype(bf16)
        grad_descent = dot_nt(key_scaled, late_one_bf)
        back_key = dot_nn(descent, late_one_bf)
        back_error = dot_nn(active, late_two_bf)
        weight_grad = key_twice * back_key + error_twice * back_error
        grad_state_weight = lane_sum(jnp.where(low, weight_grad, 0.0))
        grad_write_weight = lane_sum(jnp.where(low, 0.0, weight_grad))
        write_grads = jnp.where(wide == head, grad_state_weight, write_grads)
        write_grads = jnp.where(wide == 8 + head, grad_write_weight, write_grads)
        grad_pulled = (grad_descent * slope).astype(bf16)
        back_error = back_error * scale
        back_error = back_error + swap_halves(back_error) + dot_nn(grad_pulled, swap)
        back_error = jnp.where(low, back_error, 0.0)
        back_error_bf = back_error.astype(bf16)
        grad_active = dot_nt(error_scaled, late_two_bf) + dot_nt(back_error_bf, swap)
        grad_inner = (grad_descent * pulled * curve + grad_active * slope).astype(bf16)
        back_key = back_key * scale
        back_key = back_key + swap_halves(back_key) + dot_nn(grad_inner, mem)
        back_key = jnp.where(low, MEMORY_SCALE * back_key, 0.0)
        grad_key = grad_key + (back_key if head == 0 else swap_halves(back_key))
        grad_value = grad_value - (back_error if head == 0 else swap_halves(back_error))
        write_one = dot_tn(grad_inner, key_bf)
        write_two = dot_tn(grad_pulled, error_bf) + dot_tn(active, back_error_bf)
        dmem_ref[head] += jnp.where(low, read_one + write_one, swap_halves(read_two + write_two))

        factor, blend = state_factors(scan["totals"], head, low)
        same = late_one * state_one + late_two * state_two
        cross = late_one * swap_halves(state_one) + late_two * swap_halves(state_two)
        same_low = jnp.sum(lane_sum(jnp.where(low, same, 0.0)), axis=0, keepdims=True)
        same_high = jnp.sum(lane_sum(jnp.where(low, 0.0, same)), axis=0, keepdims=True)
        cross_high = jnp.sum(lane_sum(jnp.where(low, 0.0, cross)), axis=0, keepdims=True)
        keep_start = jnp.where(sublane == head, same_low, keep_start)
        fade_start = jnp.where(sublane == head, same_high, fade_start)
        mix_start = jnp.where(sublane == head, cross_high, mix_start)
        for member, old, read in ((0, late_one, read_one), (1, late_two, read_two)):
            turned = jnp.where(low, blend * swap_halves(old), read)
            late[head, member] = factor * old + turned

    lane = lane_index((8, SEG))
    write_rows = jnp.transpose(write_grads)
    grad_state_rows, grad_write_rows = write_rows[0:8], write_rows[8:16]
    written = scan["written"]
    keep_grads = chain_rows(scan["carry"], grad_state_rows * written, keep_start, lane)
    mix_grads = chain_rows(scan["carry"], grad_write_rows * written, mix_start, lane)
    mix_next = scan["carry"] * mix_grads + grad_write_rows * written
    fade_grads = chain_rows(scan["fade"], mix_next, fade_start, lane)
    grad_written = grad_state_rows * scan["keep_after"] + grad_write_rows * scan["reach"]
    grad_carry = keep_grads * scan["keep_after"] + mix_grads * scan["reach"]
    grad_fade = fade_grads * scan["fade_after"]
    used = sublane < heads
    forget, momentum, step = scan["forget"], scan["momentum"], scan["step"]
    forget_back = -grad_fade * scan["keep"] * forget * (1.0 - forget)
    momentum_back = grad_carry * scan["keep"] * momentum * (1.0 - momentum)
    step_back = -THETA_SCALE * grad_written * scan["live"] * step * (1.0 - step)
    gate_back = jnp.concatenate(
        [
            jnp.where(used, forget_back, 0.0),
            jnp.where(used, momentum_back, 0.0),
            jnp.where(used, step_back, 0.0),
            jnp.zeros((LANES - 24, SEG), f32),
        ],
        axis=0,
    )
    gate_back = jnp.transpose(gate_back)
    dbias_ref[0:1, :] += jnp.sum(gate_back, axis=0, keepdims=True)
    draw_ref[:, 3 * LANES :] = gate_back.astype(bf16)

    key_carry[...] = carry_key
    value_carry[...] = carry_value
    grad_mixed = jnp.concatenate(
        [
            unit_pair_pull(query_unit, query_inverse, grad_query, low),
            unit_pair_pull(key_unit, key_inverse, grad_key, low),
            grad_value,
        ],
        axis=1,
    )
    back = conv_ref[0:1, :] * grad_mixed
    dconv_ref[0:1, :] += jnp.sum(grad_mixed * ext[8 : 8 + SEG, :], axis=0, keepdims=True)
    for offset in range(1, 4):
        kept = jnp.where(place >= offset, grad_mixed, 0.0)
        member = offset - 1
        shifted_rows[member, SEG : SEG + 8, :] = shifted_rows[member, 0:8, :]
        shifted_rows[member, 0:SEG, :] = kept
        back = back + conv_ref[offset : offset + 1, :] * shifted_rows[
            member, offset : offset + SEG, :
        ]
        dconv_ref[offset : offset + 1, :] += jnp.sum(
            kept * ext[8 - offset : 8 - offset + SEG, :], axis=0, keepdims=True
        )
    draw_ref[:, : 3 * LANES] = back.astype(bf16)


def block_of(shape, index):
    return pl.BlockSpec(shape, index)


def whole_of(array):
    zeros = (0,) * array.ndim
    return pl.BlockSpec(array.shape, lambda n: zeros)


def mix_forward(collective, plan, heads, raw, gates, live, *constants):
    length = raw.shape[0]
    count = length // SEG
    row_block = pl.BlockSpec((SEG, LANES), lambda n: (n, 0))
    smem = pl.BlockSpec(memory_space=pltpu.SMEM)
    carried_in, carried_out = plan.specs(True)
    return pl.pallas_call(
        partial(forward_kernel, heads, plan),
        grid=(count,),
        in_specs=[
            pl.BlockSpec((SEG, 3 * LANES), lambda n: (n, 0)),
            row_block,
            pl.BlockSpec((1, 8, SEG), lambda n: (n, 0, 0)),
        ]
        + [whole_of(member) for member in constants[:4]]
        + [smem, smem]
        + carried_in,
        out_specs=[
            row_block,
            row_block,
            row_block,
            pl.BlockSpec((SEG, 8), lambda n: (n, 0)),
            pl.BlockSpec((1, heads, 2, MH, LANES), lambda n: (n, 0, 0, 0, 0)),
        ]
        + carried_out,
        out_shape=[
            jax.ShapeDtypeStruct((length, LANES), bf16),
            jax.ShapeDtypeStruct((length, LANES), bf16),
            jax.ShapeDtypeStruct((length, LANES), bf16),
            jax.ShapeDtypeStruct((length, 8), f32),
            jax.ShapeDtypeStruct((count, heads, 2, MH, LANES), bf16),
        ]
        + plan.shapes,
        scratch_shapes=[
            pltpu.VMEM((SEG + 8, 3 * LANES), f32),
            pltpu.VMEM((SEG, LANES), bf16),
            pltpu.VMEM((SEG, LANES), bf16),
            pltpu.VMEM((8, SEG), f32),
            pltpu.VMEM((heads, 2, MH, LANES), f32),
        ]
        + plan.scratch,
        compiler_params=pltpu.CompilerParams(
            dimension_semantics=("arbitrary",),
            collective_id=collective,
            has_side_effects=True,
            vmem_limit_bytes=VMEM_GRANT,
        ),
        name="mix_forward",
    )(raw, gates, live, *constants, *plan.arrays)


def mix_backward(
    collective, plan, heads, raw, gates, live, keys, values, totals, states, grad, *constants
):
    length = raw.shape[0]
    count = length // SEG

    def here(n):
        return count - 1 - n

    def before(n):
        return jnp.maximum(count - 2 - n, 0)

    row_block = pl.BlockSpec((SEG, LANES), lambda n: (here(n), 0))
    prev_block = pl.BlockSpec((SEG, LANES), lambda n: (before(n), 0))
    tail_rows = SEG // 16
    smem = pl.BlockSpec(memory_space=pltpu.SMEM)
    carried_in, carried_out = plan.specs(True)
    return pl.pallas_call(
        partial(backward_kernel, heads, plan),
        grid=(count,),
        in_specs=[
            pl.BlockSpec((SEG, 3 * LANES), lambda n: (here(n), 0)),
            pl.BlockSpec((16, 3 * LANES), lambda n: (jnp.maximum(here(n) * tail_rows - 1, 0), 0)),
            row_block,
            pl.BlockSpec((1, 8, SEG), lambda n: (here(n), 0, 0)),
            pl.BlockSpec((1, 8, SEG), lambda n: (before(n), 0, 0)),
            row_block,
            prev_block,
            row_block,
            prev_block,
            pl.BlockSpec((SEG, 8), lambda n: (here(n), 0)),
            pl.BlockSpec((1, heads, 2, MH, LANES), lambda n: (here(n), 0, 0, 0, 0)),
            row_block,
        ]
        + [whole_of(member) for member in constants[:4]]
        + [smem, smem]
        + carried_in,
        out_specs=[
            pl.BlockSpec((SEG, 4 * LANES), lambda n: (here(n), 0)),
            pl.BlockSpec((heads, MH, LANES), lambda n: (0, 0, 0)),
            pl.BlockSpec((8, 3 * LANES), lambda n: (0, 0)),
            pl.BlockSpec((2 * P_SIZE, LANES), lambda n: (0, 0)),
            pl.BlockSpec((8, LANES), lambda n: (0, 0)),
        ]
        + carried_out,
        out_shape=[
            jax.ShapeDtypeStruct((length, 4 * LANES), bf16),
            jax.ShapeDtypeStruct((heads, MH, LANES), f32),
            jax.ShapeDtypeStruct((8, 3 * LANES), f32),
            jax.ShapeDtypeStruct((2 * P_SIZE, LANES), f32),
            jax.ShapeDtypeStruct((8, LANES), f32),
        ]
        + plan.shapes,
        scratch_shapes=[
            pltpu.VMEM((SEG + 8, 3 * LANES), f32),
            pltpu.VMEM((3, SEG + 8, 3 * LANES), f32),
            pltpu.VMEM((SEG, LANES), f32),
            pltpu.VMEM((SEG, LANES), f32),
            pltpu.VMEM((heads, 2, MH, LANES), f32),
        ]
        + plan.scratch,
        compiler_params=pltpu.CompilerParams(
            dimension_semantics=("arbitrary",),
            collective_id=collective,
            has_side_effects=True,
            vmem_limit_bytes=VMEM_GRANT,
        ),
        name="mix_backward",
    )(
        raw,
        raw,
        gates,
        live,
        live,
        keys,
        keys,
        values,
        values,
        totals,
        states,
        grad,
        *constants,
        *plan.arrays,
    )


class PlaneGather:
    def __init__(self, seqs, source, target, sems):
        self.source, self.target = source, target
        self.local, self.far_send, self.far_recv = sems[:3]
        self.near_send, self.near_recv, self.relay_send, self.relay_recv = sems[3:]
        self.chips = seqs // 2
        self.relayed = self.chips == 4
        self.seq, self.line = lax.axis_index("seq"), lax.axis_index("fsdp")
        self.chip, self.core = self.seq // 2, lax.rem(self.seq, 2)
        self.half = source.shape[0] // 2

    @staticmethod
    def sems(seqs):
        dma = pltpu.SemaphoreType.DMA
        return [dma((1,))] + [dma((seqs // 2,))] * 4 + [dma((2,))] * 2

    def chip_at(self, k):
        side = math.isqrt(self.chips)
        across = lax.rem(lax.rem(self.chip, side) + lax.rem(k, side), side)
        along = lax.rem(self.chip // side + k // side, side)
        return along * side + across

    def copy(self, source, target, send, recv, place):
        return pltpu.make_async_remote_copy(
            src_ref=source,
            dst_ref=target,
            send_sem=send,
            recv_sem=recv,
            device_id=(place, self.line),
            device_id_type=MESH,
        )

    def own(self):
        return pltpu.make_async_copy(self.source, self.target.at[self.seq], self.local.at[0])

    def far(self, q, slot):
        place = 2 * q + self.core
        block = self.target.at[2 * slot + self.core]
        return self.copy(self.source, block, self.far_send.at[q], self.far_recv.at[slot], place)

    def near(self, q, side):
        block = self.target.at[2 * q + (self.core if side == 0 else 1 - self.core)]
        place = 2 * self.chip + 1 - self.core
        return self.copy(block, block, self.near_send.at[q], self.near_recv.at[q], place)

    def near_own(self):
        block = self.target.at[self.seq]
        place = 2 * self.chip + 1 - self.core
        send, recv = self.near_send.at[self.chip], self.near_recv.at[self.chip]
        return self.copy(self.source, block, send, recv, place)

    def relay(self, part, q, to):
        rows = pl.ds(part * self.half, self.half)
        block = self.target.at[2 * q + self.core, rows]
        send, recv = self.relay_send.at[part], self.relay_recv.at[part]
        return self.copy(block, block, send, recv, 2 * to + self.core)

    def loop(self, first, body):
        def step(k, carry):
            body(k)
            return carry

        lax.fori_loop(first, self.chips, step, 0)

    def start(self):
        self.near_own().start()
        if self.relayed:
            for k in (1, 2):
                self.far(self.chip_at(k), self.chip).start()
        else:
            self.loop(1, lambda k: self.far(self.chip_at(k), self.chip).start())
        self.own().start()

    def step(self, k):
        q = self.chip_at(k)

        @pl.when(k == 0)
        def _():
            self.own().wait()

        if self.relayed:
            across, along, diagonal = (self.chip_at(i) for i in (1, 2, 3))

            @pl.when(k == 1)
            def _():
                self.far(across, across).wait_recv()
                self.relay(0, across, along).start()
                self.near(across, 0).start()
                self.far(along, along).wait_recv()
                self.relay(1, along, across).start()
                self.near(along, 0).start()

            @pl.when(k == 3)
            def _():
                self.relay(0, diagonal, along).wait_recv()
                self.relay(1, diagonal, across).wait_recv()
                self.near(diagonal, 0).start()

        else:

            @pl.when(k > 0)
            def _():
                self.far(q, q).wait_recv()
                self.near(q, 0).start()

        self.near(q, 1).wait_recv()

    def finish(self):
        self.near_own().wait_send()
        self.loop(1, lambda k: self.near(self.chip_at(k), 0).wait_send())
        if self.relayed:
            across, along = self.chip_at(1), self.chip_at(2)
            self.far(across, across).wait_send()
            self.far(along, along).wait_send()
            self.relay(0, across, along).wait_send()
            self.relay(1, along, across).wait_send()
        else:
            self.loop(1, lambda k: self.far(self.chip_at(k), self.chip_at(k)).wait_send())


def exchange_phases(axes, counts, inputs, outputs, scratch):
    seqs, lines = axes
    chips = seqs // 2
    devices = seqs * lines
    seq, line = lax.axis_index("seq"), lax.axis_index("fsdp")
    me = seq * lines + line
    chip, core = seq // 2, lax.rem(seq, 2)
    sibling = (2 * chip + 1 - core, line)

    def twin(q):
        return (2 * q + core, line)

    def point(i):
        return (i // lines, lax.rem(i, lines))

    def loop(first, last, body):
        def step(k, carry):
            body(k)
            return carry

        lax.fori_loop(first, last, step, 0)

    position = 0
    groups = []
    for count in counts:
        groups.append((inputs[position : position + count], outputs[position : position + count]))
        position += count
    scratch = list(scratch)

    def take(number):
        taken = scratch[:number]
        del scratch[:number]
        return taken

    starts = []

    sums = []
    for source, target in zip(*groups[5]):
        pair, landed, pair_send, pair_recv, far_send, far_recv = take(6)

        def pair_copy(q, source=source, pair=pair, send=pair_send, recv=pair_recv):
            return pltpu.make_async_remote_copy(
                src_ref=source.at[2 * q + 1 - core],
                dst_ref=pair.at[q],
                send_sem=send.at[q],
                recv_sem=recv.at[q],
                device_id=sibling,
                device_id_type=MESH,
            )

        def far_copy(q, slot, pair=pair, landed=landed, send=far_send, recv=far_recv):
            return pltpu.make_async_remote_copy(
                src_ref=pair.at[q],
                dst_ref=landed.at[slot],
                send_sem=send.at[q],
                recv_sem=recv.at[slot],
                device_id=twin(q),
                device_id_type=MESH,
            )

        starts.append(
            lambda f=pair_copy: loop(1, chips + 1, lambda k: f(lax.rem(chip + k, chips)).start())
        )
        sums.append((source, target, pair, landed, pair_copy, far_copy))

    spread = []
    for source, target in zip(*groups[0]):
        gather = PlaneGather(seqs, source, target, take(7))
        starts.append(gather.start)
        spread.append(gather)

    direct = []
    for kind, (sources, targets) in (
        ("plane", groups[1]),
        ("line", groups[2]),
        ("every", groups[3]),
        ("all", groups[4]),
    ):
        for source, target in zip(sources, targets):
            local, send, recv = take(3)
            if kind == "plane":
                number, mine = seqs, seq
            elif kind == "line":
                number, mine = lines, line
            else:
                number, mine = devices, me

            def piece(i, source=source, kind=kind, number=number):
                if kind == "all" or (kind == "line" and source.ndim == 2):
                    return source
                if kind == "every" and source.shape[0] != number:
                    return source.at[i // lines]
                return source.at[i]

            def place(i, kind=kind):
                if kind == "plane":
                    return (i, line)
                if kind == "line":
                    return (seq, i)
                return point(i)

            def copy(i, slot, target=target, send=send, recv=recv, piece=piece, place=place):
                return pltpu.make_async_remote_copy(
                    src_ref=piece(i),
                    dst_ref=target.at[slot],
                    send_sem=send.at[i],
                    recv_sem=recv.at[slot],
                    device_id=place(i),
                    device_id_type=MESH,
                )

            def own(target=target, local=local, piece=piece, mine=mine):
                return pltpu.make_async_copy(piece(mine), target.at[mine], local.at[0])

            def start(copy=copy, own=own, mine=mine, number=number):
                loop(1, number, lambda k: copy(lax.rem(mine + k, number), mine).start())
                own().start()

            starts.append(start)
            direct.append((own, copy, mine, number))

    relays = []
    for source, target in zip(*groups[6]):
        local, plane_send, plane_recv, line_send, line_recv = take(5)

        def copy(i, slot, source=source, target=target, send=plane_send, recv=plane_recv):
            return pltpu.make_async_remote_copy(
                src_ref=source.at[i],
                dst_ref=target.at[line, slot],
                send_sem=send.at[i],
                recv_sem=recv.at[slot],
                device_id=(i, line),
                device_id_type=MESH,
            )

        def own(source=source, target=target, local=local):
            return pltpu.make_async_copy(source.at[seq], target.at[line, seq], local.at[0])

        def onward(i, slot, target=target, send=line_send, recv=line_recv):
            return pltpu.make_async_remote_copy(
                src_ref=target.at[slot],
                dst_ref=target.at[slot],
                send_sem=send.at[i],
                recv_sem=recv.at[slot],
                device_id=(seq, i),
                device_id_type=MESH,
            )

        def start(copy=copy, own=own):
            loop(1, seqs, lambda k: copy(lax.rem(seq + k, seqs), seq).start())
            own().start()

        starts.insert(0, start)
        relays.append((own, copy, onward))

    merges = []
    rows = 32
    for source, target in zip(*groups[7]):
        landed, summed, local, line_send, line_recv, plane_send, plane_recv = take(7)

        def copy(i, slot, source=source, landed=landed, send=line_send, recv=line_recv):
            return pltpu.make_async_remote_copy(
                src_ref=source.at[i],
                dst_ref=landed.at[slot],
                send_sem=send.at[i],
                recv_sem=recv.at[slot],
                device_id=(seq, i),
                device_id_type=MESH,
            )

        def own(source=source, landed=landed, local=local):
            return pltpu.make_async_copy(source.at[line], landed.at[line], local.at[0])

        def onward(i, slot, summed=summed, target=target, send=plane_send, recv=plane_recv):
            return pltpu.make_async_remote_copy(
                src_ref=summed.at[i],
                dst_ref=target.at[slot],
                send_sem=send.at[i],
                recv_sem=recv.at[slot],
                device_id=(i, line),
                device_id_type=MESH,
            )

        def keep(summed=summed, target=target, local=local):
            return pltpu.make_async_copy(summed.at[seq], target.at[seq], local.at[0])

        def start(copy=copy, own=own):
            loop(1, lines, lambda k: copy(lax.rem(line + k, lines), line).start())
            own().start()

        starts.insert(0, start)
        merges.append((landed, summed, own, copy, onward, keep))

    def begin():
        for start in starts:
            start()

    def middle():
        for source, target, pair, landed, pair_copy, far_copy in sums:

            def combine(k, source=source, pair=pair, pair_copy=pair_copy, far_copy=far_copy):
                q = lax.rem(chip + k, chips)
                pair_copy(q).wait_recv()

                def add(r):
                    part = pl.ds(pl.multiple_of(r * rows, rows), rows)
                    both = source[2 * q + core, part, :].astype(f32) + pair[q, part, :].astype(f32)
                    pair[q, part, :] = both.astype(bf16)

                loop(0, source.shape[1] // rows, add)

                @pl.when(k < chips)
                def _():
                    far_copy(q, chip).start()

            loop(1, chips + 1, combine)
        for own, copy, onward in relays:
            loop(1, seqs, lambda k, f=copy: f(lax.rem(seq + k, seqs), lax.rem(seq + k, seqs)).wait_recv())
            own().wait()
            loop(1, lines, lambda k, f=onward: f(lax.rem(line + k, lines), line).start())
        for gather in spread:
            gather.step(0)
            gather.step(1)
        for landed, summed, own, copy, onward, keep in merges:
            loop(1, lines, lambda k, f=copy: f(lax.rem(line + k, lines), lax.rem(line + k, lines)).wait_recv())
            own().wait()

            def add_up(k, landed=landed, summed=summed, onward=onward):
                i = lax.rem(seq + k, seqs)
                whole = landed[0, i].astype(f32)
                for member in range(1, lines):
                    whole = whole + landed[member, i].astype(f32)
                summed[i] = whole.astype(bf16)

                @pl.when(k < seqs)
                def _():
                    onward(i, seq).start()

            loop(1, seqs + 1, add_up)
            keep().start()

    def finish():
        for own, copy, mine, number in direct:

            def end(k, copy=copy, mine=mine, number=number):
                i = lax.rem(mine + k, number)
                copy(i, i).wait_recv()
                copy(i, i).wait_send()

            loop(1, number, end)
            own().wait()
        for own, copy, onward in relays:
            loop(1, seqs, lambda k, f=copy: f(lax.rem(seq + k, seqs), seq).wait_send())

            def end_relay(k, onward=onward):
                i = lax.rem(line + k, lines)
                onward(i, i).wait_recv()
                onward(i, line).wait_send()

            loop(1, lines, end_relay)
        for gather in spread:
            gather.loop(2, gather.step)
            gather.finish()
        for source, target, pair, landed, pair_copy, far_copy in sums:

            def end_sum(k, far_copy=far_copy):
                q = lax.rem(chip + k, chips)
                far_copy(q, q).wait_recv()

            loop(1, chips, end_sum)

            def add_all(r, target=target, pair=pair, landed=landed):
                part = pl.ds(pl.multiple_of(r * rows, rows), rows)
                whole = pair[chip, part, :].astype(f32)
                for k in range(1, chips):
                    whole = whole + landed[lax.rem(chip + k, chips), part, :].astype(f32)
                target[part, :] = whole

            loop(0, target.shape[0] // rows, add_all)
            loop(1, chips, lambda k, f=far_copy: f(lax.rem(chip + k, chips), chip).wait_send())
            loop(0, chips, lambda q, f=pair_copy: f(q).wait_send())
        for landed, summed, own, copy, onward, keep in merges:
            loop(1, lines, lambda k, f=copy: f(lax.rem(line + k, lines), line).wait_send())

            def end_merge(k, onward=onward):
                i = lax.rem(seq + k, seqs)
                onward(i, i).wait_recv()
                onward(i, seq).wait_send()

            loop(1, seqs, end_merge)
            keep().wait()

    return begin, middle, finish


def greet_all(axes, kinds):
    seqs, lines = axes
    seq, line = lax.axis_index("seq"), lax.axis_index("fsdp")
    barrier = pltpu.get_barrier_semaphore()

    def signal(place):
        pl.semaphore_signal(barrier, inc=1, device_id=place, device_id_type=MESH)

    def loop(last, body):
        def step(k, carry):
            body(k)
            return carry

        lax.fori_loop(1, last, step, 0)

    if "all" in kinds:
        devices = seqs * lines
        me = seq * lines + line

        def greet(k):
            i = lax.rem(me + k, devices)
            signal((i // lines, lax.rem(i, lines)))

        loop(devices, greet)
        pl.semaphore_wait(barrier, devices - 1)
        return
    met = 0
    if "plane" in kinds:
        loop(seqs, lambda k: signal((lax.rem(seq + k, seqs), line)))
        met += seqs - 1
    if "line" in kinds:
        loop(lines, lambda k: signal((seq, lax.rem(line + k, lines))))
        met += lines - 1
    pl.semaphore_wait(barrier, met)


KINDS = ("gathers", "planes", "to_line", "everys", "alls", "scatters", "relays", "merges")


class Exchange:
    def __init__(self, **arrays):
        self.axes = seqs, lines = lax.axis_size("seq"), lax.axis_size("fsdp")
        chips, devices = seqs // 2, seqs * lines
        dma = pltpu.SemaphoreType.DMA
        groups = [tuple(arrays.get(kind, ())) for kind in KINDS]
        self.counts = tuple(len(group) for group in groups)
        self.arrays = [array for group in groups for array in group]
        scratch = {kind: [] for kind in KINDS}
        shapes, self.in_vmem = [], []
        kinds = set()
        for kind, group in zip(KINDS, groups):
            for array in group:
                shape, dtype = array.shape, array.dtype
                if kind == "gathers":
                    scratch[kind] += PlaneGather.sems(seqs)
                    shape = (seqs,) + shape
                elif kind == "planes":
                    scratch[kind] += [dma((1,)), dma((seqs,)), dma((seqs,))]
                elif kind == "to_line":
                    scratch[kind] += [dma((1,)), dma((lines,)), dma((lines,))]
                    shape = (lines,) + shape[-2:]
                elif kind == "everys":
                    scratch[kind] += [dma((1,)), dma((devices,)), dma((devices,))]
                    shape = (devices,) + shape[1:]
                elif kind == "alls":
                    scratch[kind] += [dma((1,)), dma((devices,)), dma((devices,))]
                    shape = (devices,) + shape
                elif kind == "scatters":
                    half = pltpu.VMEM((chips,) + shape[1:], bf16)
                    scratch[kind] += [half, half] + [dma((chips,))] * 4
                    shape, dtype = shape[1:], f32
                elif kind == "relays":
                    scratch[kind] += [dma((1,))] + [dma((seqs,))] * 2 + [dma((lines,))] * 2
                    shape = (lines,) + shape
                else:
                    scratch[kind] += [pltpu.VMEM(shape, bf16), pltpu.VMEM(shape[1:], bf16), dma((1,))]
                    scratch[kind] += [dma((lines,))] * 2 + [dma((seqs,))] * 2
                    shape = shape[1:]
                shapes.append(jax.ShapeDtypeStruct(shape, dtype))
                self.in_vmem.append(kind == "scatters")
                if kind in ("everys", "alls"):
                    kinds.add("all")
                if kind not in ("to_line",):
                    kinds.add("plane")
                if kind in ("to_line", "relays", "merges"):
                    kinds.add("line")
        self.kinds = kinds
        self.shapes = shapes
        order = ("scatters", "gathers", "planes", "to_line", "everys", "alls", "relays", "merges")
        self.scratch = [member for kind in order for member in scratch[kind]]

    def specs(self, gridded):
        if gridded:
            vmem = [
                pl.BlockSpec(
                    array.shape, lambda n, z=(0,) * array.ndim: z, pipeline_mode=pl.Buffered(1)
                )
                for array in self.arrays
            ]
            out = [
                pl.BlockSpec(array.shape, lambda n, z=(0,) * len(array.shape): z)
                for array in self.shapes
            ]
        else:
            vmem = out = [pl.BlockSpec(memory_space=pltpu.VMEM)] * len(self.arrays)
        plain = pl.BlockSpec(memory_space=pl.ANY)
        first = [one if inside else plain for one, inside in zip(vmem, self.in_vmem)]
        second = [one if inside else plain for one, inside in zip(out, self.in_vmem)]
        return first, second

    def phases(self, inputs, outputs, scratch):
        return exchange_phases(self.axes, self.counts, inputs, outputs, scratch)


def exchange_kernel(plan, *refs):
    number = len(plan.arrays)
    greet_all(plan.axes, plan.kinds)
    for phase in plan.phases(refs[:number], refs[number : 2 * number], refs[2 * number :]):
        phase()


def exchange(name, collective, **arrays):
    plan = Exchange(**arrays)
    in_specs, out_specs = plan.specs(False)
    return pl.pallas_call(
        partial(exchange_kernel, plan),
        out_shape=plan.shapes,
        in_specs=in_specs,
        out_specs=out_specs,
        scratch_shapes=plan.scratch,
        compiler_params=pltpu.CompilerParams(
            collective_id=collective, has_side_effects=True, vmem_limit_bytes=VMEM_GRANT
        ),
        name=name,
    )(*plan.arrays)


def round_up(number, step):
    return -(-number // step) * step


class Sizes:
    def __init__(self, seqs, lines):
        self.seqs, self.lines = seqs, lines
        self.chips, self.devices = seqs // 2, seqs * lines
        self.groups = min(HEAD_COUNT, seqs)
        self.copies = seqs // self.groups
        self.heads = HEAD_COUNT // self.groups
        self.width = self.heads * HEAD_SIZE
        self.share = D // self.devices
        self.memory = MH // self.devices
        self.piece = D // seqs
        self.hidden = FF // lines
        self.slab = self.hidden // seqs
        self.gate_at = round_up(3 * self.share, 8)
        self.mem_at = self.gate_at + round_up(max(self.share, 2 * P_SIZE), 8)
        self.rest_at = self.mem_at + round_up(self.heads * self.memory, 8)
        self.weight_rows = round_up(self.rest_at + 8, 16)
        self.grad_mem_at = round_up(4 * self.share, 8)
        self.grad_rest_at = self.grad_mem_at + round_up(self.heads * self.memory, 8)
        self.grad_rows = round_up(self.grad_rest_at + 16, 16)


def gate_choice(sizes, group, turned):
    shape = (LANES, 3 * HEAD_COUNT) if turned else (3 * HEAD_COUNT, LANES)
    lane = lax.broadcasted_iota(jnp.int32, shape, 0 if turned else 1)
    column = lax.broadcasted_iota(jnp.int32, shape, 1 if turned else 0)
    head = lane % 8
    chosen = (lane // 8 == column // HEAD_COUNT) & (head < sizes.heads)
    chosen = chosen & (column % HEAD_COUNT == group * sizes.heads + head)
    return jnp.where(chosen, 1.0, 0.0).astype(bf16)


def first_kernel(
    sizes,
    token_ref,
    qkv_ref,
    gate_ref,
    conv_ref,
    pkey_ref,
    pvalue_ref,
    gain_one_ref,
    gain_two_ref,
    live_ref,
    mem_ref,
    ffn_gate_ref,
    ffn_up_ref,
    ffn_down_ref,
    out_ref,
    normed_out,
    raw_out,
    gate_out,
    matrix_out,
    mem_out,
    swap_out,
    gain_out,
    taps_out,
    persist_out,
    live_out,
    ffn_out,
    out_rows,
    rows_all,
    pack,
    pack_rows,
    ffn_pack,
    got,
    conv_full,
    persist_full,
    mem_full,
    matrix_full,
    *sems,
):
    seqs, lines, share, width = sizes.seqs, sizes.lines, sizes.share, sizes.width
    seq, line = lax.axis_index("seq"), lax.axis_index("fsdp")
    group = seq // sizes.copies
    axes = (seqs, lines)
    greet_all(axes, ("plane", "line"))
    gather = PlaneGather(seqs, token_ref, rows_all, sems[:7])
    gather.start()
    weights = exchange_phases(axes, (0, 0, 0, 0, 0, 0, 1, 0), [pack], [got], sems[7:12])
    ffn = exchange_phases(axes, (0, 1, 0, 0, 0, 0, 0, 0), [ffn_pack], [ffn_out], sems[12:15])
    outs = exchange_phases(axes, (0, 0, 1, 0, 0, 0, 0, 0), [out_ref], [out_rows], sems[15:18])

    gate_at, mem_at, rest_at = sizes.gate_at, sizes.mem_at, sizes.rest_at
    pack_rows[...] = jnp.zeros_like(pack_rows)
    pack_rows[gate_at : gate_at + P_SIZE, HEAD_SIZE : HEAD_SIZE + share] = pkey_ref[...].astype(f32)
    pack_rows[gate_at + P_SIZE : gate_at + 2 * P_SIZE, HEAD_SIZE : HEAD_SIZE + share] = pvalue_ref[
        ...
    ].astype(f32)
    pack_rows[rest_at : rest_at + 4, : 3 * share] = conv_ref[...].astype(f32)
    pack_rows[rest_at + 4 : rest_at + 5, :share] = gain_one_ref[...].astype(f32)
    pack_rows[rest_at + 5 : rest_at + 6, :share] = gain_two_ref[...].astype(f32)
    live = live_ref[...].astype(f32)
    pack_rows[rest_at + 6 : rest_at + 7, :] = live[:, :LANES]
    pack_rows[rest_at + 7 : rest_at + 8, :] = live[:, LANES:]
    qkv = qkv_ref[...].astype(f32)
    gate = gate_ref[...]
    for to in range(seqs):
        other = to // sizes.copies
        for part in range(3):
            first = part * D + other * width
            pack_rows[part * share : (part + 1) * share, :width] = qkv[:, first : first + width]
        chosen = dot_nn(gate, gate_choice(sizes, other, False))
        pack_rows[gate_at : gate_at + share, :HEAD_SIZE] = chosen[:, :HEAD_SIZE]
        for head in range(sizes.heads):
            first = mem_at + head * sizes.memory
            pack_rows[first : first + sizes.memory, :] = mem_ref[other * sizes.heads + head].astype(
                f32
            )
        pack[to] = pack_rows[...].astype(bf16)
    weights[0]()
    for to in range(seqs):
        columns = slice(to * sizes.slab, (to + 1) * sizes.slab)
        piece = sizes.piece
        ffn_pack[to, :piece, :] = ffn_gate_ref[:, columns]
        ffn_pack[to, piece : 2 * piece, :] = ffn_up_ref[:, columns]
        turned = jnp.transpose(ffn_down_ref[columns, :].astype(f32))
        ffn_pack[to, 2 * piece :, :] = turned.astype(bf16)
    ffn[0]()
    outs[0]()
    weights[1]()
    gather.step(0)
    gather.step(1)
    weights[2]()

    aligned = share % 16 == 0
    matrix = matrix_out if aligned else matrix_full
    lane = lane_index((share, LANES))
    for i in range(sizes.devices):
        block = got[i % lines, i // lines].astype(f32)
        rows = slice(i * share, (i + 1) * share)
        for part in range(3):
            columns = slice(part * LANES, (part + 1) * LANES)
            matrix[rows, columns] = block[part * share : (part + 1) * share].astype(matrix.dtype)
        chosen = jnp.where(lane < 24, block[gate_at : gate_at + share], 0.0)
        matrix[rows, 3 * LANES :] = chosen.astype(matrix.dtype)
        for head in range(sizes.heads):
            first = mem_at + head * sizes.memory
            mem_full[head, i * sizes.memory : (i + 1) * sizes.memory, :] = block[
                first : first + sizes.memory
            ]
        rest = block[rest_at : rest_at + 8]
        conv_full[0:4, i * 3 * share : (i + 1) * 3 * share] = rest[0:4, : 3 * share]
        gain_out[4:6, i * share : (i + 1) * share] = rest[4:6, :share]
    if not aligned:
        matrix_out[...] = matrix_full[...].astype(bf16)
    for head in range(sizes.heads):
        mem_out[head] = mem_full[head].astype(bf16)
        swap_out[head] = swap_halves(mem_full[head]).astype(bf16)
    taps_out[...] = jnp.zeros_like(taps_out)
    for part in range(3):
        whole = conv_full[:, part * D : (part + 1) * D]
        turned = pltpu.roll(whole, lax.rem(D - group * width, D), 1)
        taps_out[0:4, part * LANES : part * LANES + width] = turned[0:4, :width]
    persist_full[...] = jnp.zeros_like(persist_full)
    for part in range(width // share):
        i = group * (width // share) + part
        block = got[lax.rem(i, lines), i // lines].astype(f32)
        persist_full[:, part * share : (part + 1) * share] = block[
            gate_at : gate_at + 2 * P_SIZE, HEAD_SIZE : HEAD_SIZE + share
        ]
    persist_out[...] = persist_full[...].astype(bf16)
    for s in range(seqs):
        block = got[line, s].astype(f32)
        live_out[s] = jnp.zeros((8, SEG), f32)
        live_out[s, 0:1, :LANES] = block[rest_at + 6 : rest_at + 7]
        live_out[s, 0:1, LANES:] = block[rest_at + 7 : rest_at + 8]

    gain = gain_out[4:5, :]

    def work(k, carry):
        q = gather.chip_at(k)

        @pl.when(k > 1)
        def _():
            gather.step(k)

        both = pl.ds(2 * q, 2)
        rows = rows_all[both].reshape(2 * SEG, D).astype(f32)
        normed = (rows * norm_scale(rows) * gain).astype(bf16)
        projected = dot_nn(normed, matrix_out[...])
        normed_out[both] = normed.reshape(2, SEG, D)
        raw_out[both] = projected[:, : 3 * LANES].astype(bf16).reshape(2, SEG, 3 * LANES)
        gate_out[both] = projected[:, 3 * LANES :].reshape(2, SEG, LANES)
        return carry

    lax.fori_loop(0, sizes.chips, work, 0)
    gather.finish()
    ffn[2]()
    outs[2]()


def first_call(sizes, tokens, *operands):
    seqs, lines = sizes.seqs, sizes.lines
    dma = pltpu.SemaphoreType.DMA
    any_spec, vmem_spec = pl.BlockSpec(memory_space=pl.ANY), pl.BlockSpec(memory_space=pltpu.VMEM)
    shape = jax.ShapeDtypeStruct
    matrix_shape = (D, 4 * LANES)
    return pl.pallas_call(
        partial(first_kernel, sizes),
        out_shape=[
            shape((seqs, SEG, D), bf16),
            shape((seqs, SEG, 3 * LANES), bf16),
            shape((seqs, SEG, LANES), f32),
            shape(matrix_shape, bf16),
            shape((sizes.heads, MH, LANES), bf16),
            shape((sizes.heads, MH, LANES), bf16),
            shape((8, D), f32),
            shape((8, 3 * LANES), f32),
            shape((2 * P_SIZE, LANES), bf16),
            shape((seqs, 8, SEG), f32),
            shape((seqs, 3 * sizes.piece, sizes.slab), bf16),
            shape((lines, sizes.share, D), bf16),
        ],
        in_specs=[any_spec] + [vmem_spec] * 12 + [any_spec],
        out_specs=[vmem_spec] * 10 + [any_spec] * 2,
        scratch_shapes=[
            pltpu.VMEM((seqs, SEG, D), bf16),
            pltpu.VMEM((seqs, sizes.weight_rows, LANES), bf16),
            pltpu.VMEM((sizes.weight_rows, LANES), f32),
            pltpu.VMEM((seqs, 3 * sizes.piece, sizes.slab), bf16),
            pltpu.VMEM((lines, seqs, sizes.weight_rows, LANES), bf16),
            pltpu.VMEM((8, 3 * D), f32),
            pltpu.VMEM((2 * P_SIZE, LANES), f32),
            pltpu.VMEM((sizes.heads, MH, LANES), f32),
            pltpu.VMEM((8, LANES) if sizes.share % 16 == 0 else matrix_shape, f32),
        ]
        + PlaneGather.sems(seqs)
        + [dma((1,)), dma((seqs,)), dma((seqs,)), dma((lines,)), dma((lines,))]
        + [dma((1,)), dma((seqs,)), dma((seqs,))]
        + [dma((1,)), dma((lines,)), dma((lines,))],
        compiler_params=pltpu.CompilerParams(
            collective_id=0, has_side_effects=True, vmem_limit_bytes=VMEM_GRANT
        ),
        name="first",
    )(tokens, *operands)


def ffn_kernel(
    sizes,
    rows_ref,
    cot_ref,
    weight_ref,
    sum_ref,
    down_ref,
    grad_ref,
    rows_all,
    other,
    pair,
    landed,
    cot_slot,
    down_slot,
    both_matrix,
    down_matrix,
    both_grad,
    down_grad,
    acts,
    part,
    blocks,
    block_sem,
    pair_send,
    pair_recv,
    back_send,
    back_recv,
    cot_sem,
    down_sem,
    *gather_sems,
):
    seqs, lines, chips = sizes.seqs, sizes.lines, sizes.chips
    hidden_size, slab, piece = sizes.slab * sizes.lines, sizes.slab, sizes.piece
    seq, line = lax.axis_index("seq"), lax.axis_index("fsdp")
    chip, core = seq // 2, lax.rem(seq, 2)
    sibling = (2 * chip + 1 - core, line)

    def loop(first, last, body):
        def step(k, carry):
            body(k)
            return carry

        lax.fori_loop(first, last, step, 0)

    def remote(source, target, send, recv, place):
        return pltpu.make_async_remote_copy(
            src_ref=source,
            dst_ref=target,
            send_sem=send,
            recv_sem=recv,
            device_id=place,
            device_id_type=MESH,
        )

    gather = PlaneGather(seqs, rows_ref, rows_all, gather_sems)

    def order(j):
        return jnp.where(j >= 2, 5 - j, j) if chips == 4 else j

    def chip_at(j):
        return gather.chip_at(order(j))

    def to_pair(j):
        q, slot = chip_at(j), lax.rem(j, 2)
        return remote(other.at[slot], pair.at[q], pair_send.at[slot], pair_recv.at[q], sibling)

    def back(q, slot):
        place = (2 * q + core, line)
        return remote(pair.at[q], landed.at[slot], back_send.at[q], back_recv.at[slot], place)

    def cot_copy(j, slot):
        return pltpu.make_async_copy(
            cot_ref.at[pl.ds(2 * chip_at(j), 2)], cot_slot.at[slot], cot_sem.at[slot]
        )

    def down_copy(j):
        slot = lax.rem(j, 2)
        return pltpu.make_async_copy(
            down_slot.at[slot], down_ref.at[pl.ds(2 * chip_at(j), 2)], down_sem.at[slot]
        )

    greet_all((seqs, lines), ("plane",))
    gather.start()
    cot_copy(0, 0).start()
    slots = blocks.shape[0]

    def weight_copy(f):
        return pltpu.make_async_copy(weight_ref.at[f], blocks.at[f % slots], block_sem.at[f % slots])

    def grad_copy(f):
        return pltpu.make_async_copy(blocks.at[f % slots], grad_ref.at[f], block_sem.at[f % slots])

    for f in range(slots):
        weight_copy(f).start()
    for f in range(lines):
        weight_copy(f).wait()
        columns = slice(f * slab, (f + 1) * slab)
        up_columns = slice(hidden_size + f * slab, hidden_size + (f + 1) * slab)
        for s in range(seqs):
            rows = slice(s * piece, (s + 1) * piece)
            both_matrix[rows, columns] = blocks[f % slots, s, :piece, :]
            both_matrix[rows, up_columns] = blocks[f % slots, s, piece : 2 * piece, :]
            down_matrix[rows, columns] = blocks[f % slots, s, 2 * piece :, :]
        if f + slots < lines:
            weight_copy(f + slots).start()

    def forth(j):
        k, q = order(j), chip_at(j)
        gather.step(k)
        cot_copy(j, lax.rem(j, 2)).wait()

        @pl.when(jnp.logical_and(j > 0, j + 1 < chips))
        def _():
            cot_copy(j + 1, lax.rem(j + 1, 2)).start()

        rows = rows_all[pl.ds(2 * q, 2)].reshape(2 * SEG, D)
        cot = cot_slot[lax.rem(j, 2)].reshape(2 * SEG, D)
        grad_hidden = dot_nn(cot, down_matrix[...])
        ups = dot_nn(rows, both_matrix[...])
        gate_act, up_act = ups[:, :hidden_size], ups[:, hidden_size:]
        sigmoid = jax.nn.sigmoid(gate_act)
        swish = gate_act * sigmoid
        slope = sigmoid * (1.0 + gate_act - swish)
        acts[j, :, :hidden_size] = (grad_hidden * up_act * slope).astype(bf16)
        acts[j, :, hidden_size : 2 * hidden_size] = (grad_hidden * swish).astype(bf16)
        acts[j, :, 2 * hidden_size :] = (swish * up_act).astype(bf16)
        part[...] = dot_nt(acts[j, :, : 2 * hidden_size], both_matrix[...])

        @pl.when(j >= 2)
        def _():
            to_pair(j - 2).wait_send()

        theirs = part[pl.ds(pl.multiple_of((1 - core) * SEG, SEG), SEG), :].astype(bf16)
        other[lax.rem(j, 2)] = theirs
        to_pair(j).start()
        to_pair(j).wait_recv()
        own = part[pl.ds(pl.multiple_of(core * SEG, SEG), SEG), :] + pair[q].astype(f32)

        @pl.when(j == 0)
        def _():
            sum_ref[...] = own

        @pl.when(j > 0)
        def _():
            pair[q] = own.astype(bf16)
            back(q, chip).start()

    def weigh(j):
        q = chip_at(j)
        slot = lax.rem(j, 2)

        @pl.when(j > 0)
        def _():
            cot_copy(j, slot).wait()

            @pl.when(j + 1 < chips)
            def _():
                cot_copy(j + 1, lax.rem(j + 1, 2)).start()

        @pl.when(j >= 2)
        def _():
            down_copy(j - 2).wait()

        hidden = acts[j, :, 2 * hidden_size :]
        down_slot[slot] = dot_nt(hidden, down_matrix[...]).astype(bf16).reshape(2, SEG, D)
        down_copy(j).start()
        rows = rows_all[pl.ds(2 * q, 2)].reshape(2 * SEG, D)
        cot = cot_slot[slot].reshape(2 * SEG, D)
        both_new = dot_tn(rows, acts[j, :, : 2 * hidden_size])
        down_new = dot_tn(cot, hidden)

        @pl.when(j == 0)
        def _():
            both_grad[...] = both_new
            down_grad[...] = down_new

        @pl.when(j > 0)
        def _():
            both_grad[...] += both_new
            down_grad[...] += down_new

    forth(jnp.int32(0))
    weigh(jnp.int32(0))
    cot_copy(1, 1).start()
    loop(1, chips, forth)
    cot_copy(1, 1).start()
    loop(1, chips, weigh)
    for f in range(lines):
        if f >= slots:
            grad_copy(f - slots).wait()
        columns = slice(f * slab, (f + 1) * slab)
        up_columns = slice(hidden_size + f * slab, hidden_size + (f + 1) * slab)
        for s in range(seqs):
            rows = slice(s * piece, (s + 1) * piece)
            blocks[f % slots, s, :piece, :] = both_grad[rows, columns].astype(bf16)
            blocks[f % slots, s, piece : 2 * piece, :] = both_grad[rows, up_columns].astype(bf16)
            blocks[f % slots, s, 2 * piece :, :] = down_grad[rows, columns].astype(bf16)
        grad_copy(f).start()
    for f in range(lines - slots, lines):
        grad_copy(f).wait()
    loop(chips - 2, chips, lambda j: down_copy(j).wait())
    gather.finish()
    loop(chips - 2, chips, lambda j: to_pair(j).wait_send())

    def end(j):
        q = chip_at(j)
        back(q, chip).wait_send()
        back(q, q).wait_recv()
        sum_ref[...] += landed[q].astype(f32)

    loop(1, chips, end)


def feed_forward(sizes, rows, cot, weights):
    seqs, lines, chips = sizes.seqs, sizes.lines, sizes.chips
    hidden = sizes.slab * lines
    dma = pltpu.SemaphoreType.DMA
    any_spec, vmem_spec = pl.BlockSpec(memory_space=pl.ANY), pl.BlockSpec(memory_space=pltpu.VMEM)
    half = pltpu.VMEM((chips, SEG, D), bf16)
    slots = lines if lines <= 4 else 2
    return pl.pallas_call(
        partial(ffn_kernel, sizes),
        out_shape=[
            jax.ShapeDtypeStruct((SEG, D), f32),
            jax.ShapeDtypeStruct((seqs, SEG, D), bf16),
            jax.ShapeDtypeStruct(weights.shape, bf16),
        ],
        in_specs=[vmem_spec, any_spec, any_spec],
        out_specs=[vmem_spec, any_spec, any_spec],
        scratch_shapes=[
            pltpu.VMEM((seqs, SEG, D), bf16),
            pltpu.VMEM((2, SEG, D), bf16),
            half,
            half,
            pltpu.VMEM((2, 2, SEG, D), bf16),
            pltpu.VMEM((2, 2, SEG, D), bf16),
            pltpu.VMEM((D, 2 * hidden), bf16),
            pltpu.VMEM((D, hidden), bf16),
            pltpu.VMEM((D, 2 * hidden), f32),
            pltpu.VMEM((D, hidden), f32),
            pltpu.VMEM((chips, 2 * SEG, 3 * hidden), bf16),
            pltpu.VMEM((2 * SEG, D), f32),
            pltpu.VMEM((slots,) + weights.shape[1:], bf16),
            dma((slots,)),
        ]
        + [dma((2,)), dma((chips,)), dma((chips,)), dma((chips,))]
        + [dma((2,)), dma((2,))]
        + PlaneGather.sems(seqs),
        compiler_params=pltpu.CompilerParams(
            collective_id=2, has_side_effects=True, vmem_limit_bytes=VMEM_GRANT
        ),
        name="feed_forward",
    )(rows, cot, weights)


def last_kernel(
    sizes,
    grad_ref,
    normed_ref,
    matrix_ref,
    mem_ref,
    taps_ref,
    persist_ref,
    bias_ref,
    gain_two_ref,
    ffn_ref,
    out_ref,
    token_ref,
    middle_ref,
    gain_ref,
    qkv_ref,
    gate_ref,
    own_gain_ref,
    token_grad,
    qkv_grad,
    gate_grad,
    mem_grad,
    conv_grad,
    persist_grad,
    out_grad,
    gain_one_grad,
    gain_two_grad,
    ffn_gate_grad,
    ffn_up_grad,
    ffn_down_grad,
    bias_grad,
    normed_slot,
    matrix_grad,
    pack,
    pack_rows,
    pack_landed,
    pack_sums,
    pack_got,
    out_blocks,
    out_got,
    persist_got,
    ffn_got,
    other,
    pair,
    landed,
    conv_full,
    normed_sem,
    pair_send,
    pair_recv,
    back_send,
    back_recv,
    *sems,
):
    seqs, lines, chips = sizes.seqs, sizes.lines, sizes.chips
    share, width, heads = sizes.share, sizes.width, sizes.heads
    seq, line = lax.axis_index("seq"), lax.axis_index("fsdp")
    me = seq * lines + line
    group = seq // sizes.copies
    chip, core = seq // 2, lax.rem(seq, 2)
    sibling = (2 * chip + 1 - core, line)
    side = math.isqrt(chips)

    def chip_at(k):
        across = lax.rem(lax.rem(chip, side) + lax.rem(k, side), side)
        along = lax.rem(chip // side + k // side, side)
        return along * side + across

    def loop(first, last, body):
        def step(k, carry):
            body(k)
            return carry

        lax.fori_loop(first, last, step, 0)

    def remote(source, target, send, recv, place):
        return pltpu.make_async_remote_copy(
            src_ref=source,
            dst_ref=target,
            send_sem=send,
            recv_sem=recv,
            device_id=place,
            device_id_type=MESH,
        )

    def to_pair(k):
        q, slot = chip_at(lax.rem(k, chips)), lax.rem(k, 2)
        return remote(other.at[slot], pair.at[q], pair_send.at[slot], pair_recv.at[q], sibling)

    def back(q, slot):
        place = (2 * q + core, line)
        return remote(pair.at[q], landed.at[slot], back_send.at[q], back_recv.at[slot], place)

    def normed_copy(q, slot):
        return pltpu.make_async_copy(
            normed_ref.at[pl.ds(2 * q, 2)], normed_slot.at[slot], normed_sem.at[slot]
        )

    axes = (seqs, lines)
    greet_all(axes, ("plane", "line"))
    ffn = exchange_phases(axes, (0, 1, 0, 0, 0, 0, 0, 0), [ffn_ref], [ffn_got], sems[0:3])
    outs = exchange_phases(
        axes, (0, 0, 2, 0, 0, 0, 0, 0), [out_blocks, persist_ref], [out_got, persist_got], sems[3:9]
    )
    grads = exchange_phases(
        axes, (0, 0, 0, 0, 0, 0, 0, 1), [pack], [pack_got], [pack_landed, pack_sums, *sems[9:14]]
    )
    normed_copy(0, 0).start()
    ffn[0]()

    def gather_grad(q):
        slot = lax.rem(q, 2)

        @pl.when(q + 1 < chips)
        def _():
            normed_copy(q + 1, lax.rem(q + 1, 2)).start()

        normed_copy(q, slot).wait()
        grad = grad_ref[pl.ds(2 * q, 2)].reshape(2 * SEG, 4 * LANES)
        new = dot_tn(normed_slot[slot].reshape(2 * SEG, D), grad)

        @pl.when(q == 0)
        def _():
            matrix_grad[...] = new

        @pl.when(q > 0)
        def _():
            matrix_grad[...] += new

    loop(0, chips, gather_grad)
    mem_at, rest_at = sizes.grad_mem_at, sizes.grad_rest_at
    pack_rows[...] = jnp.zeros_like(pack_rows)
    for tap in range(4):
        for part in range(3):
            at = rest_at + 3 * tap + part
            pack_rows[at : at + 1, :] = taps_ref[tap : tap + 1, part * LANES : (part + 1) * LANES]
    pack_rows[rest_at + 12 : rest_at + 13, :] = bias_ref[0:1, :]
    for i in range(sizes.devices):
        rows = slice(i * share, (i + 1) * share)
        for part in range(4):
            pack_rows[part * share : (part + 1) * share, :] = matrix_grad[
                rows, part * LANES : (part + 1) * LANES
            ]
        for head in range(heads):
            first = mem_at + head * sizes.memory
            pack_rows[first : first + sizes.memory, :] = mem_ref[
                head, i * sizes.memory : (i + 1) * sizes.memory, :
            ]
        pack_rows[rest_at + 13 : rest_at + 14, :share] = gain_two_ref[0:1, rows]
        pack[i % lines, i // lines] = pack_rows[...].astype(bf16)
    grads[0]()
    for f in range(lines):
        out_blocks[f] = out_ref[f * share : (f + 1) * share, :].astype(bf16)
    outs[0]()

    def spread(k):
        q = chip_at(lax.rem(k, chips))
        grad = grad_ref[pl.ds(2 * q, 2)].reshape(2 * SEG, 4 * LANES)
        if sizes.copies > 1:
            grad = grad * jnp.where(lax.rem(seq, sizes.copies) == 0, 1.0, 0.0).astype(bf16)
        whole = dot_nt(grad, matrix_ref[...])
        first_core, second_core = whole[:SEG], whole[SEG:]

        @pl.when(k >= 3)
        def _():
            to_pair(k - 2).wait_send()

        other[lax.rem(k, 2)] = jnp.where(core == 0, second_core, first_core).astype(bf16)
        to_pair(k).start()
        own = jnp.where(core == 0, first_core, second_core)
        to_pair(k).wait_recv()
        own = own + pair[q].astype(f32)

        @pl.when(k == chips)
        def _():
            token_grad[...] = own

        @pl.when(k < chips)
        def _():
            pair[q] = own.astype(bf16)
            back(q, chip).start()

    loop(1, chips + 1, spread)
    grads[1]()

    def add_back(k):
        q = chip_at(k)
        back(q, q).wait_recv()
        token_grad[...] += landed[q].astype(f32)

    loop(1, chips, add_back)
    rows = token_ref[...].astype(f32)
    scale = norm_scale(rows)
    token_grad[...] = middle_ref[...] + norm_pull(rows, scale, gain_ref[4:5, :], token_grad[...])

    ffn[2]()
    piece, slab = sizes.piece, sizes.slab
    for s in range(seqs):
        columns = slice(s * slab, (s + 1) * slab)
        ffn_gate_grad[:, columns] = ffn_got[s, :piece, :].astype(f32)
        ffn_up_grad[:, columns] = ffn_got[s, piece : 2 * piece, :].astype(f32)
        ffn_down_grad[columns, :] = jnp.transpose(ffn_got[s, 2 * piece :, :].astype(f32))
    outs[2]()
    out_sum = out_got[0].astype(f32)
    persist_sum = persist_got[0]
    for f in range(1, lines):
        out_sum = out_sum + out_got[f].astype(f32)
        persist_sum = persist_sum + persist_got[f]
    out_grad[...] = out_sum
    inside = lax.rem(LANES - (me * share - group * width), LANES)
    persist_grad[...] = pltpu.roll(persist_sum, inside, 1)[:, :share]

    grads[2]()
    gates = jnp.zeros((share, 3 * HEAD_COUNT), f32)
    bias = jnp.zeros((8, 3 * HEAD_COUNT), f32)
    gain_two = jnp.zeros((1, share), f32)
    conv_full[...] = jnp.zeros_like(conv_full)
    for s in range(seqs):
        block = pack_got[s].astype(f32)
        gain_two = gain_two + block[rest_at + 13 : rest_at + 14, :share]
        if s % sizes.copies:
            continue
        other_group = s // sizes.copies
        for part in range(3):
            first = part * D + other_group * width
            qkv_grad[:, first : first + width] = block[
                part * share : (part + 1) * share, :width
            ]
            for tap in range(4):
                at = rest_at + 3 * tap + part
                conv_full[tap : tap + 1, first : first + width] = block[at : at + 1, :width]
        choice = gate_choice(sizes, other_group, True)
        gates = gates + dot_nn(block[3 * share : 4 * share].astype(bf16), choice)
        rest = block[rest_at + 8 : rest_at + 16].astype(bf16)
        bias = bias + dot_nn(rest, choice)
        for head in range(heads):
            first = mem_at + head * sizes.memory
            mem_grad[other_group * heads + head] = block[first : first + sizes.memory]
    gate_grad[...] = gates
    bias_grad[...] = bias[4:5]
    gain_two_grad[...] = gain_two
    along = jnp.sum(qkv_grad[...] * qkv_ref[...].astype(f32), axis=1, keepdims=True)
    along = along + jnp.sum(gates * gate_ref[...].astype(f32), axis=1, keepdims=True)
    gain_one_grad[...] = along / own_gain_ref[...].astype(f32)
    turned = pltpu.roll(conv_full[...], lax.rem(3 * D - me * 3 * share, 3 * D), 1)
    conv_grad[...] = turned[:, : 3 * share]

    def end(k):
        q = chip_at(k)
        back(q, chip).wait_send()

    loop(1, chips, end)
    loop(chips - 1, chips + 1, lambda k: to_pair(k).wait_send())


def last_call(sizes, *operands):
    seqs, lines, chips, share = sizes.seqs, sizes.lines, sizes.chips, sizes.share
    dma = pltpu.SemaphoreType.DMA
    any_spec, vmem_spec = pl.BlockSpec(memory_space=pl.ANY), pl.BlockSpec(memory_space=pltpu.VMEM)
    shape = jax.ShapeDtypeStruct
    half = pltpu.VMEM((chips, SEG, D), bf16)
    in_specs = [vmem_spec] * len(operands)
    in_specs[1] = any_spec
    in_specs[8] = any_spec
    pack_shape = (lines, seqs, sizes.grad_rows, LANES)
    return pl.pallas_call(
        partial(last_kernel, sizes),
        out_shape=[
            shape((SEG, D), f32),
            shape((share, 3 * D), f32),
            shape((share, 3 * HEAD_COUNT), f32),
            shape((HEAD_COUNT, sizes.memory, LANES), f32),
            shape((8, 3 * share), f32),
            shape((2 * P_SIZE, share), f32),
            shape((share, D), f32),
            shape((share, 1), f32),
            shape((1, share), f32),
            shape((sizes.piece, sizes.hidden), f32),
            shape((sizes.piece, sizes.hidden), f32),
            shape((sizes.hidden, sizes.piece), f32),
            shape((1, 3 * HEAD_COUNT), f32),
        ],
        in_specs=in_specs,
        out_specs=[vmem_spec] * 13,
        scratch_shapes=[
            pltpu.VMEM((2, 2, SEG, D), bf16),
            pltpu.VMEM((D, 4 * LANES), f32),
            pltpu.VMEM(pack_shape, bf16),
            pltpu.VMEM(pack_shape[2:], f32),
            pltpu.VMEM(pack_shape, bf16),
            pltpu.VMEM(pack_shape[1:], bf16),
            pltpu.VMEM(pack_shape[1:], bf16),
            pltpu.VMEM((lines, share, D), bf16),
            pltpu.VMEM((lines, share, D), bf16),
            pltpu.VMEM((lines, 2 * P_SIZE, LANES), f32),
            pltpu.VMEM((seqs, 3 * sizes.piece, sizes.slab), bf16),
            pltpu.VMEM((2, SEG, D), bf16),
            half,
            half,
            pltpu.VMEM((8, 3 * D), f32),
            dma((2,)),
        ]
        + [dma((2,)), dma((chips,)), dma((chips,)), dma((chips,))]
        + [dma((1,)), dma((seqs,)), dma((seqs,))]
        + [dma((1,)), dma((lines,)), dma((lines,))] * 2
        + [dma((1,)), dma((lines,)), dma((lines,)), dma((seqs,)), dma((seqs,))],
        compiler_params=pltpu.CompilerParams(
            collective_id=5, has_side_effects=True, vmem_limit_bytes=VMEM_GRANT
        ),
        name="last",
    )(*operands)


def norm_scale(values):
    return lax.rsqrt(jnp.mean(values * values, axis=-1, keepdims=True) + NORM_EPS)


def norm_pull(values, scale, gain, grad):
    inner = jnp.mean(grad * gain * values, axis=-1, keepdims=True)
    return scale * (grad * gain - values * (scale * scale) * inner)


def widen(rows, width):
    return jnp.pad(rows, [(0, 0)] * (rows.ndim - 1) + [(0, width - rows.shape[-1])])


def on_device(
    tokens,
    norm1_gain,
    qkv_weight,
    gate_weight,
    conv_weight,
    memory_w1,
    memory_w2,
    persistent_keys,
    persistent_values,
    out_weight,
    norm2_gain,
    ffn_gate,
    ffn_up,
    ffn_down,
    gate_bias,
    doc_lengths,
    live_mask,
    cotangent,
):
    sizes = Sizes(lax.axis_size("seq"), lax.axis_size("fsdp"))
    seqs, lines, groups = sizes.seqs, sizes.lines, sizes.groups
    heads, width, share = sizes.heads, sizes.width, sizes.share
    length = seqs * SEG
    memory_pack = jnp.concatenate([memory_w1.transpose(0, 2, 1), memory_w2], axis=2)
    (
        normed,
        raw,
        gates,
        matrix,
        memory_both,
        memory_turned,
        gains,
        taps,
        persistent,
        live,
        ffn_part,
        out_rows,
    ) = first_call(
        sizes,
        tokens[0],
        qkv_weight,
        gate_weight,
        conv_weight,
        persistent_keys,
        persistent_values,
        norm1_gain[None],
        norm2_gain[None],
        live_mask,
        memory_pack,
        ffn_gate,
        ffn_up,
        ffn_down,
        out_weight,
    )
    ffn_full = lax.all_gather(ffn_part, "fsdp")

    constants = (taps, memory_both, memory_turned, persistent, doc_lengths, gate_bias)
    raw = raw.reshape(length, 3 * LANES)
    gates = gates.reshape(length, LANES)
    plan = Exchange(gathers=[out_rows.reshape(lines * share, D), cotangent[0]])
    mixed, keys, values, totals, states, out_matrix, cot_rows = mix_forward(
        6, plan, heads, raw, gates, live, *constants
    )
    out_matrix = out_matrix.reshape(D, D)

    (mixed_got,) = exchange("to_segments", 1, planes=[mixed.reshape(seqs, SEG, LANES)])
    combined = mixed_got[:: sizes.copies, :, :width].transpose(1, 0, 2).reshape(SEG, D)
    inputs = tokens[0].astype(f32)
    gain_two = gains[5:6]
    middle = inputs + jnp.dot(combined, out_matrix, preferred_element_type=f32)
    scale_two = norm_scale(middle)
    normed_two_own = (middle * scale_two * gain_two).astype(bf16)

    grad_normed_two, down_part, ffn_grads = feed_forward(sizes, normed_two_own, cot_rows, ffn_full)
    ffn_grads = lax.psum_scatter(ffn_grads, "fsdp")

    grad_middle = cotangent[0].astype(f32) + norm_pull(middle, scale_two, gain_two, grad_normed_two)
    grad_gain_two = jnp.sum(grad_normed_two * middle * scale_two, axis=0, keepdims=True)
    grad_branch = grad_middle.astype(bf16)
    grad_combined = dot_nt(grad_branch, out_matrix).astype(bf16)
    grad_out = dot_tn(combined, grad_branch).astype(bf16)
    plan = Exchange(scatters=[down_part, grad_out.reshape(seqs, sizes.piece, D)])
    blocks = widen(grad_combined.reshape(SEG, groups, width).transpose(1, 0, 2), LANES)
    if sizes.copies > 1:
        blocks = jnp.repeat(blocks, sizes.copies, axis=0)
    (grad_mixed,) = exchange("to_heads", 4, planes=[blocks])

    grad_all, grad_memory, grad_taps, grad_persistent, grad_bias, down_sum, grad_out = mix_backward(
        7,
        plan,
        heads,
        raw,
        gates,
        live,
        keys,
        values,
        totals,
        states,
        grad_mixed.reshape(length, LANES),
        *constants,
    )
    output = (middle + down_sum).astype(bf16)
    (
        input_grad,
        grad_qkv,
        grad_gate,
        grad_memory,
        grad_conv,
        grad_persistent,
        grad_out,
        grad_gain_one,
        grad_gain_two,
        grad_ffn_gate,
        grad_ffn_up,
        grad_ffn_down,
        grad_bias,
    ) = last_call(
        sizes,
        grad_all.reshape(seqs, SEG, 4 * LANES),
        normed,
        matrix,
        grad_memory,
        grad_taps,
        grad_persistent,
        grad_bias,
        grad_gain_two,
        ffn_grads,
        grad_out,
        tokens[0],
        grad_middle,
        gains,
        qkv_weight,
        gate_weight,
        norm1_gain[:, None],
    )
    return (
        output[None],
        input_grad[None],
        grad_gain_one[:, 0],
        grad_qkv,
        grad_gate,
        grad_conv[:4],
        grad_memory[..., :HEAD_SIZE].transpose(0, 2, 1),
        grad_memory[..., HEAD_SIZE:],
        grad_persistent[:P_SIZE],
        grad_persistent[P_SIZE:],
        grad_out,
        grad_gain_two[0],
        grad_ffn_gate,
        grad_ffn_up,
        grad_ffn_down,
        grad_bias.reshape(3, HEAD_COUNT) * jnp.array([[3.0], [1.0], [1.0]], f32),
    )


def solution(mesh):
    return jax.shard_map(
        on_device,
        mesh=mesh,
        in_specs=(
            P("fsdp", "seq", None),
            P(("seq", "fsdp")),
            P(("seq", "fsdp"), None),
            P(("seq", "fsdp"), None),
            P(None, ("seq", "fsdp")),
            P(None, None, ("seq", "fsdp")),
            P(None, ("seq", "fsdp"), None),
            P(None, ("seq", "fsdp")),
            P(None, ("seq", "fsdp")),
            P(("seq", "fsdp"), None),
            P(("seq", "fsdp")),
            P("seq", "fsdp"),
            P("seq", "fsdp"),
            P("fsdp", "seq"),
            P(),
            P("fsdp", None),
            P("fsdp", "seq"),
            P("fsdp", "seq", None),
        ),
        out_specs=(
            P("fsdp", "seq", None),
            P("fsdp", "seq", None),
            P(("seq", "fsdp")),
            P(("seq", "fsdp"), None),
            P(("seq", "fsdp"), None),
            P(None, ("seq", "fsdp")),
            P(None, None, ("seq", "fsdp")),
            P(None, ("seq", "fsdp"), None),
            P(None, ("seq", "fsdp")),
            P(None, ("seq", "fsdp")),
            P(("seq", "fsdp"), None),
            P(("seq", "fsdp")),
            P("seq", "fsdp"),
            P("seq", "fsdp"),
            P("fsdp", "seq"),
            P(),
        ),
        check_vma=False,
    )
```

```python
import math
from functools import partial

import jax
import jax.numpy as jnp
from jax import lax
from jax.experimental import pallas as pl
from jax.experimental.pallas import tpu as pltpu
from jax.sharding import PartitionSpec as P

HEAD_COUNT = 16
HEAD_SIZE = 64
D = 1024
FF = 4096
MH = 256
P_SIZE = 16
SEG = 256
LANES = 128

NORM_EPS = 1e-05
UNIT_EPS = 1e-06
SCORE_SCALE = 8.0
MEMORY_SCALE = 8.0
THETA_SCALE = 0.0005
MASKED = -1000000000.0
LEAST_SHIFT = -30.0
VMEM_GRANT = 62 * 1024 * 1024
MESH = pl.DeviceIdType.MESH

f32 = jnp.float32
bf16 = jnp.bfloat16


def dot_nt(left, right):
    return lax.dot_general(left, right, (((1,), (1,)), ((), ())), preferred_element_type=f32)


def dot_nn(left, right):
    return lax.dot_general(left, right, (((1,), (0,)), ((), ())), preferred_element_type=f32)


def dot_tn(left, right):
    return lax.dot_general(left, right, (((0,), (0,)), ((), ())), preferred_element_type=f32)


def lane_index(shape):
    return lax.broadcasted_iota(jnp.int32, shape, 1)


def swap_halves(rows):
    return pltpu.roll(rows, HEAD_SIZE, 1)


def lane_sum(rows):
    return jnp.sum(rows, axis=1, keepdims=True)


def unit_pair(rows, low):
    squares = rows * rows
    first = lane_sum(jnp.where(low, squares, 0.0))
    second = lane_sum(jnp.where(low, 0.0, squares))
    inverse = jnp.where(low, lax.rsqrt(first + UNIT_EPS), lax.rsqrt(second + UNIT_EPS))
    return rows * inverse, inverse


def unit_pair_pull(unit, inverse, grad, low):
    along = unit * grad
    first = lane_sum(jnp.where(low, along, 0.0))
    second = lane_sum(jnp.where(low, 0.0, along))
    return inverse * (grad - unit * jnp.where(low, first, second))


def mix_taps(ext_ref, conv_ref, place):
    mixed = conv_ref[0:1, :] * ext_ref[8 : 8 + SEG, :]
    for offset in range(1, 4):
        kept = jnp.where(place >= offset, ext_ref[8 - offset : 8 - offset + SEG, :], 0.0)
        mixed = mixed + conv_ref[offset : offset + 1, :] * kept
    return mixed


def places(length_ref, positions):
    start = jnp.int32(0)
    begin = jnp.zeros_like(positions)
    for document in range(1, length_ref.shape[1]):
        start = start + length_ref[0, document - 1]
        begin = jnp.where(positions >= start, start, begin)
    return positions - begin


def gate_scan(heads, first_head, gate_columns, bias_ref, place_row, live):
    lane = lane_index((8, SEG))
    sublane = lax.broadcasted_iota(jnp.int32, (8, SEG), 0)
    gate_rows = jnp.transpose(gate_columns)
    shifts = []
    for kind, (scale, shift) in enumerate(((3.0, -7.5), (1.0, 1.5), (1.0, 0.0))):
        bias = jnp.zeros((8, SEG), f32)
        for head in range(heads):
            own = scale * bias_ref[kind, first_head + head] + shift
            bias = jnp.where(sublane == head, own, bias)
        shifts.append(bias)
    keep = jnp.where(place_row < 1, 0.0, 1.0)
    forget = jax.nn.sigmoid(gate_rows[0:8] + shifts[0])
    momentum = jax.nn.sigmoid(gate_rows[8:16] + shifts[1])
    step = jax.nn.sigmoid(gate_rows[16:24] + shifts[2])
    carry = keep * momentum
    fade = keep * (1.0 - forget)
    keep_all, mix_all, fade_all = carry, carry, fade
    distance = 1
    while distance < SEG:
        inside = lane < SEG - distance
        turn = SEG - distance
        keep_next = jnp.where(inside, pltpu.roll(keep_all, turn, 1), 1.0)
        mix_next = jnp.where(inside, pltpu.roll(mix_all, turn, 1), 0.0)
        fade_next = jnp.where(inside, pltpu.roll(fade_all, turn, 1), 1.0)
        mix_all = mix_next * keep_all + fade_next * mix_all
        keep_all = keep_next * keep_all
        fade_all = fade_next * fade_all
        distance *= 2
    inside = lane < SEG - 1
    keep_after = jnp.where(inside, pltpu.roll(keep_all, SEG - 1, 1), 1.0)
    mix_after = jnp.where(inside, pltpu.roll(mix_all, SEG - 1, 1), 0.0)
    fade_after = jnp.where(inside, pltpu.roll(fade_all, SEG - 1, 1), 1.0)
    written = -THETA_SCALE * step * live
    return dict(
        keep=keep,
        live=live,
        forget=forget,
        momentum=momentum,
        step=step,
        carry=carry,
        fade=fade,
        keep_after=keep_after,
        reach=mix_after + fade_after,
        fade_after=fade_after,
        written=written,
        totals=(keep_all, mix_all, fade_all),
    )


def write_columns(scan):
    rows = jnp.concatenate(
        [scan["written"] * scan["keep_after"], scan["written"] * scan["reach"]], axis=0
    )
    return jnp.transpose(rows)


def state_factors(totals, head, low):
    keep_all, mix_all, fade_all = (member[head : head + 1, 0:1] for member in totals)
    return jnp.where(low, keep_all, fade_all), mix_all


def half_swish(inner):
    turn = jnp.tanh(0.5 * inner)
    sigmoid = 0.5 * turn + 0.5
    active = inner * sigmoid
    slope = sigmoid + active * (1.0 - sigmoid)
    return turn, sigmoid, active, slope


def fill_bias(bias_ref, place, live_prev, live_now):
    row = lax.broadcasted_iota(jnp.int32, (SEG, SEG), 0)
    gap = row - lane_index((SEG, SEG))
    hidden_prev = jnp.where(live_prev > 0.5, 0.0, MASKED)
    hidden_now = jnp.where(live_now > 0.5, 0.0, MASKED)
    bias_ref[:, :SEG] = jnp.where((gap < 0) & (gap + SEG <= place), hidden_prev, MASKED)
    bias_ref[:, SEG : 2 * SEG] = jnp.where((gap >= 0) & (gap <= place), hidden_now, MASKED)


def fill_persistent(bias_ref, keys_all, values_all, persist_ref):
    lane = lane_index((SEG, LANES))
    bias_ref[:, 2 * SEG :] = jnp.where(lane < P_SIZE, 0.0, MASKED)
    keys_all[2 * SEG :, :] = jnp.zeros((LANES, LANES), bf16)
    values_all[2 * SEG :, :] = jnp.zeros((LANES, LANES), bf16)
    pkeys = persist_ref[0:P_SIZE, :].astype(f32) * (1.0 / SCORE_SCALE)
    keys_all[2 * SEG : 2 * SEG + P_SIZE, :] = pkeys.astype(bf16)
    values_all[2 * SEG : 2 * SEG + P_SIZE, :] = persist_ref[P_SIZE:, :]


def forward_kernel(heads, plan, *refs):
    carried = len(plan.arrays)
    own, refs = refs[:9], refs[9:]
    sent, refs = refs[:carried], refs[carried:]
    made, refs = refs[:5], refs[5:]
    got, refs = refs[:carried], refs[carried:]
    begin, middle, finish = plan.phases(sent, got, refs[6:])
    at, last = pl.program_id(0), pl.num_programs(0) - 1

    @pl.when(at == 0)
    def _():
        greet_all(plan.axes, plan.kinds)
        begin()

    forward_step(heads, *own, *made, *refs[:6])

    @pl.when(at == (5 * last) // 8)
    def _():
        middle()

    @pl.when(at == last)
    def _():
        finish()


def forward_step(
    heads,
    raw_ref,
    gate_ref,
    live_ref,
    conv_ref,
    mem_ref,
    swap_ref,
    persist_ref,
    length_ref,
    bias_ref,
    comb_ref,
    key_out,
    value_out,
    total_out,
    state_out,
    ext,
    keys_all,
    values_all,
    live_prev,
    state,
    hidden,
):
    at = pl.program_id(0)

    @pl.when(at == 0)
    def _():
        ext[0:8, :] = jnp.zeros((8, 3 * LANES), f32)
        keys_all[SEG : 2 * SEG, :] = jnp.zeros((SEG, LANES), bf16)
        values_all[SEG : 2 * SEG, :] = jnp.zeros((SEG, LANES), bf16)
        live_prev[...] = jnp.zeros_like(live_prev)
        state[...] = jnp.zeros_like(state)
        fill_persistent(hidden, keys_all, values_all, persist_ref)

    low = lane_index((SEG, LANES)) < HEAD_SIZE
    ext[8 : 8 + SEG, :] = raw_ref[...].astype(f32)
    place = places(length_ref, at * SEG + lax.broadcasted_iota(jnp.int32, (SEG, 1), 0))
    place_row = places(length_ref, at * SEG + lane_index((1, SEG)))
    first_head = (lax.axis_index("seq") * HEAD_COUNT) // lax.axis_size("seq")
    mixed = mix_taps(ext, conv_ref, place)
    ext[0:8, :] = ext[SEG : SEG + 8, :]
    query_unit, _ = unit_pair(mixed[:, :LANES], low)
    key_unit, _ = unit_pair(mixed[:, LANES : 2 * LANES], low)
    value = mixed[:, 2 * LANES :]
    keys_all[0:SEG, :] = keys_all[SEG : 2 * SEG, :]
    values_all[0:SEG, :] = values_all[SEG : 2 * SEG, :]
    keys_all[SEG : 2 * SEG, :] = key_unit.astype(bf16)
    values_all[SEG : 2 * SEG, :] = value.astype(bf16)
    key_out[...] = keys_all[SEG : 2 * SEG, :]
    value_out[...] = values_all[SEG : 2 * SEG, :]
    scan = gate_scan(heads, first_head, gate_ref[...], bias_ref, place_row, live_ref[0, 0:1, :])
    columns = write_columns(scan)
    fill_bias(hidden, place, live_prev[0:1, :], scan["live"])
    live_prev[...] = jnp.broadcast_to(scan["live"], (8, SEG))
    older = jnp.where(place > lax.broadcasted_iota(jnp.int32, (SEG, 1), 0), 1.0, 0.0)
    query = query_unit * SCORE_SCALE
    key = key_unit * MEMORY_SCALE
    queries = (query, swap_halves(query))
    keys = (key, swap_halves(key))
    values = (value, swap_halves(value))
    every = range(heads)
    owns = (low, jnp.logical_not(low))

    mems, swaps = [mem_ref[head] for head in every], [swap_ref[head] for head in every]
    states = [(state[head, 0], state[head, 1]) for head in every]
    for head in every:
        state_out[0, head, 0] = states[head][0].astype(bf16)
        state_out[0, head, 1] = states[head][1].astype(bf16)
    scores = [
        dot_nt(jnp.where(owns[head], query, 0.0).astype(bf16), keys_all[...]) for head in every
    ]
    key_cuts = [jnp.where(low, keys[head], 0.0) for head in every]
    inners = [dot_nt(key_cuts[head].astype(bf16), mems[head]) for head in every]
    firsts = [jnp.where(low, mems[head].astype(f32), states[head][0]).astype(bf16) for head in every]
    seconds = [
        jnp.where(low, swaps[head].astype(f32), states[head][1]).astype(bf16) for head in every
    ]
    asked = [
        jnp.where(low, queries[head], older * queries[1 - head]).astype(bf16) for head in every
    ]
    asked = [dot_nt(asked[head], firsts[head]) for head in every]
    log_totals = jnp.zeros((SEG, 8), f32)
    combined = jnp.zeros((SEG, LANES), f32)
    attended = []
    for head in every:
        shown = scores[head] + hidden[...]
        highest = jnp.max(shown[:, 2 * SEG :], axis=1, keepdims=True)
        highest = jnp.maximum(highest, LEAST_SHIFT)
        weights = jnp.exp(shown - highest)
        summed = lane_sum(weights)
        attended.append(dot_nn(weights.astype(bf16), values_all[...]) * (1.0 / summed))
        log_totals = jnp.where(lane_index((SEG, 8)) == head, highest + jnp.log(summed), log_totals)
    total_out[...] = log_totals
    actives, slopes = [], []
    for head in every:
        _, _, active, slope = half_swish(inners[head])
        actives.append(active.astype(bf16))
        slopes.append(slope)
    errors = [
        jnp.where(low, dot_nn(actives[head], swaps[head]) - values[head], 0.0) for head in every
    ]
    answers = []
    for head in every:
        _, _, active, _ = half_swish(asked[head])
        answers.append(dot_nn(active.astype(bf16), seconds[head]))
    descents = [
        (dot_nt(errors[head].astype(bf16), swaps[head]) * slopes[head]).astype(bf16)
        for head in every
    ]
    for head in every:
        answer = answers[head]
        turned = swap_halves(answer)
        if head == 0:
            recalled = jnp.where(low, answer + older * turned, 0.0)
        else:
            recalled = jnp.where(low, 0.0, turned + older * answer)
        combined = combined + jnp.where(owns[head], attended[head], 0.0) + recalled
    comb_ref[...] = combined.astype(bf16)
    for head in every:
        scale = jnp.where(low, columns[:, head : head + 1], columns[:, 8 + head : 9 + head])
        key_scaled = (jnp.where(low, keys[head], keys[1 - head]) * scale).astype(bf16)
        error_scaled = ((errors[head] + swap_halves(errors[head])) * scale).astype(bf16)
        factor, blend = state_factors(scan["totals"], head, low)
        for member, added in (
            (0, dot_tn(descents[head], key_scaled)),
            (1, dot_tn(actives[head], error_scaled)),
        ):
            old = states[head][member]
            turned = jnp.where(low, 0.0, blend * swap_halves(old))
            state[head, member] = factor * old + turned + added


def chain_rows(factor, term, start, lane):
    distance = 1
    while distance < SEG:
        inside = lane >= distance
        factor_before = jnp.where(inside, pltpu.roll(factor, distance, 1), 1.0)
        term_before = jnp.where(inside, pltpu.roll(term, distance, 1), 0.0)
        term = term + factor * term_before
        factor = factor * factor_before
        distance *= 2
    after = factor * start + term
    return jnp.where(lane == 0, start, pltpu.roll(after, 1, 1))


def backward_kernel(heads, plan, *refs):
    carried = len(plan.arrays)
    own, refs = refs[:18], refs[18:]
    sent, refs = refs[:carried], refs[carried:]
    made, refs = refs[:5], refs[5:]
    got, refs = refs[:carried], refs[carried:]
    begin, middle, finish = plan.phases(sent, got, refs[8:])
    at, last = pl.program_id(0), pl.num_programs(0) - 1

    @pl.when(at == 0)
    def _():
        greet_all(plan.axes, plan.kinds)
        begin()

    backward_step(heads, *own, *made, *refs[:8])

    @pl.when(at == 1)
    def _():
        middle()

    @pl.when(at == last)
    def _():
        finish()


def backward_step(
    heads,
    raw_ref,
    tail_ref,
    gate_ref,
    live_ref,
    live_prev_ref,
    key_ref,
    key_prev_ref,
    value_ref,
    value_prev_ref,
    total_ref,
    state_ref,
    grad_ref,
    conv_ref,
    mem_ref,
    swap_ref,
    persist_ref,
    length_ref,
    bias_ref,
    draw_ref,
    dmem_ref,
    dconv_ref,
    dpersist_ref,
    dbias_ref,
    ext,
    shifted_rows,
    key_carry,
    value_carry,
    late,
    keys_all,
    values_all,
    hidden,
):
    at = pl.program_id(0)

    @pl.when(at == 0)
    def _():
        dmem_ref[...] = jnp.zeros_like(dmem_ref)
        dconv_ref[...] = jnp.zeros_like(dconv_ref)
        dpersist_ref[...] = jnp.zeros_like(dpersist_ref)
        dbias_ref[...] = jnp.zeros_like(dbias_ref)
        shifted_rows[:, 0:8, :] = jnp.zeros((3, 8, 3 * LANES), f32)
        key_carry[...] = jnp.zeros_like(key_carry)
        value_carry[...] = jnp.zeros_like(value_carry)
        late[...] = jnp.zeros_like(late)
        fill_persistent(hidden, keys_all, values_all, persist_ref)

    low = lane_index((SEG, LANES)) < HEAD_SIZE
    ext[0:8, :] = tail_ref[8:16, :].astype(f32)
    ext[8 : 8 + SEG, :] = raw_ref[...].astype(f32)
    here = (pl.num_programs(0) - 1 - at) * SEG
    place = places(length_ref, here + lax.broadcasted_iota(jnp.int32, (SEG, 1), 0))
    place_row = places(length_ref, here + lane_index((1, SEG)))
    first_head = (lax.axis_index("seq") * HEAD_COUNT) // lax.axis_size("seq")
    mixed = mix_taps(ext, conv_ref, place)
    query_unit, query_inverse = unit_pair(mixed[:, :LANES], low)
    key_unit, key_inverse = unit_pair(mixed[:, LANES : 2 * LANES], low)
    value = mixed[:, 2 * LANES :]
    keys_all[0:SEG, :] = key_prev_ref[...]
    values_all[0:SEG, :] = value_prev_ref[...]
    keys_all[SEG : 2 * SEG, :] = key_ref[...]
    values_all[SEG : 2 * SEG, :] = value_ref[...]
    scan = gate_scan(heads, first_head, gate_ref[...], bias_ref, place_row, live_ref[0, 0:1, :])
    columns = write_columns(scan)
    fill_bias(hidden, place, live_prev_ref[0, 0:1, :], scan["live"])
    older = jnp.where(place > lax.broadcasted_iota(jnp.int32, (SEG, 1), 0), 1.0, 0.0)
    grad = grad_ref[...].astype(f32)
    query = query_unit * SCORE_SCALE
    key = key_unit * MEMORY_SCALE
    queries = (query, swap_halves(query))
    keys = (key, swap_halves(key))
    values = (value, swap_halves(value))
    grads = (grad, swap_halves(grad))
    every = range(heads)
    owns = (low, jnp.logical_not(low))
    grad_query = jnp.zeros((SEG, LANES), f32)
    grad_key = key_carry[...]
    grad_value = value_carry[...]
    wide = lane_index((SEG, LANES))
    write_grads = jnp.zeros((SEG, LANES), f32)
    sublane = lax.broadcasted_iota(jnp.int32, (8, 1), 0)
    keep_start = jnp.zeros((8, 1), f32)
    mix_start = jnp.zeros((8, 1), f32)
    fade_start = jnp.zeros((8, 1), f32)

    query_own = [jnp.where(owns[head], query, 0.0).astype(bf16) for head in every]
    grad_own = [jnp.where(owns[head], grad, 0.0).astype(bf16) for head in every]
    scores = [dot_nt(query_own[head], keys_all[...]) for head in every]
    prob_grads = [dot_nt(grad_own[head], values_all[...]) for head in every]
    probs, score_grads = [], []
    for head in every:
        prob = jnp.exp(scores[head] + hidden[...] - total_ref[:, head : head + 1])
        spread = lane_sum(prob * prob_grads[head])
        score_grads.append((prob * (prob_grads[head] - spread)).astype(bf16))
        probs.append(prob.astype(bf16))
    back_keys = dot_tn(score_grads[0], query_own[0])
    back_values = dot_tn(probs[0], grad_own[0])
    for head in every[1:]:
        back_keys = back_keys + dot_tn(score_grads[head], query_own[head])
        back_values = back_values + dot_tn(probs[head], grad_own[head])
    for head in every:
        back = dot_nn(score_grads[head], keys_all[...])
        grad_query = grad_query + jnp.where(owns[head], SCORE_SCALE * back, 0.0)
    key_carry[...] = back_keys[0:SEG]
    value_carry[...] = back_values[0:SEG]
    grad_key = grad_key + back_keys[SEG : 2 * SEG]
    grad_value = grad_value + back_values[SEG : 2 * SEG]
    back_pkeys = back_keys[2 * SEG : 2 * SEG + P_SIZE] * (1.0 / SCORE_SCALE)
    dpersist_ref[0:P_SIZE, :] += back_pkeys
    dpersist_ref[P_SIZE:, :] += back_values[2 * SEG : 2 * SEG + P_SIZE]

    mems, swaps = [mem_ref[head] for head in every], [swap_ref[head] for head in every]
    states = [[state_ref[0, head, member].astype(f32) for member in range(2)] for head in every]
    lates = [[late[head, member] for member in range(2)] for head in every]
    firsts = [jnp.where(low, mems[head].astype(f32), states[head][0]).astype(bf16) for head in every]
    seconds = [
        jnp.where(low, swaps[head].astype(f32), states[head][1]).astype(bf16) for head in every
    ]
    asked = [
        jnp.where(low, queries[head], older * queries[1 - head]).astype(bf16) for head in every
    ]
    told = [jnp.where(low, grads[head], older * grads[1 - head]).astype(bf16) for head in every]
    key_bfs = [jnp.where(low, keys[head], 0.0).astype(bf16) for head in every]
    read_inners = [dot_nt(asked[head], firsts[head]) for head in every]
    read_grads = [dot_nt(told[head], seconds[head]) for head in every]
    inners = [dot_nt(key_bfs[head], mems[head]) for head in every]
    key_twices = [jnp.where(low, keys[head], keys[1 - head]) for head in every]
    scales = [
        jnp.where(low, columns[:, head : head + 1], columns[:, 8 + head : 9 + head])
        for head in every
    ]
    late_bfs = [[member.astype(bf16) for member in lates[head]] for head in every]
    key_scaled = [(key_twices[head] * scales[head]).astype(bf16) for head in every]
    grad_descents = [dot_nt(key_scaled[head], late_bfs[head][0]) for head in every]
    read_backs, reads = [], []
    for head in every:
        _, _, active, slope = half_swish(read_inners[head])
        grad_inner = (read_grads[head] * slope).astype(bf16)
        read_backs.append(dot_nn(grad_inner, firsts[head]))
        reads.append((dot_tn(grad_inner, asked[head]), dot_tn(active.astype(bf16), told[head])))
    actives, slopes, curves = [], [], []
    for head in every:
        turn, _, active, slope = half_swish(inners[head])
        actives.append(active.astype(bf16))
        slopes.append(slope)
        curves.append(0.5 - turn * (slope - 0.5))
    errors = [
        jnp.where(low, dot_nn(actives[head], swaps[head]) - values[head], 0.0) for head in every
    ]
    error_bfs = [error.astype(bf16) for error in errors]
    pulled = [dot_nt(error_bfs[head], swaps[head]) for head in every]
    active_backs = [dot_nn(actives[head], late_bfs[head][1]) for head in every]
    for head in every:
        back = read_backs[head]
        turned = swap_halves(back)
        if head == 0:
            back = jnp.where(low, MEMORY_SCALE * (back + older * turned), 0.0)
        else:
            back = jnp.where(low, 0.0, MEMORY_SCALE * (turned + older * back))
        grad_query = grad_query + back
    descents = [(pulled[head] * slopes[head]).astype(bf16) for head in every]
    grad_pulled = [(grad_descents[head] * slopes[head]).astype(bf16) for head in every]
    curved = [grad_descents[head] * pulled[head] * curves[head] for head in every]
    back_keys = [dot_nn(descents[head], late_bfs[head][0]) for head in every]
    pulled_backs = [dot_nn(grad_pulled[head], swaps[head]) for head in every]
    error_twices = [errors[head] + swap_halves(errors[head]) for head in every]
    error_scaled = [(error_twices[head] * scales[head]).astype(bf16) for head in every]
    error_backs = []
    for head in every:
        weight_grad = key_twices[head] * back_keys[head] + error_twices[head] * active_backs[head]
        grad_state_weight = lane_sum(jnp.where(low, weight_grad, 0.0))
        grad_write_weight = lane_sum(jnp.where(low, 0.0, weight_grad))
        write_grads = jnp.where(wide == head, grad_state_weight, write_grads)
        write_grads = jnp.where(wide == 8 + head, grad_write_weight, write_grads)
        back = active_backs[head] * scales[head]
        back = jnp.where(low, back + swap_halves(back) + pulled_backs[head], 0.0)
        error_backs.append(back)
        grad_value = grad_value - (back if head == 0 else swap_halves(back))
    back_bfs = [back.astype(bf16) for back in error_backs]
    grad_actives = [
        dot_nt(error_scaled[head], late_bfs[head][1]) + dot_nt(back_bfs[head], swaps[head])
        for head in every
    ]
    grad_inners = [
        (curved[head] + grad_actives[head] * slopes[head]).astype(bf16) for head in every
    ]
    for head in every:
        back = back_keys[head] * scales[head]
        back = back + swap_halves(back) + dot_nn(grad_inners[head], mems[head])
        back = jnp.where(low, MEMORY_SCALE * back, 0.0)
        grad_key = grad_key + (back if head == 0 else swap_halves(back))
        write_one = dot_tn(grad_inners[head], key_bfs[head])
        write_two = dot_tn(grad_pulled[head], error_bfs[head])
        write_two = write_two + dot_tn(actives[head], back_bfs[head])
        read_one, read_two = reads[head]
        dmem_ref[head] += jnp.where(low, read_one + write_one, swap_halves(read_two + write_two))

        (late_one, late_two), (state_one, state_two) = lates[head], states[head]
        factor, blend = state_factors(scan["totals"], head, low)
        same = late_one * state_one + late_two * state_two
        cross = late_one * swap_halves(state_one) + late_two * swap_halves(state_two)
        same_low = jnp.sum(lane_sum(jnp.where(low, same, 0.0)), axis=0, keepdims=True)
        same_high = jnp.sum(lane_sum(jnp.where(low, 0.0, same)), axis=0, keepdims=True)
        cross_high = jnp.sum(lane_sum(jnp.where(low, 0.0, cross)), axis=0, keepdims=True)
        keep_start = jnp.where(sublane == head, same_low, keep_start)
        fade_start = jnp.where(sublane == head, same_high, fade_start)
        mix_start = jnp.where(sublane == head, cross_high, mix_start)
        for member, old, read in ((0, late_one, read_one), (1, late_two, read_two)):
            turned = jnp.where(low, blend * swap_halves(old), read)
            late[head, member] = factor * old + turned

    lane = lane_index((8, SEG))
    write_rows = jnp.transpose(write_grads)
    grad_state_rows, grad_write_rows = write_rows[0:8], write_rows[8:16]
    written = scan["written"]
    keep_grads = chain_rows(scan["carry"], grad_state_rows * written, keep_start, lane)
    mix_grads = chain_rows(scan["carry"], grad_write_rows * written, mix_start, lane)
    mix_next = scan["carry"] * mix_grads + grad_write_rows * written
    fade_grads = chain_rows(scan["fade"], mix_next, fade_start, lane)
    grad_written = grad_state_rows * scan["keep_after"] + grad_write_rows * scan["reach"]
    grad_carry = keep_grads * scan["keep_after"] + mix_grads * scan["reach"]
    grad_fade = fade_grads * scan["fade_after"]
    used = sublane < heads
    forget, momentum, step = scan["forget"], scan["momentum"], scan["step"]
    forget_back = -grad_fade * scan["keep"] * forget * (1.0 - forget)
    momentum_back = grad_carry * scan["keep"] * momentum * (1.0 - momentum)
    step_back = -THETA_SCALE * grad_written * scan["live"] * step * (1.0 - step)
    gate_back = jnp.concatenate(
        [
            jnp.where(used, forget_back, 0.0),
            jnp.where(used, momentum_back, 0.0),
            jnp.where(used, step_back, 0.0),
            jnp.zeros((LANES - 24, SEG), f32),
        ],
        axis=0,
    )
    gate_back = jnp.transpose(gate_back)
    dbias_ref[0:1, :] += jnp.sum(gate_back, axis=0, keepdims=True)
    draw_ref[:, 3 * LANES :] = gate_back.astype(bf16)

    grad_mixed = jnp.concatenate(
        [
            unit_pair_pull(query_unit, query_inverse, grad_query, low),
            unit_pair_pull(key_unit, key_inverse, grad_key, low),
            grad_value,
        ],
        axis=1,
    )
    back = conv_ref[0:1, :] * grad_mixed
    dconv_ref[0:1, :] += jnp.sum(grad_mixed * ext[8 : 8 + SEG, :], axis=0, keepdims=True)
    for offset in range(1, 4):
        kept = jnp.where(place >= offset, grad_mixed, 0.0)
        member = offset - 1
        shifted_rows[member, SEG : SEG + 8, :] = shifted_rows[member, 0:8, :]
        shifted_rows[member, 0:SEG, :] = kept
        back = back + conv_ref[offset : offset + 1, :] * shifted_rows[
            member, offset : offset + SEG, :
        ]
        dconv_ref[offset : offset + 1, :] += jnp.sum(
            kept * ext[8 - offset : 8 - offset + SEG, :], axis=0, keepdims=True
        )
    draw_ref[:, : 3 * LANES] = back.astype(bf16)


def whole_of(array):
    zeros = (0,) * array.ndim
    return pl.BlockSpec(array.shape, lambda n: zeros)


def mix_forward(collective, plan, heads, raw, gates, live, *constants):
    length = raw.shape[0]
    count = length // SEG
    row_block = pl.BlockSpec((SEG, LANES), lambda n: (n, 0))
    smem = pl.BlockSpec(memory_space=pltpu.SMEM)
    carried_in, carried_out = plan.specs(True)
    return pl.pallas_call(
        partial(forward_kernel, heads, plan),
        grid=(count,),
        in_specs=[
            pl.BlockSpec((SEG, 3 * LANES), lambda n: (n, 0)),
            row_block,
            pl.BlockSpec((1, 8, SEG), lambda n: (n, 0, 0)),
        ]
        + [whole_of(member) for member in constants[:4]]
        + [smem, smem]
        + carried_in,
        out_specs=[
            row_block,
            row_block,
            row_block,
            pl.BlockSpec((SEG, 8), lambda n: (n, 0)),
            pl.BlockSpec((1, heads, 2, MH, LANES), lambda n: (n, 0, 0, 0, 0)),
        ]
        + carried_out,
        out_shape=[
            jax.ShapeDtypeStruct((length, LANES), bf16),
            jax.ShapeDtypeStruct((length, LANES), bf16),
            jax.ShapeDtypeStruct((length, LANES), bf16),
            jax.ShapeDtypeStruct((length, 8), f32),
            jax.ShapeDtypeStruct((count, heads, 2, MH, LANES), bf16),
        ]
        + plan.shapes,
        scratch_shapes=[
            pltpu.VMEM((SEG + 8, 3 * LANES), f32),
            pltpu.VMEM((2 * SEG + LANES, LANES), bf16),
            pltpu.VMEM((2 * SEG + LANES, LANES), bf16),
            pltpu.VMEM((8, SEG), f32),
            pltpu.VMEM((heads, 2, MH, LANES), f32),
            pltpu.VMEM((SEG, 2 * SEG + LANES), f32),
        ]
        + plan.scratch,
        compiler_params=pltpu.CompilerParams(
            dimension_semantics=("arbitrary",),
            collective_id=collective,
            has_side_effects=True,
            vmem_limit_bytes=VMEM_GRANT,
        ),
        name="mix_forward",
    )(raw, gates, live, *constants, *plan.arrays)


def mix_backward(
    collective, plan, heads, raw, gates, live, keys, values, totals, states, grad, *constants
):
    length = raw.shape[0]
    count = length // SEG

    def here(n):
        return count - 1 - n

    def before(n):
        return jnp.maximum(count - 2 - n, 0)

    row_block = pl.BlockSpec((SEG, LANES), lambda n: (here(n), 0))
    prev_block = pl.BlockSpec((SEG, LANES), lambda n: (before(n), 0))
    tail_rows = SEG // 16
    smem = pl.BlockSpec(memory_space=pltpu.SMEM)
    carried_in, carried_out = plan.specs(True)
    return pl.pallas_call(
        partial(backward_kernel, heads, plan),
        grid=(count,),
        in_specs=[
            pl.BlockSpec((SEG, 3 * LANES), lambda n: (here(n), 0)),
            pl.BlockSpec((16, 3 * LANES), lambda n: (jnp.maximum(here(n) * tail_rows - 1, 0), 0)),
            row_block,
            pl.BlockSpec((1, 8, SEG), lambda n: (here(n), 0, 0)),
            pl.BlockSpec((1, 8, SEG), lambda n: (before(n), 0, 0)),
            row_block,
            prev_block,
            row_block,
            prev_block,
            pl.BlockSpec((SEG, 8), lambda n: (here(n), 0)),
            pl.BlockSpec((1, heads, 2, MH, LANES), lambda n: (here(n), 0, 0, 0, 0)),
            row_block,
        ]
        + [whole_of(member) for member in constants[:4]]
        + [smem, smem]
        + carried_in,
        out_specs=[
            pl.BlockSpec((SEG, 4 * LANES), lambda n: (here(n), 0)),
            pl.BlockSpec((heads, MH, LANES), lambda n: (0, 0, 0)),
            pl.BlockSpec((8, 3 * LANES), lambda n: (0, 0)),
            pl.BlockSpec((2 * P_SIZE, LANES), lambda n: (0, 0)),
            pl.BlockSpec((8, LANES), lambda n: (0, 0)),
        ]
        + carried_out,
        out_shape=[
            jax.ShapeDtypeStruct((length, 4 * LANES), bf16),
            jax.ShapeDtypeStruct((heads, MH, LANES), f32),
            jax.ShapeDtypeStruct((8, 3 * LANES), f32),
            jax.ShapeDtypeStruct((2 * P_SIZE, LANES), f32),
            jax.ShapeDtypeStruct((8, LANES), f32),
        ]
        + plan.shapes,
        scratch_shapes=[
            pltpu.VMEM((SEG + 8, 3 * LANES), f32),
            pltpu.VMEM((3, SEG + 8, 3 * LANES), f32),
            pltpu.VMEM((SEG, LANES), f32),
            pltpu.VMEM((SEG, LANES), f32),
            pltpu.VMEM((heads, 2, MH, LANES), f32),
            pltpu.VMEM((2 * SEG + LANES, LANES), bf16),
            pltpu.VMEM((2 * SEG + LANES, LANES), bf16),
            pltpu.VMEM((SEG, 2 * SEG + LANES), f32),
        ]
        + plan.scratch,
        compiler_params=pltpu.CompilerParams(
            dimension_semantics=("arbitrary",),
            collective_id=collective,
            has_side_effects=True,
            vmem_limit_bytes=VMEM_GRANT,
        ),
        name="mix_backward",
    )(
        raw,
        raw,
        gates,
        live,
        live,
        keys,
        keys,
        values,
        values,
        totals,
        states,
        grad,
        *constants,
        *plan.arrays,
    )


class PlaneGather:
    def __init__(self, seqs, source, target, sems):
        self.source, self.target = source, target
        self.local, self.far_send, self.far_recv = sems[:3]
        self.near_send, self.near_recv, self.relay_send, self.relay_recv = sems[3:]
        self.chips = seqs // 2
        self.relayed = self.chips == 4
        self.seq, self.line = lax.axis_index("seq"), lax.axis_index("fsdp")
        self.chip, self.core = self.seq // 2, lax.rem(self.seq, 2)
        self.half = source.shape[0] // 2

    @staticmethod
    def sems(seqs):
        dma = pltpu.SemaphoreType.DMA
        return [dma((1,))] + [dma((seqs // 2,))] * 4 + [dma((2,))] * 2

    def chip_at(self, k):
        side = math.isqrt(self.chips)
        across = lax.rem(lax.rem(self.chip, side) + lax.rem(k, side), side)
        along = lax.rem(self.chip // side + k // side, side)
        return along * side + across

    def copy(self, source, target, send, recv, place):
        return pltpu.make_async_remote_copy(
            src_ref=source,
            dst_ref=target,
            send_sem=send,
            recv_sem=recv,
            device_id=(place, self.line),
            device_id_type=MESH,
        )

    def own(self):
        return pltpu.make_async_copy(self.source, self.target.at[self.seq], self.local.at[0])

    def far(self, q, slot):
        place = 2 * q + self.core
        block = self.target.at[2 * slot + self.core]
        return self.copy(self.source, block, self.far_send.at[q], self.far_recv.at[slot], place)

    def near(self, q, side):
        block = self.target.at[2 * q + (self.core if side == 0 else 1 - self.core)]
        place = 2 * self.chip + 1 - self.core
        return self.copy(block, block, self.near_send.at[q], self.near_recv.at[q], place)

    def near_own(self):
        block = self.target.at[self.seq]
        place = 2 * self.chip + 1 - self.core
        send, recv = self.near_send.at[self.chip], self.near_recv.at[self.chip]
        return self.copy(self.source, block, send, recv, place)

    def relay(self, part, q, to):
        rows = pl.ds(part * self.half, self.half)
        block = self.target.at[2 * q + self.core, rows]
        send, recv = self.relay_send.at[part], self.relay_recv.at[part]
        return self.copy(block, block, send, recv, 2 * to + self.core)

    def loop(self, first, body):
        def step(k, carry):
            body(k)
            return carry

        lax.fori_loop(first, self.chips, step, 0)

    def start(self):
        self.near_own().start()
        if self.relayed:
            for k in (1, 2):
                self.far(self.chip_at(k), self.chip).start()
        else:
            self.loop(1, lambda k: self.far(self.chip_at(k), self.chip).start())
        self.own().start()

    def step(self, k):
        q = self.chip_at(k)

        @pl.when(k == 0)
        def _():
            self.own().wait()

        if self.relayed:
            across, along, diagonal = (self.chip_at(i) for i in (1, 2, 3))

            @pl.when(k == 1)
            def _():
                self.far(across, across).wait_recv()
                self.relay(0, across, along).start()
                self.near(across, 0).start()
                self.far(along, along).wait_recv()
                self.relay(1, along, across).start()
                self.near(along, 0).start()

            @pl.when(k == 3)
            def _():
                self.relay(0, diagonal, along).wait_recv()
                self.relay(1, diagonal, across).wait_recv()
                self.near(diagonal, 0).start()

        else:

            @pl.when(k > 0)
            def _():
                self.far(q, q).wait_recv()
                self.near(q, 0).start()

        self.near(q, 1).wait_recv()

    def finish(self):
        self.near_own().wait_send()
        self.loop(1, lambda k: self.near(self.chip_at(k), 0).wait_send())
        if self.relayed:
            across, along = self.chip_at(1), self.chip_at(2)
            self.far(across, across).wait_send()
            self.far(along, along).wait_send()
            self.relay(0, across, along).wait_send()
            self.relay(1, along, across).wait_send()
        else:
            self.loop(1, lambda k: self.far(self.chip_at(k), self.chip_at(k)).wait_send())

class LineGather:
    def __init__(self, lines, source, target, sems, keep=True):
        self.lines, self.source, self.target = lines, source, target
        self.local, self.send, self.recv = sems
        self.keep = keep
        self.seq, self.line = lax.axis_index("seq"), lax.axis_index("fsdp")

    @staticmethod
    def sems(lines):
        dma = pltpu.SemaphoreType.DMA
        return [dma((1,)), dma((lines,)), dma((lines,))]

    def at(self, k):
        return lax.rem(self.line + k, self.lines)

    def copy(self, source, target, send, recv, to):
        return pltpu.make_async_remote_copy(
            src_ref=source,
            dst_ref=target,
            send_sem=send,
            recv_sem=recv,
            device_id=(self.seq, to),
            device_id_type=MESH,
        )

    def own(self):
        return pltpu.make_async_copy(self.source, self.target.at[self.line], self.local.at[0])

    def far(self, i, slot):
        source = self.source if self.keep else self.target.at[self.line]
        return self.copy(source, self.target.at[slot], self.send.at[i], self.recv.at[slot], i)

    def loop(self, body):
        def step(k, carry):
            body(k)
            return carry

        lax.fori_loop(1, self.lines, step, 0)

    def start_one(self, k):
        self.far(self.at(k), self.line).start()

    def start(self):
        self.loop(self.start_one)
        if self.keep:
            self.own().start()

    def arrive(self):
        if self.keep:
            self.own().wait()
        self.loop(lambda k: self.far(self.at(k), self.at(k)).wait_recv())

    def finish(self):
        self.loop(lambda k: self.far(self.at(k), self.at(k)).wait_send())


class LineSum:
    def __init__(self, lines, source, landed, target, sems):
        self.lines, self.source, self.landed, self.target = lines, source, landed, target
        self.send, self.recv, self.relay_send, self.relay_recv = sems
        self.seq, self.line = lax.axis_index("seq"), lax.axis_index("fsdp")
        self.relayed = lines == 4
        self.half = source.shape[1] // 2

    @staticmethod
    def sems(lines):
        dma = pltpu.SemaphoreType.DMA
        return [dma((lines,)), dma((lines,)), dma((2,)), dma((2,))]

    def at(self, k):
        return lax.rem(self.line + k, self.lines)

    def copy(self, source, target, send, recv, to):
        return pltpu.make_async_remote_copy(
            src_ref=source,
            dst_ref=target,
            send_sem=send,
            recv_sem=recv,
            device_id=(self.seq, to),
            device_id_type=MESH,
        )

    def far(self, i, slot):
        return self.copy(
            self.source.at[i], self.landed.at[slot], self.send.at[i], self.recv.at[slot], i
        )

    def relay(self, part, to):
        rows = pl.ds(part * self.half, self.half)
        return self.copy(
            self.source.at[self.at(2), rows],
            self.landed.at[to, rows],
            self.relay_send.at[part],
            self.relay_recv.at[part],
            to,
        )

    def loop(self, body):
        def step(k, carry):
            body(k)
            return carry

        lax.fori_loop(1, self.lines, step, 0)

    def start(self):
        if self.relayed:
            self.relay(0, self.at(1)).start()
            self.relay(1, self.at(3)).start()
        else:
            self.loop(lambda k: self.far(self.at(k), self.line).start())

    def middle(self):
        if not self.relayed:
            return
        for part, to in ((0, self.at(1)), (1, self.at(3))):
            rows = pl.ds(part * self.half, self.half)
            block = self.landed.at[self.line, rows]
            send, recv = self.relay_send.at[part], self.relay_recv.at[part]
            self.copy(block, block, send, recv, to).wait_recv()

            def add(i, carry, to=to, part=part):
                at = part * self.half + i
                both = self.source[to, at].astype(f32) + self.landed[self.line, at].astype(f32)
                self.source[to, at] = both.astype(bf16)
                return carry

            lax.fori_loop(0, self.half, add, 0)
            self.far(to, self.line).start()

    def others(self):
        return (self.at(1), self.at(3)) if self.relayed else [self.at(k) for k in range(1, self.lines)]

    def arrive(self):
        for i in self.others():
            self.far(i, i).wait_recv()

    def total(self, i):
        whole = self.source[self.line, i].astype(f32)
        for other in self.others():
            whole = whole + self.landed[other, i].astype(f32)
        return whole

    def finish(self):
        for i in self.others():
            self.far(i, i).wait_send()
        if self.relayed:
            self.relay(0, self.at(1)).wait_send()
            self.relay(1, self.at(3)).wait_send()


def exchange_phases(axes, counts, inputs, outputs, scratch):
    seqs, lines = axes
    chips = seqs // 2
    devices = seqs * lines
    seq, line = lax.axis_index("seq"), lax.axis_index("fsdp")
    me = seq * lines + line
    chip, core = seq // 2, lax.rem(seq, 2)
    sibling = (2 * chip + 1 - core, line)

    def twin(q):
        return (2 * q + core, line)

    def point(i):
        return (i // lines, lax.rem(i, lines))

    def loop(first, last, body):
        def step(k, carry):
            body(k)
            return carry

        lax.fori_loop(first, last, step, 0)

    position = 0
    groups = []
    for count in counts:
        groups.append((inputs[position : position + count], outputs[position : position + count]))
        position += count
    scratch = list(scratch)

    def take(number):
        taken = scratch[:number]
        del scratch[:number]
        return taken

    starts = []

    sums = []
    for source, target in zip(*groups[5]):
        pair, landed, pair_send, pair_recv, far_send, far_recv = take(6)

        def pair_copy(q, source=source, pair=pair, send=pair_send, recv=pair_recv):
            return pltpu.make_async_remote_copy(
                src_ref=source.at[2 * q + 1 - core],
                dst_ref=pair.at[q],
                send_sem=send.at[q],
                recv_sem=recv.at[q],
                device_id=sibling,
                device_id_type=MESH,
            )

        def far_copy(q, slot, pair=pair, landed=landed, send=far_send, recv=far_recv):
            return pltpu.make_async_remote_copy(
                src_ref=pair.at[q],
                dst_ref=landed.at[slot],
                send_sem=send.at[q],
                recv_sem=recv.at[slot],
                device_id=twin(q),
                device_id_type=MESH,
            )

        starts.append(
            lambda f=pair_copy: loop(1, chips + 1, lambda k: f(lax.rem(chip + k, chips)).start())
        )
        sums.append((source, target, pair, landed, pair_copy, far_copy))

    spread = []
    for source, target in zip(*groups[0]):
        gather = PlaneGather(seqs, source, target, take(7))
        starts.append(gather.start)
        spread.append(gather)

    direct = []
    for kind, (sources, targets) in (
        ("plane", groups[1]),
        ("line", groups[2]),
        ("every", groups[3]),
        ("all", groups[4]),
    ):
        for source, target in zip(sources, targets):
            local, send, recv = take(3)
            if kind == "plane":
                number, mine = seqs, seq
            elif kind == "line":
                number, mine = lines, line
            else:
                number, mine = devices, me

            def piece(i, source=source, kind=kind, number=number):
                if kind == "all" or (kind == "line" and source.ndim == 2):
                    return source
                if kind == "every" and source.shape[0] != number:
                    return source.at[i // lines]
                return source.at[i]

            def place(i, kind=kind):
                if kind == "plane":
                    return (i, line)
                if kind == "line":
                    return (seq, i)
                return point(i)

            def copy(i, slot, target=target, send=send, recv=recv, piece=piece, place=place):
                return pltpu.make_async_remote_copy(
                    src_ref=piece(i),
                    dst_ref=target.at[slot],
                    send_sem=send.at[i],
                    recv_sem=recv.at[slot],
                    device_id=place(i),
                    device_id_type=MESH,
                )

            def own(target=target, local=local, piece=piece, mine=mine):
                return pltpu.make_async_copy(piece(mine), target.at[mine], local.at[0])

            def start(copy=copy, own=own, mine=mine, number=number):
                loop(1, number, lambda k: copy(lax.rem(mine + k, number), mine).start())
                own().start()

            starts.append(start)
            direct.append((own, copy, mine, number))

    merges = []
    rows = 32
    for source, target in zip(*groups[7]):
        landed, summed, local, plane_send, plane_recv = take(5)
        line_sum = LineSum(lines, source, landed, target, take(4))

        def onward(i, slot, summed=summed, target=target, send=plane_send, recv=plane_recv):
            return pltpu.make_async_remote_copy(
                src_ref=summed.at[i],
                dst_ref=target.at[slot],
                send_sem=send.at[i],
                recv_sem=recv.at[slot],
                device_id=(i, line),
                device_id_type=MESH,
            )

        def keep(summed=summed, target=target, local=local):
            return pltpu.make_async_copy(summed.at[seq], target.at[seq], local.at[0])

        starts.insert(0, line_sum.start)
        merges.append((summed, line_sum, onward, keep))

    line_gathers = []
    for source, target in zip(*groups[8]):
        gather = LineGather(lines, source, target, take(3))
        starts.append(gather.start)
        line_gathers.append(gather)

    def begin():
        for start in starts:
            start()

    def middle():
        for source, target, pair, landed, pair_copy, far_copy in sums:

            def combine(k, source=source, pair=pair, pair_copy=pair_copy, far_copy=far_copy):
                q = lax.rem(chip + k, chips)
                pair_copy(q).wait_recv()

                def add(r):
                    part = pl.ds(pl.multiple_of(r * rows, rows), rows)
                    both = source[2 * q + core, part, :].astype(f32) + pair[q, part, :].astype(f32)
                    pair[q, part, :] = both.astype(bf16)

                loop(0, source.shape[1] // rows, add)

                @pl.when(k < chips)
                def _():
                    far_copy(q, chip).start()

            loop(1, chips + 1, combine)
        for gather in spread:
            gather.step(0)
            gather.step(1)
        for summed, line_sum, onward, keep in merges:
            line_sum.middle()
            line_sum.arrive()

            def add_up(k, summed=summed, line_sum=line_sum, onward=onward):
                i = lax.rem(seq + k, seqs)
                summed[i] = line_sum.total(i).astype(bf16)

                @pl.when(k < seqs)
                def _():
                    onward(i, seq).start()

            loop(1, seqs + 1, add_up)
            keep().start()

    def finish():
        for gather in spread:
            gather.loop(2, gather.step)
        for own, copy, mine, number in direct:

            def end(k, copy=copy, mine=mine, number=number):
                i = lax.rem(mine + k, number)
                copy(i, i).wait_recv()
                copy(i, i).wait_send()

            loop(1, number, end)
            own().wait()
        for gather in spread:
            gather.finish()
        for gather in line_gathers:
            gather.arrive()
            gather.finish()
        for source, target, pair, landed, pair_copy, far_copy in sums:

            def end_sum(k, far_copy=far_copy):
                q = lax.rem(chip + k, chips)
                far_copy(q, q).wait_recv()

            loop(1, chips, end_sum)

            def add_all(r, target=target, pair=pair, landed=landed):
                part = pl.ds(pl.multiple_of(r * rows, rows), rows)
                whole = pair[chip, part, :].astype(f32)
                for k in range(1, chips):
                    whole = whole + landed[lax.rem(chip + k, chips), part, :].astype(f32)
                target[part, :] = whole

            loop(0, target.shape[0] // rows, add_all)
            loop(1, chips, lambda k, f=far_copy: f(lax.rem(chip + k, chips), chip).wait_send())
            loop(0, chips, lambda q, f=pair_copy: f(q).wait_send())
        for summed, line_sum, onward, keep in merges:
            line_sum.finish()

            def end_merge(k, onward=onward):
                i = lax.rem(seq + k, seqs)
                onward(i, i).wait_recv()
                onward(i, seq).wait_send()

            loop(1, seqs, end_merge)
            keep().wait()

    return begin, middle, finish


def greet_all(axes, kinds):
    seqs, lines = axes
    seq, line = lax.axis_index("seq"), lax.axis_index("fsdp")
    barrier = pltpu.get_barrier_semaphore()

    def signal(place):
        pl.semaphore_signal(barrier, inc=1, device_id=place, device_id_type=MESH)

    def loop(last, body):
        def step(k, carry):
            body(k)
            return carry

        lax.fori_loop(1, last, step, 0)

    if "all" in kinds:
        devices = seqs * lines
        me = seq * lines + line

        def greet(k):
            i = lax.rem(me + k, devices)
            signal((i // lines, lax.rem(i, lines)))

        loop(devices, greet)
        pl.semaphore_wait(barrier, devices - 1)
        return
    met = 0
    if "plane" in kinds:
        loop(seqs, lambda k: signal((lax.rem(seq + k, seqs), line)))
        met += seqs - 1
    if "line" in kinds:
        loop(lines, lambda k: signal((seq, lax.rem(line + k, lines))))
        met += lines - 1
    pl.semaphore_wait(barrier, met)


KINDS = (
    "gathers",
    "planes",
    "to_line",
    "everys",
    "alls",
    "scatters",
    "relays",
    "merges",
    "line_gathers",
)


class Exchange:
    def __init__(self, **arrays):
        self.axes = seqs, lines = lax.axis_size("seq"), lax.axis_size("fsdp")
        chips, devices = seqs // 2, seqs * lines
        dma = pltpu.SemaphoreType.DMA
        groups = [tuple(arrays.get(kind, ())) for kind in KINDS]
        self.counts = tuple(len(group) for group in groups)
        self.arrays = [array for group in groups for array in group]
        scratch = {kind: [] for kind in KINDS}
        shapes, self.in_vmem = [], []
        kinds = set()
        for kind, group in zip(KINDS, groups):
            for array in group:
                shape, dtype = array.shape, array.dtype
                if kind == "gathers":
                    scratch[kind] += PlaneGather.sems(seqs)
                    shape = (seqs,) + shape
                elif kind == "planes":
                    scratch[kind] += [dma((1,)), dma((seqs,)), dma((seqs,))]
                elif kind == "to_line":
                    scratch[kind] += [dma((1,)), dma((lines,)), dma((lines,))]
                    shape = (lines,) + shape[-2:]
                elif kind == "everys":
                    scratch[kind] += [dma((1,)), dma((devices,)), dma((devices,))]
                    shape = (devices,) + shape[1:]
                elif kind == "alls":
                    scratch[kind] += [dma((1,)), dma((devices,)), dma((devices,))]
                    shape = (devices,) + shape
                elif kind == "scatters":
                    half = pltpu.VMEM((chips,) + shape[1:], bf16)
                    scratch[kind] += [half, half] + [dma((chips,))] * 4
                    shape, dtype = shape[1:], f32
                elif kind == "line_gathers":
                    scratch[kind] += LineGather.sems(lines)
                    shape = (lines,) + shape
                else:
                    raise ValueError(kind)
                shapes.append(jax.ShapeDtypeStruct(shape, dtype))
                self.in_vmem.append(kind == "scatters")
                if kind in ("everys", "alls"):
                    kinds.add("all")
                kinds.add("line" if kind in ("to_line", "line_gathers") else "plane")
        self.kinds = kinds
        self.shapes = shapes
        order = ("scatters", "gathers", "planes", "to_line", "everys", "alls", "line_gathers")
        self.scratch = [member for kind in order for member in scratch[kind]]

    def specs(self, gridded):
        if gridded:
            vmem = [
                pl.BlockSpec(
                    array.shape, lambda n, z=(0,) * array.ndim: z, pipeline_mode=pl.Buffered(1)
                )
                for array in self.arrays
            ]
            out = [
                pl.BlockSpec(array.shape, lambda n, z=(0,) * len(array.shape): z)
                for array in self.shapes
            ]
        else:
            vmem = out = [pl.BlockSpec(memory_space=pltpu.VMEM)] * len(self.arrays)
        plain = pl.BlockSpec(memory_space=pl.ANY)
        first = [one if inside else plain for one, inside in zip(vmem, self.in_vmem)]
        second = [one if inside else plain for one, inside in zip(out, self.in_vmem)]
        return first, second

    def phases(self, inputs, outputs, scratch):
        return exchange_phases(self.axes, self.counts, inputs, outputs, scratch)


PLANE = (0, 1, 0, 0, 0, 0, 0, 0, 0)
TO_LINE = (0, 0, 1, 0, 0, 0, 0, 0, 0)

MERGE = (0, 0, 0, 0, 0, 0, 0, 1, 0)


def round_up(number, step):
    return -(-number // step) * step


class Sizes:
    def __init__(self, seqs, lines):
        self.seqs, self.lines = seqs, lines
        self.chips, self.devices = seqs // 2, seqs * lines
        self.groups = min(HEAD_COUNT, seqs)
        self.copies = seqs // self.groups
        self.heads = HEAD_COUNT // self.groups
        self.width = self.heads * HEAD_SIZE
        self.share = D // self.devices
        self.memory = MH // self.devices
        self.piece = D // seqs
        self.hidden = FF // lines
        self.slab = self.hidden // seqs
        self.gate_at = round_up(3 * self.share, 8)
        self.mem_at = self.gate_at + round_up(max(self.share, 2 * P_SIZE), 8)
        self.rest_at = self.mem_at + round_up(self.heads * self.memory, 8)
        self.weight_rows = round_up(self.rest_at + 8, 16)
        self.grad_mem_at = round_up(4 * self.share, 8)
        self.grad_rest_at = self.grad_mem_at + round_up(self.heads * self.memory, 8)
        self.grad_rows = round_up(self.grad_rest_at + 16, 16)


def gate_choice(sizes, group, turned):
    shape = (LANES, 3 * HEAD_COUNT) if turned else (3 * HEAD_COUNT, LANES)
    lane = lax.broadcasted_iota(jnp.int32, shape, 0 if turned else 1)
    column = lax.broadcasted_iota(jnp.int32, shape, 1 if turned else 0)
    head = lane % 8
    chosen = (lane // 8 == column // HEAD_COUNT) & (head < sizes.heads)
    chosen = chosen & (column % HEAD_COUNT == group * sizes.heads + head)
    return jnp.where(chosen, 1.0, 0.0).astype(bf16)


def first_kernel(
    sizes,
    token_ref,
    qkv_ref,
    gate_ref,
    conv_ref,
    pkey_ref,
    pvalue_ref,
    gain_one_ref,
    gain_two_ref,
    live_ref,
    mem_ref,
    ffn_gate_ref,
    ffn_up_ref,
    ffn_down_ref,
    out_ref,
    normed_out,
    raw_out,
    gate_out,
    matrix_out,
    mem_out,
    swap_out,
    gain_out,
    taps_out,
    persist_out,
    live_out,
    ffn_out,
    ffn_relayed,
    out_rows,
    out_all,
    rows_all,
    pack,
    pack_rows,
    ffn_pack,
    ffn_relay,
    got,
    conv_full,
    persist_full,
    mem_full,
    matrix_full,
    *sems,
):
    seqs, lines, share, width = sizes.seqs, sizes.lines, sizes.share, sizes.width
    seq, line = lax.axis_index("seq"), lax.axis_index("fsdp")
    group = seq // sizes.copies
    axes = (seqs, lines)
    greet_all(axes, ("plane", "line"))
    gather = PlaneGather(seqs, token_ref, rows_all, sems[:7])
    weights = exchange_phases(axes, PLANE, [pack], [got.at[line]], sems[7:10])
    weights_line = LineGather(lines, None, got, sems[10:13], keep=False)
    ffn = exchange_phases(axes, PLANE, [ffn_pack], [ffn_out], sems[13:16])
    outs = exchange_phases(axes, TO_LINE, [out_ref], [out_rows], sems[16:19])
    relay = exchange_phases(axes, PLANE, [ffn_relay], [ffn_relayed.at[line]], sems[19:22])
    relay_line = LineGather(lines, None, ffn_relayed, sems[22:25], keep=False)
    out_gather = PlaneGather(seqs, out_rows, out_all, sems[25:32])
    for to in range(seqs):
        ffn_relay[to] = ffn_gate_ref[:, to * sizes.slab : (to + 1) * sizes.slab]
    relay[0]()
    outs[0]()

    gate_at, mem_at, rest_at = sizes.gate_at, sizes.mem_at, sizes.rest_at
    pack_rows[...] = jnp.zeros_like(pack_rows)
    pack_rows[gate_at : gate_at + P_SIZE, HEAD_SIZE : HEAD_SIZE + share] = pkey_ref[...].astype(f32)
    pack_rows[gate_at + P_SIZE : gate_at + 2 * P_SIZE, HEAD_SIZE : HEAD_SIZE + share] = pvalue_ref[
        ...
    ].astype(f32)
    pack_rows[rest_at : rest_at + 4, : 3 * share] = conv_ref[...].astype(f32)
    pack_rows[rest_at + 4 : rest_at + 5, :share] = gain_one_ref[...].astype(f32)
    pack_rows[rest_at + 5 : rest_at + 6, :share] = gain_two_ref[...].astype(f32)
    live = live_ref[...].astype(f32)
    pack_rows[rest_at + 6 : rest_at + 7, :] = live[:, :LANES]
    pack_rows[rest_at + 7 : rest_at + 8, :] = live[:, LANES:]
    qkv = qkv_ref[...].astype(f32)
    gate = gate_ref[...]
    for to in range(seqs):
        other = to // sizes.copies
        for part in range(3):
            first = part * D + other * width
            pack_rows[part * share : (part + 1) * share, :width] = qkv[:, first : first + width]
        chosen = dot_nn(gate, gate_choice(sizes, other, False))
        pack_rows[gate_at : gate_at + share, :HEAD_SIZE] = chosen[:, :HEAD_SIZE]
        for head in range(sizes.heads):
            first = mem_at + head * sizes.memory
            pack_rows[first : first + sizes.memory, :] = mem_ref[other * sizes.heads + head].astype(
                f32
            )
        pack[to] = pack_rows[...].astype(bf16)
    weights[0]()
    gather.start()
    piece = sizes.piece
    for to in range(seqs):
        columns = slice(to * sizes.slab, (to + 1) * sizes.slab)
        ffn_pack[to, :piece, :] = ffn_up_ref[:, columns]
        turned = jnp.transpose(ffn_down_ref[columns, :].astype(f32))
        ffn_pack[to, piece:, :] = turned.astype(bf16)
    ffn[0]()
    relay[2]()
    relay_line.start_one(1)
    weights[2]()
    weights_line.start_one(1)
    weights_line.start_one(2)
    gather.step(0)
    gather.step(1)
    weights_line.start_one(3)
    outs[2]()
    out_gather.start()
    for k in range(2, lines):
        relay_line.start_one(k)
    gather.loop(2, gather.step)
    for k in range(4, lines):
        weights_line.start_one(k)
    out_gather.step(0)
    out_gather.loop(1, out_gather.step)
    weights_line.arrive()

    aligned = share % 16 == 0
    matrix = matrix_out if aligned else matrix_full
    lane = lane_index((share, LANES))
    for i in range(sizes.devices):
        block = got[i % lines, i // lines].astype(f32)
        rows = slice(i * share, (i + 1) * share)
        for part in range(3):
            columns = slice(part * LANES, (part + 1) * LANES)
            matrix[rows, columns] = block[part * share : (part + 1) * share].astype(matrix.dtype)
        chosen = jnp.where(lane < 24, block[gate_at : gate_at + share], 0.0)
        matrix[rows, 3 * LANES :] = chosen.astype(matrix.dtype)
        for head in range(sizes.heads):
            first = mem_at + head * sizes.memory
            mem_full[head, i * sizes.memory : (i + 1) * sizes.memory, :] = block[
                first : first + sizes.memory
            ]
        rest = block[rest_at : rest_at + 8]
        conv_full[0:4, i * 3 * share : (i + 1) * 3 * share] = rest[0:4, : 3 * share]
        gain_out[4:6, i * share : (i + 1) * share] = rest[4:6, :share]
    if not aligned:
        matrix_out[...] = matrix_full[...].astype(bf16)
    for head in range(sizes.heads):
        mem_out[head] = mem_full[head].astype(bf16)
        swap_out[head] = swap_halves(mem_full[head]).astype(bf16)
    taps_out[...] = jnp.zeros_like(taps_out)
    for part in range(3):
        whole = conv_full[:, part * D : (part + 1) * D]
        turned = pltpu.roll(whole, lax.rem(D - group * width, D), 1)
        taps_out[0:4, part * LANES : part * LANES + width] = turned[0:4, :width]
    persist_full[...] = jnp.zeros_like(persist_full)
    for part in range(width // share):
        i = group * (width // share) + part
        block = got[lax.rem(i, lines), i // lines].astype(f32)
        persist_full[:, part * share : (part + 1) * share] = block[
            gate_at : gate_at + 2 * P_SIZE, HEAD_SIZE : HEAD_SIZE + share
        ]
    persist_out[...] = persist_full[...].astype(bf16)
    for s in range(seqs):
        block = got[line, s].astype(f32)
        live_out[s] = jnp.zeros((8, SEG), f32)
        live_out[s, 0:1, :LANES] = block[rest_at + 6 : rest_at + 7]
        live_out[s, 0:1, LANES:] = block[rest_at + 7 : rest_at + 8]

    gain = gain_out[4:5, :]

    def work(k, carry):
        q = gather.chip_at(k)
        both = pl.ds(2 * q, 2)
        rows = rows_all[both].reshape(2 * SEG, D).astype(f32)
        normed = (rows * norm_scale(rows) * gain).astype(bf16)
        projected = dot_nn(normed, matrix_out[...])
        normed_out[both] = normed.reshape(2, SEG, D)
        raw_out[both] = projected[:, : 3 * LANES].astype(bf16).reshape(2, SEG, 3 * LANES)
        gate_out[both] = projected[:, 3 * LANES :].reshape(2, SEG, LANES)
        return carry

    lax.fori_loop(0, sizes.chips, work, 0)
    gather.finish()
    out_gather.finish()
    ffn[2]()
    weights_line.finish()
    relay_line.arrive()
    relay_line.finish()


def first_call(sizes, tokens, *operands):
    seqs, lines = sizes.seqs, sizes.lines
    dma = pltpu.SemaphoreType.DMA
    any_spec, vmem_spec = pl.BlockSpec(memory_space=pl.ANY), pl.BlockSpec(memory_space=pltpu.VMEM)
    shape = jax.ShapeDtypeStruct
    matrix_shape = (D, 4 * LANES)
    return pl.pallas_call(
        partial(first_kernel, sizes),
        out_shape=[
            shape((seqs, SEG, D), bf16),
            shape((seqs, SEG, 3 * LANES), bf16),
            shape((seqs, SEG, LANES), f32),
            shape(matrix_shape, bf16),
            shape((sizes.heads, MH, LANES), bf16),
            shape((sizes.heads, MH, LANES), bf16),
            shape((8, D), f32),
            shape((8, 3 * LANES), f32),
            shape((2 * P_SIZE, LANES), bf16),
            shape((seqs, 8, SEG), f32),
            shape((seqs, 2 * sizes.piece, sizes.slab), bf16),
            shape((lines, seqs, sizes.piece, sizes.slab), bf16),
            shape((lines, sizes.share, D), bf16),
            shape((seqs, lines, sizes.share, D), bf16),
        ],
        in_specs=[any_spec] + [vmem_spec] * 12 + [any_spec],
        out_specs=[vmem_spec] * 10 + [any_spec] * 4,
        scratch_shapes=[
            pltpu.VMEM((seqs, SEG, D), bf16),
            pltpu.VMEM((seqs, sizes.weight_rows, LANES), bf16),
            pltpu.VMEM((sizes.weight_rows, LANES), f32),
            pltpu.VMEM((seqs, 2 * sizes.piece, sizes.slab), bf16),
            pltpu.VMEM((seqs, sizes.piece, sizes.slab), bf16),
            pltpu.VMEM((lines, seqs, sizes.weight_rows, LANES), bf16),
            pltpu.VMEM((8, 3 * D), f32),
            pltpu.VMEM((2 * P_SIZE, LANES), f32),
            pltpu.VMEM((sizes.heads, MH, LANES), f32),
            pltpu.VMEM((8, LANES) if sizes.share % 16 == 0 else matrix_shape, f32),
        ]
        + PlaneGather.sems(seqs)
        + [dma((1,)), dma((seqs,)), dma((seqs,))]
        + LineGather.sems(lines)
        + [dma((1,)), dma((seqs,)), dma((seqs,))]
        + [dma((1,)), dma((lines,)), dma((lines,))]
        + [dma((1,)), dma((seqs,)), dma((seqs,))]
        + LineGather.sems(lines)
        + PlaneGather.sems(seqs),
        compiler_params=pltpu.CompilerParams(
            collective_id=0, has_side_effects=True, vmem_limit_bytes=VMEM_GRANT
        ),
        name="first",
    )(tokens, *operands)


def middle_kernel(
    sizes,
    mixed_ref,
    token_ref,
    cot_own_ref,
    out_ref,
    gain_ref,
    cot_ref,
    gate_weight_ref,
    weight_ref,
    middle_ref,
    grad_middle_ref,
    gain_grad_ref,
    out_grad_ref,
    grad_mixed_ref,
    down_ref,
    grad_ref,
    mixed_got,
    combined,
    rows_ref,
    sum_ref,
    rows_all,
    other,
    pair,
    landed,
    cot_slot,
    down_slot,
    both_matrix,
    down_matrix,
    both_grad,
    down_grad,
    acts,
    blocks,
    block_sem,
    gate_sem,
    pair_send,
    pair_recv,
    back_send,
    back_recv,
    cot_sem,
    down_sem,
    *sems,
):
    seqs, lines, chips = sizes.seqs, sizes.lines, sizes.chips
    hidden_size, slab, piece = sizes.slab * sizes.lines, sizes.slab, sizes.piece
    seq, line = lax.axis_index("seq"), lax.axis_index("fsdp")
    chip, core = seq // 2, lax.rem(seq, 2)
    sibling = (2 * chip + 1 - core, line)

    def loop(first, last, body):
        def step(k, carry):
            body(k)
            return carry

        lax.fori_loop(first, last, step, 0)

    def remote(source, target, send, recv, place):
        return pltpu.make_async_remote_copy(
            src_ref=source,
            dst_ref=target,
            send_sem=send,
            recv_sem=recv,
            device_id=place,
            device_id_type=MESH,
        )

    gather = PlaneGather(seqs, rows_ref, rows_all, sems[:7])

    chip_at = gather.chip_at

    def to_pair(j):
        q, slot = chip_at(j), lax.rem(j, 2)
        return remote(other.at[slot], pair.at[q], pair_send.at[slot], pair_recv.at[q], sibling)

    def back(q, slot):
        place = (2 * q + core, line)
        return remote(pair.at[q], landed.at[slot], back_send.at[q], back_recv.at[slot], place)

    resident = chips <= 4

    def cot_copy(j, slot):
        if resident:
            both = pl.ds(2 * chip_at(j), 2)
            return pltpu.make_async_copy(cot_ref.at[both], cot_slot.at[both], cot_sem.at[j])
        return pltpu.make_async_copy(
            cot_ref.at[pl.ds(2 * chip_at(j), 2)], cot_slot.at[slot], cot_sem.at[slot]
        )

    def down_copy(j):
        slot = j % 2 if isinstance(j, int) else lax.rem(j, 2)
        return pltpu.make_async_copy(
            down_slot.at[slot], down_ref.at[pl.ds(2 * chip_at(j), 2)], down_sem.at[slot]
        )

    axes = (seqs, lines)
    to_segments = exchange_phases(axes, PLANE, [mixed_ref], [mixed_got], sems[7:10])
    to_heads = exchange_phases(axes, PLANE, [mixed_got], [grad_mixed_ref], sems[10:13])
    greet_all(axes, ("plane",))
    to_segments[0]()
    if resident:
        for j in range(chips):
            cot_copy(j, 0).start()
    else:
        cot_copy(0, 0).start()
    slots = blocks.shape[0]

    def gate_copy(f):
        target = blocks.at[f % slots, :, pl.ds(0, piece)]
        return pltpu.make_async_copy(gate_weight_ref.at[f], target, gate_sem.at[f % slots])

    def weight_copy(f):
        target = blocks.at[f % slots, :, pl.ds(piece, 2 * piece)]
        return pltpu.make_async_copy(weight_ref.at[f], target, block_sem.at[f % slots])

    def grad_copy(f):
        return pltpu.make_async_copy(blocks.at[f % slots], grad_ref.at[f], block_sem.at[f % slots])

    for f in range(slots):
        gate_copy(f).start()
        weight_copy(f).start()
    for f in range(lines):
        gate_copy(f).wait()
        weight_copy(f).wait()
        columns = slice(f * slab, (f + 1) * slab)
        up_columns = slice(hidden_size + f * slab, hidden_size + (f + 1) * slab)
        for s in range(seqs):
            rows = slice(s * piece, (s + 1) * piece)
            both_matrix[rows, columns] = blocks[f % slots, s, :piece, :]
            both_matrix[rows, up_columns] = blocks[f % slots, s, piece : 2 * piece, :]
            down_matrix[rows, columns] = blocks[f % slots, s, 2 * piece :, :]
        if f + slots < lines:
            gate_copy(f + slots).start()
            weight_copy(f + slots).start()

    width, copies = sizes.width, sizes.copies
    to_segments[2]()
    for group in range(sizes.groups):
        combined[:, group * width : (group + 1) * width] = mixed_got[group * copies, :, :width]
    middle = token_ref[...].astype(f32) + dot_nn(combined[...], out_ref[...])
    middle_ref[...] = middle
    rows_ref[...] = (middle * norm_scale(middle) * gain_ref[5:6, :]).astype(bf16)
    gather.start()

    def forth(j):
        q = chip_at(j)
        gather.step(j)
        cot_copy(j, lax.rem(j, 2)).wait()

        if not resident:

            @pl.when(jnp.logical_and(j > 0, j + 1 < chips))
            def _():
                cot_copy(j + 1, lax.rem(j + 1, 2)).start()

        rows = rows_all[pl.ds(2 * q, 2)].reshape(2 * SEG, D)
        cot = cot_slot[pl.ds(2 * q, 2)] if resident else cot_slot[lax.rem(j, 2)]
        cot = cot.reshape(2 * SEG, D)
        grad_hidden = dot_nn(cot, down_matrix[...])
        ups = dot_nn(rows, both_matrix[...])
        gate_act, up_act = ups[:, :hidden_size], ups[:, hidden_size:]
        sigmoid = jax.nn.sigmoid(gate_act)
        swish = gate_act * sigmoid
        slope = sigmoid * (1.0 + gate_act - swish)
        acts[q, :, :hidden_size] = (grad_hidden * up_act * slope).astype(bf16)
        acts[q, :, hidden_size : 2 * hidden_size] = (grad_hidden * swish).astype(bf16)
        acts[q, :, 2 * hidden_size :] = (swish * up_act).astype(bf16)
        theirs = acts[q, pl.ds(pl.multiple_of((1 - core) * SEG, SEG), SEG), : 2 * hidden_size]
        theirs = dot_nt(theirs, both_matrix[...])

        @pl.when(j >= 2)
        def _():
            to_pair(j - 2).wait_send()

        other[lax.rem(j, 2)] = theirs.astype(bf16)
        to_pair(j).start()
        own = acts[q, pl.ds(pl.multiple_of(core * SEG, SEG), SEG), : 2 * hidden_size]
        own = dot_nt(own, both_matrix[...])
        to_pair(j).wait_recv()
        own = own + pair[q].astype(f32)

        @pl.when(j == 0)
        def _():
            sum_ref[...] = own

        @pl.when(j > 0)
        def _():
            pair[q] = own.astype(bf16)
            back(q, chip).start()

    def weigh(j):
        q = chip_at(j)
        slot = lax.rem(j, 2)

        @pl.when(j > 0)
        def _():
            cot_copy(j, slot).wait()

            @pl.when(j + 1 < chips)
            def _():
                cot_copy(j + 1, lax.rem(j + 1, 2)).start()

        @pl.when(j >= 2)
        def _():
            down_copy(j - 2).wait()

        hidden = acts[q, :, 2 * hidden_size :]
        down_slot[slot] = dot_nt(hidden, down_matrix[...]).astype(bf16).reshape(2, SEG, D)
        down_copy(j).start()
        rows = rows_all[pl.ds(2 * q, 2)].reshape(2 * SEG, D)
        cot = cot_slot[slot].reshape(2 * SEG, D)
        both_new = dot_tn(rows, acts[q, :, : 2 * hidden_size])
        down_new = dot_tn(cot, hidden)

        @pl.when(j == 0)
        def _():
            both_grad[...] = both_new
            down_grad[...] = down_new

        @pl.when(j > 0)
        def _():
            both_grad[...] += both_new
            down_grad[...] += down_new

    def weigh_all():
        rows = rows_all[...].reshape(seqs * SEG, D)
        cot = cot_slot[...].reshape(seqs * SEG, D)
        kept = acts[...].reshape(seqs * SEG, 3 * hidden_size)
        both, hidden = kept[:, : 2 * hidden_size], kept[:, 2 * hidden_size :]
        both_grad[...] = dot_tn(rows, both)
        down_grad[...] = dot_tn(cot, hidden)
        for j in range(chips):
            if j >= 2:
                down_copy(j - 2).wait()
            back_rows = dot_nt(acts[chip_at(j), :, 2 * hidden_size :], down_matrix[...])
            down_slot[j % 2] = back_rows.astype(bf16).reshape(2, SEG, D)
            down_copy(j).start()

    if resident:
        loop(0, chips, forth)
        weigh_all()
    else:
        forth(jnp.int32(0))
        weigh(jnp.int32(0))
        cot_copy(1, 1).start()
        loop(1, chips, forth)
        cot_copy(1, 1).start()
        loop(1, chips, weigh)
    for f in range(lines):
        if f >= slots:
            grad_copy(f - slots).wait()
        columns = slice(f * slab, (f + 1) * slab)
        up_columns = slice(hidden_size + f * slab, hidden_size + (f + 1) * slab)
        for s in range(seqs):
            rows = slice(s * piece, (s + 1) * piece)
            blocks[f % slots, s, :piece, :] = both_grad[rows, columns].astype(bf16)
            blocks[f % slots, s, piece : 2 * piece, :] = both_grad[rows, up_columns].astype(bf16)
            blocks[f % slots, s, 2 * piece :, :] = down_grad[rows, columns].astype(bf16)
        grad_copy(f).start()
    for f in range(lines - slots, lines):
        grad_copy(f).wait()
    loop(chips - 2, chips, lambda j: down_copy(j).wait())
    gather.finish()
    loop(chips - 2, chips, lambda j: to_pair(j).wait_send())

    def end(j):
        q = chip_at(j)
        back(q, chip).wait_send()
        back(q, q).wait_recv()
        sum_ref[...] += landed[q].astype(f32)

    loop(1, chips, end)

    middle = middle_ref[...]
    scale = norm_scale(middle)
    grad = sum_ref[...]
    gain_grad_ref[...] = jnp.sum(grad * middle * scale, axis=0, keepdims=True)
    grad = cot_own_ref[...].astype(f32) + norm_pull(middle, scale, gain_ref[5:6, :], grad)
    grad_middle_ref[...] = grad
    branch = grad.astype(bf16)
    grad_combined = dot_nt(branch, out_ref[...]).astype(bf16)
    if width < LANES:
        mixed_got[...] = jnp.zeros_like(mixed_got)
    for to in range(seqs):
        first = to // copies * width
        mixed_got[to, :, :width] = grad_combined[:, first : first + width]
    to_heads[0]()
    out_grad = dot_tn(combined[...], branch).astype(bf16)
    out_grad_ref[...] = out_grad.reshape(seqs, piece, D)
    to_heads[2]()


def middle_call(sizes, *operands):
    seqs, lines, chips = sizes.seqs, sizes.lines, sizes.chips
    hidden = sizes.slab * lines
    dma = pltpu.SemaphoreType.DMA
    any_spec, vmem_spec = pl.BlockSpec(memory_space=pl.ANY), pl.BlockSpec(memory_space=pltpu.VMEM)
    half = pltpu.VMEM((chips, SEG, D), bf16)
    slots = lines if lines <= 4 else 2
    block_shape = (lines, seqs, 3 * sizes.piece, sizes.slab)
    cot_shape = (seqs, SEG, D) if chips <= 4 else (2, 2, SEG, D)
    shape = jax.ShapeDtypeStruct
    return pl.pallas_call(
        partial(middle_kernel, sizes),
        out_shape=[
            shape((SEG, D), f32),
            shape((SEG, D), f32),
            shape((1, D), f32),
            shape((seqs, sizes.piece, D), bf16),
            shape((seqs, SEG, LANES), bf16),
            shape((seqs, SEG, D), bf16),
            shape(block_shape, bf16),
        ],
        in_specs=[any_spec] + [vmem_spec] * 4 + [any_spec] * 3,
        out_specs=[vmem_spec] * 4 + [any_spec] * 3,
        scratch_shapes=[
            pltpu.VMEM((seqs, SEG, LANES), bf16),
            pltpu.VMEM((SEG, D), bf16),
            pltpu.VMEM((SEG, D), bf16),
            pltpu.VMEM((SEG, D), f32),
            pltpu.VMEM((seqs, SEG, D), bf16),
            pltpu.VMEM((2, SEG, D), bf16),
            half,
            half,
            pltpu.VMEM(cot_shape, bf16),
            pltpu.VMEM((2, 2, SEG, D), bf16),
            pltpu.VMEM((D, 2 * hidden), bf16),
            pltpu.VMEM((D, hidden), bf16),
            pltpu.VMEM((D, 2 * hidden), f32),
            pltpu.VMEM((D, hidden), f32),
            pltpu.VMEM((chips, 2 * SEG, 3 * hidden), bf16),
            pltpu.VMEM((slots,) + block_shape[1:], bf16),
            dma((slots,)),
            dma((slots,)),
        ]
        + [dma((2,)), dma((chips,)), dma((chips,)), dma((chips,))]
        + [dma((max(chips, 2),)), dma((2,))]
        + PlaneGather.sems(seqs)
        + [dma((1,)), dma((seqs,)), dma((seqs,))] * 2,
        compiler_params=pltpu.CompilerParams(
            collective_id=2, has_side_effects=True, vmem_limit_bytes=VMEM_GRANT
        ),
        name="middle",
    )(*operands)


def last_kernel(
    sizes,
    grad_ref,
    normed_ref,
    matrix_ref,
    mem_ref,
    taps_ref,
    persist_ref,
    bias_ref,
    gain_two_ref,
    ffn_ref,
    out_ref,
    token_grad,
    pack_got,
    out_got,
    persist_got,
    ffn_got,
    normed_slot,
    matrix_grad,
    pack,
    pack_rows,
    pack_landed,
    pack_sums,
    out_blocks,
    other,
    pair,
    landed,
    normed_sem,
    pair_send,
    pair_recv,
    back_send,
    back_recv,
    *sems,
):
    seqs, lines, chips = sizes.seqs, sizes.lines, sizes.chips
    share, heads = sizes.share, sizes.heads
    seq, line = lax.axis_index("seq"), lax.axis_index("fsdp")
    chip, core = seq // 2, lax.rem(seq, 2)
    sibling = (2 * chip + 1 - core, line)
    side = math.isqrt(chips)

    def chip_at(k):
        across = lax.rem(lax.rem(chip, side) + lax.rem(k, side), side)
        along = lax.rem(chip // side + k // side, side)
        return along * side + across

    def loop(first, last, body):
        def step(k, carry):
            body(k)
            return carry

        lax.fori_loop(first, last, step, 0)

    def remote(source, target, send, recv, place):
        return pltpu.make_async_remote_copy(
            src_ref=source,
            dst_ref=target,
            send_sem=send,
            recv_sem=recv,
            device_id=place,
            device_id_type=MESH,
        )

    def to_pair(k):
        q, slot = chip_at(lax.rem(k, chips)), lax.rem(k, 2)
        return remote(other.at[slot], pair.at[q], pair_send.at[slot], pair_recv.at[q], sibling)

    def back(q, slot):
        place = (2 * q + core, line)
        return remote(pair.at[q], landed.at[slot], back_send.at[q], back_recv.at[slot], place)

    def normed_copy(q, slot):
        return pltpu.make_async_copy(
            normed_ref.at[pl.ds(2 * q, 2)], normed_slot.at[slot], normed_sem.at[slot]
        )

    axes = (seqs, lines)
    greet_all(axes, ("plane", "line"))
    ffn = exchange_phases(axes, PLANE, [ffn_ref], [ffn_got], sems[0:3])
    outs = exchange_phases(
        axes, (0, 0, 2, 0, 0, 0, 0, 0, 0), [out_blocks, persist_ref], [out_got, persist_got], sems[3:9]
    )
    grads = exchange_phases(
        axes, MERGE, [pack], [pack_got], [pack_landed, pack_sums, *sems[9:16]]
    )
    normed_copy(0, 0).start()
    ffn[0]()

    def gather_grad(q):
        slot = lax.rem(q, 2)

        @pl.when(q + 1 < chips)
        def _():
            normed_copy(q + 1, lax.rem(q + 1, 2)).start()

        normed_copy(q, slot).wait()
        grad = grad_ref[pl.ds(2 * q, 2)].reshape(2 * SEG, 4 * LANES)
        new = dot_tn(normed_slot[slot].reshape(2 * SEG, D), grad)

        @pl.when(q == 0)
        def _():
            matrix_grad[...] = new

        @pl.when(q > 0)
        def _():
            matrix_grad[...] += new

    loop(0, chips, gather_grad)
    mem_at, rest_at = sizes.grad_mem_at, sizes.grad_rest_at
    pack_rows[...] = jnp.zeros_like(pack_rows)
    for tap in range(4):
        for part in range(3):
            at = rest_at + 3 * tap + part
            pack_rows[at : at + 1, :] = taps_ref[tap : tap + 1, part * LANES : (part + 1) * LANES]
    pack_rows[rest_at + 12 : rest_at + 13, :] = bias_ref[0:1, :]
    for i in range(sizes.devices):
        rows = slice(i * share, (i + 1) * share)
        for part in range(4):
            pack_rows[part * share : (part + 1) * share, :] = matrix_grad[
                rows, part * LANES : (part + 1) * LANES
            ]
        for head in range(heads):
            first = mem_at + head * sizes.memory
            pack_rows[first : first + sizes.memory, :] = mem_ref[
                head, i * sizes.memory : (i + 1) * sizes.memory, :
            ]
        pack_rows[rest_at + 13 : rest_at + 14, :share] = gain_two_ref[0:1, rows]
        pack[i % lines, i // lines] = pack_rows[...].astype(bf16)
    grads[0]()
    for f in range(lines):
        out_blocks[f] = out_ref[f * share : (f + 1) * share, :].astype(bf16)
    outs[0]()

    def spread(k):
        q = chip_at(lax.rem(k, chips))
        grad = grad_ref[pl.ds(2 * q, 2)].reshape(2 * SEG, 4 * LANES)
        if sizes.copies > 1:
            grad = grad * jnp.where(lax.rem(seq, sizes.copies) == 0, 1.0, 0.0).astype(bf16)
        whole = dot_nt(grad, matrix_ref[...])
        first_core, second_core = whole[:SEG], whole[SEG:]

        @pl.when(k >= 3)
        def _():
            to_pair(k - 2).wait_send()

        other[lax.rem(k, 2)] = jnp.where(core == 0, second_core, first_core).astype(bf16)
        to_pair(k).start()
        own = jnp.where(core == 0, first_core, second_core)
        to_pair(k).wait_recv()
        own = own + pair[q].astype(f32)

        @pl.when(k == chips)
        def _():
            token_grad[...] = own

        @pl.when(k < chips)
        def _():
            pair[q] = own.astype(bf16)
            back(q, chip).start()

    loop(1, chips + 1, spread)
    grads[1]()

    def add_back(k):
        q = chip_at(k)
        back(q, q).wait_recv()
        token_grad[...] += landed[q].astype(f32)

    loop(1, chips, add_back)
    ffn[2]()
    outs[2]()
    grads[2]()

    def end(k):
        q = chip_at(k)
        back(q, chip).wait_send()

    loop(1, chips, end)
    loop(chips - 1, chips + 1, lambda k: to_pair(k).wait_send())

def unpack_kernel(
    sizes,
    sum_ref,
    pack_got,
    out_got,
    persist_got,
    ffn_got,
    token_ref,
    middle_ref,
    gain_ref,
    qkv_ref,
    gate_ref,
    own_gain_ref,
    token_grad,
    qkv_grad,
    gate_grad,
    first_grad,
    second_grad,
    conv_grad,
    pkey_grad,
    pvalue_grad,
    out_grad,
    gain_one_grad,
    gain_two_grad,
    ffn_gate_grad,
    ffn_up_grad,
    ffn_down_grad,
    bias_grad,
    conv_full,
):
    seqs, lines = sizes.seqs, sizes.lines
    share, width, heads = sizes.share, sizes.width, sizes.heads
    seq, line = lax.axis_index("seq"), lax.axis_index("fsdp")
    me = seq * lines + line
    group = seq // sizes.copies
    mem_at, rest_at = sizes.grad_mem_at, sizes.grad_rest_at
    rows = token_ref[...].astype(f32)
    scale = norm_scale(rows)
    token_grad[...] = middle_ref[...] + norm_pull(rows, scale, gain_ref[4:5, :], sum_ref[...])

    piece, slab = sizes.piece, sizes.slab
    for s in range(seqs):
        columns = slice(s * slab, (s + 1) * slab)
        ffn_gate_grad[:, columns] = ffn_got[s, :piece, :].astype(f32)
        ffn_up_grad[:, columns] = ffn_got[s, piece : 2 * piece, :].astype(f32)
        ffn_down_grad[columns, :] = jnp.transpose(ffn_got[s, 2 * piece :, :].astype(f32))
    out_sum = out_got[0].astype(f32)
    persist_sum = persist_got[0]
    for f in range(1, lines):
        out_sum = out_sum + out_got[f].astype(f32)
        persist_sum = persist_sum + persist_got[f]
    out_grad[...] = out_sum
    inside = lax.rem(LANES - (me * share - group * width), LANES)
    persist_sum = pltpu.roll(persist_sum, inside, 1)[:, :share]
    pkey_grad[...] = persist_sum[:P_SIZE]
    pvalue_grad[...] = persist_sum[P_SIZE:]

    gates = jnp.zeros((share, 3 * HEAD_COUNT), f32)
    bias = jnp.zeros((8, 3 * HEAD_COUNT), f32)
    gain_two = jnp.zeros((1, share), f32)
    conv_full[...] = jnp.zeros_like(conv_full)
    for s in range(seqs):
        block = pack_got[s].astype(f32)
        gain_two = gain_two + block[rest_at + 13 : rest_at + 14, :share]
        if s % sizes.copies:
            continue
        other_group = s // sizes.copies
        for part in range(3):
            first = part * D + other_group * width
            qkv_grad[:, first : first + width] = block[
                part * share : (part + 1) * share, :width
            ]
            for tap in range(4):
                at = rest_at + 3 * tap + part
                conv_full[tap : tap + 1, first : first + width] = block[at : at + 1, :width]
        choice = gate_choice(sizes, other_group, True)
        gates = gates + dot_nn(block[3 * share : 4 * share].astype(bf16), choice)
        rest = block[rest_at + 8 : rest_at + 16].astype(bf16)
        bias = bias + dot_nn(rest, choice)
        for head in range(heads):
            first = mem_at + head * sizes.memory
            member = other_group * heads + head
            rows = block[first : first + 8]
            second_grad[member] = rows[: sizes.memory, HEAD_SIZE:]
            first_grad[member] = jnp.transpose(rows)[:HEAD_SIZE, : sizes.memory]
    gate_grad[...] = gates
    bias_grad[0:1, :] = 3.0 * bias[4:5, :HEAD_COUNT]
    bias_grad[1:2, :] = bias[4:5, HEAD_COUNT : 2 * HEAD_COUNT]
    bias_grad[2:3, :] = bias[4:5, 2 * HEAD_COUNT :]
    gain_two_grad[...] = gain_two
    along = jnp.sum(qkv_grad[...] * qkv_ref[...].astype(f32), axis=1, keepdims=True)
    along = along + jnp.sum(gates * gate_ref[...].astype(f32), axis=1, keepdims=True)
    gain_one_grad[...] = jnp.transpose(along)[0:1] / own_gain_ref[...].astype(f32)
    turned = pltpu.roll(conv_full[...], lax.rem(3 * D - me * 3 * share, 3 * D), 1)
    conv_grad[...] = turned[:4, : 3 * share]


def last_call(sizes, *operands):
    seqs, lines, chips, share = sizes.seqs, sizes.lines, sizes.chips, sizes.share
    dma = pltpu.SemaphoreType.DMA
    any_spec, vmem_spec = pl.BlockSpec(memory_space=pl.ANY), pl.BlockSpec(memory_space=pltpu.VMEM)
    shape = jax.ShapeDtypeStruct
    half = pltpu.VMEM((chips, SEG, D), bf16)
    in_specs = [vmem_spec] * len(operands)
    in_specs[1] = any_spec
    in_specs[8] = any_spec
    pack_shape = (lines, seqs, sizes.grad_rows, LANES)
    return pl.pallas_call(
        partial(last_kernel, sizes),
        out_shape=[
            shape((SEG, D), f32),
            shape(pack_shape[1:], bf16),
            shape((lines, share, D), bf16),
            shape((lines, 2 * P_SIZE, LANES), f32),
            shape((seqs, 3 * sizes.piece, sizes.slab), bf16),
        ],
        in_specs=in_specs,
        out_specs=[vmem_spec] + [any_spec] * 4,
        scratch_shapes=[
            pltpu.VMEM((2, 2, SEG, D), bf16),
            pltpu.VMEM((D, 4 * LANES), f32),
            pltpu.VMEM(pack_shape, bf16),
            pltpu.VMEM(pack_shape[2:], f32),
            pltpu.VMEM(pack_shape, bf16),
            pltpu.VMEM(pack_shape[1:], bf16),
            pltpu.VMEM((lines, share, D), bf16),
            pltpu.VMEM((2, SEG, D), bf16),
            half,
            half,
            dma((2,)),
        ]
        + [dma((2,)), dma((chips,)), dma((chips,)), dma((chips,))]
        + [dma((1,)), dma((seqs,)), dma((seqs,))]
        + [dma((1,)), dma((lines,)), dma((lines,))] * 2
        + [dma((1,)), dma((seqs,)), dma((seqs,))]
        + LineSum.sems(lines),
        compiler_params=pltpu.CompilerParams(
            collective_id=5, has_side_effects=True, vmem_limit_bytes=VMEM_GRANT
        ),
        name="last",
    )(*operands)


def unpack_call(sizes, *operands):
    share, memory = sizes.share, sizes.memory
    vmem_spec = pl.BlockSpec(memory_space=pltpu.VMEM)
    shape = jax.ShapeDtypeStruct
    return pl.pallas_call(
        partial(unpack_kernel, sizes),
        out_shape=[
            shape((SEG, D), f32),
            shape((share, 3 * D), f32),
            shape((share, 3 * HEAD_COUNT), f32),
            shape((HEAD_COUNT, HEAD_SIZE, memory), f32),
            shape((HEAD_COUNT, memory, HEAD_SIZE), f32),
            shape((4, 3 * share), f32),
            shape((P_SIZE, share), f32),
            shape((P_SIZE, share), f32),
            shape((share, D), f32),
            shape((1, share), f32),
            shape((1, share), f32),
            shape((sizes.piece, sizes.hidden), f32),
            shape((sizes.piece, sizes.hidden), f32),
            shape((sizes.hidden, sizes.piece), f32),
            shape((3, HEAD_COUNT), f32),
        ],
        in_specs=[vmem_spec] * len(operands),
        out_specs=[vmem_spec] * 15,
        scratch_shapes=[pltpu.VMEM((8, 3 * D), f32)],
        compiler_params=pltpu.CompilerParams(vmem_limit_bytes=VMEM_GRANT),
        name="unpack",
    )(*operands)


def norm_scale(values):
    return lax.rsqrt(jnp.mean(values * values, axis=-1, keepdims=True) + NORM_EPS)


def norm_pull(values, scale, gain, grad):
    inner = jnp.mean(grad * gain * values, axis=-1, keepdims=True)
    return scale * (grad * gain - values * (scale * scale) * inner)


def on_device(
    tokens,
    norm1_gain,
    qkv_weight,
    gate_weight,
    conv_weight,
    memory_w1,
    memory_w2,
    persistent_keys,
    persistent_values,
    out_weight,
    norm2_gain,
    ffn_gate,
    ffn_up,
    ffn_down,
    gate_bias,
    doc_lengths,
    live_mask,
    cotangent,
):
    sizes = Sizes(lax.axis_size("seq"), lax.axis_size("fsdp"))
    seqs, heads = sizes.seqs, sizes.heads
    length = seqs * SEG
    memory_pack = jnp.concatenate([memory_w1.transpose(0, 2, 1), memory_w2], axis=2)
    (
        normed,
        raw,
        gates,
        matrix,
        memory_both,
        memory_turned,
        gains,
        taps,
        persistent,
        live,
        ffn_part,
        ffn_gates,
        _,
        out_matrix,
    ) = first_call(
        sizes,
        tokens[0],
        qkv_weight,
        gate_weight,
        conv_weight,
        persistent_keys,
        persistent_values,
        norm1_gain[None],
        norm2_gain[None],
        live_mask,
        memory_pack,
        ffn_gate,
        ffn_up,
        ffn_down,
        out_weight,
    )

    constants = (taps, memory_both, memory_turned, persistent, doc_lengths, gate_bias)
    raw = raw.reshape(length, 3 * LANES)
    gates = gates.reshape(length, LANES)
    plan = Exchange(gathers=[cotangent[0]], line_gathers=[ffn_part])
    mixed, keys, values, totals, states, cot_rows, ffn_full = mix_forward(
        6, plan, heads, raw, gates, live, *constants
    )
    middle, grad_middle, grad_gain_two, grad_out, grad_mixed, down_part, ffn_grads = middle_call(
        sizes,
        mixed.reshape(seqs, SEG, LANES),
        tokens[0],
        cotangent[0],
        out_matrix.reshape(D, D),
        gains,
        cot_rows,
        ffn_gates,
        ffn_full,
    )
    ffn_grads = lax.psum_scatter(ffn_grads, "fsdp")
    plan = Exchange(scatters=[down_part, grad_out])
    grad_all, grad_memory, grad_taps, grad_persistent, grad_bias, down_sum, grad_out = mix_backward(
        7,
        plan,
        heads,
        raw,
        gates,
        live,
        keys,
        values,
        totals,
        states,
        grad_mixed.reshape(length, LANES),
        *constants,
    )
    output = (middle + down_sum).astype(bf16)
    token_sum, pack_got, out_got, persist_got, ffn_got = last_call(
        sizes,
        grad_all.reshape(seqs, SEG, 4 * LANES),
        normed,
        matrix,
        grad_memory,
        grad_taps,
        grad_persistent,
        grad_bias,
        grad_gain_two,
        ffn_grads,
        grad_out,
    )
    grads = unpack_call(
        sizes,
        token_sum,
        pack_got,
        out_got,
        persist_got,
        ffn_got,
        tokens[0],
        grad_middle,
        gains,
        qkv_weight,
        gate_weight,
        norm1_gain[None],
    )
    (
        input_grad,
        grad_qkv,
        grad_gate,
        grad_first,
        grad_second,
        grad_conv,
        grad_pkeys,
        grad_pvalues,
        grad_out,
        grad_gain_one,
        grad_gain_two,
        grad_ffn_gate,
        grad_ffn_up,
        grad_ffn_down,
        grad_bias,
    ) = grads
    return (
        output[None],
        input_grad[None],
        grad_gain_one[0],
        grad_qkv,
        grad_gate,
        grad_conv,
        grad_first,
        grad_second,
        grad_pkeys,
        grad_pvalues,
        grad_out,
        grad_gain_two[0],
        grad_ffn_gate,
        grad_ffn_up,
        grad_ffn_down,
        grad_bias,
    )


def solution(mesh):
    return jax.shard_map(
        on_device,
        mesh=mesh,
        in_specs=(
            P("fsdp", "seq", None),
            P(("seq", "fsdp")),
            P(("seq", "fsdp"), None),
            P(("seq", "fsdp"), None),
            P(None, ("seq", "fsdp")),
            P(None, None, ("seq", "fsdp")),
            P(None, ("seq", "fsdp"), None),
            P(None, ("seq", "fsdp")),
            P(None, ("seq", "fsdp")),
            P(("seq", "fsdp"), None),
            P(("seq", "fsdp")),
            P("seq", "fsdp"),
            P("seq", "fsdp"),
            P("fsdp", "seq"),
            P(),
            P("fsdp", None),
            P("fsdp", "seq"),
            P("fsdp", "seq", None),
        ),
        out_specs=(
            P("fsdp", "seq", None),
            P("fsdp", "seq", None),
            P(("seq", "fsdp")),
            P(("seq", "fsdp"), None),
            P(("seq", "fsdp"), None),
            P(None, ("seq", "fsdp")),
            P(None, None, ("seq", "fsdp")),
            P(None, ("seq", "fsdp"), None),
            P(None, ("seq", "fsdp")),
            P(None, ("seq", "fsdp")),
            P(("seq", "fsdp"), None),
            P(("seq", "fsdp")),
            P("seq", "fsdp"),
            P("seq", "fsdp"),
            P("fsdp", "seq"),
            P(),
        ),
        check_vma=False,
    )
```

```python
import math
from functools import partial

import jax
import jax.numpy as jnp
from jax import lax
from jax.experimental import pallas as pl
from jax.experimental.pallas import tpu as pltpu
from jax.sharding import PartitionSpec as P

HEAD_COUNT = 16
HEAD_SIZE = 64
D = 1024
FF = 4096
MH = 256
P_SIZE = 16
SEG = 256
LANES = 128

NORM_EPS = 1e-05
UNIT_EPS = 1e-06
SCORE_SCALE = 8.0
MEMORY_SCALE = 8.0
THETA_SCALE = 0.0005
MASKED = -1000000000.0
LEAST_SHIFT = -30.0
VMEM_GRANT = 62 * 1024 * 1024
MESH = pl.DeviceIdType.MESH

f32 = jnp.float32
bf16 = jnp.bfloat16


def dot_nt(left, right):
    return lax.dot_general(left, right, (((1,), (1,)), ((), ())), preferred_element_type=f32)


def dot_nn(left, right):
    return lax.dot_general(left, right, (((1,), (0,)), ((), ())), preferred_element_type=f32)


def dot_tn(left, right):
    return lax.dot_general(left, right, (((0,), (0,)), ((), ())), preferred_element_type=f32)


def lane_index(shape):
    return lax.broadcasted_iota(jnp.int32, shape, 1)


def swap_halves(rows):
    return pltpu.roll(rows, HEAD_SIZE, 1)


def lane_sum(rows):
    return jnp.sum(rows, axis=1, keepdims=True)


def unit_pair(rows, low):
    squares = rows * rows
    first = lane_sum(jnp.where(low, squares, 0.0))
    second = lane_sum(jnp.where(low, 0.0, squares))
    inverse = jnp.where(low, lax.rsqrt(first + UNIT_EPS), lax.rsqrt(second + UNIT_EPS))
    return rows * inverse, inverse


def unit_pair_pull(unit, inverse, grad, low):
    along = unit * grad
    first = lane_sum(jnp.where(low, along, 0.0))
    second = lane_sum(jnp.where(low, 0.0, along))
    return inverse * (grad - unit * jnp.where(low, first, second))


def mix_taps(ext_ref, conv_ref, place):
    mixed = conv_ref[0:1, :] * ext_ref[8 : 8 + SEG, :]
    for offset in range(1, 4):
        kept = jnp.where(place >= offset, ext_ref[8 - offset : 8 - offset + SEG, :], 0.0)
        mixed = mixed + conv_ref[offset : offset + 1, :] * kept
    return mixed


def places(length_ref, positions):
    start = jnp.int32(0)
    begin = jnp.zeros_like(positions)
    for document in range(1, length_ref.shape[1]):
        start = start + length_ref[0, document - 1]
        begin = jnp.where(positions >= start, start, begin)
    return positions - begin


def gate_scan(heads, first_head, gate_columns, bias_ref, place_row, live):
    lane = lane_index((8, SEG))
    sublane = lax.broadcasted_iota(jnp.int32, (8, SEG), 0)
    gate_rows = jnp.transpose(gate_columns)
    shifts = []
    for kind, (scale, shift) in enumerate(((3.0, -7.5), (1.0, 1.5), (1.0, 0.0))):
        bias = jnp.zeros((8, SEG), f32)
        for head in range(heads):
            own = scale * bias_ref[kind, first_head + head] + shift
            bias = jnp.where(sublane == head, own, bias)
        shifts.append(bias)
    keep = jnp.where(place_row < 1, 0.0, 1.0)
    forget = jax.nn.sigmoid(gate_rows[0:8] + shifts[0])
    momentum = jax.nn.sigmoid(gate_rows[8:16] + shifts[1])
    step = jax.nn.sigmoid(gate_rows[16:24] + shifts[2])
    carry = keep * momentum
    fade = keep * (1.0 - forget)
    keep_all, mix_all, fade_all = carry, carry, fade
    distance = 1
    while distance < SEG:
        inside = lane < SEG - distance
        turn = SEG - distance
        keep_next = jnp.where(inside, pltpu.roll(keep_all, turn, 1), 1.0)
        mix_next = jnp.where(inside, pltpu.roll(mix_all, turn, 1), 0.0)
        fade_next = jnp.where(inside, pltpu.roll(fade_all, turn, 1), 1.0)
        mix_all = mix_next * keep_all + fade_next * mix_all
        keep_all = keep_next * keep_all
        fade_all = fade_next * fade_all
        distance *= 2
    inside = lane < SEG - 1
    keep_after = jnp.where(inside, pltpu.roll(keep_all, SEG - 1, 1), 1.0)
    mix_after = jnp.where(inside, pltpu.roll(mix_all, SEG - 1, 1), 0.0)
    fade_after = jnp.where(inside, pltpu.roll(fade_all, SEG - 1, 1), 1.0)
    written = -THETA_SCALE * step * live
    return dict(
        keep=keep,
        live=live,
        forget=forget,
        momentum=momentum,
        step=step,
        carry=carry,
        fade=fade,
        keep_after=keep_after,
        reach=mix_after + fade_after,
        fade_after=fade_after,
        written=written,
        totals=(keep_all, mix_all, fade_all),
    )


def write_columns(scan):
    rows = jnp.concatenate(
        [scan["written"] * scan["keep_after"], scan["written"] * scan["reach"]], axis=0
    )
    return jnp.transpose(rows)


def state_factors(totals, head, low):
    keep_all, mix_all, fade_all = (member[head : head + 1, 0:1] for member in totals)
    return jnp.where(low, keep_all, fade_all), mix_all


def half_swish(inner):
    turn = jnp.tanh(0.5 * inner)
    sigmoid = 0.5 * turn + 0.5
    active = inner * sigmoid
    slope = sigmoid + active * (1.0 - sigmoid)
    return turn, sigmoid, active, slope


def fill_bias(bias_ref, place, live_prev, live_now):
    row = lax.broadcasted_iota(jnp.int32, (SEG, SEG), 0)
    gap = row - lane_index((SEG, SEG))
    hidden_prev = jnp.where(live_prev > 0.5, 0.0, MASKED)
    hidden_now = jnp.where(live_now > 0.5, 0.0, MASKED)
    bias_ref[:, :SEG] = jnp.where((gap < 0) & (gap + SEG <= place), hidden_prev, MASKED)
    bias_ref[:, SEG : 2 * SEG] = jnp.where((gap >= 0) & (gap <= place), hidden_now, MASKED)


def fill_persistent(bias_ref, keys_all, values_all, persist_ref):
    lane = lane_index((SEG, LANES))
    bias_ref[:, 2 * SEG :] = jnp.where(lane < P_SIZE, 0.0, MASKED)
    keys_all[2 * SEG :, :] = jnp.zeros((LANES, LANES), bf16)
    values_all[2 * SEG :, :] = jnp.zeros((LANES, LANES), bf16)
    pkeys = persist_ref[0:P_SIZE, :].astype(f32) * (1.0 / SCORE_SCALE)
    keys_all[2 * SEG : 2 * SEG + P_SIZE, :] = pkeys.astype(bf16)
    values_all[2 * SEG : 2 * SEG + P_SIZE, :] = persist_ref[P_SIZE:, :]


def forward_step(
    at,
    heads,
    raw_ref,
    gate_ref,
    live_ref,
    conv_ref,
    mem_ref,
    swap_ref,
    persist_ref,
    length_ref,
    bias_ref,
    comb_ref,
    key_out,
    value_out,
    total_out,
    state_out,
    ext,
    keys_all,
    values_all,
    live_prev,
    state,
    hidden,
):
    @pl.when(at == 0)
    def _():
        ext[0:8, :] = jnp.zeros((8, 3 * LANES), f32)
        keys_all[SEG : 2 * SEG, :] = jnp.zeros((SEG, LANES), bf16)
        values_all[SEG : 2 * SEG, :] = jnp.zeros((SEG, LANES), bf16)
        live_prev[...] = jnp.zeros_like(live_prev)
        state[...] = jnp.zeros_like(state)
        fill_persistent(hidden, keys_all, values_all, persist_ref)

    low = lane_index((SEG, LANES)) < HEAD_SIZE
    ext[8 : 8 + SEG, :] = raw_ref[...].astype(f32)
    place = places(length_ref, at * SEG + lax.broadcasted_iota(jnp.int32, (SEG, 1), 0))
    place_row = places(length_ref, at * SEG + lane_index((1, SEG)))
    first_head = (lax.axis_index("seq") * HEAD_COUNT) // lax.axis_size("seq")
    mixed = mix_taps(ext, conv_ref, place)
    ext[0:8, :] = ext[SEG : SEG + 8, :]
    query_unit, _ = unit_pair(mixed[:, :LANES], low)
    key_unit, _ = unit_pair(mixed[:, LANES : 2 * LANES], low)
    value = mixed[:, 2 * LANES :]
    keys_all[0:SEG, :] = keys_all[SEG : 2 * SEG, :]
    values_all[0:SEG, :] = values_all[SEG : 2 * SEG, :]
    keys_all[SEG : 2 * SEG, :] = key_unit.astype(bf16)
    values_all[SEG : 2 * SEG, :] = value.astype(bf16)
    key_out[...] = keys_all[SEG : 2 * SEG, :]
    value_out[...] = values_all[SEG : 2 * SEG, :]
    scan = gate_scan(heads, first_head, gate_ref[...], bias_ref, place_row, live_ref[0, 0:1, :])
    columns = write_columns(scan)
    fill_bias(hidden, place, live_prev[0:1, :], scan["live"])
    live_prev[...] = jnp.broadcast_to(scan["live"], (8, SEG))
    older = jnp.where(place > lax.broadcasted_iota(jnp.int32, (SEG, 1), 0), 1.0, 0.0)
    query = query_unit * SCORE_SCALE
    key = key_unit * MEMORY_SCALE
    queries = (query, swap_halves(query))
    keys = (key, swap_halves(key))
    values = (value, swap_halves(value))
    every = range(heads)
    owns = (low, jnp.logical_not(low))

    mems, swaps = [mem_ref[head] for head in every], [swap_ref[head] for head in every]
    states = [(state[head, 0], state[head, 1]) for head in every]
    for head in every:
        state_out[0, head, 0] = states[head][0].astype(bf16)
        state_out[0, head, 1] = states[head][1].astype(bf16)
    scores = [
        dot_nt(jnp.where(owns[head], query, 0.0).astype(bf16), keys_all[...]) for head in every
    ]
    key_cuts = [jnp.where(low, keys[head], 0.0) for head in every]
    inners = [dot_nt(key_cuts[head].astype(bf16), mems[head]) for head in every]
    firsts = [jnp.where(low, mems[head].astype(f32), states[head][0]).astype(bf16) for head in every]
    seconds = [
        jnp.where(low, swaps[head].astype(f32), states[head][1]).astype(bf16) for head in every
    ]
    asked = [
        jnp.where(low, queries[head], older * queries[1 - head]).astype(bf16) for head in every
    ]
    asked = [dot_nt(asked[head], firsts[head]) for head in every]
    log_totals = jnp.zeros((SEG, 8), f32)
    combined = jnp.zeros((SEG, LANES), f32)
    attended = []
    for head in every:
        shown = scores[head] + hidden[...]
        highest = jnp.max(shown[:, 2 * SEG :], axis=1, keepdims=True)
        highest = jnp.maximum(highest, LEAST_SHIFT)
        weights = jnp.exp(shown - highest)
        summed = lane_sum(weights)
        attended.append(dot_nn(weights.astype(bf16), values_all[...]) * (1.0 / summed))
        log_totals = jnp.where(lane_index((SEG, 8)) == head, highest + jnp.log(summed), log_totals)
    total_out[...] = log_totals
    actives, slopes = [], []
    for head in every:
        _, _, active, slope = half_swish(inners[head])
        actives.append(active.astype(bf16))
        slopes.append(slope)
    errors = [
        jnp.where(low, dot_nn(actives[head], swaps[head]) - values[head], 0.0) for head in every
    ]
    answers = []
    for head in every:
        _, _, active, _ = half_swish(asked[head])
        answers.append(dot_nn(active.astype(bf16), seconds[head]))
    descents = [
        (dot_nt(errors[head].astype(bf16), swaps[head]) * slopes[head]).astype(bf16)
        for head in every
    ]
    for head in every:
        answer = answers[head]
        turned = swap_halves(answer)
        if head == 0:
            recalled = jnp.where(low, answer + older * turned, 0.0)
        else:
            recalled = jnp.where(low, 0.0, turned + older * answer)
        combined = combined + jnp.where(owns[head], attended[head], 0.0) + recalled
    comb_ref[...] = combined.astype(bf16)
    for head in every:
        scale = jnp.where(low, columns[:, head : head + 1], columns[:, 8 + head : 9 + head])
        key_scaled = (jnp.where(low, keys[head], keys[1 - head]) * scale).astype(bf16)
        error_scaled = ((errors[head] + swap_halves(errors[head])) * scale).astype(bf16)
        factor, blend = state_factors(scan["totals"], head, low)
        for member, added in (
            (0, dot_tn(descents[head], key_scaled)),
            (1, dot_tn(actives[head], error_scaled)),
        ):
            old = states[head][member]
            turned = jnp.where(low, 0.0, blend * swap_halves(old))
            state[head, member] = factor * old + turned + added


def chain_rows(factor, term, start, lane):
    distance = 1
    while distance < SEG:
        inside = lane >= distance
        factor_before = jnp.where(inside, pltpu.roll(factor, distance, 1), 1.0)
        term_before = jnp.where(inside, pltpu.roll(term, distance, 1), 0.0)
        term = term + factor * term_before
        factor = factor * factor_before
        distance *= 2
    after = factor * start + term
    return jnp.where(lane == 0, start, pltpu.roll(after, 1, 1))


def backward_kernel(heads, plan, *refs):
    carried = len(plan.arrays)
    own, refs = refs[:18], refs[18:]
    sent, refs = refs[:carried], refs[carried:]
    made, refs = refs[:5], refs[5:]
    got, refs = refs[:carried], refs[carried:]
    begin, middle, finish = plan.phases(sent, got, refs[8:])
    at, last = pl.program_id(0), pl.num_programs(0) - 1

    @pl.when(at == 0)
    def _():
        greet_all(plan.axes, plan.kinds)
        begin()

    backward_step(heads, *own, *made, *refs[:8])

    @pl.when(at == 1)
    def _():
        middle()

    @pl.when(at == last)
    def _():
        finish()


def backward_step(
    heads,
    raw_ref,
    tail_ref,
    gate_ref,
    live_ref,
    live_prev_ref,
    key_ref,
    key_prev_ref,
    value_ref,
    value_prev_ref,
    total_ref,
    state_ref,
    grad_ref,
    conv_ref,
    mem_ref,
    swap_ref,
    persist_ref,
    length_ref,
    bias_ref,
    draw_ref,
    dmem_ref,
    dconv_ref,
    dpersist_ref,
    dbias_ref,
    ext,
    shifted_rows,
    key_carry,
    value_carry,
    late,
    keys_all,
    values_all,
    hidden,
):
    at = pl.program_id(0)

    @pl.when(at == 0)
    def _():
        dmem_ref[...] = jnp.zeros_like(dmem_ref)
        dconv_ref[...] = jnp.zeros_like(dconv_ref)
        dpersist_ref[...] = jnp.zeros_like(dpersist_ref)
        dbias_ref[...] = jnp.zeros_like(dbias_ref)
        shifted_rows[:, 0:8, :] = jnp.zeros((3, 8, 3 * LANES), f32)
        key_carry[...] = jnp.zeros_like(key_carry)
        value_carry[...] = jnp.zeros_like(value_carry)
        late[...] = jnp.zeros_like(late)
        fill_persistent(hidden, keys_all, values_all, persist_ref)

    low = lane_index((SEG, LANES)) < HEAD_SIZE
    ext[0:8, :] = tail_ref[8:16, :].astype(f32)
    ext[8 : 8 + SEG, :] = raw_ref[...].astype(f32)
    here = (pl.num_programs(0) - 1 - at) * SEG
    place = places(length_ref, here + lax.broadcasted_iota(jnp.int32, (SEG, 1), 0))
    place_row = places(length_ref, here + lane_index((1, SEG)))
    first_head = (lax.axis_index("seq") * HEAD_COUNT) // lax.axis_size("seq")
    mixed = mix_taps(ext, conv_ref, place)
    query_unit, query_inverse = unit_pair(mixed[:, :LANES], low)
    key_unit, key_inverse = unit_pair(mixed[:, LANES : 2 * LANES], low)
    value = mixed[:, 2 * LANES :]
    keys_all[0:SEG, :] = key_prev_ref[...]
    values_all[0:SEG, :] = value_prev_ref[...]
    keys_all[SEG : 2 * SEG, :] = key_ref[...]
    values_all[SEG : 2 * SEG, :] = value_ref[...]
    scan = gate_scan(heads, first_head, gate_ref[...], bias_ref, place_row, live_ref[0, 0:1, :])
    columns = write_columns(scan)
    fill_bias(hidden, place, live_prev_ref[0, 0:1, :], scan["live"])
    older = jnp.where(place > lax.broadcasted_iota(jnp.int32, (SEG, 1), 0), 1.0, 0.0)
    grad = grad_ref[...].astype(f32)
    query = query_unit * SCORE_SCALE
    key = key_unit * MEMORY_SCALE
    queries = (query, swap_halves(query))
    keys = (key, swap_halves(key))
    values = (value, swap_halves(value))
    grads = (grad, swap_halves(grad))
    every = range(heads)
    owns = (low, jnp.logical_not(low))
    grad_query = jnp.zeros((SEG, LANES), f32)
    grad_key = key_carry[...]
    grad_value = value_carry[...]
    wide = lane_index((SEG, LANES))
    write_grads = jnp.zeros((SEG, LANES), f32)
    sublane = lax.broadcasted_iota(jnp.int32, (8, 1), 0)
    keep_start = jnp.zeros((8, 1), f32)
    mix_start = jnp.zeros((8, 1), f32)
    fade_start = jnp.zeros((8, 1), f32)

    query_own = [jnp.where(owns[head], query, 0.0).astype(bf16) for head in every]
    grad_own = [jnp.where(owns[head], grad, 0.0).astype(bf16) for head in every]
    scores = [dot_nt(query_own[head], keys_all[...]) for head in every]
    prob_grads = [dot_nt(grad_own[head], values_all[...]) for head in every]
    probs, score_grads = [], []
    for head in every:
        prob = jnp.exp(scores[head] + hidden[...] - total_ref[:, head : head + 1])
        spread = lane_sum(prob * prob_grads[head])
        score_grads.append((prob * (prob_grads[head] - spread)).astype(bf16))
        probs.append(prob.astype(bf16))
    back_keys = dot_tn(score_grads[0], query_own[0])
    back_values = dot_tn(probs[0], grad_own[0])
    for head in every[1:]:
        back_keys = back_keys + dot_tn(score_grads[head], query_own[head])
        back_values = back_values + dot_tn(probs[head], grad_own[head])
    for head in every:
        back = dot_nn(score_grads[head], keys_all[...])
        grad_query = grad_query + jnp.where(owns[head], SCORE_SCALE * back, 0.0)
    key_carry[...] = back_keys[0:SEG]
    value_carry[...] = back_values[0:SEG]
    grad_key = grad_key + back_keys[SEG : 2 * SEG]
    grad_value = grad_value + back_values[SEG : 2 * SEG]
    back_pkeys = back_keys[2 * SEG : 2 * SEG + P_SIZE] * (1.0 / SCORE_SCALE)
    dpersist_ref[0:P_SIZE, :] += back_pkeys
    dpersist_ref[P_SIZE:, :] += back_values[2 * SEG : 2 * SEG + P_SIZE]

    mems, swaps = [mem_ref[head] for head in every], [swap_ref[head] for head in every]
    states = [[state_ref[0, head, member].astype(f32) for member in range(2)] for head in every]
    lates = [[late[head, member] for member in range(2)] for head in every]
    firsts = [jnp.where(low, mems[head].astype(f32), states[head][0]).astype(bf16) for head in every]
    seconds = [
        jnp.where(low, swaps[head].astype(f32), states[head][1]).astype(bf16) for head in every
    ]
    asked = [
        jnp.where(low, queries[head], older * queries[1 - head]).astype(bf16) for head in every
    ]
    told = [jnp.where(low, grads[head], older * grads[1 - head]).astype(bf16) for head in every]
    key_bfs = [jnp.where(low, keys[head], 0.0).astype(bf16) for head in every]
    read_inners = [dot_nt(asked[head], firsts[head]) for head in every]
    read_grads = [dot_nt(told[head], seconds[head]) for head in every]
    inners = [dot_nt(key_bfs[head], mems[head]) for head in every]
    key_twices = [jnp.where(low, keys[head], keys[1 - head]) for head in every]
    scales = [
        jnp.where(low, columns[:, head : head + 1], columns[:, 8 + head : 9 + head])
        for head in every
    ]
    late_bfs = [[member.astype(bf16) for member in lates[head]] for head in every]
    key_scaled = [(key_twices[head] * scales[head]).astype(bf16) for head in every]
    grad_descents = [dot_nt(key_scaled[head], late_bfs[head][0]) for head in every]
    read_backs, reads = [], []
    for head in every:
        _, _, active, slope = half_swish(read_inners[head])
        grad_inner = (read_grads[head] * slope).astype(bf16)
        read_backs.append(dot_nn(grad_inner, firsts[head]))
        reads.append((dot_tn(grad_inner, asked[head]), dot_tn(active.astype(bf16), told[head])))
    actives, slopes, curves = [], [], []
    for head in every:
        turn, _, active, slope = half_swish(inners[head])
        actives.append(active.astype(bf16))
        slopes.append(slope)
        curves.append(0.5 - turn * (slope - 0.5))
    errors = [
        jnp.where(low, dot_nn(actives[head], swaps[head]) - values[head], 0.0) for head in every
    ]
    error_bfs = [error.astype(bf16) for error in errors]
    pulled = [dot_nt(error_bfs[head], swaps[head]) for head in every]
    active_backs = [dot_nn(actives[head], late_bfs[head][1]) for head in every]
    for head in every:
        back = read_backs[head]
        turned = swap_halves(back)
        if head == 0:
            back = jnp.where(low, MEMORY_SCALE * (back + older * turned), 0.0)
        else:
            back = jnp.where(low, 0.0, MEMORY_SCALE * (turned + older * back))
        grad_query = grad_query + back
    descents = [(pulled[head] * slopes[head]).astype(bf16) for head in every]
    grad_pulled = [(grad_descents[head] * slopes[head]).astype(bf16) for head in every]
    curved = [grad_descents[head] * pulled[head] * curves[head] for head in every]
    back_keys = [dot_nn(descents[head], late_bfs[head][0]) for head in every]
    pulled_backs = [dot_nn(grad_pulled[head], swaps[head]) for head in every]
    error_twices = [errors[head] + swap_halves(errors[head]) for head in every]
    error_scaled = [(error_twices[head] * scales[head]).astype(bf16) for head in every]
    error_backs = []
    for head in every:
        weight_grad = key_twices[head] * back_keys[head] + error_twices[head] * active_backs[head]
        grad_state_weight = lane_sum(jnp.where(low, weight_grad, 0.0))
        grad_write_weight = lane_sum(jnp.where(low, 0.0, weight_grad))
        write_grads = jnp.where(wide == head, grad_state_weight, write_grads)
        write_grads = jnp.where(wide == 8 + head, grad_write_weight, write_grads)
        back = active_backs[head] * scales[head]
        back = jnp.where(low, back + swap_halves(back) + pulled_backs[head], 0.0)
        error_backs.append(back)
        grad_value = grad_value - (back if head == 0 else swap_halves(back))
    back_bfs = [back.astype(bf16) for back in error_backs]
    grad_actives = [
        dot_nt(error_scaled[head], late_bfs[head][1]) + dot_nt(back_bfs[head], swaps[head])
        for head in every
    ]
    grad_inners = [
        (curved[head] + grad_actives[head] * slopes[head]).astype(bf16) for head in every
    ]
    for head in every:
        back = back_keys[head] * scales[head]
        back = back + swap_halves(back) + dot_nn(grad_inners[head], mems[head])
        back = jnp.where(low, MEMORY_SCALE * back, 0.0)
        grad_key = grad_key + (back if head == 0 else swap_halves(back))
        write_one = dot_tn(grad_inners[head], key_bfs[head])
        write_two = dot_tn(grad_pulled[head], error_bfs[head])
        write_two = write_two + dot_tn(actives[head], back_bfs[head])
        read_one, read_two = reads[head]
        dmem_ref[head] += jnp.where(low, read_one + write_one, swap_halves(read_two + write_two))

        (late_one, late_two), (state_one, state_two) = lates[head], states[head]
        factor, blend = state_factors(scan["totals"], head, low)
        same = late_one * state_one + late_two * state_two
        cross = late_one * swap_halves(state_one) + late_two * swap_halves(state_two)
        same_low = jnp.sum(lane_sum(jnp.where(low, same, 0.0)), axis=0, keepdims=True)
        same_high = jnp.sum(lane_sum(jnp.where(low, 0.0, same)), axis=0, keepdims=True)
        cross_high = jnp.sum(lane_sum(jnp.where(low, 0.0, cross)), axis=0, keepdims=True)
        keep_start = jnp.where(sublane == head, same_low, keep_start)
        fade_start = jnp.where(sublane == head, same_high, fade_start)
        mix_start = jnp.where(sublane == head, cross_high, mix_start)
        for member, old, read in ((0, late_one, read_one), (1, late_two, read_two)):
            turned = jnp.where(low, blend * swap_halves(old), read)
            late[head, member] = factor * old + turned

    lane = lane_index((8, SEG))
    write_rows = jnp.transpose(write_grads)
    grad_state_rows, grad_write_rows = write_rows[0:8], write_rows[8:16]
    written = scan["written"]
    keep_grads = chain_rows(scan["carry"], grad_state_rows * written, keep_start, lane)
    mix_grads = chain_rows(scan["carry"], grad_write_rows * written, mix_start, lane)
    mix_next = scan["carry"] * mix_grads + grad_write_rows * written
    fade_grads = chain_rows(scan["fade"], mix_next, fade_start, lane)
    grad_written = grad_state_rows * scan["keep_after"] + grad_write_rows * scan["reach"]
    grad_carry = keep_grads * scan["keep_after"] + mix_grads * scan["reach"]
    grad_fade = fade_grads * scan["fade_after"]
    used = sublane < heads
    forget, momentum, step = scan["forget"], scan["momentum"], scan["step"]
    forget_back = -grad_fade * scan["keep"] * forget * (1.0 - forget)
    momentum_back = grad_carry * scan["keep"] * momentum * (1.0 - momentum)
    step_back = -THETA_SCALE * grad_written * scan["live"] * step * (1.0 - step)
    gate_back = jnp.concatenate(
        [
            jnp.where(used, forget_back, 0.0),
            jnp.where(used, momentum_back, 0.0),
            jnp.where(used, step_back, 0.0),
            jnp.zeros((LANES - 24, SEG), f32),
        ],
        axis=0,
    )
    gate_back = jnp.transpose(gate_back)
    dbias_ref[0:1, :] += jnp.sum(gate_back, axis=0, keepdims=True)
    draw_ref[:, 3 * LANES :] = gate_back.astype(bf16)

    grad_mixed = jnp.concatenate(
        [
            unit_pair_pull(query_unit, query_inverse, grad_query, low),
            unit_pair_pull(key_unit, key_inverse, grad_key, low),
            grad_value,
        ],
        axis=1,
    )
    back = conv_ref[0:1, :] * grad_mixed
    dconv_ref[0:1, :] += jnp.sum(grad_mixed * ext[8 : 8 + SEG, :], axis=0, keepdims=True)
    for offset in range(1, 4):
        kept = jnp.where(place >= offset, grad_mixed, 0.0)
        member = offset - 1
        shifted_rows[member, SEG : SEG + 8, :] = shifted_rows[member, 0:8, :]
        shifted_rows[member, 0:SEG, :] = kept
        back = back + conv_ref[offset : offset + 1, :] * shifted_rows[
            member, offset : offset + SEG, :
        ]
        dconv_ref[offset : offset + 1, :] += jnp.sum(
            kept * ext[8 - offset : 8 - offset + SEG, :], axis=0, keepdims=True
        )
    draw_ref[:, : 3 * LANES] = back.astype(bf16)


def whole_of(array):
    zeros = (0,) * array.ndim
    return pl.BlockSpec(array.shape, lambda n: zeros)


def mix_backward(
    collective, plan, heads, raw, gates, live, keys, values, totals, states, grad, *constants
):
    length = raw.shape[0]
    count = length // SEG

    def here(n):
        return count - 1 - n

    def before(n):
        return jnp.maximum(count - 2 - n, 0)

    row_block = pl.BlockSpec((SEG, LANES), lambda n: (here(n), 0))
    prev_block = pl.BlockSpec((SEG, LANES), lambda n: (before(n), 0))
    tail_rows = SEG // 16
    smem = pl.BlockSpec(memory_space=pltpu.SMEM)
    carried_in, carried_out = plan.specs(True)
    return pl.pallas_call(
        partial(backward_kernel, heads, plan),
        grid=(count,),
        in_specs=[
            pl.BlockSpec((SEG, 3 * LANES), lambda n: (here(n), 0)),
            pl.BlockSpec((16, 3 * LANES), lambda n: (jnp.maximum(here(n) * tail_rows - 1, 0), 0)),
            row_block,
            pl.BlockSpec((1, 8, SEG), lambda n: (here(n), 0, 0)),
            pl.BlockSpec((1, 8, SEG), lambda n: (before(n), 0, 0)),
            row_block,
            prev_block,
            row_block,
            prev_block,
            pl.BlockSpec((SEG, 8), lambda n: (here(n), 0)),
            pl.BlockSpec((1, heads, 2, MH, LANES), lambda n: (here(n), 0, 0, 0, 0)),
            row_block,
        ]
        + [whole_of(member) for member in constants[:4]]
        + [smem, smem]
        + carried_in,
        out_specs=[
            pl.BlockSpec((SEG, 4 * LANES), lambda n: (here(n), 0)),
            pl.BlockSpec((heads, MH, LANES), lambda n: (0, 0, 0)),
            pl.BlockSpec((8, 3 * LANES), lambda n: (0, 0)),
            pl.BlockSpec((2 * P_SIZE, LANES), lambda n: (0, 0)),
            pl.BlockSpec((8, LANES), lambda n: (0, 0)),
        ]
        + carried_out,
        out_shape=[
            jax.ShapeDtypeStruct((length, 4 * LANES), bf16),
            jax.ShapeDtypeStruct((heads, MH, LANES), f32),
            jax.ShapeDtypeStruct((8, 3 * LANES), f32),
            jax.ShapeDtypeStruct((2 * P_SIZE, LANES), f32),
            jax.ShapeDtypeStruct((8, LANES), f32),
        ]
        + plan.shapes,
        scratch_shapes=[
            pltpu.VMEM((SEG + 8, 3 * LANES), f32),
            pltpu.VMEM((3, SEG + 8, 3 * LANES), f32),
            pltpu.VMEM((SEG, LANES), f32),
            pltpu.VMEM((SEG, LANES), f32),
            pltpu.VMEM((heads, 2, MH, LANES), f32),
            pltpu.VMEM((2 * SEG + LANES, LANES), bf16),
            pltpu.VMEM((2 * SEG + LANES, LANES), bf16),
            pltpu.VMEM((SEG, 2 * SEG + LANES), f32),
        ]
        + plan.scratch,
        compiler_params=pltpu.CompilerParams(
            dimension_semantics=("arbitrary",),
            collective_id=collective,
            has_side_effects=True,
            vmem_limit_bytes=VMEM_GRANT,
        ),
        name="mix_backward",
    )(
        raw,
        raw,
        gates,
        live,
        live,
        keys,
        keys,
        values,
        values,
        totals,
        states,
        grad,
        *constants,
        *plan.arrays,
    )


class PlaneGather:
    def __init__(self, seqs, source, target, sems):
        self.source, self.target = source, target
        self.local, self.far_send, self.far_recv = sems[:3]
        self.near_send, self.near_recv, self.relay_send, self.relay_recv = sems[3:]
        self.chips = seqs // 2
        self.relayed = self.chips == 4
        self.seq, self.line = lax.axis_index("seq"), lax.axis_index("fsdp")
        self.chip, self.core = self.seq // 2, lax.rem(self.seq, 2)
        self.half = source.shape[0] // 2

    @staticmethod
    def sems(seqs):
        dma = pltpu.SemaphoreType.DMA
        return [dma((1,))] + [dma((seqs // 2,))] * 4 + [dma((2,))] * 2

    def chip_at(self, k):
        side = math.isqrt(self.chips)
        across = lax.rem(lax.rem(self.chip, side) + lax.rem(k, side), side)
        along = lax.rem(self.chip // side + k // side, side)
        return along * side + across

    def copy(self, source, target, send, recv, place):
        return pltpu.make_async_remote_copy(
            src_ref=source,
            dst_ref=target,
            send_sem=send,
            recv_sem=recv,
            device_id=(place, self.line),
            device_id_type=MESH,
        )

    def own(self):
        return pltpu.make_async_copy(self.source, self.target.at[self.seq], self.local.at[0])

    def far(self, q, slot):
        place = 2 * q + self.core
        block = self.target.at[2 * slot + self.core]
        return self.copy(self.source, block, self.far_send.at[q], self.far_recv.at[slot], place)

    def near(self, q, side):
        block = self.target.at[2 * q + (self.core if side == 0 else 1 - self.core)]
        place = 2 * self.chip + 1 - self.core
        return self.copy(block, block, self.near_send.at[q], self.near_recv.at[q], place)

    def near_own(self):
        block = self.target.at[self.seq]
        place = 2 * self.chip + 1 - self.core
        send, recv = self.near_send.at[self.chip], self.near_recv.at[self.chip]
        return self.copy(self.source, block, send, recv, place)

    def relay(self, part, q, to):
        rows = pl.ds(part * self.half, self.half)
        block = self.target.at[2 * q + self.core, rows]
        send, recv = self.relay_send.at[part], self.relay_recv.at[part]
        return self.copy(block, block, send, recv, 2 * to + self.core)

    def loop(self, first, body):
        def step(k, carry):
            body(k)
            return carry

        lax.fori_loop(first, self.chips, step, 0)

    def start(self):
        self.near_own().start()
        if self.relayed:
            for k in (1, 2):
                self.far(self.chip_at(k), self.chip).start()
        else:
            self.loop(1, lambda k: self.far(self.chip_at(k), self.chip).start())
        self.own().start()

    def step(self, k):
        q = self.chip_at(k)

        @pl.when(k == 0)
        def _():
            self.own().wait()

        if self.relayed:
            across, along, diagonal = (self.chip_at(i) for i in (1, 2, 3))

            @pl.when(k == 1)
            def _():
                self.far(across, across).wait_recv()
                self.relay(0, across, along).start()
                self.near(across, 0).start()
                self.far(along, along).wait_recv()
                self.relay(1, along, across).start()
                self.near(along, 0).start()

            @pl.when(k == 3)
            def _():
                self.relay(0, diagonal, along).wait_recv()
                self.relay(1, diagonal, across).wait_recv()
                self.near(diagonal, 0).start()

        else:

            @pl.when(k > 0)
            def _():
                self.far(q, q).wait_recv()
                self.near(q, 0).start()

        self.near(q, 1).wait_recv()

    def finish(self):
        self.near_own().wait_send()
        self.loop(1, lambda k: self.near(self.chip_at(k), 0).wait_send())
        if self.relayed:
            across, along = self.chip_at(1), self.chip_at(2)
            self.far(across, across).wait_send()
            self.far(along, along).wait_send()
            self.relay(0, across, along).wait_send()
            self.relay(1, along, across).wait_send()
        else:
            self.loop(1, lambda k: self.far(self.chip_at(k), self.chip_at(k)).wait_send())

class LineGather:
    def __init__(self, lines, source, target, sems, keep=True):
        self.lines, self.source, self.target, self.keep = lines, source, target, keep
        self.local, self.right_send, self.left_send, self.recv = sems
        self.seq, self.line = lax.axis_index("seq"), lax.axis_index("fsdp")

    @staticmethod
    def sems(lines):
        dma = pltpu.SemaphoreType.DMA
        return [dma((1,)), dma((lines,)), dma((lines,)), dma((lines,))]

    def own(self):
        return pltpu.make_async_copy(self.source, self.target.at[self.line], self.local.at[0])

    def hop(self, block, step, own=False):
        send = self.right_send if step > 0 else self.left_send
        return pltpu.make_async_remote_copy(
            src_ref=self.source if own and self.keep else self.target.at[block],
            dst_ref=self.target.at[block],
            send_sem=send.at[block],
            recv_sem=self.recv.at[block],
            device_id=(self.seq, lax.rem(self.line + step + self.lines, self.lines)),
            device_id_type=MESH,
        )

    def start(self):
        @pl.when(self.line < self.lines - 1)
        def _():
            self.hop(self.line, 1, True).start()

        @pl.when(self.line > 0)
        def _():
            self.hop(self.line, -1, True).start()

        if self.keep:
            self.own().start()

    def round(self, distance):
        before, after = self.line - distance, self.line + distance

        @pl.when(before >= 0)
        def _():
            self.hop(before, 1).wait_recv()

            @pl.when(self.line < self.lines - 1)
            def _():
                self.hop(before, 1).start()

        @pl.when(after < self.lines)
        def _():
            self.hop(after, -1).wait_recv()

            @pl.when(self.line > 0)
            def _():
                self.hop(after, -1).start()

    def rounds(self, first=1):
        for distance in range(first, self.lines):
            self.round(distance)

    def finish(self):
        if self.keep:
            self.own().wait()
        for distance in range(self.lines):
            before, after = self.line - distance, self.line + distance

            @pl.when(jnp.logical_and(before >= 0, self.line < self.lines - 1))
            def _(before=before):
                self.hop(before, 1).wait_send()

            @pl.when(jnp.logical_and(after < self.lines, self.line > 0))
            def _(after=after):
                self.hop(after, -1).wait_send()


class LineSum:
    def __init__(self, lines, source, landed, target, sems):
        self.lines, self.source, self.landed, self.target = lines, source, landed, target
        self.send, self.recv, self.relay_send, self.relay_recv = sems
        self.seq, self.line = lax.axis_index("seq"), lax.axis_index("fsdp")
        self.relayed = lines == 4
        self.half = source.shape[1] // 2

    @staticmethod
    def sems(lines):
        dma = pltpu.SemaphoreType.DMA
        return [dma((lines,)), dma((lines,)), dma((2,)), dma((2,))]

    def at(self, k):
        return lax.rem(self.line + k, self.lines)

    def copy(self, source, target, send, recv, to):
        return pltpu.make_async_remote_copy(
            src_ref=source,
            dst_ref=target,
            send_sem=send,
            recv_sem=recv,
            device_id=(self.seq, to),
            device_id_type=MESH,
        )

    def far(self, i, slot):
        return self.copy(
            self.source.at[i], self.landed.at[slot], self.send.at[i], self.recv.at[slot], i
        )

    def relay(self, part, to):
        rows = pl.ds(part * self.half, self.half)
        return self.copy(
            self.source.at[self.at(2), rows],
            self.landed.at[to, rows],
            self.relay_send.at[part],
            self.relay_recv.at[part],
            to,
        )

    def loop(self, body):
        def step(k, carry):
            body(k)
            return carry

        lax.fori_loop(1, self.lines, step, 0)

    def start(self):
        if self.relayed:
            self.relay(0, self.at(1)).start()
            self.relay(1, self.at(3)).start()
        else:
            self.loop(lambda k: self.far(self.at(k), self.line).start())

    def middle(self):
        if not self.relayed:
            return
        for part, to in ((0, self.at(1)), (1, self.at(3))):
            rows = pl.ds(part * self.half, self.half)
            block = self.landed.at[self.line, rows]
            send, recv = self.relay_send.at[part], self.relay_recv.at[part]
            self.copy(block, block, send, recv, to).wait_recv()

            def add(i, carry, to=to, part=part):
                at = part * self.half + i
                both = self.source[to, at].astype(f32) + self.landed[self.line, at].astype(f32)
                self.source[to, at] = both.astype(bf16)
                return carry

            lax.fori_loop(0, self.half, add, 0)
            self.far(to, self.line).start()

    def others(self):
        return (self.at(1), self.at(3)) if self.relayed else [self.at(k) for k in range(1, self.lines)]

    def arrive(self):
        for i in self.others():
            self.far(i, i).wait_recv()

    def total(self, i):
        whole = self.source[self.line, i].astype(f32)
        for other in self.others():
            whole = whole + self.landed[other, i].astype(f32)
        return whole

    def finish(self):
        for i in self.others():
            self.far(i, i).wait_send()
        if self.relayed:
            self.relay(0, self.at(1)).wait_send()
            self.relay(1, self.at(3)).wait_send()


def exchange_phases(axes, counts, inputs, outputs, scratch):
    seqs, lines = axes
    chips = seqs // 2
    devices = seqs * lines
    seq, line = lax.axis_index("seq"), lax.axis_index("fsdp")
    me = seq * lines + line
    chip, core = seq // 2, lax.rem(seq, 2)
    sibling = (2 * chip + 1 - core, line)

    def twin(q):
        return (2 * q + core, line)

    def point(i):
        return (i // lines, lax.rem(i, lines))

    def loop(first, last, body):
        def step(k, carry):
            body(k)
            return carry

        lax.fori_loop(first, last, step, 0)

    position = 0
    groups = []
    for count in counts:
        groups.append((inputs[position : position + count], outputs[position : position + count]))
        position += count
    scratch = list(scratch)

    def take(number):
        taken = scratch[:number]
        del scratch[:number]
        return taken

    starts = []

    sums = []
    for source, target in zip(*groups[5]):
        pair, landed, pair_send, pair_recv, far_send, far_recv = take(6)

        def pair_copy(q, source=source, pair=pair, send=pair_send, recv=pair_recv):
            return pltpu.make_async_remote_copy(
                src_ref=source.at[2 * q + 1 - core],
                dst_ref=pair.at[q],
                send_sem=send.at[q],
                recv_sem=recv.at[q],
                device_id=sibling,
                device_id_type=MESH,
            )

        def far_copy(q, slot, pair=pair, landed=landed, send=far_send, recv=far_recv):
            return pltpu.make_async_remote_copy(
                src_ref=pair.at[q],
                dst_ref=landed.at[slot],
                send_sem=send.at[q],
                recv_sem=recv.at[slot],
                device_id=twin(q),
                device_id_type=MESH,
            )

        starts.append(
            lambda f=pair_copy: loop(1, chips + 1, lambda k: f(lax.rem(chip + k, chips)).start())
        )
        sums.append((source, target, pair, landed, pair_copy, far_copy))

    spread = []
    for source, target in zip(*groups[0]):
        gather = PlaneGather(seqs, source, target, take(7))
        starts.append(gather.start)
        spread.append(gather)

    direct = []
    for kind, (sources, targets) in (
        ("plane", groups[1]),
        ("line", groups[2]),
        ("every", groups[3]),
        ("all", groups[4]),
    ):
        for source, target in zip(sources, targets):
            local, send, recv = take(3)
            if kind == "plane":
                number, mine = seqs, seq
            elif kind == "line":
                number, mine = lines, line
            else:
                number, mine = devices, me

            def piece(i, source=source, kind=kind, number=number):
                if kind == "all" or (kind == "line" and source.ndim == 2):
                    return source
                if kind == "every" and source.shape[0] != number:
                    return source.at[i // lines]
                return source.at[i]

            def place(i, kind=kind):
                if kind == "plane":
                    return (i, line)
                if kind == "line":
                    return (seq, i)
                return point(i)

            def copy(i, slot, target=target, send=send, recv=recv, piece=piece, place=place):
                return pltpu.make_async_remote_copy(
                    src_ref=piece(i),
                    dst_ref=target.at[slot],
                    send_sem=send.at[i],
                    recv_sem=recv.at[slot],
                    device_id=place(i),
                    device_id_type=MESH,
                )

            def own(target=target, local=local, piece=piece, mine=mine):
                return pltpu.make_async_copy(piece(mine), target.at[mine], local.at[0])

            def start(copy=copy, own=own, mine=mine, number=number):
                loop(1, number, lambda k: copy(lax.rem(mine + k, number), mine).start())
                own().start()

            starts.append(start)
            direct.append((own, copy, mine, number))

    merges = []
    rows = 32
    for source, target in zip(*groups[7]):
        landed, summed, local, plane_send, plane_recv = take(5)
        line_sum = LineSum(lines, source, landed, target, take(4))

        def onward(i, slot, summed=summed, target=target, send=plane_send, recv=plane_recv):
            return pltpu.make_async_remote_copy(
                src_ref=summed.at[i],
                dst_ref=target.at[slot],
                send_sem=send.at[i],
                recv_sem=recv.at[slot],
                device_id=(i, line),
                device_id_type=MESH,
            )

        def keep(summed=summed, target=target, local=local):
            return pltpu.make_async_copy(summed.at[seq], target.at[seq], local.at[0])

        starts.insert(0, line_sum.start)
        merges.append((summed, line_sum, onward, keep))

    def begin():
        for start in starts:
            start()

    def middle():
        for source, target, pair, landed, pair_copy, far_copy in sums:

            def combine(k, source=source, pair=pair, pair_copy=pair_copy, far_copy=far_copy):
                q = lax.rem(chip + k, chips)
                pair_copy(q).wait_recv()

                def add(r):
                    part = pl.ds(pl.multiple_of(r * rows, rows), rows)
                    both = source[2 * q + core, part, :].astype(f32) + pair[q, part, :].astype(f32)
                    pair[q, part, :] = both.astype(bf16)

                loop(0, source.shape[1] // rows, add)

                @pl.when(k < chips)
                def _():
                    far_copy(q, chip).start()

            loop(1, chips + 1, combine)
        for gather in spread:
            gather.step(0)
            gather.step(1)
        for summed, line_sum, onward, keep in merges:
            line_sum.middle()
            line_sum.arrive()

            def add_up(k, summed=summed, line_sum=line_sum, onward=onward):
                i = lax.rem(seq + k, seqs)
                summed[i] = line_sum.total(i).astype(bf16)

                @pl.when(k < seqs)
                def _():
                    onward(i, seq).start()

            loop(1, seqs + 1, add_up)
            keep().start()

    def finish():
        for gather in spread:
            gather.loop(2, gather.step)
        for own, copy, mine, number in direct:

            def end(k, copy=copy, mine=mine, number=number):
                i = lax.rem(mine + k, number)
                copy(i, i).wait_recv()
                copy(i, i).wait_send()

            loop(1, number, end)
            own().wait()
        for gather in spread:
            gather.finish()
        for source, target, pair, landed, pair_copy, far_copy in sums:

            def end_sum(k, far_copy=far_copy):
                q = lax.rem(chip + k, chips)
                far_copy(q, q).wait_recv()

            loop(1, chips, end_sum)

            def add_all(r, target=target, pair=pair, landed=landed):
                part = pl.ds(pl.multiple_of(r * rows, rows), rows)
                whole = pair[chip, part, :].astype(f32)
                for k in range(1, chips):
                    whole = whole + landed[lax.rem(chip + k, chips), part, :].astype(f32)
                target[part, :] = whole

            loop(0, target.shape[0] // rows, add_all)
            loop(1, chips, lambda k, f=far_copy: f(lax.rem(chip + k, chips), chip).wait_send())
            loop(0, chips, lambda q, f=pair_copy: f(q).wait_send())
        for summed, line_sum, onward, keep in merges:
            line_sum.finish()

            def end_merge(k, onward=onward):
                i = lax.rem(seq + k, seqs)
                onward(i, i).wait_recv()
                onward(i, seq).wait_send()

            loop(1, seqs, end_merge)
            keep().wait()

    return begin, middle, finish


def greet_all(axes, kinds):
    seqs, lines = axes
    seq, line = lax.axis_index("seq"), lax.axis_index("fsdp")
    barrier = pltpu.get_barrier_semaphore()

    def signal(place):
        pl.semaphore_signal(barrier, inc=1, device_id=place, device_id_type=MESH)

    def loop(last, body):
        def step(k, carry):
            body(k)
            return carry

        lax.fori_loop(1, last, step, 0)

    if "all" in kinds:
        devices = seqs * lines
        me = seq * lines + line

        def greet(k):
            i = lax.rem(me + k, devices)
            signal((i // lines, lax.rem(i, lines)))

        loop(devices, greet)
        pl.semaphore_wait(barrier, devices - 1)
        return
    met = 0
    if "plane" in kinds:
        loop(seqs, lambda k: signal((lax.rem(seq + k, seqs), line)))
        met += seqs - 1
    if "line" in kinds:
        loop(lines, lambda k: signal((seq, lax.rem(line + k, lines))))
        met += lines - 1
    pl.semaphore_wait(barrier, met)


KINDS = (
    "gathers",
    "planes",
    "to_line",
    "everys",
    "alls",
    "scatters",
    "relays",
    "merges",
)


class Exchange:
    def __init__(self, **arrays):
        self.axes = seqs, lines = lax.axis_size("seq"), lax.axis_size("fsdp")
        chips, devices = seqs // 2, seqs * lines
        dma = pltpu.SemaphoreType.DMA
        groups = [tuple(arrays.get(kind, ())) for kind in KINDS]
        self.counts = tuple(len(group) for group in groups)
        self.arrays = [array for group in groups for array in group]
        scratch = {kind: [] for kind in KINDS}
        shapes, self.in_vmem = [], []
        kinds = set()
        for kind, group in zip(KINDS, groups):
            for array in group:
                shape, dtype = array.shape, array.dtype
                if kind == "gathers":
                    scratch[kind] += PlaneGather.sems(seqs)
                    shape = (seqs,) + shape
                elif kind == "planes":
                    scratch[kind] += [dma((1,)), dma((seqs,)), dma((seqs,))]
                elif kind == "to_line":
                    scratch[kind] += [dma((1,)), dma((lines,)), dma((lines,))]
                    shape = (lines,) + shape[-2:]
                elif kind == "everys":
                    scratch[kind] += [dma((1,)), dma((devices,)), dma((devices,))]
                    shape = (devices,) + shape[1:]
                elif kind == "alls":
                    scratch[kind] += [dma((1,)), dma((devices,)), dma((devices,))]
                    shape = (devices,) + shape
                elif kind == "scatters":
                    half = pltpu.VMEM((chips,) + shape[1:], bf16)
                    scratch[kind] += [half, half] + [dma((chips,))] * 4
                    shape, dtype = shape[1:], f32
                else:
                    raise ValueError(kind)
                shapes.append(jax.ShapeDtypeStruct(shape, dtype))
                self.in_vmem.append(kind == "scatters")
                if kind in ("everys", "alls"):
                    kinds.add("all")
                kinds.add("line" if kind == "to_line" else "plane")
        self.kinds = kinds
        self.shapes = shapes
        order = ("scatters", "gathers", "planes", "to_line", "everys", "alls")
        self.scratch = [member for kind in order for member in scratch[kind]]

    def specs(self, gridded):
        if gridded:
            vmem = [
                pl.BlockSpec(
                    array.shape, lambda n, z=(0,) * array.ndim: z, pipeline_mode=pl.Buffered(1)
                )
                for array in self.arrays
            ]
            out = [
                pl.BlockSpec(array.shape, lambda n, z=(0,) * len(array.shape): z)
                for array in self.shapes
            ]
        else:
            vmem = out = [pl.BlockSpec(memory_space=pltpu.VMEM)] * len(self.arrays)
        plain = pl.BlockSpec(memory_space=pl.ANY)
        first = [one if inside else plain for one, inside in zip(vmem, self.in_vmem)]
        second = [one if inside else plain for one, inside in zip(out, self.in_vmem)]
        return first, second

    def phases(self, inputs, outputs, scratch):
        return exchange_phases(self.axes, self.counts, inputs, outputs, scratch)


PLANE = (0, 1, 0, 0, 0, 0, 0, 0)
TO_LINE = (0, 0, 1, 0, 0, 0, 0, 0)

MERGE = (0, 0, 0, 0, 0, 0, 0, 1)


def round_up(number, step):
    return -(-number // step) * step


class Sizes:
    def __init__(self, seqs, lines):
        self.seqs, self.lines = seqs, lines
        self.chips, self.devices = seqs // 2, seqs * lines
        self.groups = min(HEAD_COUNT, seqs)
        self.copies = seqs // self.groups
        self.heads = HEAD_COUNT // self.groups
        self.width = self.heads * HEAD_SIZE
        self.share = D // self.devices
        self.memory = MH // self.devices
        self.piece = D // seqs
        self.hidden = FF // lines
        self.slab = self.hidden // seqs
        self.gate_at = round_up(3 * self.share, 8)
        self.mem_at = self.gate_at + round_up(max(self.share, 2 * P_SIZE), 8)
        self.rest_at = self.mem_at + round_up(self.heads * self.memory, 8)
        self.weight_rows = round_up(self.rest_at + 8, 16)
        self.grad_mem_at = round_up(4 * self.share, 8)
        self.grad_rest_at = self.grad_mem_at + round_up(self.heads * self.memory, 8)
        self.grad_rows = round_up(self.grad_rest_at + 16, 16)


def gate_choice(sizes, group, turned):
    shape = (LANES, 3 * HEAD_COUNT) if turned else (3 * HEAD_COUNT, LANES)
    lane = lax.broadcasted_iota(jnp.int32, shape, 0 if turned else 1)
    column = lax.broadcasted_iota(jnp.int32, shape, 1 if turned else 0)
    head = lane % 8
    chosen = (lane // 8 == column // HEAD_COUNT) & (head < sizes.heads)
    chosen = chosen & (column % HEAD_COUNT == group * sizes.heads + head)
    return jnp.where(chosen, 1.0, 0.0).astype(bf16)


def first_kernel(
    sizes,
    token_ref,
    qkv_ref,
    gate_ref,
    conv_ref,
    pkey_ref,
    pvalue_ref,
    gain_one_ref,
    gain_two_ref,
    live_ref,
    mem_ref,
    ffn_gate_ref,
    ffn_up_ref,
    ffn_down_ref,
    out_ref,
    cot_ref,
    length_ref,
    bias_ref,
    raw_out,
    gate_out,
    matrix_out,
    mem_out,
    swap_out,
    gain_out,
    taps_out,
    persist_out,
    live_out,
    mixed_out,
    key_out,
    value_out,
    total_out,
    state_out,
    normed_out,
    ffn_out,
    ffn_rest,
    ffn_relayed,
    out_rows,
    out_all,
    cot_all,
    rows_all,
    pack,
    pack_rows,
    ffn_pack,
    ffn_relay,
    got,
    conv_full,
    persist_full,
    mem_full,
    matrix_full,
    ext,
    keys_all,
    values_all,
    live_prev,
    state,
    hidden,
    normed_sem,
    *sems,
):
    seqs, lines, share, width = sizes.seqs, sizes.lines, sizes.share, sizes.width
    seq, line = lax.axis_index("seq"), lax.axis_index("fsdp")
    group = seq // sizes.copies
    axes = (seqs, lines)
    greet_all(axes, ("plane", "line"))
    gather = PlaneGather(seqs, token_ref, rows_all, sems[:7])
    weights = exchange_phases(axes, PLANE, [pack], [got.at[line]], sems[7:10])
    weights_line = LineGather(lines, None, got, sems[10:14], keep=False)
    ffn = exchange_phases(axes, PLANE, [ffn_pack], [ffn_out], sems[14:17])
    outs = exchange_phases(axes, TO_LINE, [out_ref], [out_rows], sems[17:20])
    relay = exchange_phases(axes, PLANE, [ffn_relay], [ffn_relayed.at[line]], sems[20:23])
    relay_line = LineGather(lines, None, ffn_relayed, sems[23:27], keep=False)
    out_gather = PlaneGather(seqs, out_rows, out_all, sems[27:34])
    cot_gather = PlaneGather(seqs, cot_ref, cot_all, sems[34:41])
    piece = sizes.piece
    rest_line = LineGather(lines, ffn_out, ffn_rest, sems[41:45])
    for to in range(seqs):
        ffn_relay[to] = ffn_gate_ref[:, to * sizes.slab : (to + 1) * sizes.slab]
    relay[0]()
    outs[0]()

    gate_at, mem_at, rest_at = sizes.gate_at, sizes.mem_at, sizes.rest_at
    pack_rows[...] = jnp.zeros_like(pack_rows)
    pack_rows[gate_at : gate_at + P_SIZE, HEAD_SIZE : HEAD_SIZE + share] = pkey_ref[...].astype(f32)
    pack_rows[gate_at + P_SIZE : gate_at + 2 * P_SIZE, HEAD_SIZE : HEAD_SIZE + share] = pvalue_ref[
        ...
    ].astype(f32)
    pack_rows[rest_at : rest_at + 4, : 3 * share] = conv_ref[...].astype(f32)
    pack_rows[rest_at + 4 : rest_at + 5, :share] = gain_one_ref[...].astype(f32)
    pack_rows[rest_at + 5 : rest_at + 6, :share] = gain_two_ref[...].astype(f32)
    live = live_ref[...].astype(f32)
    pack_rows[rest_at + 6 : rest_at + 7, :] = live[:, :LANES]
    pack_rows[rest_at + 7 : rest_at + 8, :] = live[:, LANES:]
    qkv = qkv_ref[...].astype(f32)
    gate = gate_ref[...]
    for to in range(seqs):
        other = to // sizes.copies
        for part in range(3):
            first = part * D + other * width
            pack_rows[part * share : (part + 1) * share, :width] = qkv[:, first : first + width]
        chosen = dot_nn(gate, gate_choice(sizes, other, False))
        pack_rows[gate_at : gate_at + share, :HEAD_SIZE] = chosen[:, :HEAD_SIZE]
        for head in range(sizes.heads):
            first = mem_at + head * sizes.memory
            pack_rows[first : first + sizes.memory, :] = mem_ref[other * sizes.heads + head].astype(
                f32
            )
        pack[to] = pack_rows[...].astype(bf16)
    weights[0]()
    gather.start()
    for to in range(seqs):
        columns = slice(to * sizes.slab, (to + 1) * sizes.slab)
        ffn_pack[to, :piece, :] = ffn_up_ref[:, columns]
        turned = jnp.transpose(ffn_down_ref[columns, :].astype(f32))
        ffn_pack[to, piece:, :] = turned.astype(bf16)
    ffn[0]()
    weights[2]()
    weights_line.start()
    gather.step(0)
    gather.step(1)
    weights_line.round(1)
    outs[2]()
    out_gather.start()
    gather.loop(2, gather.step)
    weights_line.rounds(2)
    relay[2]()
    relay_line.start()
    cot_gather.start()
    ffn[2]()
    rest_line.start()

    aligned = share % 16 == 0
    matrix = matrix_out if aligned else matrix_full
    lane = lane_index((share, LANES))
    for i in range(sizes.devices):
        block = got[i % lines, i // lines].astype(f32)
        rows = slice(i * share, (i + 1) * share)
        for part in range(3):
            columns = slice(part * LANES, (part + 1) * LANES)
            matrix[rows, columns] = block[part * share : (part + 1) * share].astype(matrix.dtype)
        chosen = jnp.where(lane < 24, block[gate_at : gate_at + share], 0.0)
        matrix[rows, 3 * LANES :] = chosen.astype(matrix.dtype)
        for head in range(sizes.heads):
            first = mem_at + head * sizes.memory
            mem_full[head, i * sizes.memory : (i + 1) * sizes.memory, :] = block[
                first : first + sizes.memory
            ]
        rest = block[rest_at : rest_at + 8]
        conv_full[0:4, i * 3 * share : (i + 1) * 3 * share] = rest[0:4, : 3 * share]
        gain_out[4:6, i * share : (i + 1) * share] = rest[4:6, :share]
    if not aligned:
        matrix_out[...] = matrix_full[...].astype(bf16)
    for head in range(sizes.heads):
        mem_out[head] = mem_full[head].astype(bf16)
        swap_out[head] = swap_halves(mem_full[head]).astype(bf16)
    taps_out[...] = jnp.zeros_like(taps_out)
    for part in range(3):
        whole = conv_full[:, part * D : (part + 1) * D]
        turned = pltpu.roll(whole, lax.rem(D - group * width, D), 1)
        taps_out[0:4, part * LANES : part * LANES + width] = turned[0:4, :width]
    persist_full[...] = jnp.zeros_like(persist_full)
    for part in range(width // share):
        i = group * (width // share) + part
        block = got[lax.rem(i, lines), i // lines].astype(f32)
        persist_full[:, part * share : (part + 1) * share] = block[
            gate_at : gate_at + 2 * P_SIZE, HEAD_SIZE : HEAD_SIZE + share
        ]
    persist_out[...] = persist_full[...].astype(bf16)
    for s in range(seqs):
        block = got[line, s].astype(f32)
        live_out[s] = jnp.zeros((8, SEG), f32)
        live_out[s, 0:1, :LANES] = block[rest_at + 6 : rest_at + 7]
        live_out[s, 0:1, LANES:] = block[rest_at + 7 : rest_at + 8]

    gain = gain_out[4:5, :]
    gather.finish()

    def normed_copy(q):
        both = pl.ds(2 * q, 2)
        return pltpu.make_async_copy(rows_all.at[both], normed_out.at[both], normed_sem.at[q])

    def work(q, carry):
        both = pl.ds(2 * q, 2)
        rows = rows_all[both].reshape(2 * SEG, D).astype(f32)
        normed = (rows * norm_scale(rows) * gain).astype(bf16)
        projected = dot_nn(normed, matrix_out[...])
        rows_all[both] = normed.reshape(2, SEG, D)
        normed_copy(q).start()
        raw_out[both] = projected[:, : 3 * LANES].astype(bf16).reshape(2, SEG, 3 * LANES)
        gate_out[both] = projected[:, 3 * LANES :].reshape(2, SEG, LANES)
        return carry

    lax.fori_loop(0, sizes.chips, work, 0)

    def segment(n, carry):
        @pl.when(n == 1)
        def _():
            relay_line.round(1)

        @pl.when(n == 2)
        def _():
            out_gather.step(0)
            out_gather.step(1)
            cot_gather.step(0)
            cot_gather.step(1)

        @pl.when(n == 3)
        def _():
            relay_line.round(2)

        @pl.when(n == 4)
        def _():
            rest_line.round(1)

        @pl.when(n == 6)
        def _():
            out_gather.loop(2, out_gather.step)
            cot_gather.loop(2, cot_gather.step)

        forward_step(
            n,
            sizes.heads,
            raw_out.at[n],
            gate_out.at[n],
            live_out.at[pl.ds(n, 1)],
            taps_out,
            mem_out,
            swap_out,
            persist_out,
            length_ref,
            bias_ref,
            mixed_out.at[n],
            key_out.at[n],
            value_out.at[n],
            total_out.at[n],
            state_out.at[pl.ds(n, 1)],
            ext,
            keys_all,
            values_all,
            live_prev,
            state,
            hidden,
        )
        return carry

    lax.fori_loop(0, seqs, segment, 0)
    lax.fori_loop(0, sizes.chips, lambda q, carry: (normed_copy(q).wait(), carry)[1], 0)
    out_gather.finish()
    cot_gather.finish()
    weights_line.finish()
    relay_line.rounds(3)
    rest_line.rounds(2)
    relay_line.finish()
    rest_line.finish()


def first_call(sizes, *operands):
    seqs, lines, heads = sizes.seqs, sizes.lines, sizes.heads
    dma = pltpu.SemaphoreType.DMA
    any_spec, vmem_spec = pl.BlockSpec(memory_space=pl.ANY), pl.BlockSpec(memory_space=pltpu.VMEM)
    smem_spec = pl.BlockSpec(memory_space=pltpu.SMEM)
    shape = jax.ShapeDtypeStruct
    matrix_shape = (D, 4 * LANES)
    return pl.pallas_call(
        partial(first_kernel, sizes),
        out_shape=[
            shape((seqs, SEG, 3 * LANES), bf16),
            shape((seqs, SEG, LANES), f32),
            shape(matrix_shape, bf16),
            shape((heads, MH, LANES), bf16),
            shape((heads, MH, LANES), bf16),
            shape((8, D), f32),
            shape((8, 3 * LANES), f32),
            shape((2 * P_SIZE, LANES), bf16),
            shape((seqs, 8, SEG), f32),
            shape((seqs, SEG, LANES), bf16),
            shape((seqs, SEG, LANES), bf16),
            shape((seqs, SEG, LANES), bf16),
            shape((seqs, SEG, 8), f32),
            shape((seqs, heads, 2, MH, LANES), bf16),
            shape((seqs, SEG, D), bf16),
            shape((seqs, 2 * sizes.piece, sizes.slab), bf16),
            shape((lines, seqs, 2 * sizes.piece, sizes.slab), bf16),
            shape((lines, seqs, sizes.piece, sizes.slab), bf16),
            shape((lines, sizes.share, D), bf16),
            shape((seqs, lines, sizes.share, D), bf16),
            shape((seqs, SEG, D), bf16),
        ],
        in_specs=[any_spec] + [vmem_spec] * 12 + [any_spec] * 2 + [smem_spec] * 2,
        out_specs=[vmem_spec] * 14 + [any_spec] * 7,
        scratch_shapes=[
            pltpu.VMEM((seqs, SEG, D), bf16),
            pltpu.VMEM((seqs, sizes.weight_rows, LANES), bf16),
            pltpu.VMEM((sizes.weight_rows, LANES), f32),
            pltpu.VMEM((seqs, 2 * sizes.piece, sizes.slab), bf16),
            pltpu.VMEM((seqs, sizes.piece, sizes.slab), bf16),
            pltpu.VMEM((lines, seqs, sizes.weight_rows, LANES), bf16),
            pltpu.VMEM((8, 3 * D), f32),
            pltpu.VMEM((2 * P_SIZE, LANES), f32),
            pltpu.VMEM((heads, MH, LANES), f32),
            pltpu.VMEM((8, LANES) if sizes.share % 16 == 0 else matrix_shape, f32),
            pltpu.VMEM((SEG + 8, 3 * LANES), f32),
            pltpu.VMEM((2 * SEG + LANES, LANES), bf16),
            pltpu.VMEM((2 * SEG + LANES, LANES), bf16),
            pltpu.VMEM((8, SEG), f32),
            pltpu.VMEM((heads, 2, MH, LANES), f32),
            pltpu.VMEM((SEG, 2 * SEG + LANES), f32),
            dma((sizes.chips,)),
        ]
        + PlaneGather.sems(seqs)
        + [dma((1,)), dma((seqs,)), dma((seqs,))]
        + LineGather.sems(lines)
        + [dma((1,)), dma((seqs,)), dma((seqs,))]
        + [dma((1,)), dma((lines,)), dma((lines,))]
        + [dma((1,)), dma((seqs,)), dma((seqs,))]
        + LineGather.sems(lines)
        + PlaneGather.sems(seqs) * 2
        + LineGather.sems(lines),
        compiler_params=pltpu.CompilerParams(
            collective_id=0, has_side_effects=True, vmem_limit_bytes=VMEM_GRANT
        ),
        name="first",
    )(*operands)


def middle_kernel(
    sizes,
    mixed_ref,
    token_ref,
    cot_own_ref,
    out_ref,
    gain_ref,
    cot_ref,
    gate_weight_ref,
    weight_ref,
    middle_ref,
    grad_middle_ref,
    gain_grad_ref,
    out_grad_ref,
    grad_mixed_ref,
    down_ref,
    grad_ref,
    mixed_got,
    combined,
    rows_ref,
    sum_ref,
    rows_all,
    other,
    pair,
    landed,
    cot_slot,
    down_slot,
    both_matrix,
    down_matrix,
    both_grad,
    down_grad,
    acts,
    blocks,
    block_sem,
    gate_sem,
    pair_send,
    pair_recv,
    back_send,
    back_recv,
    cot_sem,
    down_sem,
    *sems,
):
    seqs, lines, chips = sizes.seqs, sizes.lines, sizes.chips
    hidden_size, slab, piece = sizes.slab * sizes.lines, sizes.slab, sizes.piece
    seq, line = lax.axis_index("seq"), lax.axis_index("fsdp")
    chip, core = seq // 2, lax.rem(seq, 2)
    sibling = (2 * chip + 1 - core, line)

    def loop(first, last, body):
        def step(k, carry):
            body(k)
            return carry

        lax.fori_loop(first, last, step, 0)

    def remote(source, target, send, recv, place):
        return pltpu.make_async_remote_copy(
            src_ref=source,
            dst_ref=target,
            send_sem=send,
            recv_sem=recv,
            device_id=place,
            device_id_type=MESH,
        )

    gather = PlaneGather(seqs, rows_ref, rows_all, sems[:7])

    chip_at = gather.chip_at

    def to_pair(j):
        q, slot = chip_at(j), lax.rem(j, 2)
        return remote(other.at[slot], pair.at[q], pair_send.at[slot], pair_recv.at[q], sibling)

    def back(q, slot):
        place = (2 * q + core, line)
        return remote(pair.at[q], landed.at[slot], back_send.at[q], back_recv.at[slot], place)

    resident = chips <= 4

    def cot_copy(j, slot):
        if resident:
            both = pl.ds(2 * chip_at(j), 2)
            return pltpu.make_async_copy(cot_ref.at[both], cot_slot.at[both], cot_sem.at[j])
        return pltpu.make_async_copy(
            cot_ref.at[pl.ds(2 * chip_at(j), 2)], cot_slot.at[slot], cot_sem.at[slot]
        )

    def down_copy(j):
        slot = j % 2 if isinstance(j, int) else lax.rem(j, 2)
        return pltpu.make_async_copy(
            down_slot.at[slot], down_ref.at[pl.ds(2 * chip_at(j), 2)], down_sem.at[slot]
        )

    axes = (seqs, lines)
    to_segments = exchange_phases(axes, PLANE, [mixed_ref], [mixed_got], sems[7:10])
    to_heads = exchange_phases(axes, PLANE, [mixed_got], [grad_mixed_ref], sems[10:13])
    greet_all(axes, ("plane",))
    to_segments[0]()
    if resident:
        for j in range(chips):
            cot_copy(j, 0).start()
    else:
        cot_copy(0, 0).start()
    slots = blocks.shape[0]

    def gate_copy(f):
        target = blocks.at[f % slots, :, pl.ds(0, piece)]
        return pltpu.make_async_copy(gate_weight_ref.at[f], target, gate_sem.at[f % slots])

    def weight_copy(f):
        target = blocks.at[f % slots, :, pl.ds(piece, 2 * piece)]
        return pltpu.make_async_copy(weight_ref.at[f], target, block_sem.at[f % slots])

    def grad_copy(f):
        return pltpu.make_async_copy(blocks.at[f % slots], grad_ref.at[f], block_sem.at[f % slots])

    for f in range(slots):
        gate_copy(f).start()
        weight_copy(f).start()
    for f in range(lines):
        gate_copy(f).wait()
        weight_copy(f).wait()
        columns = slice(f * slab, (f + 1) * slab)
        up_columns = slice(hidden_size + f * slab, hidden_size + (f + 1) * slab)
        for s in range(seqs):
            rows = slice(s * piece, (s + 1) * piece)
            both_matrix[rows, columns] = blocks[f % slots, s, :piece, :]
            both_matrix[rows, up_columns] = blocks[f % slots, s, piece : 2 * piece, :]
            down_matrix[rows, columns] = blocks[f % slots, s, 2 * piece :, :]
        if f + slots < lines:
            gate_copy(f + slots).start()
            weight_copy(f + slots).start()

    width, copies = sizes.width, sizes.copies
    to_segments[2]()
    for group in range(sizes.groups):
        combined[:, group * width : (group + 1) * width] = mixed_got[group * copies, :, :width]
    middle = token_ref[...].astype(f32) + dot_nn(combined[...], out_ref[...])
    middle_ref[...] = middle
    rows_ref[...] = (middle * norm_scale(middle) * gain_ref[5:6, :]).astype(bf16)
    gather.start()

    def forth(j):
        q = chip_at(j)
        gather.step(j)
        cot_copy(j, lax.rem(j, 2)).wait()

        if not resident:

            @pl.when(jnp.logical_and(j > 0, j + 1 < chips))
            def _():
                cot_copy(j + 1, lax.rem(j + 1, 2)).start()

        rows = rows_all[pl.ds(2 * q, 2)].reshape(2 * SEG, D)
        cot = cot_slot[pl.ds(2 * q, 2)] if resident else cot_slot[lax.rem(j, 2)]
        cot = cot.reshape(2 * SEG, D)
        grad_hidden = dot_nn(cot, down_matrix[...])
        ups = dot_nn(rows, both_matrix[...])
        gate_act, up_act = ups[:, :hidden_size], ups[:, hidden_size:]
        sigmoid = jax.nn.sigmoid(gate_act)
        swish = gate_act * sigmoid
        slope = sigmoid * (1.0 + gate_act - swish)
        acts[q, :, :hidden_size] = (grad_hidden * up_act * slope).astype(bf16)
        acts[q, :, hidden_size : 2 * hidden_size] = (grad_hidden * swish).astype(bf16)
        acts[q, :, 2 * hidden_size :] = (swish * up_act).astype(bf16)
        theirs = acts[q, pl.ds(pl.multiple_of((1 - core) * SEG, SEG), SEG), : 2 * hidden_size]
        theirs = dot_nt(theirs, both_matrix[...])

        @pl.when(j >= 2)
        def _():
            to_pair(j - 2).wait_send()

        other[lax.rem(j, 2)] = theirs.astype(bf16)
        to_pair(j).start()
        own = acts[q, pl.ds(pl.multiple_of(core * SEG, SEG), SEG), : 2 * hidden_size]
        own = dot_nt(own, both_matrix[...])
        to_pair(j).wait_recv()
        own = own + pair[q].astype(f32)

        @pl.when(j == 0)
        def _():
            sum_ref[...] = own

        @pl.when(j > 0)
        def _():
            pair[q] = own.astype(bf16)
            back(q, chip).start()

    def weigh(j):
        q = chip_at(j)
        slot = lax.rem(j, 2)

        @pl.when(j > 0)
        def _():
            cot_copy(j, slot).wait()

            @pl.when(j + 1 < chips)
            def _():
                cot_copy(j + 1, lax.rem(j + 1, 2)).start()

        @pl.when(j >= 2)
        def _():
            down_copy(j - 2).wait()

        hidden = acts[q, :, 2 * hidden_size :]
        down_slot[slot] = dot_nt(hidden, down_matrix[...]).astype(bf16).reshape(2, SEG, D)
        down_copy(j).start()
        rows = rows_all[pl.ds(2 * q, 2)].reshape(2 * SEG, D)
        cot = cot_slot[slot].reshape(2 * SEG, D)
        both_new = dot_tn(rows, acts[q, :, : 2 * hidden_size])
        down_new = dot_tn(cot, hidden)

        @pl.when(j == 0)
        def _():
            both_grad[...] = both_new
            down_grad[...] = down_new

        @pl.when(j > 0)
        def _():
            both_grad[...] += both_new
            down_grad[...] += down_new

    def weigh_all():
        rows = rows_all[...].reshape(seqs * SEG, D)
        cot = cot_slot[...].reshape(seqs * SEG, D)
        kept = acts[...].reshape(seqs * SEG, 3 * hidden_size)
        both, hidden = kept[:, : 2 * hidden_size], kept[:, 2 * hidden_size :]
        both_grad[...] = dot_tn(rows, both)
        down_grad[...] = dot_tn(cot, hidden)
        for j in range(chips):
            if j >= 2:
                down_copy(j - 2).wait()
            back_rows = dot_nt(acts[chip_at(j), :, 2 * hidden_size :], down_matrix[...])
            down_slot[j % 2] = back_rows.astype(bf16).reshape(2, SEG, D)
            down_copy(j).start()

    if resident:
        loop(0, chips, forth)
        weigh_all()
    else:
        forth(jnp.int32(0))
        weigh(jnp.int32(0))
        cot_copy(1, 1).start()
        loop(1, chips, forth)
        cot_copy(1, 1).start()
        loop(1, chips, weigh)
    for f in range(lines):
        if f >= slots:
            grad_copy(f - slots).wait()
        columns = slice(f * slab, (f + 1) * slab)
        up_columns = slice(hidden_size + f * slab, hidden_size + (f + 1) * slab)
        for s in range(seqs):
            rows = slice(s * piece, (s + 1) * piece)
            blocks[f % slots, s, :piece, :] = both_grad[rows, columns].astype(bf16)
            blocks[f % slots, s, piece : 2 * piece, :] = both_grad[rows, up_columns].astype(bf16)
            blocks[f % slots, s, 2 * piece :, :] = down_grad[rows, columns].astype(bf16)
        grad_copy(f).start()
    for f in range(lines - slots, lines):
        grad_copy(f).wait()
    loop(chips - 2, chips, lambda j: down_copy(j).wait())
    gather.finish()
    loop(chips - 2, chips, lambda j: to_pair(j).wait_send())

    def end(j):
        q = chip_at(j)
        back(q, chip).wait_send()
        back(q, q).wait_recv()
        sum_ref[...] += landed[q].astype(f32)

    loop(1, chips, end)

    middle = middle_ref[...]
    scale = norm_scale(middle)
    grad = sum_ref[...]
    gain_grad_ref[...] = jnp.sum(grad * middle * scale, axis=0, keepdims=True)
    grad = cot_own_ref[...].astype(f32) + norm_pull(middle, scale, gain_ref[5:6, :], grad)
    grad_middle_ref[...] = grad
    branch = grad.astype(bf16)
    grad_combined = dot_nt(branch, out_ref[...]).astype(bf16)
    if width < LANES:
        mixed_got[...] = jnp.zeros_like(mixed_got)
    for to in range(seqs):
        first = to // copies * width
        mixed_got[to, :, :width] = grad_combined[:, first : first + width]
    to_heads[0]()
    out_grad = dot_tn(combined[...], branch).astype(bf16)
    out_grad_ref[...] = out_grad.reshape(seqs, piece, D)
    to_heads[2]()


def middle_call(sizes, *operands):
    seqs, lines, chips = sizes.seqs, sizes.lines, sizes.chips
    hidden = sizes.slab * lines
    dma = pltpu.SemaphoreType.DMA
    any_spec, vmem_spec = pl.BlockSpec(memory_space=pl.ANY), pl.BlockSpec(memory_space=pltpu.VMEM)
    half = pltpu.VMEM((chips, SEG, D), bf16)
    slots = lines if lines <= 4 else 2
    block_shape = (lines, seqs, 3 * sizes.piece, sizes.slab)
    cot_shape = (seqs, SEG, D) if chips <= 4 else (2, 2, SEG, D)
    shape = jax.ShapeDtypeStruct
    return pl.pallas_call(
        partial(middle_kernel, sizes),
        out_shape=[
            shape((SEG, D), f32),
            shape((SEG, D), f32),
            shape((1, D), f32),
            shape((seqs, sizes.piece, D), bf16),
            shape((seqs, SEG, LANES), bf16),
            shape((seqs, SEG, D), bf16),
            shape(block_shape, bf16),
        ],
        in_specs=[any_spec] + [vmem_spec] * 4 + [any_spec] * 3,
        out_specs=[vmem_spec] * 4 + [any_spec] * 3,
        scratch_shapes=[
            pltpu.VMEM((seqs, SEG, LANES), bf16),
            pltpu.VMEM((SEG, D), bf16),
            pltpu.VMEM((SEG, D), bf16),
            pltpu.VMEM((SEG, D), f32),
            pltpu.VMEM((seqs, SEG, D), bf16),
            pltpu.VMEM((2, SEG, D), bf16),
            half,
            half,
            pltpu.VMEM(cot_shape, bf16),
            pltpu.VMEM((2, 2, SEG, D), bf16),
            pltpu.VMEM((D, 2 * hidden), bf16),
            pltpu.VMEM((D, hidden), bf16),
            pltpu.VMEM((D, 2 * hidden), f32),
            pltpu.VMEM((D, hidden), f32),
            pltpu.VMEM((chips, 2 * SEG, 3 * hidden), bf16),
            pltpu.VMEM((slots,) + block_shape[1:], bf16),
            dma((slots,)),
            dma((slots,)),
        ]
        + [dma((2,)), dma((chips,)), dma((chips,)), dma((chips,))]
        + [dma((max(chips, 2),)), dma((2,))]
        + PlaneGather.sems(seqs)
        + [dma((1,)), dma((seqs,)), dma((seqs,))] * 2,
        compiler_params=pltpu.CompilerParams(
            collective_id=2, has_side_effects=True, vmem_limit_bytes=VMEM_GRANT
        ),
        name="middle",
    )(*operands)


def last_kernel(
    sizes,
    grad_ref,
    normed_ref,
    matrix_ref,
    mem_ref,
    taps_ref,
    persist_ref,
    bias_ref,
    gain_two_ref,
    ffn_ref,
    out_ref,
    token_grad,
    pack_got,
    out_got,
    persist_got,
    ffn_got,
    normed_slot,
    matrix_grad,
    pack,
    pack_rows,
    pack_landed,
    pack_sums,
    out_blocks,
    other,
    pair,
    landed,
    normed_sem,
    pair_send,
    pair_recv,
    back_send,
    back_recv,
    *sems,
):
    seqs, lines, chips = sizes.seqs, sizes.lines, sizes.chips
    share, heads = sizes.share, sizes.heads
    seq, line = lax.axis_index("seq"), lax.axis_index("fsdp")
    chip, core = seq // 2, lax.rem(seq, 2)
    sibling = (2 * chip + 1 - core, line)
    side = math.isqrt(chips)

    def chip_at(k):
        across = lax.rem(lax.rem(chip, side) + lax.rem(k, side), side)
        along = lax.rem(chip // side + k // side, side)
        return along * side + across

    def loop(first, last, body):
        def step(k, carry):
            body(k)
            return carry

        lax.fori_loop(first, last, step, 0)

    def remote(source, target, send, recv, place):
        return pltpu.make_async_remote_copy(
            src_ref=source,
            dst_ref=target,
            send_sem=send,
            recv_sem=recv,
            device_id=place,
            device_id_type=MESH,
        )

    def to_pair(k):
        q, slot = chip_at(lax.rem(k, chips)), lax.rem(k, 2)
        return remote(other.at[slot], pair.at[q], pair_send.at[slot], pair_recv.at[q], sibling)

    def back(q, slot):
        place = (2 * q + core, line)
        return remote(pair.at[q], landed.at[slot], back_send.at[q], back_recv.at[slot], place)

    def normed_copy(q, slot):
        return pltpu.make_async_copy(
            normed_ref.at[pl.ds(2 * q, 2)], normed_slot.at[slot], normed_sem.at[slot]
        )

    axes = (seqs, lines)
    greet_all(axes, ("plane", "line"))
    ffn = exchange_phases(axes, PLANE, [ffn_ref], [ffn_got], sems[0:3])
    outs = exchange_phases(
        axes, (0, 0, 2, 0, 0, 0, 0, 0), [out_blocks, persist_ref], [out_got, persist_got], sems[3:9]
    )
    grads = exchange_phases(
        axes, MERGE, [pack], [pack_got], [pack_landed, pack_sums, *sems[9:16]]
    )
    normed_copy(0, 0).start()
    ffn[0]()

    def gather_grad(q):
        slot = lax.rem(q, 2)

        @pl.when(q + 1 < chips)
        def _():
            normed_copy(q + 1, lax.rem(q + 1, 2)).start()

        normed_copy(q, slot).wait()
        grad = grad_ref[pl.ds(2 * q, 2)].reshape(2 * SEG, 4 * LANES)
        new = dot_tn(normed_slot[slot].reshape(2 * SEG, D), grad)

        @pl.when(q == 0)
        def _():
            matrix_grad[...] = new

        @pl.when(q > 0)
        def _():
            matrix_grad[...] += new

    loop(0, chips, gather_grad)
    mem_at, rest_at = sizes.grad_mem_at, sizes.grad_rest_at
    pack_rows[...] = jnp.zeros_like(pack_rows)
    for tap in range(4):
        for part in range(3):
            at = rest_at + 3 * tap + part
            pack_rows[at : at + 1, :] = taps_ref[tap : tap + 1, part * LANES : (part + 1) * LANES]
    pack_rows[rest_at + 12 : rest_at + 13, :] = bias_ref[0:1, :]
    for i in range(sizes.devices):
        rows = slice(i * share, (i + 1) * share)
        for part in range(4):
            pack_rows[part * share : (part + 1) * share, :] = matrix_grad[
                rows, part * LANES : (part + 1) * LANES
            ]
        for head in range(heads):
            first = mem_at + head * sizes.memory
            pack_rows[first : first + sizes.memory, :] = mem_ref[
                head, i * sizes.memory : (i + 1) * sizes.memory, :
            ]
        pack_rows[rest_at + 13 : rest_at + 14, :share] = gain_two_ref[0:1, rows]
        pack[i % lines, i // lines] = pack_rows[...].astype(bf16)
    grads[0]()
    for f in range(lines):
        out_blocks[f] = out_ref[f * share : (f + 1) * share, :].astype(bf16)
    outs[0]()

    def spread(k):
        q = chip_at(lax.rem(k, chips))
        grad = grad_ref[pl.ds(2 * q, 2)].reshape(2 * SEG, 4 * LANES)
        if sizes.copies > 1:
            grad = grad * jnp.where(lax.rem(seq, sizes.copies) == 0, 1.0, 0.0).astype(bf16)
        whole = dot_nt(grad, matrix_ref[...])
        first_core, second_core = whole[:SEG], whole[SEG:]

        @pl.when(k >= 3)
        def _():
            to_pair(k - 2).wait_send()

        other[lax.rem(k, 2)] = jnp.where(core == 0, second_core, first_core).astype(bf16)
        to_pair(k).start()
        own = jnp.where(core == 0, first_core, second_core)
        to_pair(k).wait_recv()
        own = own + pair[q].astype(f32)

        @pl.when(k == chips)
        def _():
            token_grad[...] = own

        @pl.when(k < chips)
        def _():
            pair[q] = own.astype(bf16)
            back(q, chip).start()

    loop(1, chips + 1, spread)
    grads[1]()

    def add_back(k):
        q = chip_at(k)
        back(q, q).wait_recv()
        token_grad[...] += landed[q].astype(f32)

    loop(1, chips, add_back)
    ffn[2]()
    outs[2]()
    grads[2]()

    def end(k):
        q = chip_at(k)
        back(q, chip).wait_send()

    loop(1, chips, end)
    loop(chips - 1, chips + 1, lambda k: to_pair(k).wait_send())

def unpack_kernel(
    sizes,
    sum_ref,
    pack_got,
    out_got,
    persist_got,
    ffn_got,
    token_ref,
    middle_ref,
    gain_ref,
    qkv_ref,
    gate_ref,
    own_gain_ref,
    rows_ref,
    down_ref,
    output_ref,
    token_grad,
    qkv_grad,
    gate_grad,
    first_grad,
    second_grad,
    conv_grad,
    pkey_grad,
    pvalue_grad,
    out_grad,
    gain_one_grad,
    gain_two_grad,
    ffn_gate_grad,
    ffn_up_grad,
    ffn_down_grad,
    bias_grad,
    conv_full,
):
    seqs, lines = sizes.seqs, sizes.lines
    share, width, heads = sizes.share, sizes.width, sizes.heads
    seq, line = lax.axis_index("seq"), lax.axis_index("fsdp")
    me = seq * lines + line
    group = seq // sizes.copies
    mem_at, rest_at = sizes.grad_mem_at, sizes.grad_rest_at
    output_ref[...] = (rows_ref[...] + down_ref[...]).astype(bf16)
    rows = token_ref[...].astype(f32)
    scale = norm_scale(rows)
    token_grad[...] = middle_ref[...] + norm_pull(rows, scale, gain_ref[4:5, :], sum_ref[...])

    piece, slab = sizes.piece, sizes.slab
    for s in range(seqs):
        columns = slice(s * slab, (s + 1) * slab)
        ffn_gate_grad[:, columns] = ffn_got[s, :piece, :].astype(f32)
        ffn_up_grad[:, columns] = ffn_got[s, piece : 2 * piece, :].astype(f32)
        ffn_down_grad[columns, :] = jnp.transpose(ffn_got[s, 2 * piece :, :].astype(f32))
    out_sum = out_got[0].astype(f32)
    persist_sum = persist_got[0]
    for f in range(1, lines):
        out_sum = out_sum + out_got[f].astype(f32)
        persist_sum = persist_sum + persist_got[f]
    out_grad[...] = out_sum
    inside = lax.rem(LANES - (me * share - group * width), LANES)
    persist_sum = pltpu.roll(persist_sum, inside, 1)[:, :share]
    pkey_grad[...] = persist_sum[:P_SIZE]
    pvalue_grad[...] = persist_sum[P_SIZE:]

    gates = jnp.zeros((share, 3 * HEAD_COUNT), f32)
    bias = jnp.zeros((8, 3 * HEAD_COUNT), f32)
    gain_two = jnp.zeros((1, share), f32)
    conv_full[...] = jnp.zeros_like(conv_full)
    for s in range(seqs):
        block = pack_got[s].astype(f32)
        gain_two = gain_two + block[rest_at + 13 : rest_at + 14, :share]
        if s % sizes.copies:
            continue
        other_group = s // sizes.copies
        for part in range(3):
            first = part * D + other_group * width
            qkv_grad[:, first : first + width] = block[
                part * share : (part + 1) * share, :width
            ]
            for tap in range(4):
                at = rest_at + 3 * tap + part
                conv_full[tap : tap + 1, first : first + width] = block[at : at + 1, :width]
        choice = gate_choice(sizes, other_group, True)
        gates = gates + dot_nn(block[3 * share : 4 * share].astype(bf16), choice)
        rest = block[rest_at + 8 : rest_at + 16].astype(bf16)
        bias = bias + dot_nn(rest, choice)
        for head in range(heads):
            first = mem_at + head * sizes.memory
            member = other_group * heads + head
            rows = block[first : first + 8]
            second_grad[member] = rows[: sizes.memory, HEAD_SIZE:]
            first_grad[member] = jnp.transpose(rows)[:HEAD_SIZE, : sizes.memory]
    gate_grad[...] = gates
    bias_grad[0:1, :] = 3.0 * bias[4:5, :HEAD_COUNT]
    bias_grad[1:2, :] = bias[4:5, HEAD_COUNT : 2 * HEAD_COUNT]
    bias_grad[2:3, :] = bias[4:5, 2 * HEAD_COUNT :]
    gain_two_grad[...] = gain_two
    along = jnp.sum(qkv_grad[...] * qkv_ref[...].astype(f32), axis=1, keepdims=True)
    along = along + jnp.sum(gates * gate_ref[...].astype(f32), axis=1, keepdims=True)
    gain_one_grad[...] = jnp.transpose(along)[0:1] / own_gain_ref[...].astype(f32)
    turned = pltpu.roll(conv_full[...], lax.rem(3 * D - me * 3 * share, 3 * D), 1)
    conv_grad[...] = turned[:4, : 3 * share]


def last_call(sizes, *operands):
    seqs, lines, chips, share = sizes.seqs, sizes.lines, sizes.chips, sizes.share
    dma = pltpu.SemaphoreType.DMA
    any_spec, vmem_spec = pl.BlockSpec(memory_space=pl.ANY), pl.BlockSpec(memory_space=pltpu.VMEM)
    shape = jax.ShapeDtypeStruct
    half = pltpu.VMEM((chips, SEG, D), bf16)
    in_specs = [vmem_spec] * len(operands)
    in_specs[1] = any_spec
    in_specs[8] = any_spec
    pack_shape = (lines, seqs, sizes.grad_rows, LANES)
    return pl.pallas_call(
        partial(last_kernel, sizes),
        out_shape=[
            shape((SEG, D), f32),
            shape(pack_shape[1:], bf16),
            shape((lines, share, D), bf16),
            shape((lines, 2 * P_SIZE, LANES), f32),
            shape((seqs, 3 * sizes.piece, sizes.slab), bf16),
        ],
        in_specs=in_specs,
        out_specs=[vmem_spec] + [any_spec] * 4,
        scratch_shapes=[
            pltpu.VMEM((2, 2, SEG, D), bf16),
            pltpu.VMEM((D, 4 * LANES), f32),
            pltpu.VMEM(pack_shape, bf16),
            pltpu.VMEM(pack_shape[2:], f32),
            pltpu.VMEM(pack_shape, bf16),
            pltpu.VMEM(pack_shape[1:], bf16),
            pltpu.VMEM((lines, share, D), bf16),
            pltpu.VMEM((2, SEG, D), bf16),
            half,
            half,
            dma((2,)),
        ]
        + [dma((2,)), dma((chips,)), dma((chips,)), dma((chips,))]
        + [dma((1,)), dma((seqs,)), dma((seqs,))]
        + [dma((1,)), dma((lines,)), dma((lines,))] * 2
        + [dma((1,)), dma((seqs,)), dma((seqs,))]
        + LineSum.sems(lines),
        compiler_params=pltpu.CompilerParams(
            collective_id=5, has_side_effects=True, vmem_limit_bytes=VMEM_GRANT
        ),
        name="last",
    )(*operands)


def unpack_call(sizes, *operands):
    share, memory = sizes.share, sizes.memory
    vmem_spec = pl.BlockSpec(memory_space=pltpu.VMEM)
    shape = jax.ShapeDtypeStruct
    return pl.pallas_call(
        partial(unpack_kernel, sizes),
        out_shape=[
            shape((SEG, D), bf16),
            shape((SEG, D), f32),
            shape((share, 3 * D), f32),
            shape((share, 3 * HEAD_COUNT), f32),
            shape((HEAD_COUNT, HEAD_SIZE, memory), f32),
            shape((HEAD_COUNT, memory, HEAD_SIZE), f32),
            shape((4, 3 * share), f32),
            shape((P_SIZE, share), f32),
            shape((P_SIZE, share), f32),
            shape((share, D), f32),
            shape((1, share), f32),
            shape((1, share), f32),
            shape((sizes.piece, sizes.hidden), f32),
            shape((sizes.piece, sizes.hidden), f32),
            shape((sizes.hidden, sizes.piece), f32),
            shape((3, HEAD_COUNT), f32),
        ],
        in_specs=[vmem_spec] * len(operands),
        out_specs=[vmem_spec] * 16,
        scratch_shapes=[pltpu.VMEM((8, 3 * D), f32)],
        compiler_params=pltpu.CompilerParams(vmem_limit_bytes=VMEM_GRANT),
        name="unpack",
    )(*operands)


def norm_scale(values):
    return lax.rsqrt(jnp.mean(values * values, axis=-1, keepdims=True) + NORM_EPS)


def norm_pull(values, scale, gain, grad):
    inner = jnp.mean(grad * gain * values, axis=-1, keepdims=True)
    return scale * (grad * gain - values * (scale * scale) * inner)


def on_device(
    tokens,
    norm1_gain,
    qkv_weight,
    gate_weight,
    conv_weight,
    memory_w1,
    memory_w2,
    persistent_keys,
    persistent_values,
    out_weight,
    norm2_gain,
    ffn_gate,
    ffn_up,
    ffn_down,
    gate_bias,
    doc_lengths,
    live_mask,
    cotangent,
):
    sizes = Sizes(lax.axis_size("seq"), lax.axis_size("fsdp"))
    seqs, heads = sizes.seqs, sizes.heads
    length = seqs * SEG
    memory_pack = jnp.concatenate([memory_w1.transpose(0, 2, 1), memory_w2], axis=2)
    (
        raw,
        gates,
        matrix,
        memory_both,
        memory_turned,
        gains,
        taps,
        persistent,
        live,
        mixed,
        keys,
        values,
        totals,
        states,
        normed,
        _,
        ffn_rest,
        ffn_gates,
        _,
        out_matrix,
        cot_rows,
    ) = first_call(
        sizes,
        tokens[0],
        qkv_weight,
        gate_weight,
        conv_weight,
        persistent_keys,
        persistent_values,
        norm1_gain[None],
        norm2_gain[None],
        live_mask,
        memory_pack,
        ffn_gate,
        ffn_up,
        ffn_down,
        out_weight,
        cotangent[0],
        doc_lengths,
        gate_bias,
    )
    constants = (taps, memory_both, memory_turned, persistent, doc_lengths, gate_bias)
    middle, grad_middle, grad_gain_two, grad_out, grad_mixed, down_part, ffn_grads = middle_call(
        sizes,
        mixed,
        tokens[0],
        cotangent[0],
        out_matrix.reshape(D, D),
        gains,
        cot_rows,
        ffn_gates,
        ffn_rest,
    )
    ffn_grads = lax.psum_scatter(ffn_grads, "fsdp")
    plan = Exchange(scatters=[down_part, grad_out])
    grad_all, grad_memory, grad_taps, grad_persistent, grad_bias, down_sum, grad_out = mix_backward(
        7,
        plan,
        heads,
        raw.reshape(length, 3 * LANES),
        gates.reshape(length, LANES),
        live,
        keys.reshape(length, LANES),
        values.reshape(length, LANES),
        totals.reshape(length, 8),
        states,
        grad_mixed.reshape(length, LANES),
        *constants,
    )
    token_sum, pack_got, out_got, persist_got, ffn_got = last_call(
        sizes,
        grad_all.reshape(seqs, SEG, 4 * LANES),
        normed,
        matrix,
        grad_memory,
        grad_taps,
        grad_persistent,
        grad_bias,
        grad_gain_two,
        ffn_grads,
        grad_out,
    )
    grads = unpack_call(
        sizes,
        token_sum,
        pack_got,
        out_got,
        persist_got,
        ffn_got,
        tokens[0],
        grad_middle,
        gains,
        qkv_weight,
        gate_weight,
        norm1_gain[None],
        middle,
        down_sum,
    )
    (
        output,
        input_grad,
        grad_qkv,
        grad_gate,
        grad_first,
        grad_second,
        grad_conv,
        grad_pkeys,
        grad_pvalues,
        grad_out,
        grad_gain_one,
        grad_gain_two,
        grad_ffn_gate,
        grad_ffn_up,
        grad_ffn_down,
        grad_bias,
    ) = grads
    return (
        output[None],
        input_grad[None],
        grad_gain_one[0],
        grad_qkv,
        grad_gate,
        grad_conv,
        grad_first,
        grad_second,
        grad_pkeys,
        grad_pvalues,
        grad_out,
        grad_gain_two[0],
        grad_ffn_gate,
        grad_ffn_up,
        grad_ffn_down,
        grad_bias,
    )


def solution(mesh):
    return jax.shard_map(
        on_device,
        mesh=mesh,
        in_specs=(
            P("fsdp", "seq", None),
            P(("seq", "fsdp")),
            P(("seq", "fsdp"), None),
            P(("seq", "fsdp"), None),
            P(None, ("seq", "fsdp")),
            P(None, None, ("seq", "fsdp")),
            P(None, ("seq", "fsdp"), None),
            P(None, ("seq", "fsdp")),
            P(None, ("seq", "fsdp")),
            P(("seq", "fsdp"), None),
            P(("seq", "fsdp")),
            P("seq", "fsdp"),
            P("seq", "fsdp"),
            P("fsdp", "seq"),
            P(),
            P("fsdp", None),
            P("fsdp", "seq"),
            P("fsdp", "seq", None),
        ),
        out_specs=(
            P("fsdp", "seq", None),
            P("fsdp", "seq", None),
            P(("seq", "fsdp")),
            P(("seq", "fsdp"), None),
            P(("seq", "fsdp"), None),
            P(None, ("seq", "fsdp")),
            P(None, None, ("seq", "fsdp")),
            P(None, ("seq", "fsdp"), None),
            P(None, ("seq", "fsdp")),
            P(None, ("seq", "fsdp")),
            P(("seq", "fsdp"), None),
            P(("seq", "fsdp")),
            P("seq", "fsdp"),
            P("seq", "fsdp"),
            P("fsdp", "seq"),
            P(),
        ),
        check_vma=False,
    )
```

```python
import math
from functools import partial

import jax
import jax.numpy as jnp
from jax import lax
from jax.experimental import pallas as pl
from jax.experimental.pallas import tpu as pltpu
from jax.sharding import PartitionSpec as P

HEAD_COUNT = 16
HEAD_SIZE = 64
D = 1024
FF = 4096
MH = 256
P_SIZE = 16
SEG = 256
LANES = 128

NORM_EPS = 1e-05
UNIT_EPS = 1e-06
SCORE_SCALE = 8.0
MEMORY_SCALE = 8.0
THETA_SCALE = 0.0005
MASKED = -1000000000.0
LEAST_SHIFT = -30.0
VMEM_GRANT = 62 * 1024 * 1024
MESH = pl.DeviceIdType.MESH

f32 = jnp.float32
bf16 = jnp.bfloat16


def dot_nt(left, right):
    return lax.dot_general(left, right, (((1,), (1,)), ((), ())), preferred_element_type=f32)


def dot_nn(left, right):
    return lax.dot_general(left, right, (((1,), (0,)), ((), ())), preferred_element_type=f32)


def dot_tn(left, right):
    return lax.dot_general(left, right, (((0,), (0,)), ((), ())), preferred_element_type=f32)


def lane_index(shape):
    return lax.broadcasted_iota(jnp.int32, shape, 1)


def swap_halves(rows):
    return pltpu.roll(rows, HEAD_SIZE, 1)


def lane_sum(rows):
    return jnp.sum(rows, axis=1, keepdims=True)


def unit_pair(rows, low):
    squares = rows * rows
    first = lane_sum(jnp.where(low, squares, 0.0))
    second = lane_sum(jnp.where(low, 0.0, squares))
    inverse = jnp.where(low, lax.rsqrt(first + UNIT_EPS), lax.rsqrt(second + UNIT_EPS))
    return rows * inverse, inverse


def unit_pair_pull(unit, inverse, grad, low):
    along = unit * grad
    first = lane_sum(jnp.where(low, along, 0.0))
    second = lane_sum(jnp.where(low, 0.0, along))
    return inverse * (grad - unit * jnp.where(low, first, second))


def mix_taps(ext_ref, conv_ref, place):
    mixed = conv_ref[0:1, :] * ext_ref[8 : 8 + SEG, :]
    for offset in range(1, 4):
        kept = jnp.where(place >= offset, ext_ref[8 - offset : 8 - offset + SEG, :], 0.0)
        mixed = mixed + conv_ref[offset : offset + 1, :] * kept
    return mixed


def places(length_ref, positions):
    start = jnp.int32(0)
    begin = jnp.zeros_like(positions)
    for document in range(1, length_ref.shape[1]):
        start = start + length_ref[0, document - 1]
        begin = jnp.where(positions >= start, start, begin)
    return positions - begin


def gate_scan(heads, first_head, gate_columns, bias_ref, place_row, live):
    lane = lane_index((8, SEG))
    sublane = lax.broadcasted_iota(jnp.int32, (8, SEG), 0)
    gate_rows = jnp.transpose(gate_columns)
    shifts = []
    for kind, (scale, shift) in enumerate(((3.0, -7.5), (1.0, 1.5), (1.0, 0.0))):
        bias = jnp.zeros((8, SEG), f32)
        for head in range(heads):
            own = scale * bias_ref[kind, first_head + head] + shift
            bias = jnp.where(sublane == head, own, bias)
        shifts.append(bias)
    keep = jnp.where(place_row < 1, 0.0, 1.0)
    forget = jax.nn.sigmoid(gate_rows[0:8] + shifts[0])
    momentum = jax.nn.sigmoid(gate_rows[8:16] + shifts[1])
    step = jax.nn.sigmoid(gate_rows[16:24] + shifts[2])
    carry = keep * momentum
    fade = keep * (1.0 - forget)
    keep_all, mix_all, fade_all = carry, carry, fade
    distance = 1
    while distance < SEG:
        inside = lane < SEG - distance
        turn = SEG - distance
        keep_next = jnp.where(inside, pltpu.roll(keep_all, turn, 1), 1.0)
        mix_next = jnp.where(inside, pltpu.roll(mix_all, turn, 1), 0.0)
        fade_next = jnp.where(inside, pltpu.roll(fade_all, turn, 1), 1.0)
        mix_all = mix_next * keep_all + fade_next * mix_all
        keep_all = keep_next * keep_all
        fade_all = fade_next * fade_all
        distance *= 2
    inside = lane < SEG - 1
    keep_after = jnp.where(inside, pltpu.roll(keep_all, SEG - 1, 1), 1.0)
    mix_after = jnp.where(inside, pltpu.roll(mix_all, SEG - 1, 1), 0.0)
    fade_after = jnp.where(inside, pltpu.roll(fade_all, SEG - 1, 1), 1.0)
    written = -THETA_SCALE * step * live
    return dict(
        keep=keep,
        live=live,
        forget=forget,
        momentum=momentum,
        step=step,
        carry=carry,
        fade=fade,
        keep_after=keep_after,
        reach=mix_after + fade_after,
        fade_after=fade_after,
        written=written,
        totals=(keep_all, mix_all, fade_all),
    )


def write_columns(scan):
    rows = jnp.concatenate(
        [scan["written"] * scan["keep_after"], scan["written"] * scan["reach"]], axis=0
    )
    return jnp.transpose(rows)


def state_factors(totals, head, low):
    keep_all, mix_all, fade_all = (member[head : head + 1, 0:1] for member in totals)
    return jnp.where(low, keep_all, fade_all), mix_all


def half_swish(inner):
    turn = jnp.tanh(0.5 * inner)
    sigmoid = 0.5 * turn + 0.5
    active = inner * sigmoid
    slope = sigmoid + active * (1.0 - sigmoid)
    return turn, sigmoid, active, slope


def fill_bias(bias_ref, place, live_prev, live_now):
    row = lax.broadcasted_iota(jnp.int32, (SEG, SEG), 0)
    gap = row - lane_index((SEG, SEG))
    hidden_prev = jnp.where(live_prev > 0.5, 0.0, MASKED)
    hidden_now = jnp.where(live_now > 0.5, 0.0, MASKED)
    bias_ref[:, :SEG] = jnp.where((gap < 0) & (gap + SEG <= place), hidden_prev, MASKED)
    bias_ref[:, SEG : 2 * SEG] = jnp.where((gap >= 0) & (gap <= place), hidden_now, MASKED)


def fill_persistent(bias_ref, keys_all, values_all, persist_ref):
    lane = lane_index((SEG, LANES))
    bias_ref[:, 2 * SEG :] = jnp.where(lane < P_SIZE, 0.0, MASKED)
    keys_all[2 * SEG :, :] = jnp.zeros((LANES, LANES), bf16)
    values_all[2 * SEG :, :] = jnp.zeros((LANES, LANES), bf16)
    pkeys = persist_ref[0:P_SIZE, :].astype(f32) * (1.0 / SCORE_SCALE)
    keys_all[2 * SEG : 2 * SEG + P_SIZE, :] = pkeys.astype(bf16)
    values_all[2 * SEG : 2 * SEG + P_SIZE, :] = persist_ref[P_SIZE:, :]


def forward_step(
    at,
    heads,
    raw_ref,
    gate_ref,
    live_ref,
    conv_ref,
    mem_ref,
    swap_ref,
    persist_ref,
    length_ref,
    bias_ref,
    comb_ref,
    key_out,
    value_out,
    total_out,
    state_out,
    ext,
    keys_all,
    values_all,
    live_prev,
    state,
    hidden,
):
    @pl.when(at == 0)
    def _():
        ext[0:8, :] = jnp.zeros((8, 3 * LANES), f32)
        keys_all[SEG : 2 * SEG, :] = jnp.zeros((SEG, LANES), bf16)
        values_all[SEG : 2 * SEG, :] = jnp.zeros((SEG, LANES), bf16)
        live_prev[...] = jnp.zeros_like(live_prev)
        state[...] = jnp.zeros_like(state)
        fill_persistent(hidden, keys_all, values_all, persist_ref)

    low = lane_index((SEG, LANES)) < HEAD_SIZE
    ext[8 : 8 + SEG, :] = raw_ref[...].astype(f32)
    place = places(length_ref, at * SEG + lax.broadcasted_iota(jnp.int32, (SEG, 1), 0))
    place_row = places(length_ref, at * SEG + lane_index((1, SEG)))
    first_head = (lax.axis_index("seq") * HEAD_COUNT) // lax.axis_size("seq")
    mixed = mix_taps(ext, conv_ref, place)
    ext[0:8, :] = ext[SEG : SEG + 8, :]
    query_unit, _ = unit_pair(mixed[:, :LANES], low)
    key_unit, _ = unit_pair(mixed[:, LANES : 2 * LANES], low)
    value = mixed[:, 2 * LANES :]
    keys_all[0:SEG, :] = keys_all[SEG : 2 * SEG, :]
    values_all[0:SEG, :] = values_all[SEG : 2 * SEG, :]
    keys_all[SEG : 2 * SEG, :] = key_unit.astype(bf16)
    values_all[SEG : 2 * SEG, :] = value.astype(bf16)
    key_out[...] = keys_all[SEG : 2 * SEG, :]
    value_out[...] = values_all[SEG : 2 * SEG, :]
    scan = gate_scan(heads, first_head, gate_ref[...], bias_ref, place_row, live_ref[0, 0:1, :])
    columns = write_columns(scan)
    fill_bias(hidden, place, live_prev[0:1, :], scan["live"])
    live_prev[...] = jnp.broadcast_to(scan["live"], (8, SEG))
    older = jnp.where(place > lax.broadcasted_iota(jnp.int32, (SEG, 1), 0), 1.0, 0.0)
    query = query_unit * SCORE_SCALE
    key = key_unit * MEMORY_SCALE
    queries = (query, swap_halves(query))
    keys = (key, swap_halves(key))
    values = (value, swap_halves(value))
    every = range(heads)
    owns = (low, jnp.logical_not(low))

    mems, swaps = [mem_ref[head] for head in every], [swap_ref[head] for head in every]
    states = [(state[head, 0], state[head, 1]) for head in every]
    for head in every:
        state_out[0, head, 0] = states[head][0].astype(bf16)
        state_out[0, head, 1] = states[head][1].astype(bf16)
    scores = [
        dot_nt(jnp.where(owns[head], query, 0.0).astype(bf16), keys_all[...]) for head in every
    ]
    key_cuts = [jnp.where(low, keys[head], 0.0) for head in every]
    inners = [dot_nt(key_cuts[head].astype(bf16), mems[head]) for head in every]
    firsts = [jnp.where(low, mems[head].astype(f32), states[head][0]).astype(bf16) for head in every]
    seconds = [
        jnp.where(low, swaps[head].astype(f32), states[head][1]).astype(bf16) for head in every
    ]
    asked = [
        jnp.where(low, queries[head], older * queries[1 - head]).astype(bf16) for head in every
    ]
    asked = [dot_nt(asked[head], firsts[head]) for head in every]
    log_totals = jnp.zeros((SEG, 8), f32)
    combined = jnp.zeros((SEG, LANES), f32)
    attended = []
    for head in every:
        shown = scores[head] + hidden[...]
        highest = jnp.max(shown[:, 2 * SEG :], axis=1, keepdims=True)
        highest = jnp.maximum(highest, LEAST_SHIFT)
        weights = jnp.exp(shown - highest)
        summed = lane_sum(weights)
        attended.append(dot_nn(weights.astype(bf16), values_all[...]) * (1.0 / summed))
        log_totals = jnp.where(lane_index((SEG, 8)) == head, highest + jnp.log(summed), log_totals)
    total_out[...] = log_totals
    actives, slopes = [], []
    for head in every:
        _, _, active, slope = half_swish(inners[head])
        actives.append(active.astype(bf16))
        slopes.append(slope)
    errors = [
        jnp.where(low, dot_nn(actives[head], swaps[head]) - values[head], 0.0) for head in every
    ]
    answers = []
    for head in every:
        _, _, active, _ = half_swish(asked[head])
        answers.append(dot_nn(active.astype(bf16), seconds[head]))
    descents = [
        (dot_nt(errors[head].astype(bf16), swaps[head]) * slopes[head]).astype(bf16)
        for head in every
    ]
    for head in every:
        answer = answers[head]
        turned = swap_halves(answer)
        if head == 0:
            recalled = jnp.where(low, answer + older * turned, 0.0)
        else:
            recalled = jnp.where(low, 0.0, turned + older * answer)
        combined = combined + jnp.where(owns[head], attended[head], 0.0) + recalled
    comb_ref[...] = combined.astype(bf16)
    for head in every:
        scale = jnp.where(low, columns[:, head : head + 1], columns[:, 8 + head : 9 + head])
        key_scaled = (jnp.where(low, keys[head], keys[1 - head]) * scale).astype(bf16)
        error_scaled = ((errors[head] + swap_halves(errors[head])) * scale).astype(bf16)
        factor, blend = state_factors(scan["totals"], head, low)
        for member, added in (
            (0, dot_tn(descents[head], key_scaled)),
            (1, dot_tn(actives[head], error_scaled)),
        ):
            old = states[head][member]
            turned = jnp.where(low, 0.0, blend * swap_halves(old))
            state[head, member] = factor * old + turned + added


def chain_rows(factor, term, start, lane):
    distance = 1
    while distance < SEG:
        inside = lane >= distance
        factor_before = jnp.where(inside, pltpu.roll(factor, distance, 1), 1.0)
        term_before = jnp.where(inside, pltpu.roll(term, distance, 1), 0.0)
        term = term + factor * term_before
        factor = factor * factor_before
        distance *= 2
    after = factor * start + term
    return jnp.where(lane == 0, start, pltpu.roll(after, 1, 1))


def backward_kernel(heads, plan, *refs):
    carried = len(plan.arrays)
    own, refs = refs[:18], refs[18:]
    sent, refs = refs[:carried], refs[carried:]
    made, refs = refs[:5], refs[5:]
    got, refs = refs[:carried], refs[carried:]
    begin, middle, finish = plan.phases(sent, got, refs[8:])
    at, last = pl.program_id(0), pl.num_programs(0) - 1

    @pl.when(at == 0)
    def _():
        greet_all(plan.axes, plan.kinds)
        begin()

    backward_step(heads, *own, *made, *refs[:8])

    @pl.when(at == 1)
    def _():
        middle()

    @pl.when(at == last)
    def _():
        finish()


def backward_step(
    heads,
    raw_ref,
    tail_ref,
    gate_ref,
    live_ref,
    live_prev_ref,
    key_ref,
    key_prev_ref,
    value_ref,
    value_prev_ref,
    total_ref,
    state_ref,
    grad_ref,
    conv_ref,
    mem_ref,
    swap_ref,
    persist_ref,
    length_ref,
    bias_ref,
    draw_ref,
    dmem_ref,
    dconv_ref,
    dpersist_ref,
    dbias_ref,
    ext,
    shifted_rows,
    key_carry,
    value_carry,
    late,
    keys_all,
    values_all,
    hidden,
):
    at = pl.program_id(0)

    @pl.when(at == 0)
    def _():
        dmem_ref[...] = jnp.zeros_like(dmem_ref)
        dconv_ref[...] = jnp.zeros_like(dconv_ref)
        dpersist_ref[...] = jnp.zeros_like(dpersist_ref)
        dbias_ref[...] = jnp.zeros_like(dbias_ref)
        shifted_rows[:, 0:8, :] = jnp.zeros((3, 8, 3 * LANES), f32)
        key_carry[...] = jnp.zeros_like(key_carry)
        value_carry[...] = jnp.zeros_like(value_carry)
        late[...] = jnp.zeros_like(late)
        fill_persistent(hidden, keys_all, values_all, persist_ref)

    low = lane_index((SEG, LANES)) < HEAD_SIZE
    ext[0:8, :] = tail_ref[8:16, :].astype(f32)
    ext[8 : 8 + SEG, :] = raw_ref[...].astype(f32)
    here = (pl.num_programs(0) - 1 - at) * SEG
    place = places(length_ref, here + lax.broadcasted_iota(jnp.int32, (SEG, 1), 0))
    place_row = places(length_ref, here + lane_index((1, SEG)))
    first_head = (lax.axis_index("seq") * HEAD_COUNT) // lax.axis_size("seq")
    mixed = mix_taps(ext, conv_ref, place)
    query_unit, query_inverse = unit_pair(mixed[:, :LANES], low)
    key_unit, key_inverse = unit_pair(mixed[:, LANES : 2 * LANES], low)
    value = mixed[:, 2 * LANES :]
    keys_all[0:SEG, :] = key_prev_ref[...]
    values_all[0:SEG, :] = value_prev_ref[...]
    keys_all[SEG : 2 * SEG, :] = key_ref[...]
    values_all[SEG : 2 * SEG, :] = value_ref[...]
    scan = gate_scan(heads, first_head, gate_ref[...], bias_ref, place_row, live_ref[0, 0:1, :])
    columns = write_columns(scan)
    fill_bias(hidden, place, live_prev_ref[0, 0:1, :], scan["live"])
    older = jnp.where(place > lax.broadcasted_iota(jnp.int32, (SEG, 1), 0), 1.0, 0.0)
    grad = grad_ref[...].astype(f32)
    query = query_unit * SCORE_SCALE
    key = key_unit * MEMORY_SCALE
    queries = (query, swap_halves(query))
    keys = (key, swap_halves(key))
    values = (value, swap_halves(value))
    grads = (grad, swap_halves(grad))
    every = range(heads)
    owns = (low, jnp.logical_not(low))
    grad_query = jnp.zeros((SEG, LANES), f32)
    grad_key = key_carry[...]
    grad_value = value_carry[...]
    wide = lane_index((SEG, LANES))
    write_grads = jnp.zeros((SEG, LANES), f32)
    sublane = lax.broadcasted_iota(jnp.int32, (8, 1), 0)
    keep_start = jnp.zeros((8, 1), f32)
    mix_start = jnp.zeros((8, 1), f32)
    fade_start = jnp.zeros((8, 1), f32)

    query_own = [jnp.where(owns[head], query, 0.0).astype(bf16) for head in every]
    grad_own = [jnp.where(owns[head], grad, 0.0).astype(bf16) for head in every]
    scores = [dot_nt(query_own[head], keys_all[...]) for head in every]
    prob_grads = [dot_nt(grad_own[head], values_all[...]) for head in every]
    probs, score_grads = [], []
    for head in every:
        prob = jnp.exp(scores[head] + hidden[...] - total_ref[:, head : head + 1])
        spread = lane_sum(prob * prob_grads[head])
        score_grads.append((prob * (prob_grads[head] - spread)).astype(bf16))
        probs.append(prob.astype(bf16))
    back_keys = dot_tn(score_grads[0], query_own[0])
    back_values = dot_tn(probs[0], grad_own[0])
    for head in every[1:]:
        back_keys = back_keys + dot_tn(score_grads[head], query_own[head])
        back_values = back_values + dot_tn(probs[head], grad_own[head])
    for head in every:
        back = dot_nn(score_grads[head], keys_all[...])
        grad_query = grad_query + jnp.where(owns[head], SCORE_SCALE * back, 0.0)
    key_carry[...] = back_keys[0:SEG]
    value_carry[...] = back_values[0:SEG]
    grad_key = grad_key + back_keys[SEG : 2 * SEG]
    grad_value = grad_value + back_values[SEG : 2 * SEG]
    back_pkeys = back_keys[2 * SEG : 2 * SEG + P_SIZE] * (1.0 / SCORE_SCALE)
    dpersist_ref[0:P_SIZE, :] += back_pkeys
    dpersist_ref[P_SIZE:, :] += back_values[2 * SEG : 2 * SEG + P_SIZE]

    mems, swaps = [mem_ref[head] for head in every], [swap_ref[head] for head in every]
    states = [[state_ref[0, head, member].astype(f32) for member in range(2)] for head in every]
    lates = [[late[head, member] for member in range(2)] for head in every]
    firsts = [jnp.where(low, mems[head].astype(f32), states[head][0]).astype(bf16) for head in every]
    seconds = [
        jnp.where(low, swaps[head].astype(f32), states[head][1]).astype(bf16) for head in every
    ]
    asked = [
        jnp.where(low, queries[head], older * queries[1 - head]).astype(bf16) for head in every
    ]
    told = [jnp.where(low, grads[head], older * grads[1 - head]).astype(bf16) for head in every]
    key_bfs = [jnp.where(low, keys[head], 0.0).astype(bf16) for head in every]
    read_inners = [dot_nt(asked[head], firsts[head]) for head in every]
    read_grads = [dot_nt(told[head], seconds[head]) for head in every]
    inners = [dot_nt(key_bfs[head], mems[head]) for head in every]
    key_twices = [jnp.where(low, keys[head], keys[1 - head]) for head in every]
    scales = [
        jnp.where(low, columns[:, head : head + 1], columns[:, 8 + head : 9 + head])
        for head in every
    ]
    late_bfs = [[member.astype(bf16) for member in lates[head]] for head in every]
    key_scaled = [(key_twices[head] * scales[head]).astype(bf16) for head in every]
    grad_descents = [dot_nt(key_scaled[head], late_bfs[head][0]) for head in every]
    read_backs, reads = [], []
    for head in every:
        _, _, active, slope = half_swish(read_inners[head])
        grad_inner = (read_grads[head] * slope).astype(bf16)
        read_backs.append(dot_nn(grad_inner, firsts[head]))
        reads.append((dot_tn(grad_inner, asked[head]), dot_tn(active.astype(bf16), told[head])))
    actives, slopes, curves = [], [], []
    for head in every:
        turn, _, active, slope = half_swish(inners[head])
        actives.append(active.astype(bf16))
        slopes.append(slope)
        curves.append(0.5 - turn * (slope - 0.5))
    errors = [
        jnp.where(low, dot_nn(actives[head], swaps[head]) - values[head], 0.0) for head in every
    ]
    error_bfs = [error.astype(bf16) for error in errors]
    pulled = [dot_nt(error_bfs[head], swaps[head]) for head in every]
    active_backs = [dot_nn(actives[head], late_bfs[head][1]) for head in every]
    for head in every:
        back = read_backs[head]
        turned = swap_halves(back)
        if head == 0:
            back = jnp.where(low, MEMORY_SCALE * (back + older * turned), 0.0)
        else:
            back = jnp.where(low, 0.0, MEMORY_SCALE * (turned + older * back))
        grad_query = grad_query + back
    descents = [(pulled[head] * slopes[head]).astype(bf16) for head in every]
    grad_pulled = [(grad_descents[head] * slopes[head]).astype(bf16) for head in every]
    curved = [grad_descents[head] * pulled[head] * curves[head] for head in every]
    back_keys = [dot_nn(descents[head], late_bfs[head][0]) for head in every]
    pulled_backs = [dot_nn(grad_pulled[head], swaps[head]) for head in every]
    error_twices = [errors[head] + swap_halves(errors[head]) for head in every]
    error_scaled = [(error_twices[head] * scales[head]).astype(bf16) for head in every]
    error_backs = []
    for head in every:
        weight_grad = key_twices[head] * back_keys[head] + error_twices[head] * active_backs[head]
        grad_state_weight = lane_sum(jnp.where(low, weight_grad, 0.0))
        grad_write_weight = lane_sum(jnp.where(low, 0.0, weight_grad))
        write_grads = jnp.where(wide == head, grad_state_weight, write_grads)
        write_grads = jnp.where(wide == 8 + head, grad_write_weight, write_grads)
        back = active_backs[head] * scales[head]
        back = jnp.where(low, back + swap_halves(back) + pulled_backs[head], 0.0)
        error_backs.append(back)
        grad_value = grad_value - (back if head == 0 else swap_halves(back))
    back_bfs = [back.astype(bf16) for back in error_backs]
    grad_actives = [
        dot_nt(error_scaled[head], late_bfs[head][1]) + dot_nt(back_bfs[head], swaps[head])
        for head in every
    ]
    grad_inners = [
        (curved[head] + grad_actives[head] * slopes[head]).astype(bf16) for head in every
    ]
    for head in every:
        back = back_keys[head] * scales[head]
        back = back + swap_halves(back) + dot_nn(grad_inners[head], mems[head])
        back = jnp.where(low, MEMORY_SCALE * back, 0.0)
        grad_key = grad_key + (back if head == 0 else swap_halves(back))
        write_one = dot_tn(grad_inners[head], key_bfs[head])
        write_two = dot_tn(grad_pulled[head], error_bfs[head])
        write_two = write_two + dot_tn(actives[head], back_bfs[head])
        read_one, read_two = reads[head]
        dmem_ref[head] += jnp.where(low, read_one + write_one, swap_halves(read_two + write_two))

        (late_one, late_two), (state_one, state_two) = lates[head], states[head]
        factor, blend = state_factors(scan["totals"], head, low)
        same = late_one * state_one + late_two * state_two
        cross = late_one * swap_halves(state_one) + late_two * swap_halves(state_two)
        same_low = jnp.sum(lane_sum(jnp.where(low, same, 0.0)), axis=0, keepdims=True)
        same_high = jnp.sum(lane_sum(jnp.where(low, 0.0, same)), axis=0, keepdims=True)
        cross_high = jnp.sum(lane_sum(jnp.where(low, 0.0, cross)), axis=0, keepdims=True)
        keep_start = jnp.where(sublane == head, same_low, keep_start)
        fade_start = jnp.where(sublane == head, same_high, fade_start)
        mix_start = jnp.where(sublane == head, cross_high, mix_start)
        for member, old, read in ((0, late_one, read_one), (1, late_two, read_two)):
            turned = jnp.where(low, blend * swap_halves(old), read)
            late[head, member] = factor * old + turned

    lane = lane_index((8, SEG))
    write_rows = jnp.transpose(write_grads)
    grad_state_rows, grad_write_rows = write_rows[0:8], write_rows[8:16]
    written = scan["written"]
    keep_grads = chain_rows(scan["carry"], grad_state_rows * written, keep_start, lane)
    mix_grads = chain_rows(scan["carry"], grad_write_rows * written, mix_start, lane)
    mix_next = scan["carry"] * mix_grads + grad_write_rows * written
    fade_grads = chain_rows(scan["fade"], mix_next, fade_start, lane)
    grad_written = grad_state_rows * scan["keep_after"] + grad_write_rows * scan["reach"]
    grad_carry = keep_grads * scan["keep_after"] + mix_grads * scan["reach"]
    grad_fade = fade_grads * scan["fade_after"]
    used = sublane < heads
    forget, momentum, step = scan["forget"], scan["momentum"], scan["step"]
    forget_back = -grad_fade * scan["keep"] * forget * (1.0 - forget)
    momentum_back = grad_carry * scan["keep"] * momentum * (1.0 - momentum)
    step_back = -THETA_SCALE * grad_written * scan["live"] * step * (1.0 - step)
    gate_back = jnp.concatenate(
        [
            jnp.where(used, forget_back, 0.0),
            jnp.where(used, momentum_back, 0.0),
            jnp.where(used, step_back, 0.0),
            jnp.zeros((LANES - 24, SEG), f32),
        ],
        axis=0,
    )
    gate_back = jnp.transpose(gate_back)
    dbias_ref[0:1, :] += jnp.sum(gate_back, axis=0, keepdims=True)
    draw_ref[:, 3 * LANES :] = gate_back.astype(bf16)

    grad_mixed = jnp.concatenate(
        [
            unit_pair_pull(query_unit, query_inverse, grad_query, low),
            unit_pair_pull(key_unit, key_inverse, grad_key, low),
            grad_value,
        ],
        axis=1,
    )
    back = conv_ref[0:1, :] * grad_mixed
    dconv_ref[0:1, :] += jnp.sum(grad_mixed * ext[8 : 8 + SEG, :], axis=0, keepdims=True)
    for offset in range(1, 4):
        kept = jnp.where(place >= offset, grad_mixed, 0.0)
        member = offset - 1
        shifted_rows[member, SEG : SEG + 8, :] = shifted_rows[member, 0:8, :]
        shifted_rows[member, 0:SEG, :] = kept
        back = back + conv_ref[offset : offset + 1, :] * shifted_rows[
            member, offset : offset + SEG, :
        ]
        dconv_ref[offset : offset + 1, :] += jnp.sum(
            kept * ext[8 - offset : 8 - offset + SEG, :], axis=0, keepdims=True
        )
    draw_ref[:, : 3 * LANES] = back.astype(bf16)


def whole_of(array):
    zeros = (0,) * array.ndim
    return pl.BlockSpec(array.shape, lambda n: zeros)


def mix_backward(
    collective, plan, heads, raw, gates, live, keys, values, totals, states, grad, *constants
):
    length = raw.shape[0]
    count = length // SEG

    def here(n):
        return count - 1 - n

    def before(n):
        return jnp.maximum(count - 2 - n, 0)

    row_block = pl.BlockSpec((SEG, LANES), lambda n: (here(n), 0))
    prev_block = pl.BlockSpec((SEG, LANES), lambda n: (before(n), 0))
    tail_rows = SEG // 16
    smem = pl.BlockSpec(memory_space=pltpu.SMEM)
    carried_in, carried_out = plan.specs(True)
    return pl.pallas_call(
        partial(backward_kernel, heads, plan),
        grid=(count,),
        in_specs=[
            pl.BlockSpec((SEG, 3 * LANES), lambda n: (here(n), 0)),
            pl.BlockSpec((16, 3 * LANES), lambda n: (jnp.maximum(here(n) * tail_rows - 1, 0), 0)),
            row_block,
            pl.BlockSpec((1, 8, SEG), lambda n: (here(n), 0, 0)),
            pl.BlockSpec((1, 8, SEG), lambda n: (before(n), 0, 0)),
            row_block,
            prev_block,
            row_block,
            prev_block,
            pl.BlockSpec((SEG, 8), lambda n: (here(n), 0)),
            pl.BlockSpec((1, heads, 2, MH, LANES), lambda n: (here(n), 0, 0, 0, 0)),
            row_block,
        ]
        + [whole_of(member) for member in constants[:4]]
        + [smem, smem]
        + carried_in,
        out_specs=[
            pl.BlockSpec((SEG, 4 * LANES), lambda n: (here(n), 0)),
            pl.BlockSpec((heads, MH, LANES), lambda n: (0, 0, 0)),
            pl.BlockSpec((8, 3 * LANES), lambda n: (0, 0)),
            pl.BlockSpec((2 * P_SIZE, LANES), lambda n: (0, 0)),
            pl.BlockSpec((8, LANES), lambda n: (0, 0)),
        ]
        + carried_out,
        out_shape=[
            jax.ShapeDtypeStruct((length, 4 * LANES), bf16),
            jax.ShapeDtypeStruct((heads, MH, LANES), f32),
            jax.ShapeDtypeStruct((8, 3 * LANES), f32),
            jax.ShapeDtypeStruct((2 * P_SIZE, LANES), f32),
            jax.ShapeDtypeStruct((8, LANES), f32),
        ]
        + plan.shapes,
        scratch_shapes=[
            pltpu.VMEM((SEG + 8, 3 * LANES), f32),
            pltpu.VMEM((3, SEG + 8, 3 * LANES), f32),
            pltpu.VMEM((SEG, LANES), f32),
            pltpu.VMEM((SEG, LANES), f32),
            pltpu.VMEM((heads, 2, MH, LANES), f32),
            pltpu.VMEM((2 * SEG + LANES, LANES), bf16),
            pltpu.VMEM((2 * SEG + LANES, LANES), bf16),
            pltpu.VMEM((SEG, 2 * SEG + LANES), f32),
        ]
        + plan.scratch,
        compiler_params=pltpu.CompilerParams(
            dimension_semantics=("arbitrary",),
            collective_id=collective,
            has_side_effects=True,
            vmem_limit_bytes=VMEM_GRANT,
        ),
        name="mix_backward",
    )(
        raw,
        raw,
        gates,
        live,
        live,
        keys,
        keys,
        values,
        values,
        totals,
        states,
        grad,
        *constants,
        *plan.arrays,
    )


class PlaneGather:
    def __init__(self, seqs, source, target, sems):
        self.source, self.target = source, target
        self.local, self.far_send, self.far_recv = sems[:3]
        self.near_send, self.near_recv, self.relay_send, self.relay_recv = sems[3:]
        self.chips = seqs // 2
        self.relayed = self.chips == 4
        self.seq, self.line = lax.axis_index("seq"), lax.axis_index("fsdp")
        self.chip, self.core = self.seq // 2, lax.rem(self.seq, 2)
        self.half = source.shape[0] // 2

    @staticmethod
    def sems(seqs):
        dma = pltpu.SemaphoreType.DMA
        return [dma((1,))] + [dma((seqs // 2,))] * 4 + [dma((2,))] * 2

    def chip_at(self, k):
        side = math.isqrt(self.chips)
        across = lax.rem(lax.rem(self.chip, side) + lax.rem(k, side), side)
        along = lax.rem(self.chip // side + k // side, side)
        return along * side + across

    def copy(self, source, target, send, recv, place):
        return pltpu.make_async_remote_copy(
            src_ref=source,
            dst_ref=target,
            send_sem=send,
            recv_sem=recv,
            device_id=(place, self.line),
            device_id_type=MESH,
        )

    def own(self):
        return pltpu.make_async_copy(self.source, self.target.at[self.seq], self.local.at[0])

    def far(self, q, slot):
        place = 2 * q + self.core
        block = self.target.at[2 * slot + self.core]
        return self.copy(self.source, block, self.far_send.at[q], self.far_recv.at[slot], place)

    def near(self, q, side):
        block = self.target.at[2 * q + (self.core if side == 0 else 1 - self.core)]
        place = 2 * self.chip + 1 - self.core
        return self.copy(block, block, self.near_send.at[q], self.near_recv.at[q], place)

    def near_own(self):
        block = self.target.at[self.seq]
        place = 2 * self.chip + 1 - self.core
        send, recv = self.near_send.at[self.chip], self.near_recv.at[self.chip]
        return self.copy(self.source, block, send, recv, place)

    def relay(self, part, q, to):
        rows = pl.ds(part * self.half, self.half)
        block = self.target.at[2 * q + self.core, rows]
        send, recv = self.relay_send.at[part], self.relay_recv.at[part]
        return self.copy(block, block, send, recv, 2 * to + self.core)

    def loop(self, first, body):
        def step(k, carry):
            body(k)
            return carry

        lax.fori_loop(first, self.chips, step, 0)

    def start(self):
        self.near_own().start()
        if self.relayed:
            for k in (1, 2):
                self.far(self.chip_at(k), self.chip).start()
        else:
            self.loop(1, lambda k: self.far(self.chip_at(k), self.chip).start())
        self.own().start()

    def step(self, k):
        q = self.chip_at(k)

        @pl.when(k == 0)
        def _():
            self.own().wait()

        if self.relayed:
            across, along, diagonal = (self.chip_at(i) for i in (1, 2, 3))

            @pl.when(k == 1)
            def _():
                self.far(across, across).wait_recv()
                self.relay(0, across, along).start()
                self.near(across, 0).start()
                self.far(along, along).wait_recv()
                self.relay(1, along, across).start()
                self.near(along, 0).start()

            @pl.when(k == 3)
            def _():
                self.relay(0, diagonal, along).wait_recv()
                self.relay(1, diagonal, across).wait_recv()
                self.near(diagonal, 0).start()

        else:

            @pl.when(k > 0)
            def _():
                self.far(q, q).wait_recv()
                self.near(q, 0).start()

        self.near(q, 1).wait_recv()

    def finish(self):
        self.near_own().wait_send()
        self.loop(1, lambda k: self.near(self.chip_at(k), 0).wait_send())
        if self.relayed:
            across, along = self.chip_at(1), self.chip_at(2)
            self.far(across, across).wait_send()
            self.far(along, along).wait_send()
            self.relay(0, across, along).wait_send()
            self.relay(1, along, across).wait_send()
        else:
            self.loop(1, lambda k: self.far(self.chip_at(k), self.chip_at(k)).wait_send())

class LineGather:
    def __init__(self, lines, source, target, sems, keep=True):
        self.lines, self.source, self.target, self.keep = lines, source, target, keep
        self.local, self.right_send, self.left_send, self.recv = sems
        self.seq, self.line = lax.axis_index("seq"), lax.axis_index("fsdp")

    @staticmethod
    def sems(lines):
        dma = pltpu.SemaphoreType.DMA
        return [dma((1,)), dma((lines,)), dma((lines,)), dma((lines,))]

    def own(self):
        return pltpu.make_async_copy(self.source, self.target.at[self.line], self.local.at[0])

    def hop(self, block, step, own=False):
        send = self.right_send if step > 0 else self.left_send
        return pltpu.make_async_remote_copy(
            src_ref=self.source if own and self.keep else self.target.at[block],
            dst_ref=self.target.at[block],
            send_sem=send.at[block],
            recv_sem=self.recv.at[block],
            device_id=(self.seq, lax.rem(self.line + step + self.lines, self.lines)),
            device_id_type=MESH,
        )

    def start(self):
        @pl.when(self.line < self.lines - 1)
        def _():
            self.hop(self.line, 1, True).start()

        @pl.when(self.line > 0)
        def _():
            self.hop(self.line, -1, True).start()

        if self.keep:
            self.own().start()

    def round(self, distance):
        before, after = self.line - distance, self.line + distance

        @pl.when(before >= 0)
        def _():
            self.hop(before, 1).wait_recv()

            @pl.when(self.line < self.lines - 1)
            def _():
                self.hop(before, 1).start()

        @pl.when(after < self.lines)
        def _():
            self.hop(after, -1).wait_recv()

            @pl.when(self.line > 0)
            def _():
                self.hop(after, -1).start()

    def rounds(self, first=1):
        for distance in range(first, self.lines):
            self.round(distance)

    def finish(self):
        if self.keep:
            self.own().wait()
        for distance in range(self.lines):
            before, after = self.line - distance, self.line + distance

            @pl.when(jnp.logical_and(before >= 0, self.line < self.lines - 1))
            def _(before=before):
                self.hop(before, 1).wait_send()

            @pl.when(jnp.logical_and(after < self.lines, self.line > 0))
            def _(after=after):
                self.hop(after, -1).wait_send()


class LineSum:
    def __init__(self, lines, source, landed, target, sems):
        self.lines, self.source, self.landed, self.target = lines, source, landed, target
        self.send, self.recv, self.relay_send, self.relay_recv = sems
        self.seq, self.line = lax.axis_index("seq"), lax.axis_index("fsdp")
        self.relayed = lines == 4
        self.half = source.shape[1] // 2

    @staticmethod
    def sems(lines):
        dma = pltpu.SemaphoreType.DMA
        return [dma((lines,)), dma((lines,)), dma((2,)), dma((2,))]

    def at(self, k):
        return lax.rem(self.line + k, self.lines)

    def copy(self, source, target, send, recv, to):
        return pltpu.make_async_remote_copy(
            src_ref=source,
            dst_ref=target,
            send_sem=send,
            recv_sem=recv,
            device_id=(self.seq, to),
            device_id_type=MESH,
        )

    def far(self, i, slot):
        return self.copy(
            self.source.at[i], self.landed.at[slot], self.send.at[i], self.recv.at[slot], i
        )

    def relay(self, part, to):
        rows = pl.ds(part * self.half, self.half)
        return self.copy(
            self.source.at[self.at(2), rows],
            self.landed.at[to, rows],
            self.relay_send.at[part],
            self.relay_recv.at[part],
            to,
        )

    def loop(self, body):
        def step(k, carry):
            body(k)
            return carry

        lax.fori_loop(1, self.lines, step, 0)

    def start(self):
        if self.relayed:
            self.relay(0, self.at(1)).start()
            self.relay(1, self.at(3)).start()
        else:
            self.loop(lambda k: self.far(self.at(k), self.line).start())

    def middle(self):
        if not self.relayed:
            return
        for part, to in ((0, self.at(1)), (1, self.at(3))):
            rows = pl.ds(part * self.half, self.half)
            block = self.landed.at[self.line, rows]
            send, recv = self.relay_send.at[part], self.relay_recv.at[part]
            self.copy(block, block, send, recv, to).wait_recv()

            def add(i, carry, to=to, part=part):
                at = part * self.half + i
                both = self.source[to, at].astype(f32) + self.landed[self.line, at].astype(f32)
                self.source[to, at] = both.astype(bf16)
                return carry

            lax.fori_loop(0, self.half, add, 0)
            self.far(to, self.line).start()

    def others(self):
        return (self.at(1), self.at(3)) if self.relayed else [self.at(k) for k in range(1, self.lines)]

    def arrive(self):
        for i in self.others():
            self.far(i, i).wait_recv()

    def total(self, i):
        whole = self.source[self.line, i].astype(f32)
        for other in self.others():
            whole = whole + self.landed[other, i].astype(f32)
        return whole

    def finish(self):
        for i in self.others():
            self.far(i, i).wait_send()
        if self.relayed:
            self.relay(0, self.at(1)).wait_send()
            self.relay(1, self.at(3)).wait_send()


def exchange_phases(axes, counts, inputs, outputs, scratch):
    seqs, lines = axes
    chips = seqs // 2
    devices = seqs * lines
    seq, line = lax.axis_index("seq"), lax.axis_index("fsdp")
    me = seq * lines + line
    chip, core = seq // 2, lax.rem(seq, 2)
    sibling = (2 * chip + 1 - core, line)

    def twin(q):
        return (2 * q + core, line)

    def point(i):
        return (i // lines, lax.rem(i, lines))

    def loop(first, last, body):
        def step(k, carry):
            body(k)
            return carry

        lax.fori_loop(first, last, step, 0)

    position = 0
    groups = []
    for count in counts:
        groups.append((inputs[position : position + count], outputs[position : position + count]))
        position += count
    scratch = list(scratch)

    def take(number):
        taken = scratch[:number]
        del scratch[:number]
        return taken

    starts = []

    sums = []
    for source, target in zip(*groups[5]):
        pair, landed, pair_send, pair_recv, far_send, far_recv = take(6)

        def pair_copy(q, source=source, pair=pair, send=pair_send, recv=pair_recv):
            return pltpu.make_async_remote_copy(
                src_ref=source.at[2 * q + 1 - core],
                dst_ref=pair.at[q],
                send_sem=send.at[q],
                recv_sem=recv.at[q],
                device_id=sibling,
                device_id_type=MESH,
            )

        def far_copy(q, slot, pair=pair, landed=landed, send=far_send, recv=far_recv):
            return pltpu.make_async_remote_copy(
                src_ref=pair.at[q],
                dst_ref=landed.at[slot],
                send_sem=send.at[q],
                recv_sem=recv.at[slot],
                device_id=twin(q),
                device_id_type=MESH,
            )

        starts.append(
            lambda f=pair_copy: loop(1, chips + 1, lambda k: f(lax.rem(chip + k, chips)).start())
        )
        sums.append((source, target, pair, landed, pair_copy, far_copy))

    spread = []
    for source, target in zip(*groups[0]):
        gather = PlaneGather(seqs, source, target, take(7))
        starts.append(gather.start)
        spread.append(gather)

    direct = []
    for kind, (sources, targets) in (
        ("plane", groups[1]),
        ("line", groups[2]),
        ("every", groups[3]),
        ("all", groups[4]),
    ):
        for source, target in zip(sources, targets):
            local, send, recv = take(3)
            if kind == "plane":
                number, mine = seqs, seq
            elif kind == "line":
                number, mine = lines, line
            else:
                number, mine = devices, me

            def piece(i, source=source, kind=kind, number=number):
                if kind == "all" or (kind == "line" and source.ndim == 2):
                    return source
                if kind == "every" and source.shape[0] != number:
                    return source.at[i // lines]
                return source.at[i]

            def place(i, kind=kind):
                if kind == "plane":
                    return (i, line)
                if kind == "line":
                    return (seq, i)
                return point(i)

            def copy(i, slot, target=target, send=send, recv=recv, piece=piece, place=place):
                return pltpu.make_async_remote_copy(
                    src_ref=piece(i),
                    dst_ref=target.at[slot],
                    send_sem=send.at[i],
                    recv_sem=recv.at[slot],
                    device_id=place(i),
                    device_id_type=MESH,
                )

            def own(target=target, local=local, piece=piece, mine=mine):
                return pltpu.make_async_copy(piece(mine), target.at[mine], local.at[0])

            def start(copy=copy, own=own, mine=mine, number=number):
                loop(1, number, lambda k: copy(lax.rem(mine + k, number), mine).start())
                own().start()

            starts.append(start)
            direct.append((own, copy, mine, number))

    merges = []
    rows = 32
    for source, target in zip(*groups[7]):
        landed, summed, local, plane_send, plane_recv = take(5)
        line_sum = LineSum(lines, source, landed, target, take(4))

        def onward(i, slot, summed=summed, target=target, send=plane_send, recv=plane_recv):
            return pltpu.make_async_remote_copy(
                src_ref=summed.at[i],
                dst_ref=target.at[slot],
                send_sem=send.at[i],
                recv_sem=recv.at[slot],
                device_id=(i, line),
                device_id_type=MESH,
            )

        def keep(summed=summed, target=target, local=local):
            return pltpu.make_async_copy(summed.at[seq], target.at[seq], local.at[0])

        starts.insert(0, line_sum.start)
        merges.append((summed, line_sum, onward, keep))

    def begin():
        for start in starts:
            start()

    def middle():
        for source, target, pair, landed, pair_copy, far_copy in sums:

            def combine(k, source=source, pair=pair, pair_copy=pair_copy, far_copy=far_copy):
                q = lax.rem(chip + k, chips)
                pair_copy(q).wait_recv()

                def add(r):
                    part = pl.ds(pl.multiple_of(r * rows, rows), rows)
                    both = source[2 * q + core, part, :].astype(f32) + pair[q, part, :].astype(f32)
                    pair[q, part, :] = both.astype(bf16)

                loop(0, source.shape[1] // rows, add)

                @pl.when(k < chips)
                def _():
                    far_copy(q, chip).start()

            loop(1, chips + 1, combine)
        for gather in spread:
            gather.step(0)
            gather.step(1)
        for summed, line_sum, onward, keep in merges:
            line_sum.middle()
            line_sum.arrive()

            def add_up(k, summed=summed, line_sum=line_sum, onward=onward):
                i = lax.rem(seq + k, seqs)
                summed[i] = line_sum.total(i).astype(bf16)

                @pl.when(k < seqs)
                def _():
                    onward(i, seq).start()

            loop(1, seqs + 1, add_up)
            keep().start()

    def finish():
        for gather in spread:
            gather.loop(2, gather.step)
        for own, copy, mine, number in direct:

            def end(k, copy=copy, mine=mine, number=number):
                i = lax.rem(mine + k, number)
                copy(i, i).wait_recv()
                copy(i, i).wait_send()

            loop(1, number, end)
            own().wait()
        for gather in spread:
            gather.finish()
        for source, target, pair, landed, pair_copy, far_copy in sums:

            def end_sum(k, far_copy=far_copy):
                q = lax.rem(chip + k, chips)
                far_copy(q, q).wait_recv()

            loop(1, chips, end_sum)

            def add_all(r, target=target, pair=pair, landed=landed):
                part = pl.ds(pl.multiple_of(r * rows, rows), rows)
                whole = pair[chip, part, :].astype(f32)
                for k in range(1, chips):
                    whole = whole + landed[lax.rem(chip + k, chips), part, :].astype(f32)
                target[part, :] = whole

            loop(0, target.shape[0] // rows, add_all)
            loop(1, chips, lambda k, f=far_copy: f(lax.rem(chip + k, chips), chip).wait_send())
            loop(0, chips, lambda q, f=pair_copy: f(q).wait_send())
        for summed, line_sum, onward, keep in merges:
            line_sum.finish()

            def end_merge(k, onward=onward):
                i = lax.rem(seq + k, seqs)
                onward(i, i).wait_recv()
                onward(i, seq).wait_send()

            loop(1, seqs, end_merge)
            keep().wait()

    return begin, middle, finish


def greet_all(axes, kinds):
    seqs, lines = axes
    seq, line = lax.axis_index("seq"), lax.axis_index("fsdp")
    barrier = pltpu.get_barrier_semaphore()

    def signal(place):
        pl.semaphore_signal(barrier, inc=1, device_id=place, device_id_type=MESH)

    def loop(last, body):
        def step(k, carry):
            body(k)
            return carry

        lax.fori_loop(1, last, step, 0)

    if "all" in kinds:
        devices = seqs * lines
        me = seq * lines + line

        def greet(k):
            i = lax.rem(me + k, devices)
            signal((i // lines, lax.rem(i, lines)))

        loop(devices, greet)
        pl.semaphore_wait(barrier, devices - 1)
        return
    met = 0
    if "plane" in kinds:
        loop(seqs, lambda k: signal((lax.rem(seq + k, seqs), line)))
        met += seqs - 1
    if "line" in kinds:
        loop(lines, lambda k: signal((seq, lax.rem(line + k, lines))))
        met += lines - 1
    pl.semaphore_wait(barrier, met)


KINDS = (
    "gathers",
    "planes",
    "to_line",
    "everys",
    "alls",
    "scatters",
    "relays",
    "merges",
)


class Exchange:
    def __init__(self, **arrays):
        self.axes = seqs, lines = lax.axis_size("seq"), lax.axis_size("fsdp")
        chips, devices = seqs // 2, seqs * lines
        dma = pltpu.SemaphoreType.DMA
        groups = [tuple(arrays.get(kind, ())) for kind in KINDS]
        self.counts = tuple(len(group) for group in groups)
        self.arrays = [array for group in groups for array in group]
        scratch = {kind: [] for kind in KINDS}
        shapes, self.in_vmem = [], []
        kinds = set()
        for kind, group in zip(KINDS, groups):
            for array in group:
                shape, dtype = array.shape, array.dtype
                if kind == "gathers":
                    scratch[kind] += PlaneGather.sems(seqs)
                    shape = (seqs,) + shape
                elif kind == "planes":
                    scratch[kind] += [dma((1,)), dma((seqs,)), dma((seqs,))]
                elif kind == "to_line":
                    scratch[kind] += [dma((1,)), dma((lines,)), dma((lines,))]
                    shape = (lines,) + shape[-2:]
                elif kind == "everys":
                    scratch[kind] += [dma((1,)), dma((devices,)), dma((devices,))]
                    shape = (devices,) + shape[1:]
                elif kind == "alls":
                    scratch[kind] += [dma((1,)), dma((devices,)), dma((devices,))]
                    shape = (devices,) + shape
                elif kind == "scatters":
                    half = pltpu.VMEM((chips,) + shape[1:], bf16)
                    scratch[kind] += [half, half] + [dma((chips,))] * 4
                    shape, dtype = shape[1:], f32
                else:
                    raise ValueError(kind)
                shapes.append(jax.ShapeDtypeStruct(shape, dtype))
                self.in_vmem.append(kind == "scatters")
                if kind in ("everys", "alls"):
                    kinds.add("all")
                kinds.add("line" if kind == "to_line" else "plane")
        self.kinds = kinds
        self.shapes = shapes
        order = ("scatters", "gathers", "planes", "to_line", "everys", "alls")
        self.scratch = [member for kind in order for member in scratch[kind]]

    def specs(self, gridded):
        if gridded:
            vmem = [
                pl.BlockSpec(
                    array.shape, lambda n, z=(0,) * array.ndim: z, pipeline_mode=pl.Buffered(1)
                )
                for array in self.arrays
            ]
            out = [
                pl.BlockSpec(array.shape, lambda n, z=(0,) * len(array.shape): z)
                for array in self.shapes
            ]
        else:
            vmem = out = [pl.BlockSpec(memory_space=pltpu.VMEM)] * len(self.arrays)
        plain = pl.BlockSpec(memory_space=pl.ANY)
        first = [one if inside else plain for one, inside in zip(vmem, self.in_vmem)]
        second = [one if inside else plain for one, inside in zip(out, self.in_vmem)]
        return first, second

    def phases(self, inputs, outputs, scratch):
        return exchange_phases(self.axes, self.counts, inputs, outputs, scratch)


PLANE = (0, 1, 0, 0, 0, 0, 0, 0)
TO_LINE = (0, 0, 1, 0, 0, 0, 0, 0)

MERGE = (0, 0, 0, 0, 0, 0, 0, 1)


def round_up(number, step):
    return -(-number // step) * step


class Sizes:
    def __init__(self, seqs, lines):
        self.seqs, self.lines = seqs, lines
        self.chips, self.devices = seqs // 2, seqs * lines
        self.groups = min(HEAD_COUNT, seqs)
        self.copies = seqs // self.groups
        self.heads = HEAD_COUNT // self.groups
        self.width = self.heads * HEAD_SIZE
        self.share = D // self.devices
        self.memory = MH // self.devices
        self.piece = D // seqs
        self.hidden = FF // lines
        self.slab = self.hidden // seqs
        self.gate_at = round_up(3 * self.share, 8)
        self.mem_at = self.gate_at + round_up(max(self.share, 2 * P_SIZE), 8)
        self.rest_at = self.mem_at + round_up(self.heads * self.memory, 8)
        self.weight_rows = round_up(self.rest_at + 8, 16)
        self.grad_mem_at = round_up(4 * self.share, 8)
        self.grad_rest_at = self.grad_mem_at + round_up(self.heads * self.memory, 8)
        self.grad_rows = round_up(self.grad_rest_at + 16, 16)


def gate_choice(sizes, group, turned):
    shape = (LANES, 3 * HEAD_COUNT) if turned else (3 * HEAD_COUNT, LANES)
    lane = lax.broadcasted_iota(jnp.int32, shape, 0 if turned else 1)
    column = lax.broadcasted_iota(jnp.int32, shape, 1 if turned else 0)
    head = lane % 8
    chosen = (lane // 8 == column // HEAD_COUNT) & (head < sizes.heads)
    chosen = chosen & (column % HEAD_COUNT == group * sizes.heads + head)
    return jnp.where(chosen, 1.0, 0.0).astype(bf16)


def first_kernel(
    sizes,
    token_ref,
    qkv_ref,
    gate_ref,
    conv_ref,
    pkey_ref,
    pvalue_ref,
    gain_one_ref,
    gain_two_ref,
    live_ref,
    first_ref,
    second_ref,
    ffn_gate_ref,
    ffn_up_ref,
    ffn_down_ref,
    out_ref,
    cot_ref,
    length_ref,
    bias_ref,
    raw_out,
    gate_out,
    matrix_out,
    mem_out,
    swap_out,
    gain_out,
    taps_out,
    persist_out,
    live_out,
    key_out,
    value_out,
    total_out,
    state_out,
    mixed_got,
    normed_out,
    ffn_out,
    ffn_rest,
    ffn_relayed,
    out_rows,
    out_all,
    cot_all,
    rows_all,
    pack,
    pack_rows,
    ffn_pack,
    ffn_relay,
    got,
    conv_full,
    persist_full,
    mem_full,
    matrix_full,
    ext,
    keys_all,
    values_all,
    live_prev,
    state,
    hidden,
    normed_sem,
    mixed_out,
    mixed_local,
    mixed_send,
    mixed_recv,
    *sems,
):
    seqs, lines, share, width = sizes.seqs, sizes.lines, sizes.share, sizes.width
    seq, line = lax.axis_index("seq"), lax.axis_index("fsdp")
    group = seq // sizes.copies
    axes = (seqs, lines)
    greet_all(axes, ("plane", "line"))
    gather = PlaneGather(seqs, token_ref, rows_all, sems[:7])
    weights = exchange_phases(axes, PLANE, [pack], [got.at[line]], sems[7:10])
    weights_line = LineGather(lines, None, got, sems[10:14], keep=False)
    ffn = exchange_phases(axes, PLANE, [ffn_pack], [ffn_out], sems[14:17])
    outs = exchange_phases(axes, TO_LINE, [out_ref], [out_rows], sems[17:20])
    relay = exchange_phases(axes, PLANE, [ffn_relay], [ffn_relayed.at[line]], sems[20:23])
    relay_line = LineGather(lines, None, ffn_relayed, sems[23:27], keep=False)
    out_gather = PlaneGather(seqs, out_rows, out_all, sems[27:34])
    cot_gather = PlaneGather(seqs, cot_ref, cot_all, sems[34:41])
    piece = sizes.piece
    rest_line = LineGather(lines, ffn_out, ffn_rest, sems[41:45])
    for to in range(seqs):
        ffn_relay[to] = ffn_gate_ref[:, to * sizes.slab : (to + 1) * sizes.slab]
    relay[0]()
    outs[0]()
    relay[2]()
    relay_line.start()

    gate_at, mem_at, rest_at = sizes.gate_at, sizes.mem_at, sizes.rest_at
    pack_rows[...] = jnp.zeros_like(pack_rows)
    pack_rows[gate_at : gate_at + P_SIZE, HEAD_SIZE : HEAD_SIZE + share] = pkey_ref[...].astype(f32)
    pack_rows[gate_at + P_SIZE : gate_at + 2 * P_SIZE, HEAD_SIZE : HEAD_SIZE + share] = pvalue_ref[
        ...
    ].astype(f32)
    pack_rows[rest_at : rest_at + 4, : 3 * share] = conv_ref[...].astype(f32)
    pack_rows[rest_at + 4 : rest_at + 5, :share] = gain_one_ref[...].astype(f32)
    pack_rows[rest_at + 5 : rest_at + 6, :share] = gain_two_ref[...].astype(f32)
    live = live_ref[...].astype(f32)
    pack_rows[rest_at + 6 : rest_at + 7, :] = live[:, :LANES]
    pack_rows[rest_at + 7 : rest_at + 8, :] = live[:, LANES:]
    qkv = qkv_ref[...].astype(f32)
    gate = gate_ref[...]
    for to in range(seqs):
        other = to // sizes.copies
        for part in range(3):
            first = part * D + other * width
            pack_rows[part * share : (part + 1) * share, :width] = qkv[:, first : first + width]
        chosen = dot_nn(gate, gate_choice(sizes, other, False))
        pack_rows[gate_at : gate_at + share, :HEAD_SIZE] = chosen[:, :HEAD_SIZE]
        for head in range(sizes.heads):
            rows = slice(mem_at + head * sizes.memory, mem_at + (head + 1) * sizes.memory)
            member = other * sizes.heads + head
            pack_rows[rows, :HEAD_SIZE] = first_ref[member].astype(f32)
            pack_rows[rows, HEAD_SIZE:] = second_ref[member].astype(f32)
        pack[to] = pack_rows[...].astype(bf16)
    weights[0]()
    gather.start()
    for to in range(seqs):
        columns = slice(to * sizes.slab, (to + 1) * sizes.slab)
        ffn_pack[to, :piece, :] = ffn_up_ref[:, columns]
        turned = jnp.transpose(ffn_down_ref[columns, :].astype(f32))
        ffn_pack[to, piece:, :] = turned.astype(bf16)
    ffn[0]()
    weights[2]()
    weights_line.start()
    gather.step(0)
    gather.step(1)
    weights_line.round(1)
    outs[2]()
    out_gather.start()
    gather.loop(2, gather.step)
    weights_line.rounds(2)
    relay_line.round(1)
    cot_gather.start()
    ffn[2]()
    rest_line.start()

    aligned = share % 16 == 0
    matrix = matrix_out if aligned else matrix_full
    lane = lane_index((share, LANES))
    for i in range(sizes.devices):
        block = got[i % lines, i // lines].astype(f32)
        rows = slice(i * share, (i + 1) * share)
        for part in range(3):
            columns = slice(part * LANES, (part + 1) * LANES)
            matrix[rows, columns] = block[part * share : (part + 1) * share].astype(matrix.dtype)
        chosen = jnp.where(lane < 24, block[gate_at : gate_at + share], 0.0)
        matrix[rows, 3 * LANES :] = chosen.astype(matrix.dtype)
        for head in range(sizes.heads):
            first = mem_at + head * sizes.memory
            mem_full[head, i * sizes.memory : (i + 1) * sizes.memory, :] = block[
                first : first + sizes.memory
            ]
        rest = block[rest_at : rest_at + 8]
        conv_full[0:4, i * 3 * share : (i + 1) * 3 * share] = rest[0:4, : 3 * share]
        gain_out[4:6, i * share : (i + 1) * share] = rest[4:6, :share]
    if not aligned:
        matrix_out[...] = matrix_full[...].astype(bf16)
    for head in range(sizes.heads):
        mem_out[head] = mem_full[head].astype(bf16)
        swap_out[head] = swap_halves(mem_full[head]).astype(bf16)
    taps_out[...] = jnp.zeros_like(taps_out)
    for part in range(3):
        whole = conv_full[:, part * D : (part + 1) * D]
        turned = pltpu.roll(whole, lax.rem(D - group * width, D), 1)
        taps_out[0:4, part * LANES : part * LANES + width] = turned[0:4, :width]
    persist_full[...] = jnp.zeros_like(persist_full)
    for part in range(width // share):
        i = group * (width // share) + part
        block = got[lax.rem(i, lines), i // lines].astype(f32)
        persist_full[:, part * share : (part + 1) * share] = block[
            gate_at : gate_at + 2 * P_SIZE, HEAD_SIZE : HEAD_SIZE + share
        ]
    persist_out[...] = persist_full[...].astype(bf16)
    for s in range(seqs):
        block = got[line, s].astype(f32)
        live_out[s] = jnp.zeros((8, SEG), f32)
        live_out[s, 0:1, :LANES] = block[rest_at + 6 : rest_at + 7]
        live_out[s, 0:1, LANES:] = block[rest_at + 7 : rest_at + 8]

    gain = gain_out[4:5, :]
    gather.finish()

    def normed_copy(q):
        both = pl.ds(2 * q, 2)
        return pltpu.make_async_copy(rows_all.at[both], normed_out.at[both], normed_sem.at[q])

    def work(q, carry):
        both = pl.ds(2 * q, 2)
        rows = rows_all[both].reshape(2 * SEG, D).astype(f32)
        normed = (rows * norm_scale(rows) * gain).astype(bf16)
        projected = dot_nn(normed, matrix_out[...])
        rows_all[both] = normed.reshape(2, SEG, D)
        normed_copy(q).start()
        raw_out[both] = projected[:, : 3 * LANES].astype(bf16).reshape(2, SEG, 3 * LANES)
        gate_out[both] = projected[:, 3 * LANES :].reshape(2, SEG, LANES)
        return carry

    lax.fori_loop(0, sizes.chips, work, 0)

    def mixed_own():
        return pltpu.make_async_copy(mixed_out.at[seq], mixed_got.at[seq], mixed_local.at[0])

    def mixed_copy(to, slot):
        return pltpu.make_async_remote_copy(
            src_ref=mixed_out.at[to],
            dst_ref=mixed_got.at[slot],
            send_sem=mixed_send.at[to],
            recv_sem=mixed_recv.at[slot],
            device_id=(to, line),
            device_id_type=MESH,
        )

    def segment(n, carry):
        @pl.when(n == 1)
        def _():
            relay_line.round(2)

        @pl.when(n == 2)
        def _():
            out_gather.step(0)
            out_gather.step(1)
            cot_gather.step(0)
            cot_gather.step(1)

        @pl.when(n == 3)
        def _():
            rest_line.round(1)

        @pl.when(n == 6)
        def _():
            out_gather.loop(2, out_gather.step)
            cot_gather.loop(2, cot_gather.step)

        forward_step(
            n,
            sizes.heads,
            raw_out.at[n],
            gate_out.at[n],
            live_out.at[pl.ds(n, 1)],
            taps_out,
            mem_out,
            swap_out,
            persist_out,
            length_ref,
            bias_ref,
            mixed_out.at[n],
            key_out.at[n],
            value_out.at[n],
            total_out.at[n],
            state_out.at[pl.ds(n, 1)],
            ext,
            keys_all,
            values_all,
            live_prev,
            state,
            hidden,
        )

        @pl.when(n == seq)
        def _():
            mixed_own().start()

        @pl.when(n != seq)
        def _():
            mixed_copy(n, seq).start()

        return carry

    lax.fori_loop(0, seqs, segment, 0)
    lax.fori_loop(0, sizes.chips, lambda q, carry: (normed_copy(q).wait(), carry)[1], 0)
    out_gather.finish()
    cot_gather.finish()

    def mixed_end(k, carry):
        i = lax.rem(seq + k, seqs)
        mixed_copy(i, i).wait_recv()
        mixed_copy(i, i).wait_send()
        return carry

    mixed_own().wait()
    lax.fori_loop(1, seqs, mixed_end, 0)
    weights_line.finish()
    relay_line.rounds(3)
    rest_line.rounds(2)
    relay_line.finish()
    rest_line.finish()


def first_call(sizes, *operands):
    seqs, lines, heads = sizes.seqs, sizes.lines, sizes.heads
    dma = pltpu.SemaphoreType.DMA
    any_spec, vmem_spec = pl.BlockSpec(memory_space=pl.ANY), pl.BlockSpec(memory_space=pltpu.VMEM)
    smem_spec = pl.BlockSpec(memory_space=pltpu.SMEM)
    shape = jax.ShapeDtypeStruct
    matrix_shape = (D, 4 * LANES)
    return pl.pallas_call(
        partial(first_kernel, sizes),
        out_shape=[
            shape((seqs, SEG, 3 * LANES), bf16),
            shape((seqs, SEG, LANES), f32),
            shape(matrix_shape, bf16),
            shape((heads, MH, LANES), bf16),
            shape((heads, MH, LANES), bf16),
            shape((8, D), f32),
            shape((8, 3 * LANES), f32),
            shape((2 * P_SIZE, LANES), bf16),
            shape((seqs, 8, SEG), f32),
            shape((seqs, SEG, LANES), bf16),
            shape((seqs, SEG, LANES), bf16),
            shape((seqs, SEG, 8), f32),
            shape((seqs, heads, 2, MH, LANES), bf16),
            shape((seqs, SEG, LANES), bf16),
            shape((seqs, SEG, D), bf16),
            shape((seqs, 2 * sizes.piece, sizes.slab), bf16),
            shape((lines, seqs, 2 * sizes.piece, sizes.slab), bf16),
            shape((lines, seqs, sizes.piece, sizes.slab), bf16),
            shape((lines, sizes.share, D), bf16),
            shape((seqs, lines, sizes.share, D), bf16),
            shape((seqs, SEG, D), bf16),
        ],
        in_specs=[any_spec] + [vmem_spec] * 13 + [any_spec] * 2 + [smem_spec] * 2,
        out_specs=[vmem_spec] * 13 + [any_spec] * 8,
        scratch_shapes=[
            pltpu.VMEM((seqs, SEG, D), bf16),
            pltpu.VMEM((seqs, sizes.weight_rows, LANES), bf16),
            pltpu.VMEM((sizes.weight_rows, LANES), f32),
            pltpu.VMEM((seqs, 2 * sizes.piece, sizes.slab), bf16),
            pltpu.VMEM((seqs, sizes.piece, sizes.slab), bf16),
            pltpu.VMEM((lines, seqs, sizes.weight_rows, LANES), bf16),
            pltpu.VMEM((8, 3 * D), f32),
            pltpu.VMEM((2 * P_SIZE, LANES), f32),
            pltpu.VMEM((heads, MH, LANES), f32),
            pltpu.VMEM((8, LANES) if sizes.share % 16 == 0 else matrix_shape, f32),
            pltpu.VMEM((SEG + 8, 3 * LANES), f32),
            pltpu.VMEM((2 * SEG + LANES, LANES), bf16),
            pltpu.VMEM((2 * SEG + LANES, LANES), bf16),
            pltpu.VMEM((8, SEG), f32),
            pltpu.VMEM((heads, 2, MH, LANES), f32),
            pltpu.VMEM((SEG, 2 * SEG + LANES), f32),
            dma((sizes.chips,)),
            pltpu.VMEM((seqs, SEG, LANES), bf16),
            dma((1,)),
            dma((seqs,)),
            dma((seqs,)),
        ]
        + PlaneGather.sems(seqs)
        + [dma((1,)), dma((seqs,)), dma((seqs,))]
        + LineGather.sems(lines)
        + [dma((1,)), dma((seqs,)), dma((seqs,))]
        + [dma((1,)), dma((lines,)), dma((lines,))]
        + [dma((1,)), dma((seqs,)), dma((seqs,))]
        + LineGather.sems(lines)
        + PlaneGather.sems(seqs) * 2
        + LineGather.sems(lines),
        compiler_params=pltpu.CompilerParams(
            collective_id=0, has_side_effects=True, vmem_limit_bytes=VMEM_GRANT
        ),
        name="first",
    )(*operands)


def middle_kernel(
    sizes,
    mixed_ref,
    token_ref,
    cot_own_ref,
    out_ref,
    gain_ref,
    cot_ref,
    gate_weight_ref,
    weight_ref,
    middle_ref,
    grad_middle_ref,
    gain_grad_ref,
    out_grad_ref,
    grad_mixed_ref,
    down_ref,
    grad_ref,
    mixed_got,
    combined,
    rows_ref,
    sum_ref,
    rows_all,
    other,
    pair,
    landed,
    cot_slot,
    down_slot,
    both_matrix,
    down_matrix,
    both_grad,
    down_grad,
    acts,
    blocks,
    block_sem,
    gate_sem,
    pair_send,
    pair_recv,
    back_send,
    back_recv,
    cot_sem,
    down_sem,
    *sems,
):
    seqs, lines, chips = sizes.seqs, sizes.lines, sizes.chips
    hidden_size, slab, piece = sizes.slab * sizes.lines, sizes.slab, sizes.piece
    seq, line = lax.axis_index("seq"), lax.axis_index("fsdp")
    chip, core = seq // 2, lax.rem(seq, 2)
    sibling = (2 * chip + 1 - core, line)

    def loop(first, last, body):
        def step(k, carry):
            body(k)
            return carry

        lax.fori_loop(first, last, step, 0)

    def remote(source, target, send, recv, place):
        return pltpu.make_async_remote_copy(
            src_ref=source,
            dst_ref=target,
            send_sem=send,
            recv_sem=recv,
            device_id=place,
            device_id_type=MESH,
        )

    gather = PlaneGather(seqs, rows_ref, rows_all, sems[:7])

    chip_at = gather.chip_at

    def to_pair(j):
        q, slot = chip_at(j), lax.rem(j, 2)
        return remote(other.at[slot], pair.at[q], pair_send.at[slot], pair_recv.at[q], sibling)

    def back(q, slot):
        place = (2 * q + core, line)
        return remote(pair.at[q], landed.at[slot], back_send.at[q], back_recv.at[slot], place)

    resident = chips <= 4

    def cot_copy(j, slot):
        if resident:
            both = pl.ds(2 * chip_at(j), 2)
            return pltpu.make_async_copy(cot_ref.at[both], cot_slot.at[both], cot_sem.at[j])
        return pltpu.make_async_copy(
            cot_ref.at[pl.ds(2 * chip_at(j), 2)], cot_slot.at[slot], cot_sem.at[slot]
        )

    def down_copy(j):
        slot = j % 2 if isinstance(j, int) else lax.rem(j, 2)
        return pltpu.make_async_copy(
            down_slot.at[slot], down_ref.at[pl.ds(2 * chip_at(j), 2)], down_sem.at[slot]
        )

    axes = (seqs, lines)
    to_segment = pltpu.make_async_copy(mixed_ref, mixed_got, sems[7].at[0])
    to_heads = exchange_phases(axes, PLANE, [mixed_got], [grad_mixed_ref], sems[10:13])
    greet_all(axes, ("plane",))
    to_segment.start()
    if resident:
        for j in range(chips):
            cot_copy(j, 0).start()
    else:
        cot_copy(0, 0).start()
    slots = blocks.shape[0]

    def gate_copy(f):
        target = blocks.at[f % slots, :, pl.ds(0, piece)]
        return pltpu.make_async_copy(gate_weight_ref.at[f], target, gate_sem.at[f % slots])

    def weight_copy(f):
        target = blocks.at[f % slots, :, pl.ds(piece, 2 * piece)]
        return pltpu.make_async_copy(weight_ref.at[f], target, block_sem.at[f % slots])

    def grad_copy(f):
        return pltpu.make_async_copy(blocks.at[f % slots], grad_ref.at[f], block_sem.at[f % slots])

    for f in range(slots):
        gate_copy(f).start()
        weight_copy(f).start()
    for f in range(lines):
        gate_copy(f).wait()
        weight_copy(f).wait()
        columns = slice(f * slab, (f + 1) * slab)
        up_columns = slice(hidden_size + f * slab, hidden_size + (f + 1) * slab)
        for s in range(seqs):
            rows = slice(s * piece, (s + 1) * piece)
            both_matrix[rows, columns] = blocks[f % slots, s, :piece, :]
            both_matrix[rows, up_columns] = blocks[f % slots, s, piece : 2 * piece, :]
            down_matrix[rows, columns] = blocks[f % slots, s, 2 * piece :, :]
        if f + slots < lines:
            gate_copy(f + slots).start()
            weight_copy(f + slots).start()

    width, copies = sizes.width, sizes.copies
    to_segment.wait()
    for group in range(sizes.groups):
        combined[:, group * width : (group + 1) * width] = mixed_got[group * copies, :, :width]
    middle = token_ref[...].astype(f32) + dot_nn(combined[...], out_ref[...])
    middle_ref[...] = middle
    rows_ref[...] = (middle * norm_scale(middle) * gain_ref[5:6, :]).astype(bf16)
    gather.start()

    def forth(j):
        q = chip_at(j)
        gather.step(j)
        cot_copy(j, lax.rem(j, 2)).wait()

        if not resident:

            @pl.when(jnp.logical_and(j > 0, j + 1 < chips))
            def _():
                cot_copy(j + 1, lax.rem(j + 1, 2)).start()

        rows = rows_all[pl.ds(2 * q, 2)].reshape(2 * SEG, D)
        cot = cot_slot[pl.ds(2 * q, 2)] if resident else cot_slot[lax.rem(j, 2)]
        cot = cot.reshape(2 * SEG, D)
        grad_hidden = dot_nn(cot, down_matrix[...])
        ups = dot_nn(rows, both_matrix[...])
        gate_act, up_act = ups[:, :hidden_size], ups[:, hidden_size:]
        sigmoid = jax.nn.sigmoid(gate_act)
        swish = gate_act * sigmoid
        slope = sigmoid * (1.0 + gate_act - swish)
        acts[q, :, :hidden_size] = (grad_hidden * up_act * slope).astype(bf16)
        acts[q, :, hidden_size : 2 * hidden_size] = (grad_hidden * swish).astype(bf16)
        acts[q, :, 2 * hidden_size :] = (swish * up_act).astype(bf16)
        theirs = acts[q, pl.ds(pl.multiple_of((1 - core) * SEG, SEG), SEG), : 2 * hidden_size]
        theirs = dot_nt(theirs, both_matrix[...])

        @pl.when(j >= 2)
        def _():
            to_pair(j - 2).wait_send()

        other[lax.rem(j, 2)] = theirs.astype(bf16)
        to_pair(j).start()
        own = acts[q, pl.ds(pl.multiple_of(core * SEG, SEG), SEG), : 2 * hidden_size]
        own = dot_nt(own, both_matrix[...])
        to_pair(j).wait_recv()
        own = own + pair[q].astype(f32)

        @pl.when(j == 0)
        def _():
            sum_ref[...] = own

        @pl.when(j > 0)
        def _():
            pair[q] = own.astype(bf16)
            back(q, chip).start()

    def weigh(j):
        q = chip_at(j)
        slot = lax.rem(j, 2)

        @pl.when(j > 0)
        def _():
            cot_copy(j, slot).wait()

            @pl.when(j + 1 < chips)
            def _():
                cot_copy(j + 1, lax.rem(j + 1, 2)).start()

        @pl.when(j >= 2)
        def _():
            down_copy(j - 2).wait()

        hidden = acts[q, :, 2 * hidden_size :]
        down_slot[slot] = dot_nt(hidden, down_matrix[...]).astype(bf16).reshape(2, SEG, D)
        down_copy(j).start()
        rows = rows_all[pl.ds(2 * q, 2)].reshape(2 * SEG, D)
        cot = cot_slot[slot].reshape(2 * SEG, D)
        both_new = dot_tn(rows, acts[q, :, : 2 * hidden_size])
        down_new = dot_tn(cot, hidden)

        @pl.when(j == 0)
        def _():
            both_grad[...] = both_new
            down_grad[...] = down_new

        @pl.when(j > 0)
        def _():
            both_grad[...] += both_new
            down_grad[...] += down_new

    def weigh_all():
        rows = rows_all[...].reshape(seqs * SEG, D)
        cot = cot_slot[...].reshape(seqs * SEG, D)
        kept = acts[...].reshape(seqs * SEG, 3 * hidden_size)
        both, hidden = kept[:, : 2 * hidden_size], kept[:, 2 * hidden_size :]
        both_grad[...] = dot_tn(rows, both)
        down_grad[...] = dot_tn(cot, hidden)
        for j in range(chips):
            if j >= 2:
                down_copy(j - 2).wait()
            back_rows = dot_nt(acts[chip_at(j), :, 2 * hidden_size :], down_matrix[...])
            down_slot[j % 2] = back_rows.astype(bf16).reshape(2, SEG, D)
            down_copy(j).start()

    if resident:
        loop(0, chips, forth)
        weigh_all()
    else:
        forth(jnp.int32(0))
        weigh(jnp.int32(0))
        cot_copy(1, 1).start()
        loop(1, chips, forth)
        cot_copy(1, 1).start()
        loop(1, chips, weigh)
    for f in range(lines):
        if f >= slots:
            grad_copy(f - slots).wait()
        columns = slice(f * slab, (f + 1) * slab)
        up_columns = slice(hidden_size + f * slab, hidden_size + (f + 1) * slab)
        for s in range(seqs):
            rows = slice(s * piece, (s + 1) * piece)
            blocks[f % slots, s, :piece, :] = both_grad[rows, columns].astype(bf16)
            blocks[f % slots, s, piece : 2 * piece, :] = both_grad[rows, up_columns].astype(bf16)
            blocks[f % slots, s, 2 * piece :, :] = down_grad[rows, columns].astype(bf16)
        grad_copy(f).start()
    for f in range(lines - slots, lines):
        grad_copy(f).wait()
    loop(chips - 2, chips, lambda j: down_copy(j).wait())
    gather.finish()
    loop(chips - 2, chips, lambda j: to_pair(j).wait_send())

    def end(j):
        q = chip_at(j)
        back(q, chip).wait_send()
        back(q, q).wait_recv()
        sum_ref[...] += landed[q].astype(f32)

    loop(1, chips, end)

    middle = middle_ref[...]
    scale = norm_scale(middle)
    grad = sum_ref[...]
    gain_grad_ref[...] = jnp.sum(grad * middle * scale, axis=0, keepdims=True)
    grad = cot_own_ref[...].astype(f32) + norm_pull(middle, scale, gain_ref[5:6, :], grad)
    grad_middle_ref[...] = grad
    branch = grad.astype(bf16)
    grad_combined = dot_nt(branch, out_ref[...]).astype(bf16)
    if width < LANES:
        mixed_got[...] = jnp.zeros_like(mixed_got)
    for to in range(seqs):
        first = to // copies * width
        mixed_got[to, :, :width] = grad_combined[:, first : first + width]
    to_heads[0]()
    out_grad = dot_tn(combined[...], branch).astype(bf16)
    out_grad_ref[...] = out_grad.reshape(seqs, piece, D)
    to_heads[2]()


def middle_call(sizes, *operands):
    seqs, lines, chips = sizes.seqs, sizes.lines, sizes.chips
    hidden = sizes.slab * lines
    dma = pltpu.SemaphoreType.DMA
    any_spec, vmem_spec = pl.BlockSpec(memory_space=pl.ANY), pl.BlockSpec(memory_space=pltpu.VMEM)
    half = pltpu.VMEM((chips, SEG, D), bf16)
    slots = lines if lines <= 4 else 2
    block_shape = (lines, seqs, 3 * sizes.piece, sizes.slab)
    cot_shape = (seqs, SEG, D) if chips <= 4 else (2, 2, SEG, D)
    shape = jax.ShapeDtypeStruct
    return pl.pallas_call(
        partial(middle_kernel, sizes),
        out_shape=[
            shape((SEG, D), f32),
            shape((SEG, D), f32),
            shape((1, D), f32),
            shape((seqs, sizes.piece, D), bf16),
            shape((seqs, SEG, LANES), bf16),
            shape((seqs, SEG, D), bf16),
            shape(block_shape, bf16),
        ],
        in_specs=[any_spec] + [vmem_spec] * 4 + [any_spec] * 3,
        out_specs=[vmem_spec] * 4 + [any_spec] * 3,
        scratch_shapes=[
            pltpu.VMEM((seqs, SEG, LANES), bf16),
            pltpu.VMEM((SEG, D), bf16),
            pltpu.VMEM((SEG, D), bf16),
            pltpu.VMEM((SEG, D), f32),
            pltpu.VMEM((seqs, SEG, D), bf16),
            pltpu.VMEM((2, SEG, D), bf16),
            half,
            half,
            pltpu.VMEM(cot_shape, bf16),
            pltpu.VMEM((2, 2, SEG, D), bf16),
            pltpu.VMEM((D, 2 * hidden), bf16),
            pltpu.VMEM((D, hidden), bf16),
            pltpu.VMEM((D, 2 * hidden), f32),
            pltpu.VMEM((D, hidden), f32),
            pltpu.VMEM((chips, 2 * SEG, 3 * hidden), bf16),
            pltpu.VMEM((slots,) + block_shape[1:], bf16),
            dma((slots,)),
            dma((slots,)),
        ]
        + [dma((2,)), dma((chips,)), dma((chips,)), dma((chips,))]
        + [dma((max(chips, 2),)), dma((2,))]
        + PlaneGather.sems(seqs)
        + [dma((1,)), dma((seqs,)), dma((seqs,))] * 2,
        compiler_params=pltpu.CompilerParams(
            collective_id=2, has_side_effects=True, vmem_limit_bytes=VMEM_GRANT
        ),
        name="middle",
    )(*operands)


def last_kernel(
    sizes,
    grad_ref,
    normed_ref,
    matrix_ref,
    mem_ref,
    taps_ref,
    persist_ref,
    bias_ref,
    gain_two_ref,
    ffn_ref,
    out_ref,
    token_grad,
    pack_got,
    out_got,
    persist_got,
    ffn_got,
    normed_slot,
    matrix_grad,
    pack,
    pack_rows,
    pack_landed,
    pack_sums,
    out_blocks,
    other,
    pair,
    landed,
    normed_sem,
    pair_send,
    pair_recv,
    back_send,
    back_recv,
    *sems,
):
    seqs, lines, chips = sizes.seqs, sizes.lines, sizes.chips
    share, heads = sizes.share, sizes.heads
    seq, line = lax.axis_index("seq"), lax.axis_index("fsdp")
    chip, core = seq // 2, lax.rem(seq, 2)
    sibling = (2 * chip + 1 - core, line)
    side = math.isqrt(chips)

    def chip_at(k):
        across = lax.rem(lax.rem(chip, side) + lax.rem(k, side), side)
        along = lax.rem(chip // side + k // side, side)
        return along * side + across

    def loop(first, last, body):
        def step(k, carry):
            body(k)
            return carry

        lax.fori_loop(first, last, step, 0)

    def remote(source, target, send, recv, place):
        return pltpu.make_async_remote_copy(
            src_ref=source,
            dst_ref=target,
            send_sem=send,
            recv_sem=recv,
            device_id=place,
            device_id_type=MESH,
        )

    def to_pair(k):
        q, slot = chip_at(lax.rem(k, chips)), lax.rem(k, 2)
        return remote(other.at[slot], pair.at[q], pair_send.at[slot], pair_recv.at[q], sibling)

    def back(q, slot):
        place = (2 * q + core, line)
        return remote(pair.at[q], landed.at[slot], back_send.at[q], back_recv.at[slot], place)

    def normed_copy(q, slot):
        return pltpu.make_async_copy(
            normed_ref.at[pl.ds(2 * q, 2)], normed_slot.at[slot], normed_sem.at[slot]
        )

    axes = (seqs, lines)
    greet_all(axes, ("plane", "line"))
    ffn = exchange_phases(axes, PLANE, [ffn_ref], [ffn_got], sems[0:3])
    outs = exchange_phases(
        axes, (0, 0, 2, 0, 0, 0, 0, 0), [out_blocks, persist_ref], [out_got, persist_got], sems[3:9]
    )
    grads = exchange_phases(
        axes, MERGE, [pack], [pack_got], [pack_landed, pack_sums, *sems[9:16]]
    )
    normed_copy(0, 0).start()
    ffn[0]()

    def gather_grad(q):
        slot = lax.rem(q, 2)

        @pl.when(q + 1 < chips)
        def _():
            normed_copy(q + 1, lax.rem(q + 1, 2)).start()

        normed_copy(q, slot).wait()
        grad = grad_ref[pl.ds(2 * q, 2)].reshape(2 * SEG, 4 * LANES)
        new = dot_tn(normed_slot[slot].reshape(2 * SEG, D), grad)

        @pl.when(q == 0)
        def _():
            matrix_grad[...] = new

        @pl.when(q > 0)
        def _():
            matrix_grad[...] += new

    loop(0, chips, gather_grad)
    mem_at, rest_at = sizes.grad_mem_at, sizes.grad_rest_at
    pack_rows[...] = jnp.zeros_like(pack_rows)
    for tap in range(4):
        for part in range(3):
            at = rest_at + 3 * tap + part
            pack_rows[at : at + 1, :] = taps_ref[tap : tap + 1, part * LANES : (part + 1) * LANES]
    pack_rows[rest_at + 12 : rest_at + 13, :] = bias_ref[0:1, :]
    for i in range(sizes.devices):
        rows = slice(i * share, (i + 1) * share)
        for part in range(4):
            pack_rows[part * share : (part + 1) * share, :] = matrix_grad[
                rows, part * LANES : (part + 1) * LANES
            ]
        for head in range(heads):
            first = mem_at + head * sizes.memory
            pack_rows[first : first + sizes.memory, :] = mem_ref[
                head, i * sizes.memory : (i + 1) * sizes.memory, :
            ]
        pack_rows[rest_at + 13 : rest_at + 14, :share] = gain_two_ref[0:1, rows]
        pack[i % lines, i // lines] = pack_rows[...].astype(bf16)
    grads[0]()
    for f in range(lines):
        out_blocks[f] = out_ref[f * share : (f + 1) * share, :].astype(bf16)
    outs[0]()

    def spread(k):
        q = chip_at(lax.rem(k, chips))
        grad = grad_ref[pl.ds(2 * q, 2)].reshape(2 * SEG, 4 * LANES)
        if sizes.copies > 1:
            grad = grad * jnp.where(lax.rem(seq, sizes.copies) == 0, 1.0, 0.0).astype(bf16)
        whole = dot_nt(grad, matrix_ref[...])
        first_core, second_core = whole[:SEG], whole[SEG:]

        @pl.when(k >= 3)
        def _():
            to_pair(k - 2).wait_send()

        other[lax.rem(k, 2)] = jnp.where(core == 0, second_core, first_core).astype(bf16)
        to_pair(k).start()
        own = jnp.where(core == 0, first_core, second_core)
        to_pair(k).wait_recv()
        own = own + pair[q].astype(f32)

        @pl.when(k == chips)
        def _():
            token_grad[...] = own

        @pl.when(k < chips)
        def _():
            pair[q] = own.astype(bf16)
            back(q, chip).start()

    loop(1, chips + 1, spread)
    grads[1]()

    def add_back(k):
        q = chip_at(k)
        back(q, q).wait_recv()
        token_grad[...] += landed[q].astype(f32)

    loop(1, chips, add_back)
    ffn[2]()
    outs[2]()
    grads[2]()

    def end(k):
        q = chip_at(k)
        back(q, chip).wait_send()

    loop(1, chips, end)
    loop(chips - 1, chips + 1, lambda k: to_pair(k).wait_send())

def unpack_kernel(
    sizes,
    sum_ref,
    pack_got,
    out_got,
    persist_got,
    ffn_got,
    token_ref,
    middle_ref,
    gain_ref,
    qkv_ref,
    gate_ref,
    own_gain_ref,
    rows_ref,
    down_ref,
    output_ref,
    token_grad,
    qkv_grad,
    gate_grad,
    first_grad,
    second_grad,
    conv_grad,
    pkey_grad,
    pvalue_grad,
    out_grad,
    gain_one_grad,
    gain_two_grad,
    ffn_gate_grad,
    ffn_up_grad,
    ffn_down_grad,
    bias_grad,
    conv_full,
):
    seqs, lines = sizes.seqs, sizes.lines
    share, width, heads = sizes.share, sizes.width, sizes.heads
    seq, line = lax.axis_index("seq"), lax.axis_index("fsdp")
    me = seq * lines + line
    group = seq // sizes.copies
    mem_at, rest_at = sizes.grad_mem_at, sizes.grad_rest_at
    output_ref[...] = (rows_ref[...] + down_ref[...]).astype(bf16)
    rows = token_ref[...].astype(f32)
    scale = norm_scale(rows)
    token_grad[...] = middle_ref[...] + norm_pull(rows, scale, gain_ref[4:5, :], sum_ref[...])

    piece, slab = sizes.piece, sizes.slab
    for s in range(seqs):
        columns = slice(s * slab, (s + 1) * slab)
        ffn_gate_grad[:, columns] = ffn_got[s, :piece, :].astype(f32)
        ffn_up_grad[:, columns] = ffn_got[s, piece : 2 * piece, :].astype(f32)
        ffn_down_grad[columns, :] = jnp.transpose(ffn_got[s, 2 * piece :, :].astype(f32))
    out_sum = out_got[0].astype(f32)
    persist_sum = persist_got[0]
    for f in range(1, lines):
        out_sum = out_sum + out_got[f].astype(f32)
        persist_sum = persist_sum + persist_got[f]
    out_grad[...] = out_sum
    inside = lax.rem(LANES - (me * share - group * width), LANES)
    persist_sum = pltpu.roll(persist_sum, inside, 1)[:, :share]
    pkey_grad[...] = persist_sum[:P_SIZE]
    pvalue_grad[...] = persist_sum[P_SIZE:]

    gates = jnp.zeros((share, 3 * HEAD_COUNT), f32)
    bias = jnp.zeros((8, 3 * HEAD_COUNT), f32)
    gain_two = jnp.zeros((1, share), f32)
    conv_full[...] = jnp.zeros_like(conv_full)
    for s in range(seqs):
        block = pack_got[s].astype(f32)
        gain_two = gain_two + block[rest_at + 13 : rest_at + 14, :share]
        if s % sizes.copies:
            continue
        other_group = s // sizes.copies
        for part in range(3):
            first = part * D + other_group * width
            qkv_grad[:, first : first + width] = block[
                part * share : (part + 1) * share, :width
            ]
            for tap in range(4):
                at = rest_at + 3 * tap + part
                conv_full[tap : tap + 1, first : first + width] = block[at : at + 1, :width]
        choice = gate_choice(sizes, other_group, True)
        gates = gates + dot_nn(block[3 * share : 4 * share].astype(bf16), choice)
        rest = block[rest_at + 8 : rest_at + 16].astype(bf16)
        bias = bias + dot_nn(rest, choice)
        for head in range(heads):
            first = mem_at + head * sizes.memory
            member = other_group * heads + head
            rows = block[first : first + 8]
            second_grad[member] = rows[: sizes.memory, HEAD_SIZE:]
            first_grad[member] = rows[: sizes.memory, :HEAD_SIZE]
    gate_grad[...] = gates
    bias_grad[0:1, :] = 3.0 * bias[4:5, :HEAD_COUNT]
    bias_grad[1:2, :] = bias[4:5, HEAD_COUNT : 2 * HEAD_COUNT]
    bias_grad[2:3, :] = bias[4:5, 2 * HEAD_COUNT :]
    gain_two_grad[...] = gain_two
    along = jnp.sum(qkv_grad[...] * qkv_ref[...].astype(f32), axis=1, keepdims=True)
    along = along + jnp.sum(gates * gate_ref[...].astype(f32), axis=1, keepdims=True)
    gain_one_grad[...] = jnp.transpose(along)[0:1] / own_gain_ref[...].astype(f32)
    turned = pltpu.roll(conv_full[...], lax.rem(3 * D - me * 3 * share, 3 * D), 1)
    conv_grad[...] = turned[:4, : 3 * share]


def last_call(sizes, *operands):
    seqs, lines, chips, share = sizes.seqs, sizes.lines, sizes.chips, sizes.share
    dma = pltpu.SemaphoreType.DMA
    any_spec, vmem_spec = pl.BlockSpec(memory_space=pl.ANY), pl.BlockSpec(memory_space=pltpu.VMEM)
    shape = jax.ShapeDtypeStruct
    half = pltpu.VMEM((chips, SEG, D), bf16)
    in_specs = [vmem_spec] * len(operands)
    in_specs[1] = any_spec
    in_specs[8] = any_spec
    pack_shape = (lines, seqs, sizes.grad_rows, LANES)
    return pl.pallas_call(
        partial(last_kernel, sizes),
        out_shape=[
            shape((SEG, D), f32),
            shape(pack_shape[1:], bf16),
            shape((lines, share, D), bf16),
            shape((lines, 2 * P_SIZE, LANES), f32),
            shape((seqs, 3 * sizes.piece, sizes.slab), bf16),
        ],
        in_specs=in_specs,
        out_specs=[vmem_spec] + [any_spec] * 4,
        scratch_shapes=[
            pltpu.VMEM((2, 2, SEG, D), bf16),
            pltpu.VMEM((D, 4 * LANES), f32),
            pltpu.VMEM(pack_shape, bf16),
            pltpu.VMEM(pack_shape[2:], f32),
            pltpu.VMEM(pack_shape, bf16),
            pltpu.VMEM(pack_shape[1:], bf16),
            pltpu.VMEM((lines, share, D), bf16),
            pltpu.VMEM((2, SEG, D), bf16),
            half,
            half,
            dma((2,)),
        ]
        + [dma((2,)), dma((chips,)), dma((chips,)), dma((chips,))]
        + [dma((1,)), dma((seqs,)), dma((seqs,))]
        + [dma((1,)), dma((lines,)), dma((lines,))] * 2
        + [dma((1,)), dma((seqs,)), dma((seqs,))]
        + LineSum.sems(lines),
        compiler_params=pltpu.CompilerParams(
            collective_id=5, has_side_effects=True, vmem_limit_bytes=VMEM_GRANT
        ),
        name="last",
    )(*operands)


def unpack_call(sizes, *operands):
    share, memory = sizes.share, sizes.memory
    vmem_spec = pl.BlockSpec(memory_space=pltpu.VMEM)
    shape = jax.ShapeDtypeStruct
    return pl.pallas_call(
        partial(unpack_kernel, sizes),
        out_shape=[
            shape((SEG, D), bf16),
            shape((SEG, D), f32),
            shape((share, 3 * D), f32),
            shape((share, 3 * HEAD_COUNT), f32),
            shape((HEAD_COUNT, memory, HEAD_SIZE), f32),
            shape((HEAD_COUNT, memory, HEAD_SIZE), f32),
            shape((4, 3 * share), f32),
            shape((P_SIZE, share), f32),
            shape((P_SIZE, share), f32),
            shape((share, D), f32),
            shape((1, share), f32),
            shape((1, share), f32),
            shape((sizes.piece, sizes.hidden), f32),
            shape((sizes.piece, sizes.hidden), f32),
            shape((sizes.hidden, sizes.piece), f32),
            shape((3, HEAD_COUNT), f32),
        ],
        in_specs=[vmem_spec] * len(operands),
        out_specs=[vmem_spec] * 16,
        scratch_shapes=[pltpu.VMEM((8, 3 * D), f32)],
        compiler_params=pltpu.CompilerParams(vmem_limit_bytes=VMEM_GRANT),
        name="unpack",
    )(*operands)


def norm_scale(values):
    return lax.rsqrt(jnp.mean(values * values, axis=-1, keepdims=True) + NORM_EPS)


def norm_pull(values, scale, gain, grad):
    inner = jnp.mean(grad * gain * values, axis=-1, keepdims=True)
    return scale * (grad * gain - values * (scale * scale) * inner)


def on_device(
    tokens,
    norm1_gain,
    qkv_weight,
    gate_weight,
    conv_weight,
    memory_w1,
    memory_w2,
    persistent_keys,
    persistent_values,
    out_weight,
    norm2_gain,
    ffn_gate,
    ffn_up,
    ffn_down,
    gate_bias,
    doc_lengths,
    live_mask,
    cotangent,
):
    sizes = Sizes(lax.axis_size("seq"), lax.axis_size("fsdp"))
    seqs, heads = sizes.seqs, sizes.heads
    length = seqs * SEG
    (
        raw,
        gates,
        matrix,
        memory_both,
        memory_turned,
        gains,
        taps,
        persistent,
        live,
        keys,
        values,
        totals,
        states,
        mixed,
        normed,
        _,
        ffn_rest,
        ffn_gates,
        _,
        out_matrix,
        cot_rows,
    ) = first_call(
        sizes,
        tokens[0],
        qkv_weight,
        gate_weight,
        conv_weight,
        persistent_keys,
        persistent_values,
        norm1_gain[None],
        norm2_gain[None],
        live_mask,
        memory_w1.transpose(0, 2, 1),
        memory_w2,
        ffn_gate,
        ffn_up,
        ffn_down,
        out_weight,
        cotangent[0],
        doc_lengths,
        gate_bias,
    )
    constants = (taps, memory_both, memory_turned, persistent, doc_lengths, gate_bias)
    middle, grad_middle, grad_gain_two, grad_out, grad_mixed, down_part, ffn_grads = middle_call(
        sizes,
        mixed,
        tokens[0],
        cotangent[0],
        out_matrix.reshape(D, D),
        gains,
        cot_rows,
        ffn_gates,
        ffn_rest,
    )
    ffn_grads = lax.psum_scatter(ffn_grads, "fsdp")
    plan = Exchange(scatters=[down_part, grad_out])
    grad_all, grad_memory, grad_taps, grad_persistent, grad_bias, down_sum, grad_out = mix_backward(
        7,
        plan,
        heads,
        raw.reshape(length, 3 * LANES),
        gates.reshape(length, LANES),
        live,
        keys.reshape(length, LANES),
        values.reshape(length, LANES),
        totals.reshape(length, 8),
        states,
        grad_mixed.reshape(length, LANES),
        *constants,
    )
    token_sum, pack_got, out_got, persist_got, ffn_got = last_call(
        sizes,
        grad_all.reshape(seqs, SEG, 4 * LANES),
        normed,
        matrix,
        grad_memory,
        grad_taps,
        grad_persistent,
        grad_bias,
        grad_gain_two,
        ffn_grads,
        grad_out,
    )
    grads = unpack_call(
        sizes,
        token_sum,
        pack_got,
        out_got,
        persist_got,
        ffn_got,
        tokens[0],
        grad_middle,
        gains,
        qkv_weight,
        gate_weight,
        norm1_gain[None],
        middle,
        down_sum,
    )
    (
        output,
        input_grad,
        grad_qkv,
        grad_gate,
        grad_first,
        grad_second,
        grad_conv,
        grad_pkeys,
        grad_pvalues,
        grad_out,
        grad_gain_one,
        grad_gain_two,
        grad_ffn_gate,
        grad_ffn_up,
        grad_ffn_down,
        grad_bias,
    ) = grads
    return (
        output[None],
        input_grad[None],
        grad_gain_one[0],
        grad_qkv,
        grad_gate,
        grad_conv,
        grad_first.transpose(0, 2, 1),
        grad_second,
        grad_pkeys,
        grad_pvalues,
        grad_out,
        grad_gain_two[0],
        grad_ffn_gate,
        grad_ffn_up,
        grad_ffn_down,
        grad_bias,
    )


def solution(mesh):
    return jax.shard_map(
        on_device,
        mesh=mesh,
        in_specs=(
            P("fsdp", "seq", None),
            P(("seq", "fsdp")),
            P(("seq", "fsdp"), None),
            P(("seq", "fsdp"), None),
            P(None, ("seq", "fsdp")),
            P(None, None, ("seq", "fsdp")),
            P(None, ("seq", "fsdp"), None),
            P(None, ("seq", "fsdp")),
            P(None, ("seq", "fsdp")),
            P(("seq", "fsdp"), None),
            P(("seq", "fsdp")),
            P("seq", "fsdp"),
            P("seq", "fsdp"),
            P("fsdp", "seq"),
            P(),
            P("fsdp", None),
            P("fsdp", "seq"),
            P("fsdp", "seq", None),
        ),
        out_specs=(
            P("fsdp", "seq", None),
            P("fsdp", "seq", None),
            P(("seq", "fsdp")),
            P(("seq", "fsdp"), None),
            P(("seq", "fsdp"), None),
            P(None, ("seq", "fsdp")),
            P(None, None, ("seq", "fsdp")),
            P(None, ("seq", "fsdp"), None),
            P(None, ("seq", "fsdp")),
            P(None, ("seq", "fsdp")),
            P(("seq", "fsdp"), None),
            P(("seq", "fsdp")),
            P("seq", "fsdp"),
            P("seq", "fsdp"),
            P("fsdp", "seq"),
            P(),
        ),
        check_vma=False,
    )
```

```python
import math
from functools import partial

import jax
import jax.numpy as jnp
from jax import lax
from jax.experimental import pallas as pl
from jax.experimental.pallas import tpu as pltpu
from jax.sharding import PartitionSpec as P

HEAD_COUNT = 16
HEAD_SIZE = 64
D = 1024
FF = 4096
MH = 256
P_SIZE = 16
SEG = 256
LANES = 128

NORM_EPS = 1e-05
UNIT_EPS = 1e-06
SCORE_SCALE = 8.0
MEMORY_SCALE = 8.0
THETA_SCALE = 0.0005
MASKED = -1000000000.0
LEAST_SHIFT = -30.0
VMEM_GRANT = 62 * 1024 * 1024
MESH = pl.DeviceIdType.MESH

f32 = jnp.float32
bf16 = jnp.bfloat16


def dot_nt(left, right):
    return lax.dot_general(left, right, (((1,), (1,)), ((), ())), preferred_element_type=f32)


def dot_nn(left, right):
    return lax.dot_general(left, right, (((1,), (0,)), ((), ())), preferred_element_type=f32)


def dot_tn(left, right):
    return lax.dot_general(left, right, (((0,), (0,)), ((), ())), preferred_element_type=f32)


def lane_index(shape):
    return lax.broadcasted_iota(jnp.int32, shape, 1)


def swap_halves(rows):
    return pltpu.roll(rows, HEAD_SIZE, 1)


def lane_sum(rows):
    return jnp.sum(rows, axis=1, keepdims=True)


def unit_pair(rows, low):
    squares = rows * rows
    first = lane_sum(jnp.where(low, squares, 0.0))
    second = lane_sum(jnp.where(low, 0.0, squares))
    inverse = jnp.where(low, lax.rsqrt(first + UNIT_EPS), lax.rsqrt(second + UNIT_EPS))
    return rows * inverse, inverse


def unit_pair_pull(unit, inverse, grad, low):
    along = unit * grad
    first = lane_sum(jnp.where(low, along, 0.0))
    second = lane_sum(jnp.where(low, 0.0, along))
    return inverse * (grad - unit * jnp.where(low, first, second))


def mix_taps(ext_ref, conv_ref, place):
    mixed = conv_ref[0:1, :] * ext_ref[8 : 8 + SEG, :]
    for offset in range(1, 4):
        kept = jnp.where(place >= offset, ext_ref[8 - offset : 8 - offset + SEG, :], 0.0)
        mixed = mixed + conv_ref[offset : offset + 1, :] * kept
    return mixed


def places(length_ref, positions):
    start = jnp.int32(0)
    begin = jnp.zeros_like(positions)
    for document in range(1, length_ref.shape[1]):
        start = start + length_ref[0, document - 1]
        begin = jnp.where(positions >= start, start, begin)
    return positions - begin


def gate_scan(heads, first_head, gate_columns, bias_ref, place_row, live):
    lane = lane_index((8, SEG))
    sublane = lax.broadcasted_iota(jnp.int32, (8, SEG), 0)
    gate_rows = jnp.transpose(gate_columns)
    shifts = []
    for kind, (scale, shift) in enumerate(((3.0, -7.5), (1.0, 1.5), (1.0, 0.0))):
        bias = jnp.zeros((8, SEG), f32)
        for head in range(heads):
            own = scale * bias_ref[kind, first_head + head] + shift
            bias = jnp.where(sublane == head, own, bias)
        shifts.append(bias)
    keep = jnp.where(place_row < 1, 0.0, 1.0)
    forget = jax.nn.sigmoid(gate_rows[0:8] + shifts[0])
    momentum = jax.nn.sigmoid(gate_rows[8:16] + shifts[1])
    step = jax.nn.sigmoid(gate_rows[16:24] + shifts[2])
    carry = keep * momentum
    fade = keep * (1.0 - forget)
    keep_all, mix_all, fade_all = carry, carry, fade
    distance = 1
    while distance < SEG:
        inside = lane < SEG - distance
        turn = SEG - distance
        keep_next = jnp.where(inside, pltpu.roll(keep_all, turn, 1), 1.0)
        mix_next = jnp.where(inside, pltpu.roll(mix_all, turn, 1), 0.0)
        fade_next = jnp.where(inside, pltpu.roll(fade_all, turn, 1), 1.0)
        mix_all = mix_next * keep_all + fade_next * mix_all
        keep_all = keep_next * keep_all
        fade_all = fade_next * fade_all
        distance *= 2
    inside = lane < SEG - 1
    keep_after = jnp.where(inside, pltpu.roll(keep_all, SEG - 1, 1), 1.0)
    mix_after = jnp.where(inside, pltpu.roll(mix_all, SEG - 1, 1), 0.0)
    fade_after = jnp.where(inside, pltpu.roll(fade_all, SEG - 1, 1), 1.0)
    written = -THETA_SCALE * step * live
    return dict(
        keep=keep,
        live=live,
        forget=forget,
        momentum=momentum,
        step=step,
        carry=carry,
        fade=fade,
        keep_after=keep_after,
        reach=mix_after + fade_after,
        fade_after=fade_after,
        written=written,
        totals=(keep_all, mix_all, fade_all),
    )


def write_columns(scan):
    rows = jnp.concatenate(
        [scan["written"] * scan["keep_after"], scan["written"] * scan["reach"]], axis=0
    )
    return jnp.transpose(rows)


def state_factors(totals, head, low):
    keep_all, mix_all, fade_all = (member[head : head + 1, 0:1] for member in totals)
    return jnp.where(low, keep_all, fade_all), mix_all


def half_swish(inner):
    turn = jnp.tanh(0.5 * inner)
    sigmoid = 0.5 * turn + 0.5
    active = inner * sigmoid
    slope = sigmoid + active * (1.0 - sigmoid)
    return turn, sigmoid, active, slope


def fill_bias(bias_ref, place, live_prev, live_now):
    row = lax.broadcasted_iota(jnp.int32, (SEG, SEG), 0)
    gap = row - lane_index((SEG, SEG))
    hidden_prev = jnp.where(live_prev > 0.5, 0.0, MASKED)
    hidden_now = jnp.where(live_now > 0.5, 0.0, MASKED)
    bias_ref[:, :SEG] = jnp.where((gap < 0) & (gap + SEG <= place), hidden_prev, MASKED)
    bias_ref[:, SEG : 2 * SEG] = jnp.where((gap >= 0) & (gap <= place), hidden_now, MASKED)


def fill_persistent(bias_ref, keys_all, values_all, persist_ref):
    lane = lane_index((SEG, LANES))
    bias_ref[:, 2 * SEG :] = jnp.where(lane < P_SIZE, 0.0, MASKED)
    keys_all[2 * SEG :, :] = jnp.zeros((LANES, LANES), bf16)
    values_all[2 * SEG :, :] = jnp.zeros((LANES, LANES), bf16)
    pkeys = persist_ref[0:P_SIZE, :].astype(f32) * (1.0 / SCORE_SCALE)
    keys_all[2 * SEG : 2 * SEG + P_SIZE, :] = pkeys.astype(bf16)
    values_all[2 * SEG : 2 * SEG + P_SIZE, :] = persist_ref[P_SIZE:, :]


def forward_step(
    at,
    heads,
    raw_ref,
    gate_ref,
    live_ref,
    conv_ref,
    mem_ref,
    swap_ref,
    persist_ref,
    length_ref,
    bias_ref,
    comb_ref,
    key_out,
    value_out,
    total_out,
    state_out,
    ext,
    keys_all,
    values_all,
    live_prev,
    state,
    hidden,
):
    @pl.when(at == 0)
    def _():
        ext[0:8, :] = jnp.zeros((8, 3 * LANES), f32)
        keys_all[SEG : 2 * SEG, :] = jnp.zeros((SEG, LANES), bf16)
        values_all[SEG : 2 * SEG, :] = jnp.zeros((SEG, LANES), bf16)
        live_prev[...] = jnp.zeros_like(live_prev)
        state[...] = jnp.zeros_like(state)
        fill_persistent(hidden, keys_all, values_all, persist_ref)

    low = lane_index((SEG, LANES)) < HEAD_SIZE
    ext[8 : 8 + SEG, :] = raw_ref[...].astype(f32)
    place = places(length_ref, at * SEG + lax.broadcasted_iota(jnp.int32, (SEG, 1), 0))
    place_row = places(length_ref, at * SEG + lane_index((1, SEG)))
    first_head = (lax.axis_index("seq") * HEAD_COUNT) // lax.axis_size("seq")
    mixed = mix_taps(ext, conv_ref, place)
    ext[0:8, :] = ext[SEG : SEG + 8, :]
    query_unit, _ = unit_pair(mixed[:, :LANES], low)
    key_unit, _ = unit_pair(mixed[:, LANES : 2 * LANES], low)
    value = mixed[:, 2 * LANES :]
    keys_all[0:SEG, :] = keys_all[SEG : 2 * SEG, :]
    values_all[0:SEG, :] = values_all[SEG : 2 * SEG, :]
    keys_all[SEG : 2 * SEG, :] = key_unit.astype(bf16)
    values_all[SEG : 2 * SEG, :] = value.astype(bf16)
    key_out[...] = keys_all[SEG : 2 * SEG, :]
    value_out[...] = values_all[SEG : 2 * SEG, :]
    scan = gate_scan(heads, first_head, gate_ref[...], bias_ref, place_row, live_ref[0, 0:1, :])
    columns = write_columns(scan)
    fill_bias(hidden, place, live_prev[0:1, :], scan["live"])
    live_prev[...] = jnp.broadcast_to(scan["live"], (8, SEG))
    older = jnp.where(place > lax.broadcasted_iota(jnp.int32, (SEG, 1), 0), 1.0, 0.0)
    query = query_unit * SCORE_SCALE
    key = key_unit * MEMORY_SCALE
    queries = (query, swap_halves(query))
    keys = (key, swap_halves(key))
    values = (value, swap_halves(value))
    every = range(heads)
    owns = (low, jnp.logical_not(low))

    mems, swaps = [mem_ref[head] for head in every], [swap_ref[head] for head in every]
    states = [(state[head, 0], state[head, 1]) for head in every]
    for head in every:
        state_out[0, head, 0] = states[head][0].astype(bf16)
        state_out[0, head, 1] = states[head][1].astype(bf16)
    scores = [
        dot_nt(jnp.where(owns[head], query, 0.0).astype(bf16), keys_all[...]) for head in every
    ]
    key_cuts = [jnp.where(low, keys[head], 0.0) for head in every]
    inners = [dot_nt(key_cuts[head].astype(bf16), mems[head]) for head in every]
    firsts = [jnp.where(low, mems[head].astype(f32), states[head][0]).astype(bf16) for head in every]
    seconds = [
        jnp.where(low, swaps[head].astype(f32), states[head][1]).astype(bf16) for head in every
    ]
    asked = [
        jnp.where(low, queries[head], older * queries[1 - head]).astype(bf16) for head in every
    ]
    asked = [dot_nt(asked[head], firsts[head]) for head in every]
    log_totals = jnp.zeros((SEG, 8), f32)
    combined = jnp.zeros((SEG, LANES), f32)
    attended = []
    for head in every:
        shown = scores[head] + hidden[...]
        highest = jnp.max(shown[:, 2 * SEG :], axis=1, keepdims=True)
        highest = jnp.maximum(highest, LEAST_SHIFT)
        weights = jnp.exp(shown - highest)
        summed = lane_sum(weights)
        attended.append(dot_nn(weights.astype(bf16), values_all[...]) * (1.0 / summed))
        log_totals = jnp.where(lane_index((SEG, 8)) == head, highest + jnp.log(summed), log_totals)
    total_out[...] = log_totals
    actives, slopes = [], []
    for head in every:
        _, _, active, slope = half_swish(inners[head])
        actives.append(active.astype(bf16))
        slopes.append(slope)
    errors = [
        jnp.where(low, dot_nn(actives[head], swaps[head]) - values[head], 0.0) for head in every
    ]
    answers = []
    for head in every:
        _, _, active, _ = half_swish(asked[head])
        answers.append(dot_nn(active.astype(bf16), seconds[head]))
    descents = [
        (dot_nt(errors[head].astype(bf16), swaps[head]) * slopes[head]).astype(bf16)
        for head in every
    ]
    for head in every:
        answer = answers[head]
        turned = swap_halves(answer)
        if head == 0:
            recalled = jnp.where(low, answer + older * turned, 0.0)
        else:
            recalled = jnp.where(low, 0.0, turned + older * answer)
        combined = combined + jnp.where(owns[head], attended[head], 0.0) + recalled
    comb_ref[...] = combined.astype(bf16)
    for head in every:
        scale = jnp.where(low, columns[:, head : head + 1], columns[:, 8 + head : 9 + head])
        key_scaled = (jnp.where(low, keys[head], keys[1 - head]) * scale).astype(bf16)
        error_scaled = ((errors[head] + swap_halves(errors[head])) * scale).astype(bf16)
        factor, blend = state_factors(scan["totals"], head, low)
        for member, added in (
            (0, dot_tn(descents[head], key_scaled)),
            (1, dot_tn(actives[head], error_scaled)),
        ):
            old = states[head][member]
            turned = jnp.where(low, 0.0, blend * swap_halves(old))
            state[head, member] = factor * old + turned + added


def chain_rows(factor, term, start, lane):
    distance = 1
    while distance < SEG:
        inside = lane >= distance
        factor_before = jnp.where(inside, pltpu.roll(factor, distance, 1), 1.0)
        term_before = jnp.where(inside, pltpu.roll(term, distance, 1), 0.0)
        term = term + factor * term_before
        factor = factor * factor_before
        distance *= 2
    after = factor * start + term
    return jnp.where(lane == 0, start, pltpu.roll(after, 1, 1))


def backward_kernel(heads, plan, *refs):
    carried = len(plan.arrays)
    own, refs = refs[:18], refs[18:]
    sent, refs = refs[:carried], refs[carried:]
    made, refs = refs[:5], refs[5:]
    got, refs = refs[:carried], refs[carried:]
    begin, middle, finish = plan.phases(sent, got, refs[8:])
    at, last = pl.program_id(0), pl.num_programs(0) - 1

    @pl.when(at == 0)
    def _():
        greet_all(plan.axes, plan.kinds)
        begin()

    backward_step(heads, *own, *made, *refs[:8])

    @pl.when(at == 1)
    def _():
        middle()

    @pl.when(at == last)
    def _():
        finish()


def backward_step(
    heads,
    raw_ref,
    tail_ref,
    gate_ref,
    live_ref,
    live_prev_ref,
    key_ref,
    key_prev_ref,
    value_ref,
    value_prev_ref,
    total_ref,
    state_ref,
    grad_ref,
    conv_ref,
    mem_ref,
    swap_ref,
    persist_ref,
    length_ref,
    bias_ref,
    draw_ref,
    dmem_ref,
    dconv_ref,
    dpersist_ref,
    dbias_ref,
    ext,
    shifted_rows,
    key_carry,
    value_carry,
    late,
    keys_all,
    values_all,
    hidden,
):
    at = pl.program_id(0)

    @pl.when(at == 0)
    def _():
        dmem_ref[...] = jnp.zeros_like(dmem_ref)
        dconv_ref[...] = jnp.zeros_like(dconv_ref)
        dpersist_ref[...] = jnp.zeros_like(dpersist_ref)
        dbias_ref[...] = jnp.zeros_like(dbias_ref)
        shifted_rows[:, 0:8, :] = jnp.zeros((3, 8, 3 * LANES), f32)
        key_carry[...] = jnp.zeros_like(key_carry)
        value_carry[...] = jnp.zeros_like(value_carry)
        late[...] = jnp.zeros_like(late)
        fill_persistent(hidden, keys_all, values_all, persist_ref)

    low = lane_index((SEG, LANES)) < HEAD_SIZE
    ext[0:8, :] = tail_ref[8:16, :].astype(f32)
    ext[8 : 8 + SEG, :] = raw_ref[...].astype(f32)
    here = (pl.num_programs(0) - 1 - at) * SEG
    place = places(length_ref, here + lax.broadcasted_iota(jnp.int32, (SEG, 1), 0))
    place_row = places(length_ref, here + lane_index((1, SEG)))
    first_head = (lax.axis_index("seq") * HEAD_COUNT) // lax.axis_size("seq")
    mixed = mix_taps(ext, conv_ref, place)
    query_unit, query_inverse = unit_pair(mixed[:, :LANES], low)
    key_unit, key_inverse = unit_pair(mixed[:, LANES : 2 * LANES], low)
    value = mixed[:, 2 * LANES :]
    keys_all[0:SEG, :] = key_prev_ref[...]
    values_all[0:SEG, :] = value_prev_ref[...]
    keys_all[SEG : 2 * SEG, :] = key_ref[...]
    values_all[SEG : 2 * SEG, :] = value_ref[...]
    scan = gate_scan(heads, first_head, gate_ref[...], bias_ref, place_row, live_ref[0, 0:1, :])
    columns = write_columns(scan)
    fill_bias(hidden, place, live_prev_ref[0, 0:1, :], scan["live"])
    older = jnp.where(place > lax.broadcasted_iota(jnp.int32, (SEG, 1), 0), 1.0, 0.0)
    grad = grad_ref[...].astype(f32)
    query = query_unit * SCORE_SCALE
    key = key_unit * MEMORY_SCALE
    queries = (query, swap_halves(query))
    keys = (key, swap_halves(key))
    values = (value, swap_halves(value))
    grads = (grad, swap_halves(grad))
    every = range(heads)
    owns = (low, jnp.logical_not(low))
    grad_query = jnp.zeros((SEG, LANES), f32)
    grad_key = key_carry[...]
    grad_value = value_carry[...]
    wide = lane_index((SEG, LANES))
    write_grads = jnp.zeros((SEG, LANES), f32)
    sublane = lax.broadcasted_iota(jnp.int32, (8, 1), 0)
    keep_start = jnp.zeros((8, 1), f32)
    mix_start = jnp.zeros((8, 1), f32)
    fade_start = jnp.zeros((8, 1), f32)

    query_own = [jnp.where(owns[head], query, 0.0).astype(bf16) for head in every]
    grad_own = [jnp.where(owns[head], grad, 0.0).astype(bf16) for head in every]
    scores = [dot_nt(query_own[head], keys_all[...]) for head in every]
    prob_grads = [dot_nt(grad_own[head], values_all[...]) for head in every]
    probs, score_grads = [], []
    for head in every:
        prob = jnp.exp(scores[head] + hidden[...] - total_ref[:, head : head + 1])
        spread = lane_sum(prob * prob_grads[head])
        score_grads.append((prob * (prob_grads[head] - spread)).astype(bf16))
        probs.append(prob.astype(bf16))
    back_keys = dot_tn(score_grads[0], query_own[0])
    back_values = dot_tn(probs[0], grad_own[0])
    for head in every[1:]:
        back_keys = back_keys + dot_tn(score_grads[head], query_own[head])
        back_values = back_values + dot_tn(probs[head], grad_own[head])
    for head in every:
        back = dot_nn(score_grads[head], keys_all[...])
        grad_query = grad_query + jnp.where(owns[head], SCORE_SCALE * back, 0.0)
    key_carry[...] = back_keys[0:SEG]
    value_carry[...] = back_values[0:SEG]
    grad_key = grad_key + back_keys[SEG : 2 * SEG]
    grad_value = grad_value + back_values[SEG : 2 * SEG]
    back_pkeys = back_keys[2 * SEG : 2 * SEG + P_SIZE] * (1.0 / SCORE_SCALE)
    dpersist_ref[0:P_SIZE, :] += back_pkeys
    dpersist_ref[P_SIZE:, :] += back_values[2 * SEG : 2 * SEG + P_SIZE]

    mems, swaps = [mem_ref[head] for head in every], [swap_ref[head] for head in every]
    states = [[state_ref[0, head, member].astype(f32) for member in range(2)] for head in every]
    lates = [[late[head, member] for member in range(2)] for head in every]
    firsts = [jnp.where(low, mems[head].astype(f32), states[head][0]).astype(bf16) for head in every]
    seconds = [
        jnp.where(low, swaps[head].astype(f32), states[head][1]).astype(bf16) for head in every
    ]
    asked = [
        jnp.where(low, queries[head], older * queries[1 - head]).astype(bf16) for head in every
    ]
    told = [jnp.where(low, grads[head], older * grads[1 - head]).astype(bf16) for head in every]
    key_bfs = [jnp.where(low, keys[head], 0.0).astype(bf16) for head in every]
    read_inners = [dot_nt(asked[head], firsts[head]) for head in every]
    read_grads = [dot_nt(told[head], seconds[head]) for head in every]
    inners = [dot_nt(key_bfs[head], mems[head]) for head in every]
    key_twices = [jnp.where(low, keys[head], keys[1 - head]) for head in every]
    scales = [
        jnp.where(low, columns[:, head : head + 1], columns[:, 8 + head : 9 + head])
        for head in every
    ]
    late_bfs = [[member.astype(bf16) for member in lates[head]] for head in every]
    key_scaled = [(key_twices[head] * scales[head]).astype(bf16) for head in every]
    grad_descents = [dot_nt(key_scaled[head], late_bfs[head][0]) for head in every]
    read_backs, reads = [], []
    for head in every:
        _, _, active, slope = half_swish(read_inners[head])
        grad_inner = (read_grads[head] * slope).astype(bf16)
        read_backs.append(dot_nn(grad_inner, firsts[head]))
        reads.append((dot_tn(grad_inner, asked[head]), dot_tn(active.astype(bf16), told[head])))
    actives, slopes, curves = [], [], []
    for head in every:
        turn, _, active, slope = half_swish(inners[head])
        actives.append(active.astype(bf16))
        slopes.append(slope)
        curves.append(0.5 - turn * (slope - 0.5))
    errors = [
        jnp.where(low, dot_nn(actives[head], swaps[head]) - values[head], 0.0) for head in every
    ]
    error_bfs = [error.astype(bf16) for error in errors]
    pulled = [dot_nt(error_bfs[head], swaps[head]) for head in every]
    active_backs = [dot_nn(actives[head], late_bfs[head][1]) for head in every]
    for head in every:
        back = read_backs[head]
        turned = swap_halves(back)
        if head == 0:
            back = jnp.where(low, MEMORY_SCALE * (back + older * turned), 0.0)
        else:
            back = jnp.where(low, 0.0, MEMORY_SCALE * (turned + older * back))
        grad_query = grad_query + back
    descents = [(pulled[head] * slopes[head]).astype(bf16) for head in every]
    grad_pulled = [(grad_descents[head] * slopes[head]).astype(bf16) for head in every]
    curved = [grad_descents[head] * pulled[head] * curves[head] for head in every]
    back_keys = [dot_nn(descents[head], late_bfs[head][0]) for head in every]
    pulled_backs = [dot_nn(grad_pulled[head], swaps[head]) for head in every]
    error_twices = [errors[head] + swap_halves(errors[head]) for head in every]
    error_scaled = [(error_twices[head] * scales[head]).astype(bf16) for head in every]
    error_backs = []
    for head in every:
        weight_grad = key_twices[head] * back_keys[head] + error_twices[head] * active_backs[head]
        grad_state_weight = lane_sum(jnp.where(low, weight_grad, 0.0))
        grad_write_weight = lane_sum(jnp.where(low, 0.0, weight_grad))
        write_grads = jnp.where(wide == head, grad_state_weight, write_grads)
        write_grads = jnp.where(wide == 8 + head, grad_write_weight, write_grads)
        back = active_backs[head] * scales[head]
        back = jnp.where(low, back + swap_halves(back) + pulled_backs[head], 0.0)
        error_backs.append(back)
        grad_value = grad_value - (back if head == 0 else swap_halves(back))
    back_bfs = [back.astype(bf16) for back in error_backs]
    grad_actives = [
        dot_nt(error_scaled[head], late_bfs[head][1]) + dot_nt(back_bfs[head], swaps[head])
        for head in every
    ]
    grad_inners = [
        (curved[head] + grad_actives[head] * slopes[head]).astype(bf16) for head in every
    ]
    for head in every:
        back = back_keys[head] * scales[head]
        back = back + swap_halves(back) + dot_nn(grad_inners[head], mems[head])
        back = jnp.where(low, MEMORY_SCALE * back, 0.0)
        grad_key = grad_key + (back if head == 0 else swap_halves(back))
        write_one = dot_tn(grad_inners[head], key_bfs[head])
        write_two = dot_tn(grad_pulled[head], error_bfs[head])
        write_two = write_two + dot_tn(actives[head], back_bfs[head])
        read_one, read_two = reads[head]
        dmem_ref[head] += jnp.where(low, read_one + write_one, swap_halves(read_two + write_two))

        (late_one, late_two), (state_one, state_two) = lates[head], states[head]
        factor, blend = state_factors(scan["totals"], head, low)
        same = late_one * state_one + late_two * state_two
        cross = late_one * swap_halves(state_one) + late_two * swap_halves(state_two)
        same_low = jnp.sum(lane_sum(jnp.where(low, same, 0.0)), axis=0, keepdims=True)
        same_high = jnp.sum(lane_sum(jnp.where(low, 0.0, same)), axis=0, keepdims=True)
        cross_high = jnp.sum(lane_sum(jnp.where(low, 0.0, cross)), axis=0, keepdims=True)
        keep_start = jnp.where(sublane == head, same_low, keep_start)
        fade_start = jnp.where(sublane == head, same_high, fade_start)
        mix_start = jnp.where(sublane == head, cross_high, mix_start)
        for member, old, read in ((0, late_one, read_one), (1, late_two, read_two)):
            turned = jnp.where(low, blend * swap_halves(old), read)
            late[head, member] = factor * old + turned

    lane = lane_index((8, SEG))
    write_rows = jnp.transpose(write_grads)
    grad_state_rows, grad_write_rows = write_rows[0:8], write_rows[8:16]
    written = scan["written"]
    keep_grads = chain_rows(scan["carry"], grad_state_rows * written, keep_start, lane)
    mix_grads = chain_rows(scan["carry"], grad_write_rows * written, mix_start, lane)
    mix_next = scan["carry"] * mix_grads + grad_write_rows * written
    fade_grads = chain_rows(scan["fade"], mix_next, fade_start, lane)
    grad_written = grad_state_rows * scan["keep_after"] + grad_write_rows * scan["reach"]
    grad_carry = keep_grads * scan["keep_after"] + mix_grads * scan["reach"]
    grad_fade = fade_grads * scan["fade_after"]
    used = sublane < heads
    forget, momentum, step = scan["forget"], scan["momentum"], scan["step"]
    forget_back = -grad_fade * scan["keep"] * forget * (1.0 - forget)
    momentum_back = grad_carry * scan["keep"] * momentum * (1.0 - momentum)
    step_back = -THETA_SCALE * grad_written * scan["live"] * step * (1.0 - step)
    gate_back = jnp.concatenate(
        [
            jnp.where(used, forget_back, 0.0),
            jnp.where(used, momentum_back, 0.0),
            jnp.where(used, step_back, 0.0),
            jnp.zeros((LANES - 24, SEG), f32),
        ],
        axis=0,
    )
    gate_back = jnp.transpose(gate_back)
    dbias_ref[0:1, :] += jnp.sum(gate_back, axis=0, keepdims=True)
    draw_ref[:, 3 * LANES :] = gate_back.astype(bf16)

    grad_mixed = jnp.concatenate(
        [
            unit_pair_pull(query_unit, query_inverse, grad_query, low),
            unit_pair_pull(key_unit, key_inverse, grad_key, low),
            grad_value,
        ],
        axis=1,
    )
    back = conv_ref[0:1, :] * grad_mixed
    dconv_ref[0:1, :] += jnp.sum(grad_mixed * ext[8 : 8 + SEG, :], axis=0, keepdims=True)
    for offset in range(1, 4):
        kept = jnp.where(place >= offset, grad_mixed, 0.0)
        member = offset - 1
        shifted_rows[member, SEG : SEG + 8, :] = shifted_rows[member, 0:8, :]
        shifted_rows[member, 0:SEG, :] = kept
        back = back + conv_ref[offset : offset + 1, :] * shifted_rows[
            member, offset : offset + SEG, :
        ]
        dconv_ref[offset : offset + 1, :] += jnp.sum(
            kept * ext[8 - offset : 8 - offset + SEG, :], axis=0, keepdims=True
        )
    draw_ref[:, : 3 * LANES] = back.astype(bf16)


def whole_of(array):
    zeros = (0,) * array.ndim
    return pl.BlockSpec(array.shape, lambda n: zeros)


def mix_backward(
    collective, plan, heads, raw, gates, live, keys, values, totals, states, grad, *constants
):
    length = raw.shape[0]
    count = length // SEG

    def here(n):
        return count - 1 - n

    def before(n):
        return jnp.maximum(count - 2 - n, 0)

    row_block = pl.BlockSpec((SEG, LANES), lambda n: (here(n), 0))
    prev_block = pl.BlockSpec((SEG, LANES), lambda n: (before(n), 0))
    tail_rows = SEG // 16
    smem = pl.BlockSpec(memory_space=pltpu.SMEM)
    carried_in, carried_out = plan.specs(True)
    return pl.pallas_call(
        partial(backward_kernel, heads, plan),
        grid=(count,),
        in_specs=[
            pl.BlockSpec((SEG, 3 * LANES), lambda n: (here(n), 0)),
            pl.BlockSpec((16, 3 * LANES), lambda n: (jnp.maximum(here(n) * tail_rows - 1, 0), 0)),
            row_block,
            pl.BlockSpec((1, 8, SEG), lambda n: (here(n), 0, 0)),
            pl.BlockSpec((1, 8, SEG), lambda n: (before(n), 0, 0)),
            row_block,
            prev_block,
            row_block,
            prev_block,
            pl.BlockSpec((SEG, 8), lambda n: (here(n), 0)),
            pl.BlockSpec((1, heads, 2, MH, LANES), lambda n: (here(n), 0, 0, 0, 0)),
            row_block,
        ]
        + [whole_of(member) for member in constants[:4]]
        + [smem, smem]
        + carried_in,
        out_specs=[
            pl.BlockSpec((SEG, 4 * LANES), lambda n: (here(n), 0)),
            pl.BlockSpec((heads, MH, LANES), lambda n: (0, 0, 0)),
            pl.BlockSpec((8, 3 * LANES), lambda n: (0, 0)),
            pl.BlockSpec((2 * P_SIZE, LANES), lambda n: (0, 0)),
            pl.BlockSpec((8, LANES), lambda n: (0, 0)),
        ]
        + carried_out,
        out_shape=[
            jax.ShapeDtypeStruct((length, 4 * LANES), bf16),
            jax.ShapeDtypeStruct((heads, MH, LANES), f32),
            jax.ShapeDtypeStruct((8, 3 * LANES), f32),
            jax.ShapeDtypeStruct((2 * P_SIZE, LANES), f32),
            jax.ShapeDtypeStruct((8, LANES), f32),
        ]
        + plan.shapes,
        scratch_shapes=[
            pltpu.VMEM((SEG + 8, 3 * LANES), f32),
            pltpu.VMEM((3, SEG + 8, 3 * LANES), f32),
            pltpu.VMEM((SEG, LANES), f32),
            pltpu.VMEM((SEG, LANES), f32),
            pltpu.VMEM((heads, 2, MH, LANES), f32),
            pltpu.VMEM((2 * SEG + LANES, LANES), bf16),
            pltpu.VMEM((2 * SEG + LANES, LANES), bf16),
            pltpu.VMEM((SEG, 2 * SEG + LANES), f32),
        ]
        + plan.scratch,
        compiler_params=pltpu.CompilerParams(
            dimension_semantics=("arbitrary",),
            collective_id=collective,
            has_side_effects=True,
            vmem_limit_bytes=VMEM_GRANT,
        ),
        name="mix_backward",
    )(
        raw,
        raw,
        gates,
        live,
        live,
        keys,
        keys,
        values,
        values,
        totals,
        states,
        grad,
        *constants,
        *plan.arrays,
    )


class PlaneGather:
    def __init__(self, seqs, source, target, sems):
        self.source, self.target = source, target
        self.local, self.far_send, self.far_recv = sems[:3]
        self.near_send, self.near_recv, self.relay_send, self.relay_recv = sems[3:]
        self.chips = seqs // 2
        self.relayed = self.chips == 4
        self.seq, self.line = lax.axis_index("seq"), lax.axis_index("fsdp")
        self.chip, self.core = self.seq // 2, lax.rem(self.seq, 2)
        self.half = source.shape[0] // 2

    @staticmethod
    def sems(seqs):
        dma = pltpu.SemaphoreType.DMA
        return [dma((1,))] + [dma((seqs // 2,))] * 4 + [dma((2,))] * 2

    def chip_at(self, k):
        side = math.isqrt(self.chips)
        across = lax.rem(lax.rem(self.chip, side) + lax.rem(k, side), side)
        along = lax.rem(self.chip // side + k // side, side)
        return along * side + across

    def copy(self, source, target, send, recv, place):
        return pltpu.make_async_remote_copy(
            src_ref=source,
            dst_ref=target,
            send_sem=send,
            recv_sem=recv,
            device_id=(place, self.line),
            device_id_type=MESH,
        )

    def own(self):
        return pltpu.make_async_copy(self.source, self.target.at[self.seq], self.local.at[0])

    def far(self, q, slot):
        place = 2 * q + self.core
        block = self.target.at[2 * slot + self.core]
        return self.copy(self.source, block, self.far_send.at[q], self.far_recv.at[slot], place)

    def near(self, q, side):
        block = self.target.at[2 * q + (self.core if side == 0 else 1 - self.core)]
        place = 2 * self.chip + 1 - self.core
        return self.copy(block, block, self.near_send.at[q], self.near_recv.at[q], place)

    def near_own(self):
        block = self.target.at[self.seq]
        place = 2 * self.chip + 1 - self.core
        send, recv = self.near_send.at[self.chip], self.near_recv.at[self.chip]
        return self.copy(self.source, block, send, recv, place)

    def relay(self, part, q, to):
        rows = pl.ds(part * self.half, self.half)
        block = self.target.at[2 * q + self.core, rows]
        send, recv = self.relay_send.at[part], self.relay_recv.at[part]
        return self.copy(block, block, send, recv, 2 * to + self.core)

    def loop(self, first, body):
        def step(k, carry):
            body(k)
            return carry

        lax.fori_loop(first, self.chips, step, 0)

    def start(self):
        self.near_own().start()
        if self.relayed:
            for k in (1, 2):
                self.far(self.chip_at(k), self.chip).start()
        else:
            self.loop(1, lambda k: self.far(self.chip_at(k), self.chip).start())
        self.own().start()

    def step(self, k):
        q = self.chip_at(k)

        @pl.when(k == 0)
        def _():
            self.own().wait()

        if self.relayed:
            across, along, diagonal = (self.chip_at(i) for i in (1, 2, 3))

            @pl.when(k == 1)
            def _():
                self.far(across, across).wait_recv()
                self.relay(0, across, along).start()
                self.near(across, 0).start()
                self.far(along, along).wait_recv()
                self.relay(1, along, across).start()
                self.near(along, 0).start()

            @pl.when(k == 3)
            def _():
                self.relay(0, diagonal, along).wait_recv()
                self.relay(1, diagonal, across).wait_recv()
                self.near(diagonal, 0).start()

        else:

            @pl.when(k > 0)
            def _():
                self.far(q, q).wait_recv()
                self.near(q, 0).start()

        self.near(q, 1).wait_recv()

    def finish(self):
        self.near_own().wait_send()
        self.loop(1, lambda k: self.near(self.chip_at(k), 0).wait_send())
        if self.relayed:
            across, along = self.chip_at(1), self.chip_at(2)
            self.far(across, across).wait_send()
            self.far(along, along).wait_send()
            self.relay(0, across, along).wait_send()
            self.relay(1, along, across).wait_send()
        else:
            self.loop(1, lambda k: self.far(self.chip_at(k), self.chip_at(k)).wait_send())

class LineGather:
    def __init__(self, lines, source, target, sems, keep=True):
        self.lines, self.source, self.target, self.keep = lines, source, target, keep
        self.local, self.right_send, self.left_send, self.recv = sems
        self.seq, self.line = lax.axis_index("seq"), lax.axis_index("fsdp")

    @staticmethod
    def sems(lines):
        dma = pltpu.SemaphoreType.DMA
        return [dma((1,)), dma((lines,)), dma((lines,)), dma((lines,))]

    def own(self):
        return pltpu.make_async_copy(self.source, self.target.at[self.line], self.local.at[0])

    def hop(self, block, step, own=False):
        send = self.right_send if step > 0 else self.left_send
        return pltpu.make_async_remote_copy(
            src_ref=self.source if own and self.keep else self.target.at[block],
            dst_ref=self.target.at[block],
            send_sem=send.at[block],
            recv_sem=self.recv.at[block],
            device_id=(self.seq, lax.rem(self.line + step + self.lines, self.lines)),
            device_id_type=MESH,
        )

    def start(self):
        @pl.when(self.line < self.lines - 1)
        def _():
            self.hop(self.line, 1, True).start()

        @pl.when(self.line > 0)
        def _():
            self.hop(self.line, -1, True).start()

        if self.keep:
            self.own().start()

    def round(self, distance):
        before, after = self.line - distance, self.line + distance

        @pl.when(before >= 0)
        def _():
            self.hop(before, 1).wait_recv()

            @pl.when(self.line < self.lines - 1)
            def _():
                self.hop(before, 1).start()

        @pl.when(after < self.lines)
        def _():
            self.hop(after, -1).wait_recv()

            @pl.when(self.line > 0)
            def _():
                self.hop(after, -1).start()

    def rounds(self, first=1):
        for distance in range(first, self.lines):
            self.round(distance)

    def finish(self):
        if self.keep:
            self.own().wait()
        for distance in range(self.lines):
            before, after = self.line - distance, self.line + distance

            @pl.when(jnp.logical_and(before >= 0, self.line < self.lines - 1))
            def _(before=before):
                self.hop(before, 1).wait_send()

            @pl.when(jnp.logical_and(after < self.lines, self.line > 0))
            def _(after=after):
                self.hop(after, -1).wait_send()


class LineSum:
    def __init__(self, lines, source, landed, target, sems):
        self.lines, self.source, self.landed, self.target = lines, source, landed, target
        self.send, self.recv, self.relay_send, self.relay_recv = sems
        self.seq, self.line = lax.axis_index("seq"), lax.axis_index("fsdp")
        self.relayed = lines == 4
        self.half = source.shape[1] // 2

    @staticmethod
    def sems(lines):
        dma = pltpu.SemaphoreType.DMA
        return [dma((lines,)), dma((lines,)), dma((2,)), dma((2,))]

    def at(self, k):
        return lax.rem(self.line + k, self.lines)

    def copy(self, source, target, send, recv, to):
        return pltpu.make_async_remote_copy(
            src_ref=source,
            dst_ref=target,
            send_sem=send,
            recv_sem=recv,
            device_id=(self.seq, to),
            device_id_type=MESH,
        )

    def far(self, i, slot):
        return self.copy(
            self.source.at[i], self.landed.at[slot], self.send.at[i], self.recv.at[slot], i
        )

    def relay(self, part, to):
        rows = pl.ds(part * self.half, self.half)
        return self.copy(
            self.source.at[self.at(2), rows],
            self.landed.at[to, rows],
            self.relay_send.at[part],
            self.relay_recv.at[part],
            to,
        )

    def loop(self, body):
        def step(k, carry):
            body(k)
            return carry

        lax.fori_loop(1, self.lines, step, 0)

    def start(self):
        if self.relayed:
            self.relay(0, self.at(1)).start()
            self.relay(1, self.at(3)).start()
        else:
            self.loop(lambda k: self.far(self.at(k), self.line).start())

    def middle(self):
        if not self.relayed:
            return
        for part, to in ((0, self.at(1)), (1, self.at(3))):
            rows = pl.ds(part * self.half, self.half)
            block = self.landed.at[self.line, rows]
            send, recv = self.relay_send.at[part], self.relay_recv.at[part]
            self.copy(block, block, send, recv, to).wait_recv()

            def add(i, carry, to=to, part=part):
                at = part * self.half + i
                both = self.source[to, at].astype(f32) + self.landed[self.line, at].astype(f32)
                self.source[to, at] = both.astype(bf16)
                return carry

            lax.fori_loop(0, self.half, add, 0)
            self.far(to, self.line).start()

    def others(self):
        return (self.at(1), self.at(3)) if self.relayed else [self.at(k) for k in range(1, self.lines)]

    def arrive(self):
        for i in self.others():
            self.far(i, i).wait_recv()

    def total(self, i):
        whole = self.source[self.line, i].astype(f32)
        for other in self.others():
            whole = whole + self.landed[other, i].astype(f32)
        return whole

    def finish(self):
        for i in self.others():
            self.far(i, i).wait_send()
        if self.relayed:
            self.relay(0, self.at(1)).wait_send()
            self.relay(1, self.at(3)).wait_send()


def exchange_phases(axes, counts, inputs, outputs, scratch):
    seqs, lines = axes
    chips = seqs // 2
    devices = seqs * lines
    seq, line = lax.axis_index("seq"), lax.axis_index("fsdp")
    me = seq * lines + line
    chip, core = seq // 2, lax.rem(seq, 2)
    sibling = (2 * chip + 1 - core, line)

    def twin(q):
        return (2 * q + core, line)

    def point(i):
        return (i // lines, lax.rem(i, lines))

    def loop(first, last, body):
        def step(k, carry):
            body(k)
            return carry

        lax.fori_loop(first, last, step, 0)

    position = 0
    groups = []
    for count in counts:
        groups.append((inputs[position : position + count], outputs[position : position + count]))
        position += count
    scratch = list(scratch)

    def take(number):
        taken = scratch[:number]
        del scratch[:number]
        return taken

    starts = []

    sums = []
    for source, target in zip(*groups[5]):
        pair, landed, pair_send, pair_recv, far_send, far_recv = take(6)

        def pair_copy(q, source=source, pair=pair, send=pair_send, recv=pair_recv):
            return pltpu.make_async_remote_copy(
                src_ref=source.at[2 * q + 1 - core],
                dst_ref=pair.at[q],
                send_sem=send.at[q],
                recv_sem=recv.at[q],
                device_id=sibling,
                device_id_type=MESH,
            )

        def far_copy(q, slot, pair=pair, landed=landed, send=far_send, recv=far_recv):
            return pltpu.make_async_remote_copy(
                src_ref=pair.at[q],
                dst_ref=landed.at[slot],
                send_sem=send.at[q],
                recv_sem=recv.at[slot],
                device_id=twin(q),
                device_id_type=MESH,
            )

        starts.append(
            lambda f=pair_copy: loop(1, chips + 1, lambda k: f(lax.rem(chip + k, chips)).start())
        )
        sums.append((source, target, pair, landed, pair_copy, far_copy))

    spread = []
    for source, target in zip(*groups[0]):
        gather = PlaneGather(seqs, source, target, take(7))
        starts.append(gather.start)
        spread.append(gather)

    direct = []
    for kind, (sources, targets) in (
        ("plane", groups[1]),
        ("line", groups[2]),
        ("every", groups[3]),
        ("all", groups[4]),
    ):
        for source, target in zip(sources, targets):
            local, send, recv = take(3)
            if kind == "plane":
                number, mine = seqs, seq
            elif kind == "line":
                number, mine = lines, line
            else:
                number, mine = devices, me

            def piece(i, source=source, kind=kind, number=number):
                if kind == "all" or (kind == "line" and source.ndim == 2):
                    return source
                if kind == "every" and source.shape[0] != number:
                    return source.at[i // lines]
                return source.at[i]

            def place(i, kind=kind):
                if kind == "plane":
                    return (i, line)
                if kind == "line":
                    return (seq, i)
                return point(i)

            def copy(i, slot, target=target, send=send, recv=recv, piece=piece, place=place):
                return pltpu.make_async_remote_copy(
                    src_ref=piece(i),
                    dst_ref=target.at[slot],
                    send_sem=send.at[i],
                    recv_sem=recv.at[slot],
                    device_id=place(i),
                    device_id_type=MESH,
                )

            def own(target=target, local=local, piece=piece, mine=mine):
                return pltpu.make_async_copy(piece(mine), target.at[mine], local.at[0])

            def start(copy=copy, own=own, mine=mine, number=number):
                loop(1, number, lambda k: copy(lax.rem(mine + k, number), mine).start())
                own().start()

            starts.append(start)
            direct.append((own, copy, mine, number))

    merges = []
    rows = 32
    for source, target in zip(*groups[7]):
        landed, summed, local, plane_send, plane_recv = take(5)
        line_sum = LineSum(lines, source, landed, target, take(4))

        def onward(i, slot, summed=summed, target=target, send=plane_send, recv=plane_recv):
            return pltpu.make_async_remote_copy(
                src_ref=summed.at[i],
                dst_ref=target.at[slot],
                send_sem=send.at[i],
                recv_sem=recv.at[slot],
                device_id=(i, line),
                device_id_type=MESH,
            )

        def keep(summed=summed, target=target, local=local):
            return pltpu.make_async_copy(summed.at[seq], target.at[seq], local.at[0])

        starts.insert(0, line_sum.start)
        merges.append((summed, line_sum, onward, keep))

    def begin():
        for start in starts:
            start()

    def middle():
        for source, target, pair, landed, pair_copy, far_copy in sums:

            def combine(k, source=source, pair=pair, pair_copy=pair_copy, far_copy=far_copy):
                q = lax.rem(chip + k, chips)
                pair_copy(q).wait_recv()

                def add(r):
                    part = pl.ds(pl.multiple_of(r * rows, rows), rows)
                    both = source[2 * q + core, part, :].astype(f32) + pair[q, part, :].astype(f32)
                    pair[q, part, :] = both.astype(bf16)

                loop(0, source.shape[1] // rows, add)

                @pl.when(k < chips)
                def _():
                    far_copy(q, chip).start()

            loop(1, chips + 1, combine)
        for gather in spread:
            gather.step(0)
            gather.step(1)
        for summed, line_sum, onward, keep in merges:
            line_sum.middle()
            line_sum.arrive()

            def add_up(k, summed=summed, line_sum=line_sum, onward=onward):
                i = lax.rem(seq + k, seqs)
                summed[i] = line_sum.total(i).astype(bf16)

                @pl.when(k < seqs)
                def _():
                    onward(i, seq).start()

            loop(1, seqs + 1, add_up)
            keep().start()

    def finish():
        for gather in spread:
            gather.loop(2, gather.step)
        for own, copy, mine, number in direct:

            def end(k, copy=copy, mine=mine, number=number):
                i = lax.rem(mine + k, number)
                copy(i, i).wait_recv()
                copy(i, i).wait_send()

            loop(1, number, end)
            own().wait()
        for gather in spread:
            gather.finish()
        for source, target, pair, landed, pair_copy, far_copy in sums:

            def end_sum(k, far_copy=far_copy):
                q = lax.rem(chip + k, chips)
                far_copy(q, q).wait_recv()

            loop(1, chips, end_sum)

            def add_all(r, target=target, pair=pair, landed=landed):
                part = pl.ds(pl.multiple_of(r * rows, rows), rows)
                whole = pair[chip, part, :].astype(f32)
                for k in range(1, chips):
                    whole = whole + landed[lax.rem(chip + k, chips), part, :].astype(f32)
                target[part, :] = whole

            loop(0, target.shape[0] // rows, add_all)
            loop(1, chips, lambda k, f=far_copy: f(lax.rem(chip + k, chips), chip).wait_send())
            loop(0, chips, lambda q, f=pair_copy: f(q).wait_send())
        for summed, line_sum, onward, keep in merges:
            line_sum.finish()

            def end_merge(k, onward=onward):
                i = lax.rem(seq + k, seqs)
                onward(i, i).wait_recv()
                onward(i, seq).wait_send()

            loop(1, seqs, end_merge)
            keep().wait()

    return begin, middle, finish


def greet_all(axes, kinds):
    seqs, lines = axes
    seq, line = lax.axis_index("seq"), lax.axis_index("fsdp")
    barrier = pltpu.get_barrier_semaphore()

    def signal(place):
        pl.semaphore_signal(barrier, inc=1, device_id=place, device_id_type=MESH)

    def loop(last, body):
        def step(k, carry):
            body(k)
            return carry

        lax.fori_loop(1, last, step, 0)

    if "all" in kinds:
        devices = seqs * lines
        me = seq * lines + line

        def greet(k):
            i = lax.rem(me + k, devices)
            signal((i // lines, lax.rem(i, lines)))

        loop(devices, greet)
        pl.semaphore_wait(barrier, devices - 1)
        return
    met = 0
    if "plane" in kinds:
        loop(seqs, lambda k: signal((lax.rem(seq + k, seqs), line)))
        met += seqs - 1
    if "line" in kinds:
        loop(lines, lambda k: signal((seq, lax.rem(line + k, lines))))
        met += lines - 1
    pl.semaphore_wait(barrier, met)


KINDS = (
    "gathers",
    "planes",
    "to_line",
    "everys",
    "alls",
    "scatters",
    "relays",
    "merges",
)


class Exchange:
    def __init__(self, **arrays):
        self.axes = seqs, lines = lax.axis_size("seq"), lax.axis_size("fsdp")
        chips, devices = seqs // 2, seqs * lines
        dma = pltpu.SemaphoreType.DMA
        groups = [tuple(arrays.get(kind, ())) for kind in KINDS]
        self.counts = tuple(len(group) for group in groups)
        self.arrays = [array for group in groups for array in group]
        scratch = {kind: [] for kind in KINDS}
        shapes, self.in_vmem = [], []
        kinds = set()
        for kind, group in zip(KINDS, groups):
            for array in group:
                shape, dtype = array.shape, array.dtype
                if kind == "gathers":
                    scratch[kind] += PlaneGather.sems(seqs)
                    shape = (seqs,) + shape
                elif kind == "planes":
                    scratch[kind] += [dma((1,)), dma((seqs,)), dma((seqs,))]
                elif kind == "to_line":
                    scratch[kind] += [dma((1,)), dma((lines,)), dma((lines,))]
                    shape = (lines,) + shape[-2:]
                elif kind == "everys":
                    scratch[kind] += [dma((1,)), dma((devices,)), dma((devices,))]
                    shape = (devices,) + shape[1:]
                elif kind == "alls":
                    scratch[kind] += [dma((1,)), dma((devices,)), dma((devices,))]
                    shape = (devices,) + shape
                elif kind == "scatters":
                    half = pltpu.VMEM((chips,) + shape[1:], bf16)
                    scratch[kind] += [half, half] + [dma((chips,))] * 4
                    shape, dtype = shape[1:], f32
                else:
                    raise ValueError(kind)
                shapes.append(jax.ShapeDtypeStruct(shape, dtype))
                self.in_vmem.append(kind == "scatters")
                if kind in ("everys", "alls"):
                    kinds.add("all")
                kinds.add("line" if kind == "to_line" else "plane")
        self.kinds = kinds
        self.shapes = shapes
        order = ("scatters", "gathers", "planes", "to_line", "everys", "alls")
        self.scratch = [member for kind in order for member in scratch[kind]]

    def specs(self, gridded):
        if gridded:
            vmem = [
                pl.BlockSpec(
                    array.shape, lambda n, z=(0,) * array.ndim: z, pipeline_mode=pl.Buffered(1)
                )
                for array in self.arrays
            ]
            out = [
                pl.BlockSpec(array.shape, lambda n, z=(0,) * len(array.shape): z)
                for array in self.shapes
            ]
        else:
            vmem = out = [pl.BlockSpec(memory_space=pltpu.VMEM)] * len(self.arrays)
        plain = pl.BlockSpec(memory_space=pl.ANY)
        first = [one if inside else plain for one, inside in zip(vmem, self.in_vmem)]
        second = [one if inside else plain for one, inside in zip(out, self.in_vmem)]
        return first, second

    def phases(self, inputs, outputs, scratch):
        return exchange_phases(self.axes, self.counts, inputs, outputs, scratch)


PLANE = (0, 1, 0, 0, 0, 0, 0, 0)
TO_LINE = (0, 0, 1, 0, 0, 0, 0, 0)

MERGE = (0, 0, 0, 0, 0, 0, 0, 1)


def round_up(number, step):
    return -(-number // step) * step


class Sizes:
    def __init__(self, seqs, lines):
        self.seqs, self.lines = seqs, lines
        self.chips, self.devices = seqs // 2, seqs * lines
        self.groups = min(HEAD_COUNT, seqs)
        self.copies = seqs // self.groups
        self.heads = HEAD_COUNT // self.groups
        self.width = self.heads * HEAD_SIZE
        self.share = D // self.devices
        self.memory = MH // self.devices
        self.piece = D // seqs
        self.hidden = FF // lines
        self.slab = self.hidden // seqs
        self.gate_at = round_up(3 * self.share, 8)
        self.mem_at = self.gate_at + round_up(max(self.share, 2 * P_SIZE), 8)
        self.rest_at = self.mem_at + round_up(self.heads * self.memory, 8)
        self.weight_rows = round_up(self.rest_at + 8, 16)
        self.grad_mem_at = round_up(4 * self.share, 8)
        self.grad_rest_at = self.grad_mem_at + round_up(self.heads * self.memory, 8)
        self.grad_rows = round_up(self.grad_rest_at + 16, 16)


def gate_choice(sizes, group, turned):
    shape = (LANES, 3 * HEAD_COUNT) if turned else (3 * HEAD_COUNT, LANES)
    lane = lax.broadcasted_iota(jnp.int32, shape, 0 if turned else 1)
    column = lax.broadcasted_iota(jnp.int32, shape, 1 if turned else 0)
    head = lane % 8
    chosen = (lane // 8 == column // HEAD_COUNT) & (head < sizes.heads)
    chosen = chosen & (column % HEAD_COUNT == group * sizes.heads + head)
    return jnp.where(chosen, 1.0, 0.0).astype(bf16)


def first_kernel(
    sizes,
    token_ref,
    qkv_ref,
    gate_ref,
    conv_ref,
    pkey_ref,
    pvalue_ref,
    gain_one_ref,
    gain_two_ref,
    live_ref,
    first_ref,
    second_ref,
    ffn_gate_ref,
    ffn_up_ref,
    ffn_down_ref,
    out_ref,
    cot_ref,
    length_ref,
    bias_ref,
    raw_out,
    gate_out,
    matrix_out,
    mem_out,
    swap_out,
    gain_out,
    taps_out,
    persist_out,
    live_out,
    key_out,
    value_out,
    total_out,
    state_out,
    mixed_got,
    normed_out,
    ffn_out,
    ffn_rest,
    ffn_relayed,
    out_rows,
    out_all,
    cot_all,
    rows_all,
    pack,
    pack_rows,
    ffn_pack,
    ffn_relay,
    got,
    conv_full,
    persist_full,
    mem_full,
    matrix_full,
    ext,
    keys_all,
    values_all,
    live_prev,
    state,
    hidden,
    normed_sem,
    mixed_out,
    mixed_local,
    mixed_send,
    mixed_recv,
    *sems,
):
    seqs, lines, share, width = sizes.seqs, sizes.lines, sizes.share, sizes.width
    seq, line = lax.axis_index("seq"), lax.axis_index("fsdp")
    group = seq // sizes.copies
    axes = (seqs, lines)
    greet_all(axes, ("plane", "line"))
    gather = PlaneGather(seqs, token_ref, rows_all, sems[:7])
    weights = exchange_phases(axes, PLANE, [pack], [got.at[line]], sems[7:10])
    weights_line = LineGather(lines, None, got, sems[10:14], keep=False)
    ffn = exchange_phases(axes, PLANE, [ffn_pack], [ffn_out], sems[14:17])
    outs = exchange_phases(axes, TO_LINE, [out_ref], [out_rows], sems[17:20])
    relay = exchange_phases(axes, PLANE, [ffn_relay], [ffn_relayed.at[line]], sems[20:23])
    relay_line = LineGather(lines, None, ffn_relayed, sems[23:27], keep=False)
    out_gather = PlaneGather(seqs, out_rows, out_all, sems[27:34])
    cot_gather = PlaneGather(seqs, cot_ref, cot_all, sems[34:41])
    piece = sizes.piece
    rest_line = LineGather(lines, ffn_out, ffn_rest, sems[41:45])
    for to in range(seqs):
        ffn_relay[to] = ffn_gate_ref[:, to * sizes.slab : (to + 1) * sizes.slab]
    relay[0]()
    outs[0]()
    relay[2]()
    relay_line.start()

    gate_at, mem_at, rest_at = sizes.gate_at, sizes.mem_at, sizes.rest_at
    pack_rows[...] = jnp.zeros_like(pack_rows)
    pack_rows[gate_at : gate_at + P_SIZE, HEAD_SIZE : HEAD_SIZE + share] = pkey_ref[...].astype(f32)
    pack_rows[gate_at + P_SIZE : gate_at + 2 * P_SIZE, HEAD_SIZE : HEAD_SIZE + share] = pvalue_ref[
        ...
    ].astype(f32)
    pack_rows[rest_at : rest_at + 4, : 3 * share] = conv_ref[...].astype(f32)
    pack_rows[rest_at + 4 : rest_at + 5, :share] = gain_one_ref[...].astype(f32)
    pack_rows[rest_at + 5 : rest_at + 6, :share] = gain_two_ref[...].astype(f32)
    live = live_ref[...].astype(f32)
    pack_rows[rest_at + 6 : rest_at + 7, :] = live[:, :LANES]
    pack_rows[rest_at + 7 : rest_at + 8, :] = live[:, LANES:]
    qkv = qkv_ref[...].astype(f32)
    gate = gate_ref[...]
    for to in range(seqs):
        other = to // sizes.copies
        for part in range(3):
            first = part * D + other * width
            pack_rows[part * share : (part + 1) * share, :width] = qkv[:, first : first + width]
        chosen = dot_nn(gate, gate_choice(sizes, other, False))
        pack_rows[gate_at : gate_at + share, :HEAD_SIZE] = chosen[:, :HEAD_SIZE]
        for head in range(sizes.heads):
            rows = slice(mem_at + head * sizes.memory, mem_at + (head + 1) * sizes.memory)
            member = other * sizes.heads + head
            pack_rows[rows, :HEAD_SIZE] = first_ref[member].astype(f32)
            pack_rows[rows, HEAD_SIZE:] = second_ref[member].astype(f32)
        pack[to] = pack_rows[...].astype(bf16)
    weights[0]()
    gather.start()
    for to in range(seqs):
        columns = slice(to * sizes.slab, (to + 1) * sizes.slab)
        ffn_pack[to, :piece, :] = ffn_up_ref[:, columns]
        turned = jnp.transpose(ffn_down_ref[columns, :].astype(f32))
        ffn_pack[to, piece:, :] = turned.astype(bf16)
    ffn[0]()
    weights[2]()
    weights_line.start()
    gather.step(0)
    gather.step(1)
    weights_line.round(1)
    outs[2]()
    out_gather.start()
    gather.loop(2, gather.step)
    weights_line.rounds(2)
    relay_line.round(1)
    cot_gather.start()
    ffn[2]()
    rest_line.start()

    aligned = share % 16 == 0
    matrix = matrix_out if aligned else matrix_full
    lane = lane_index((share, LANES))
    for i in range(sizes.devices):
        block = got[i % lines, i // lines].astype(f32)
        rows = slice(i * share, (i + 1) * share)
        for part in range(3):
            columns = slice(part * LANES, (part + 1) * LANES)
            matrix[rows, columns] = block[part * share : (part + 1) * share].astype(matrix.dtype)
        chosen = jnp.where(lane < 24, block[gate_at : gate_at + share], 0.0)
        matrix[rows, 3 * LANES :] = chosen.astype(matrix.dtype)
        for head in range(sizes.heads):
            first = mem_at + head * sizes.memory
            mem_full[head, i * sizes.memory : (i + 1) * sizes.memory, :] = block[
                first : first + sizes.memory
            ]
        rest = block[rest_at : rest_at + 8]
        conv_full[0:4, i * 3 * share : (i + 1) * 3 * share] = rest[0:4, : 3 * share]
        gain_out[4:6, i * share : (i + 1) * share] = rest[4:6, :share]
    if not aligned:
        matrix_out[...] = matrix_full[...].astype(bf16)
    for head in range(sizes.heads):
        mem_out[head] = mem_full[head].astype(bf16)
        swap_out[head] = swap_halves(mem_full[head]).astype(bf16)
    taps_out[...] = jnp.zeros_like(taps_out)
    for part in range(3):
        whole = conv_full[:, part * D : (part + 1) * D]
        turned = pltpu.roll(whole, lax.rem(D - group * width, D), 1)
        taps_out[0:4, part * LANES : part * LANES + width] = turned[0:4, :width]
    persist_full[...] = jnp.zeros_like(persist_full)
    for part in range(width // share):
        i = group * (width // share) + part
        block = got[lax.rem(i, lines), i // lines].astype(f32)
        persist_full[:, part * share : (part + 1) * share] = block[
            gate_at : gate_at + 2 * P_SIZE, HEAD_SIZE : HEAD_SIZE + share
        ]
    persist_out[...] = persist_full[...].astype(bf16)
    for s in range(seqs):
        block = got[line, s].astype(f32)
        live_out[s] = jnp.zeros((8, SEG), f32)
        live_out[s, 0:1, :LANES] = block[rest_at + 6 : rest_at + 7]
        live_out[s, 0:1, LANES:] = block[rest_at + 7 : rest_at + 8]

    gain = gain_out[4:5, :]
    gather.finish()

    def normed_copy(q):
        both = pl.ds(2 * q, 2)
        return pltpu.make_async_copy(rows_all.at[both], normed_out.at[both], normed_sem.at[q])

    def work(q, carry):
        both = pl.ds(2 * q, 2)
        rows = rows_all[both].reshape(2 * SEG, D).astype(f32)
        normed = (rows * norm_scale(rows) * gain).astype(bf16)
        projected = dot_nn(normed, matrix_out[...])
        rows_all[both] = normed.reshape(2, SEG, D)
        normed_copy(q).start()
        raw_out[both] = projected[:, : 3 * LANES].astype(bf16).reshape(2, SEG, 3 * LANES)
        gate_out[both] = projected[:, 3 * LANES :].reshape(2, SEG, LANES)
        return carry

    lax.fori_loop(0, sizes.chips, work, 0)

    def mixed_own():
        return pltpu.make_async_copy(mixed_out.at[seq], mixed_got.at[seq], mixed_local.at[0])

    def mixed_copy(to, slot):
        return pltpu.make_async_remote_copy(
            src_ref=mixed_out.at[to],
            dst_ref=mixed_got.at[slot],
            send_sem=mixed_send.at[to],
            recv_sem=mixed_recv.at[slot],
            device_id=(to, line),
            device_id_type=MESH,
        )

    def segment(n, carry):
        @pl.when(n == 1)
        def _():
            relay_line.round(2)

        @pl.when(n == 2)
        def _():
            out_gather.step(0)
            out_gather.step(1)
            cot_gather.step(0)
            cot_gather.step(1)

        @pl.when(n == 3)
        def _():
            rest_line.round(1)

        @pl.when(n == 6)
        def _():
            out_gather.loop(2, out_gather.step)
            cot_gather.loop(2, cot_gather.step)

        forward_step(
            n,
            sizes.heads,
            raw_out.at[n],
            gate_out.at[n],
            live_out.at[pl.ds(n, 1)],
            taps_out,
            mem_out,
            swap_out,
            persist_out,
            length_ref,
            bias_ref,
            mixed_out.at[n],
            key_out.at[n],
            value_out.at[n],
            total_out.at[n],
            state_out.at[pl.ds(n, 1)],
            ext,
            keys_all,
            values_all,
            live_prev,
            state,
            hidden,
        )

        @pl.when(n == seq)
        def _():
            mixed_own().start()

        @pl.when(n != seq)
        def _():
            mixed_copy(n, seq).start()

        return carry

    lax.fori_loop(0, seqs, segment, 0)
    lax.fori_loop(0, sizes.chips, lambda q, carry: (normed_copy(q).wait(), carry)[1], 0)
    out_gather.finish()
    cot_gather.finish()

    def mixed_end(k, carry):
        i = lax.rem(seq + k, seqs)
        mixed_copy(i, i).wait_recv()
        mixed_copy(i, i).wait_send()
        return carry

    mixed_own().wait()
    lax.fori_loop(1, seqs, mixed_end, 0)
    weights_line.finish()
    relay_line.rounds(3)
    rest_line.rounds(2)
    relay_line.finish()
    rest_line.finish()


def first_call(sizes, *operands):
    seqs, lines, heads = sizes.seqs, sizes.lines, sizes.heads
    dma = pltpu.SemaphoreType.DMA
    any_spec, vmem_spec = pl.BlockSpec(memory_space=pl.ANY), pl.BlockSpec(memory_space=pltpu.VMEM)
    smem_spec = pl.BlockSpec(memory_space=pltpu.SMEM)
    shape = jax.ShapeDtypeStruct
    matrix_shape = (D, 4 * LANES)
    return pl.pallas_call(
        partial(first_kernel, sizes),
        out_shape=[
            shape((seqs, SEG, 3 * LANES), bf16),
            shape((seqs, SEG, LANES), f32),
            shape(matrix_shape, bf16),
            shape((heads, MH, LANES), bf16),
            shape((heads, MH, LANES), bf16),
            shape((8, D), f32),
            shape((8, 3 * LANES), f32),
            shape((2 * P_SIZE, LANES), bf16),
            shape((seqs, 8, SEG), f32),
            shape((seqs, SEG, LANES), bf16),
            shape((seqs, SEG, LANES), bf16),
            shape((seqs, SEG, 8), f32),
            shape((seqs, heads, 2, MH, LANES), bf16),
            shape((seqs, SEG, LANES), bf16),
            shape((seqs, SEG, D), bf16),
            shape((seqs, 2 * sizes.piece, sizes.slab), bf16),
            shape((lines, seqs, 2 * sizes.piece, sizes.slab), bf16),
            shape((lines, seqs, sizes.piece, sizes.slab), bf16),
            shape((lines, sizes.share, D), bf16),
            shape((seqs, lines, sizes.share, D), bf16),
            shape((seqs, SEG, D), bf16),
        ],
        in_specs=[any_spec] + [vmem_spec] * 13 + [any_spec] * 2 + [smem_spec] * 2,
        out_specs=[vmem_spec] * 13 + [any_spec] * 8,
        scratch_shapes=[
            pltpu.VMEM((seqs, SEG, D), bf16),
            pltpu.VMEM((seqs, sizes.weight_rows, LANES), bf16),
            pltpu.VMEM((sizes.weight_rows, LANES), f32),
            pltpu.VMEM((seqs, 2 * sizes.piece, sizes.slab), bf16),
            pltpu.VMEM((seqs, sizes.piece, sizes.slab), bf16),
            pltpu.VMEM((lines, seqs, sizes.weight_rows, LANES), bf16),
            pltpu.VMEM((8, 3 * D), f32),
            pltpu.VMEM((2 * P_SIZE, LANES), f32),
            pltpu.VMEM((heads, MH, LANES), f32),
            pltpu.VMEM((8, LANES) if sizes.share % 16 == 0 else matrix_shape, f32),
            pltpu.VMEM((SEG + 8, 3 * LANES), f32),
            pltpu.VMEM((2 * SEG + LANES, LANES), bf16),
            pltpu.VMEM((2 * SEG + LANES, LANES), bf16),
            pltpu.VMEM((8, SEG), f32),
            pltpu.VMEM((heads, 2, MH, LANES), f32),
            pltpu.VMEM((SEG, 2 * SEG + LANES), f32),
            dma((sizes.chips,)),
            pltpu.VMEM((seqs, SEG, LANES), bf16),
            dma((1,)),
            dma((seqs,)),
            dma((seqs,)),
        ]
        + PlaneGather.sems(seqs)
        + [dma((1,)), dma((seqs,)), dma((seqs,))]
        + LineGather.sems(lines)
        + [dma((1,)), dma((seqs,)), dma((seqs,))]
        + [dma((1,)), dma((lines,)), dma((lines,))]
        + [dma((1,)), dma((seqs,)), dma((seqs,))]
        + LineGather.sems(lines)
        + PlaneGather.sems(seqs) * 2
        + LineGather.sems(lines),
        compiler_params=pltpu.CompilerParams(
            collective_id=0, has_side_effects=True, vmem_limit_bytes=VMEM_GRANT
        ),
        name="first",
    )(*operands)


def middle_kernel(
    sizes,
    mixed_ref,
    token_ref,
    cot_own_ref,
    out_ref,
    gain_ref,
    cot_ref,
    gate_weight_ref,
    weight_ref,
    middle_ref,
    grad_middle_ref,
    gain_grad_ref,
    out_grad_ref,
    grad_mixed_ref,
    down_ref,
    grad_ref,
    mixed_got,
    combined,
    rows_ref,
    sum_ref,
    rows_all,
    other,
    pair,
    landed,
    cot_slot,
    down_slot,
    both_matrix,
    down_matrix,
    both_grad,
    down_grad,
    acts,
    blocks,
    block_sem,
    gate_sem,
    pair_send,
    pair_recv,
    back_send,
    back_recv,
    cot_sem,
    down_sem,
    *sems,
):
    seqs, lines, chips = sizes.seqs, sizes.lines, sizes.chips
    hidden_size, slab, piece = sizes.slab * sizes.lines, sizes.slab, sizes.piece
    seq, line = lax.axis_index("seq"), lax.axis_index("fsdp")
    chip, core = seq // 2, lax.rem(seq, 2)
    sibling = (2 * chip + 1 - core, line)

    def loop(first, last, body):
        def step(k, carry):
            body(k)
            return carry

        lax.fori_loop(first, last, step, 0)

    def remote(source, target, send, recv, place):
        return pltpu.make_async_remote_copy(
            src_ref=source,
            dst_ref=target,
            send_sem=send,
            recv_sem=recv,
            device_id=place,
            device_id_type=MESH,
        )

    gather = PlaneGather(seqs, rows_ref, rows_all, sems[:7])

    chip_at = gather.chip_at

    def to_pair(j):
        q, slot = chip_at(j), lax.rem(j, 2)
        return remote(other.at[slot], pair.at[q], pair_send.at[slot], pair_recv.at[q], sibling)

    def back(q, slot):
        place = (2 * q + core, line)
        return remote(pair.at[q], landed.at[slot], back_send.at[q], back_recv.at[slot], place)

    resident = chips <= 4

    def cot_copy(j, slot):
        if resident:
            both = pl.ds(2 * chip_at(j), 2)
            return pltpu.make_async_copy(cot_ref.at[both], cot_slot.at[both], cot_sem.at[j])
        return pltpu.make_async_copy(
            cot_ref.at[pl.ds(2 * chip_at(j), 2)], cot_slot.at[slot], cot_sem.at[slot]
        )

    def down_copy(j):
        slot = j % 2 if isinstance(j, int) else lax.rem(j, 2)
        return pltpu.make_async_copy(
            down_slot.at[slot], down_ref.at[pl.ds(2 * chip_at(j), 2)], down_sem.at[slot]
        )

    axes = (seqs, lines)
    to_segment = pltpu.make_async_copy(mixed_ref, mixed_got, sems[7].at[0])
    to_heads = exchange_phases(axes, PLANE, [mixed_got], [grad_mixed_ref], sems[10:13])
    greet_all(axes, ("plane",))
    to_segment.start()
    if resident:
        for j in range(chips):
            cot_copy(j, 0).start()
    else:
        cot_copy(0, 0).start()
    slots = blocks.shape[0]

    def gate_copy(f):
        target = blocks.at[f % slots, :, pl.ds(0, piece)]
        return pltpu.make_async_copy(gate_weight_ref.at[f], target, gate_sem.at[f % slots])

    def weight_copy(f):
        target = blocks.at[f % slots, :, pl.ds(piece, 2 * piece)]
        return pltpu.make_async_copy(weight_ref.at[f], target, block_sem.at[f % slots])

    def grad_copy(f):
        return pltpu.make_async_copy(blocks.at[f % slots], grad_ref.at[f], block_sem.at[f % slots])

    for f in range(slots):
        gate_copy(f).start()
        weight_copy(f).start()
    for f in range(lines):
        gate_copy(f).wait()
        weight_copy(f).wait()
        columns = slice(f * slab, (f + 1) * slab)
        up_columns = slice(hidden_size + f * slab, hidden_size + (f + 1) * slab)
        for s in range(seqs):
            rows = slice(s * piece, (s + 1) * piece)
            both_matrix[rows, columns] = blocks[f % slots, s, :piece, :]
            both_matrix[rows, up_columns] = blocks[f % slots, s, piece : 2 * piece, :]
            down_matrix[rows, columns] = blocks[f % slots, s, 2 * piece :, :]
        if f + slots < lines:
            gate_copy(f + slots).start()
            weight_copy(f + slots).start()

    width, copies = sizes.width, sizes.copies
    to_segment.wait()
    for group in range(sizes.groups):
        combined[:, group * width : (group + 1) * width] = mixed_got[group * copies, :, :width]
    middle = token_ref[...].astype(f32) + dot_nn(combined[...], out_ref[...])
    middle_ref[...] = middle
    rows_ref[...] = (middle * norm_scale(middle) * gain_ref[5:6, :]).astype(bf16)
    gather.start()

    def forth(j):
        q = chip_at(j)
        gather.step(j)
        cot_copy(j, lax.rem(j, 2)).wait()

        if not resident:

            @pl.when(jnp.logical_and(j > 0, j + 1 < chips))
            def _():
                cot_copy(j + 1, lax.rem(j + 1, 2)).start()

        rows = rows_all[pl.ds(2 * q, 2)].reshape(2 * SEG, D)
        cot = cot_slot[pl.ds(2 * q, 2)] if resident else cot_slot[lax.rem(j, 2)]
        cot = cot.reshape(2 * SEG, D)
        grad_hidden = dot_nn(cot, down_matrix[...])
        ups = dot_nn(rows, both_matrix[...])
        gate_act, up_act = ups[:, :hidden_size], ups[:, hidden_size:]
        sigmoid = jax.nn.sigmoid(gate_act)
        swish = gate_act * sigmoid
        slope = sigmoid * (1.0 + gate_act - swish)
        acts[q, :, :hidden_size] = (grad_hidden * up_act * slope).astype(bf16)
        acts[q, :, hidden_size : 2 * hidden_size] = (grad_hidden * swish).astype(bf16)
        acts[q, :, 2 * hidden_size :] = (swish * up_act).astype(bf16)
        theirs = acts[q, pl.ds(pl.multiple_of((1 - core) * SEG, SEG), SEG), : 2 * hidden_size]
        theirs = dot_nt(theirs, both_matrix[...])

        @pl.when(j >= 2)
        def _():
            to_pair(j - 2).wait_send()

        other[lax.rem(j, 2)] = theirs.astype(bf16)
        to_pair(j).start()
        own = acts[q, pl.ds(pl.multiple_of(core * SEG, SEG), SEG), : 2 * hidden_size]
        own = dot_nt(own, both_matrix[...])
        to_pair(j).wait_recv()
        own = own + pair[q].astype(f32)

        @pl.when(j == 0)
        def _():
            sum_ref[...] = own

        @pl.when(j > 0)
        def _():
            pair[q] = own.astype(bf16)
            back(q, chip).start()

    def weigh(j):
        q = chip_at(j)
        slot = lax.rem(j, 2)

        @pl.when(j > 0)
        def _():
            cot_copy(j, slot).wait()

            @pl.when(j + 1 < chips)
            def _():
                cot_copy(j + 1, lax.rem(j + 1, 2)).start()

        @pl.when(j >= 2)
        def _():
            down_copy(j - 2).wait()

        hidden = acts[q, :, 2 * hidden_size :]
        down_slot[slot] = dot_nt(hidden, down_matrix[...]).astype(bf16).reshape(2, SEG, D)
        down_copy(j).start()
        rows = rows_all[pl.ds(2 * q, 2)].reshape(2 * SEG, D)
        cot = cot_slot[slot].reshape(2 * SEG, D)
        both_new = dot_tn(rows, acts[q, :, : 2 * hidden_size])
        down_new = dot_tn(cot, hidden)

        @pl.when(j == 0)
        def _():
            both_grad[...] = both_new
            down_grad[...] = down_new

        @pl.when(j > 0)
        def _():
            both_grad[...] += both_new
            down_grad[...] += down_new

    def weigh_all():
        rows = rows_all[...].reshape(seqs * SEG, D)
        cot = cot_slot[...].reshape(seqs * SEG, D)
        kept = acts[...].reshape(seqs * SEG, 3 * hidden_size)
        both, hidden = kept[:, : 2 * hidden_size], kept[:, 2 * hidden_size :]
        both_grad[...] = dot_tn(rows, both)
        down_grad[...] = dot_tn(cot, hidden)
        for j in range(chips):
            if j >= 2:
                down_copy(j - 2).wait()
            back_rows = dot_nt(acts[chip_at(j), :, 2 * hidden_size :], down_matrix[...])
            down_slot[j % 2] = back_rows.astype(bf16).reshape(2, SEG, D)
            down_copy(j).start()

    if resident:
        loop(0, chips, forth)
        weigh_all()
    else:
        forth(jnp.int32(0))
        weigh(jnp.int32(0))
        cot_copy(1, 1).start()
        loop(1, chips, forth)
        cot_copy(1, 1).start()
        loop(1, chips, weigh)
    loop(chips - 2, chips, lambda j: down_copy(j).wait())
    gather.finish()
    loop(chips - 2, chips, lambda j: to_pair(j).wait_send())

    def end(j):
        q = chip_at(j)
        back(q, chip).wait_send()
        back(q, q).wait_recv()
        sum_ref[...] += landed[q].astype(f32)

    loop(1, chips, end)

    middle = middle_ref[...]
    scale = norm_scale(middle)
    grad = sum_ref[...]
    gain_grad_ref[...] = jnp.sum(grad * middle * scale, axis=0, keepdims=True)
    grad = cot_own_ref[...].astype(f32) + norm_pull(middle, scale, gain_ref[5:6, :], grad)
    grad_middle_ref[...] = grad
    branch = grad.astype(bf16)
    grad_combined = dot_nt(branch, out_ref[...]).astype(bf16)
    if width < LANES:
        mixed_got[...] = jnp.zeros_like(mixed_got)
    for to in range(seqs):
        first = to // copies * width
        mixed_got[to, :, :width] = grad_combined[:, first : first + width]
    to_heads[0]()
    for f in range(lines):
        if f >= slots:
            grad_copy(f - slots).wait()
        columns = slice(f * slab, (f + 1) * slab)
        up_columns = slice(hidden_size + f * slab, hidden_size + (f + 1) * slab)
        for s in range(seqs):
            rows = slice(s * piece, (s + 1) * piece)
            blocks[f % slots, s, :piece, :] = both_grad[rows, columns].astype(bf16)
            blocks[f % slots, s, piece : 2 * piece, :] = both_grad[rows, up_columns].astype(bf16)
            blocks[f % slots, s, 2 * piece :, :] = down_grad[rows, columns].astype(bf16)
        grad_copy(f).start()
    for f in range(lines - slots, lines):
        grad_copy(f).wait()
    out_grad = dot_tn(combined[...], branch).astype(bf16)
    out_grad_ref[...] = out_grad.reshape(seqs, piece, D)
    to_heads[2]()


def middle_call(sizes, *operands):
    seqs, lines, chips = sizes.seqs, sizes.lines, sizes.chips
    hidden = sizes.slab * lines
    dma = pltpu.SemaphoreType.DMA
    any_spec, vmem_spec = pl.BlockSpec(memory_space=pl.ANY), pl.BlockSpec(memory_space=pltpu.VMEM)
    half = pltpu.VMEM((chips, SEG, D), bf16)
    slots = lines if lines <= 4 else 2
    block_shape = (lines, seqs, 3 * sizes.piece, sizes.slab)
    cot_shape = (seqs, SEG, D) if chips <= 4 else (2, 2, SEG, D)
    shape = jax.ShapeDtypeStruct
    return pl.pallas_call(
        partial(middle_kernel, sizes),
        out_shape=[
            shape((SEG, D), f32),
            shape((SEG, D), f32),
            shape((1, D), f32),
            shape((seqs, sizes.piece, D), bf16),
            shape((seqs, SEG, LANES), bf16),
            shape((seqs, SEG, D), bf16),
            shape(block_shape, bf16),
        ],
        in_specs=[any_spec] + [vmem_spec] * 4 + [any_spec] * 3,
        out_specs=[vmem_spec] * 4 + [any_spec] * 3,
        scratch_shapes=[
            pltpu.VMEM((seqs, SEG, LANES), bf16),
            pltpu.VMEM((SEG, D), bf16),
            pltpu.VMEM((SEG, D), bf16),
            pltpu.VMEM((SEG, D), f32),
            pltpu.VMEM((seqs, SEG, D), bf16),
            pltpu.VMEM((2, SEG, D), bf16),
            half,
            half,
            pltpu.VMEM(cot_shape, bf16),
            pltpu.VMEM((2, 2, SEG, D), bf16),
            pltpu.VMEM((D, 2 * hidden), bf16),
            pltpu.VMEM((D, hidden), bf16),
            pltpu.VMEM((D, 2 * hidden), f32),
            pltpu.VMEM((D, hidden), f32),
            pltpu.VMEM((chips, 2 * SEG, 3 * hidden), bf16),
            pltpu.VMEM((slots,) + block_shape[1:], bf16),
            dma((slots,)),
            dma((slots,)),
        ]
        + [dma((2,)), dma((chips,)), dma((chips,)), dma((chips,))]
        + [dma((max(chips, 2),)), dma((2,))]
        + PlaneGather.sems(seqs)
        + [dma((1,)), dma((seqs,)), dma((seqs,))] * 2,
        compiler_params=pltpu.CompilerParams(
            collective_id=2, has_side_effects=True, vmem_limit_bytes=VMEM_GRANT
        ),
        name="middle",
    )(*operands)


def last_kernel(
    sizes,
    grad_ref,
    normed_ref,
    matrix_ref,
    mem_ref,
    taps_ref,
    persist_ref,
    bias_ref,
    gain_two_ref,
    ffn_ref,
    out_ref,
    token_grad,
    pack_got,
    out_got,
    persist_got,
    ffn_got,
    normed_slot,
    matrix_grad,
    pack,
    pack_rows,
    pack_landed,
    pack_sums,
    out_blocks,
    other,
    pair,
    landed,
    normed_sem,
    pair_send,
    pair_recv,
    back_send,
    back_recv,
    *sems,
):
    seqs, lines, chips = sizes.seqs, sizes.lines, sizes.chips
    share, heads = sizes.share, sizes.heads
    seq, line = lax.axis_index("seq"), lax.axis_index("fsdp")
    chip, core = seq // 2, lax.rem(seq, 2)
    sibling = (2 * chip + 1 - core, line)
    side = math.isqrt(chips)

    def chip_at(k):
        across = lax.rem(lax.rem(chip, side) + lax.rem(k, side), side)
        along = lax.rem(chip // side + k // side, side)
        return along * side + across

    def loop(first, last, body):
        def step(k, carry):
            body(k)
            return carry

        lax.fori_loop(first, last, step, 0)

    def remote(source, target, send, recv, place):
        return pltpu.make_async_remote_copy(
            src_ref=source,
            dst_ref=target,
            send_sem=send,
            recv_sem=recv,
            device_id=place,
            device_id_type=MESH,
        )

    def to_pair(k):
        q, slot = chip_at(lax.rem(k, chips)), lax.rem(k, 2)
        return remote(other.at[slot], pair.at[q], pair_send.at[slot], pair_recv.at[q], sibling)

    def back(q, slot):
        place = (2 * q + core, line)
        return remote(pair.at[q], landed.at[slot], back_send.at[q], back_recv.at[slot], place)

    def normed_copy(q, slot):
        return pltpu.make_async_copy(
            normed_ref.at[pl.ds(2 * q, 2)], normed_slot.at[slot], normed_sem.at[slot]
        )

    axes = (seqs, lines)
    resident = chips <= 4
    all_normed = pltpu.make_async_copy(normed_ref, normed_slot, normed_sem.at[0])
    if resident:
        all_normed.start()
    greet_all(axes, ("plane", "line"))
    ffn = exchange_phases(axes, PLANE, [ffn_ref], [ffn_got], sems[0:3])
    outs = exchange_phases(
        axes, (0, 0, 2, 0, 0, 0, 0, 0), [out_blocks, persist_ref], [out_got, persist_got], sems[3:9]
    )
    grads = exchange_phases(
        axes, MERGE, [pack], [pack_got], [pack_landed, pack_sums, *sems[9:16]]
    )
    ffn[0]()

    def gather_grad(q):
        slot = lax.rem(q, 2)

        @pl.when(q + 1 < chips)
        def _():
            normed_copy(q + 1, lax.rem(q + 1, 2)).start()

        normed_copy(q, slot).wait()
        grad = grad_ref[pl.ds(2 * q, 2)].reshape(2 * SEG, 4 * LANES)
        new = dot_tn(normed_slot[slot].reshape(2 * SEG, D), grad)

        @pl.when(q == 0)
        def _():
            matrix_grad[...] = new

        @pl.when(q > 0)
        def _():
            matrix_grad[...] += new

    if resident:
        all_normed.wait()
        rows = normed_slot[...].reshape(seqs * SEG, D)
        matrix_grad[...] = dot_tn(rows, grad_ref[...].reshape(seqs * SEG, 4 * LANES))
    else:
        normed_copy(0, 0).start()
        loop(0, chips, gather_grad)
    mem_at, rest_at = sizes.grad_mem_at, sizes.grad_rest_at
    pack_rows[...] = jnp.zeros_like(pack_rows)
    for tap in range(4):
        for part in range(3):
            at = rest_at + 3 * tap + part
            pack_rows[at : at + 1, :] = taps_ref[tap : tap + 1, part * LANES : (part + 1) * LANES]
    pack_rows[rest_at + 12 : rest_at + 13, :] = bias_ref[0:1, :]
    for i in range(sizes.devices):
        rows = slice(i * share, (i + 1) * share)
        for part in range(4):
            pack_rows[part * share : (part + 1) * share, :] = matrix_grad[
                rows, part * LANES : (part + 1) * LANES
            ]
        for head in range(heads):
            first = mem_at + head * sizes.memory
            pack_rows[first : first + sizes.memory, :] = mem_ref[
                head, i * sizes.memory : (i + 1) * sizes.memory, :
            ]
        pack_rows[rest_at + 13 : rest_at + 14, :share] = gain_two_ref[0:1, rows]
        pack[i % lines, i // lines] = pack_rows[...].astype(bf16)
    grads[0]()
    for f in range(lines):
        out_blocks[f] = out_ref[f * share : (f + 1) * share, :].astype(bf16)
    outs[0]()

    def spread(k):
        q = chip_at(lax.rem(k, chips))
        grad = grad_ref[pl.ds(2 * q, 2)].reshape(2 * SEG, 4 * LANES)
        if sizes.copies > 1:
            grad = grad * jnp.where(lax.rem(seq, sizes.copies) == 0, 1.0, 0.0).astype(bf16)
        whole = dot_nt(grad, matrix_ref[...])
        first_core, second_core = whole[:SEG], whole[SEG:]

        @pl.when(k >= 3)
        def _():
            to_pair(k - 2).wait_send()

        other[lax.rem(k, 2)] = jnp.where(core == 0, second_core, first_core).astype(bf16)
        to_pair(k).start()
        own = jnp.where(core == 0, first_core, second_core)
        to_pair(k).wait_recv()
        own = own + pair[q].astype(f32)

        @pl.when(k == chips)
        def _():
            token_grad[...] = own

        @pl.when(k < chips)
        def _():
            pair[q] = own.astype(bf16)
            back(q, chip).start()

    loop(1, chips + 1, spread)
    grads[1]()

    def add_back(k):
        q = chip_at(k)
        back(q, q).wait_recv()
        token_grad[...] += landed[q].astype(f32)

    loop(1, chips, add_back)
    ffn[2]()
    outs[2]()
    grads[2]()

    def end(k):
        q = chip_at(k)
        back(q, chip).wait_send()

    loop(1, chips, end)
    loop(chips - 1, chips + 1, lambda k: to_pair(k).wait_send())

def unpack_kernel(
    sizes,
    sum_ref,
    pack_got,
    out_got,
    persist_got,
    ffn_got,
    token_ref,
    middle_ref,
    gain_ref,
    qkv_ref,
    gate_ref,
    own_gain_ref,
    rows_ref,
    down_ref,
    output_ref,
    token_grad,
    qkv_grad,
    gate_grad,
    first_grad,
    second_grad,
    conv_grad,
    pkey_grad,
    pvalue_grad,
    out_grad,
    gain_one_grad,
    gain_two_grad,
    ffn_gate_grad,
    ffn_up_grad,
    ffn_down_grad,
    bias_grad,
    conv_full,
):
    seqs, lines = sizes.seqs, sizes.lines
    share, width, heads = sizes.share, sizes.width, sizes.heads
    seq, line = lax.axis_index("seq"), lax.axis_index("fsdp")
    me = seq * lines + line
    group = seq // sizes.copies
    mem_at, rest_at = sizes.grad_mem_at, sizes.grad_rest_at
    output_ref[...] = (rows_ref[...] + down_ref[...]).astype(bf16)
    rows = token_ref[...].astype(f32)
    scale = norm_scale(rows)
    token_grad[...] = middle_ref[...] + norm_pull(rows, scale, gain_ref[4:5, :], sum_ref[...])

    piece, slab = sizes.piece, sizes.slab
    for s in range(seqs):
        columns = slice(s * slab, (s + 1) * slab)
        ffn_gate_grad[:, columns] = ffn_got[s, :piece, :].astype(f32)
        ffn_up_grad[:, columns] = ffn_got[s, piece : 2 * piece, :].astype(f32)
        ffn_down_grad[columns, :] = jnp.transpose(ffn_got[s, 2 * piece :, :].astype(f32))
    out_sum = out_got[0].astype(f32)
    persist_sum = persist_got[0]
    for f in range(1, lines):
        out_sum = out_sum + out_got[f].astype(f32)
        persist_sum = persist_sum + persist_got[f]
    out_grad[...] = out_sum
    inside = lax.rem(LANES - (me * share - group * width), LANES)
    persist_sum = pltpu.roll(persist_sum, inside, 1)[:, :share]
    pkey_grad[...] = persist_sum[:P_SIZE]
    pvalue_grad[...] = persist_sum[P_SIZE:]

    gates = jnp.zeros((share, 3 * HEAD_COUNT), f32)
    bias = jnp.zeros((8, 3 * HEAD_COUNT), f32)
    gain_two = jnp.zeros((1, share), f32)
    conv_full[...] = jnp.zeros_like(conv_full)
    for s in range(seqs):
        block = pack_got[s].astype(f32)
        gain_two = gain_two + block[rest_at + 13 : rest_at + 14, :share]
        if s % sizes.copies:
            continue
        other_group = s // sizes.copies
        for part in range(3):
            first = part * D + other_group * width
            qkv_grad[:, first : first + width] = block[
                part * share : (part + 1) * share, :width
            ]
            for tap in range(4):
                at = rest_at + 3 * tap + part
                conv_full[tap : tap + 1, first : first + width] = block[at : at + 1, :width]
        choice = gate_choice(sizes, other_group, True)
        gates = gates + dot_nn(block[3 * share : 4 * share].astype(bf16), choice)
        rest = block[rest_at + 8 : rest_at + 16].astype(bf16)
        bias = bias + dot_nn(rest, choice)
        for head in range(heads):
            first = mem_at + head * sizes.memory
            member = other_group * heads + head
            rows = block[first : first + 8]
            second_grad[member] = rows[: sizes.memory, HEAD_SIZE:]
            first_grad[member] = rows[: sizes.memory, :HEAD_SIZE]
    gate_grad[...] = gates
    bias_grad[0:1, :] = 3.0 * bias[4:5, :HEAD_COUNT]
    bias_grad[1:2, :] = bias[4:5, HEAD_COUNT : 2 * HEAD_COUNT]
    bias_grad[2:3, :] = bias[4:5, 2 * HEAD_COUNT :]
    gain_two_grad[...] = gain_two
    along = jnp.sum(qkv_grad[...] * qkv_ref[...].astype(f32), axis=1, keepdims=True)
    along = along + jnp.sum(gates * gate_ref[...].astype(f32), axis=1, keepdims=True)
    gain_one_grad[...] = jnp.transpose(along)[0:1] / own_gain_ref[...].astype(f32)
    turned = pltpu.roll(conv_full[...], lax.rem(3 * D - me * 3 * share, 3 * D), 1)
    conv_grad[...] = turned[:4, : 3 * share]


def last_call(sizes, *operands):
    seqs, lines, chips, share = sizes.seqs, sizes.lines, sizes.chips, sizes.share
    dma = pltpu.SemaphoreType.DMA
    any_spec, vmem_spec = pl.BlockSpec(memory_space=pl.ANY), pl.BlockSpec(memory_space=pltpu.VMEM)
    shape = jax.ShapeDtypeStruct
    half = pltpu.VMEM((chips, SEG, D), bf16)
    in_specs = [vmem_spec] * len(operands)
    in_specs[1] = any_spec
    in_specs[8] = any_spec
    pack_shape = (lines, seqs, sizes.grad_rows, LANES)
    return pl.pallas_call(
        partial(last_kernel, sizes),
        out_shape=[
            shape((SEG, D), f32),
            shape(pack_shape[1:], bf16),
            shape((lines, share, D), bf16),
            shape((lines, 2 * P_SIZE, LANES), f32),
            shape((seqs, 3 * sizes.piece, sizes.slab), bf16),
        ],
        in_specs=in_specs,
        out_specs=[vmem_spec] + [any_spec] * 4,
        scratch_shapes=[
            pltpu.VMEM((seqs, SEG, D) if chips <= 4 else (2, 2, SEG, D), bf16),
            pltpu.VMEM((D, 4 * LANES), f32),
            pltpu.VMEM(pack_shape, bf16),
            pltpu.VMEM(pack_shape[2:], f32),
            pltpu.VMEM(pack_shape, bf16),
            pltpu.VMEM(pack_shape[1:], bf16),
            pltpu.VMEM((lines, share, D), bf16),
            pltpu.VMEM((2, SEG, D), bf16),
            half,
            half,
            dma((2,)),
        ]
        + [dma((2,)), dma((chips,)), dma((chips,)), dma((chips,))]
        + [dma((1,)), dma((seqs,)), dma((seqs,))]
        + [dma((1,)), dma((lines,)), dma((lines,))] * 2
        + [dma((1,)), dma((seqs,)), dma((seqs,))]
        + LineSum.sems(lines),
        compiler_params=pltpu.CompilerParams(
            collective_id=5, has_side_effects=True, vmem_limit_bytes=VMEM_GRANT
        ),
        name="last",
    )(*operands)


def unpack_call(sizes, *operands):
    share, memory = sizes.share, sizes.memory
    vmem_spec = pl.BlockSpec(memory_space=pltpu.VMEM)
    shape = jax.ShapeDtypeStruct
    return pl.pallas_call(
        partial(unpack_kernel, sizes),
        out_shape=[
            shape((SEG, D), bf16),
            shape((SEG, D), f32),
            shape((share, 3 * D), f32),
            shape((share, 3 * HEAD_COUNT), f32),
            shape((HEAD_COUNT, memory, HEAD_SIZE), f32),
            shape((HEAD_COUNT, memory, HEAD_SIZE), f32),
            shape((4, 3 * share), f32),
            shape((P_SIZE, share), f32),
            shape((P_SIZE, share), f32),
            shape((share, D), f32),
            shape((1, share), f32),
            shape((1, share), f32),
            shape((sizes.piece, sizes.hidden), f32),
            shape((sizes.piece, sizes.hidden), f32),
            shape((sizes.hidden, sizes.piece), f32),
            shape((3, HEAD_COUNT), f32),
        ],
        in_specs=[vmem_spec] * len(operands),
        out_specs=[vmem_spec] * 16,
        scratch_shapes=[pltpu.VMEM((8, 3 * D), f32)],
        compiler_params=pltpu.CompilerParams(vmem_limit_bytes=VMEM_GRANT),
        name="unpack",
    )(*operands)


def norm_scale(values):
    return lax.rsqrt(jnp.mean(values * values, axis=-1, keepdims=True) + NORM_EPS)


def norm_pull(values, scale, gain, grad):
    inner = jnp.mean(grad * gain * values, axis=-1, keepdims=True)
    return scale * (grad * gain - values * (scale * scale) * inner)


def on_device(
    tokens,
    norm1_gain,
    qkv_weight,
    gate_weight,
    conv_weight,
    memory_w1,
    memory_w2,
    persistent_keys,
    persistent_values,
    out_weight,
    norm2_gain,
    ffn_gate,
    ffn_up,
    ffn_down,
    gate_bias,
    doc_lengths,
    live_mask,
    cotangent,
):
    sizes = Sizes(lax.axis_size("seq"), lax.axis_size("fsdp"))
    seqs, heads = sizes.seqs, sizes.heads
    length = seqs * SEG
    (
        raw,
        gates,
        matrix,
        memory_both,
        memory_turned,
        gains,
        taps,
        persistent,
        live,
        keys,
        values,
        totals,
        states,
        mixed,
        normed,
        _,
        ffn_rest,
        ffn_gates,
        _,
        out_matrix,
        cot_rows,
    ) = first_call(
        sizes,
        tokens[0],
        qkv_weight,
        gate_weight,
        conv_weight,
        persistent_keys,
        persistent_values,
        norm1_gain[None],
        norm2_gain[None],
        live_mask,
        memory_w1.transpose(0, 2, 1),
        memory_w2,
        ffn_gate,
        ffn_up,
        ffn_down,
        out_weight,
        cotangent[0],
        doc_lengths,
        gate_bias,
    )
    constants = (taps, memory_both, memory_turned, persistent, doc_lengths, gate_bias)
    middle, grad_middle, grad_gain_two, grad_out, grad_mixed, down_part, ffn_grads = middle_call(
        sizes,
        mixed,
        tokens[0],
        cotangent[0],
        out_matrix.reshape(D, D),
        gains,
        cot_rows,
        ffn_gates,
        ffn_rest,
    )
    ffn_grads = lax.psum_scatter(ffn_grads, "fsdp")
    plan = Exchange(scatters=[down_part, grad_out])
    grad_all, grad_memory, grad_taps, grad_persistent, grad_bias, down_sum, grad_out = mix_backward(
        7,
        plan,
        heads,
        raw.reshape(length, 3 * LANES),
        gates.reshape(length, LANES),
        live,
        keys.reshape(length, LANES),
        values.reshape(length, LANES),
        totals.reshape(length, 8),
        states,
        grad_mixed.reshape(length, LANES),
        *constants,
    )
    token_sum, pack_got, out_got, persist_got, ffn_got = last_call(
        sizes,
        grad_all.reshape(seqs, SEG, 4 * LANES),
        normed,
        matrix,
        grad_memory,
        grad_taps,
        grad_persistent,
        grad_bias,
        grad_gain_two,
        ffn_grads,
        grad_out,
    )
    grads = unpack_call(
        sizes,
        token_sum,
        pack_got,
        out_got,
        persist_got,
        ffn_got,
        tokens[0],
        grad_middle,
        gains,
        qkv_weight,
        gate_weight,
        norm1_gain[None],
        middle,
        down_sum,
    )
    (
        output,
        input_grad,
        grad_qkv,
        grad_gate,
        grad_first,
        grad_second,
        grad_conv,
        grad_pkeys,
        grad_pvalues,
        grad_out,
        grad_gain_one,
        grad_gain_two,
        grad_ffn_gate,
        grad_ffn_up,
        grad_ffn_down,
        grad_bias,
    ) = grads
    return (
        output[None],
        input_grad[None],
        grad_gain_one[0],
        grad_qkv,
        grad_gate,
        grad_conv,
        grad_first.transpose(0, 2, 1),
        grad_second,
        grad_pkeys,
        grad_pvalues,
        grad_out,
        grad_gain_two[0],
        grad_ffn_gate,
        grad_ffn_up,
        grad_ffn_down,
        grad_bias,
    )


def solution(mesh):
    return jax.shard_map(
        on_device,
        mesh=mesh,
        in_specs=(
            P("fsdp", "seq", None),
            P(("seq", "fsdp")),
            P(("seq", "fsdp"), None),
            P(("seq", "fsdp"), None),
            P(None, ("seq", "fsdp")),
            P(None, None, ("seq", "fsdp")),
            P(None, ("seq", "fsdp"), None),
            P(None, ("seq", "fsdp")),
            P(None, ("seq", "fsdp")),
            P(("seq", "fsdp"), None),
            P(("seq", "fsdp")),
            P("seq", "fsdp"),
            P("seq", "fsdp"),
            P("fsdp", "seq"),
            P(),
            P("fsdp", None),
            P("fsdp", "seq"),
            P("fsdp", "seq", None),
        ),
        out_specs=(
            P("fsdp", "seq", None),
            P("fsdp", "seq", None),
            P(("seq", "fsdp")),
            P(("seq", "fsdp"), None),
            P(("seq", "fsdp"), None),
            P(None, ("seq", "fsdp")),
            P(None, None, ("seq", "fsdp")),
            P(None, ("seq", "fsdp"), None),
            P(None, ("seq", "fsdp")),
            P(None, ("seq", "fsdp")),
            P(("seq", "fsdp"), None),
            P(("seq", "fsdp")),
            P("seq", "fsdp"),
            P("seq", "fsdp"),
            P("fsdp", "seq"),
            P(),
        ),
        check_vma=False,
    )
```
